32 devices in a mesh: fsdp: 4 (over x, core), seq: 8 (over z, y).
Axes of the slice: x: 2, y: 2, z: 4, core: 2. Of those that a mesh axis runs over, the one named last changes fastest.
Arguments:
- inputs: bfloat16 [8192, 768], P(('fsdp', 'seq')), may hold values from -6 to 6
- cotangent: bfloat16 [8192, 768], P(('fsdp', 'seq')), may hold values from -6 to 6
- span_order: int32 [4, 8], P('fsdp'), may hold values from 0 to 7, each once within a row
- query_weight: float32 [768, 768], P(('fsdp', 'seq')), may hold values from -0.3125 to 0.3125
- keyval_weight: float32 [768, 128], P(('fsdp', 'seq')), may hold values from -0.21875 to 0.21875
- output_weight: float32 [768, 768], P(('fsdp', 'seq')), may hold values from -1.75 to 1.75
- up_weight: float32 [768, 3072], P(('fsdp', 'seq')), may hold values from -0.21875 to 0.21875
- down_weight: float32 [3072, 768], P(('fsdp', 'seq')), may hold values from -0.109375 to 0.109375
- vectors: float32 [11, 768], P(None, ('fsdp', 'seq')), may hold values from -0.3 to 2.3, as said below
- kv_bias: float32 [128], P('seq'), may hold values from -1.8 to 1.8
- first_query: float32 [768, 768], P(('fsdp', 'seq')), may hold values from -0.00024414062 to 0.00024414062
- first_keyval: float32 [768, 128], P(('fsdp', 'seq')), may hold values from -0.00024414062 to 0.00024414062
- first_output: float32 [768, 768], P(('fsdp', 'seq')), may hold values from -7.6293945e-05 to 7.6293945e-05
- first_up: float32 [768, 3072], P(('fsdp', 'seq')), may hold values from -7.6293945e-05 to 7.6293945e-05
- first_down: float32 [3072, 768], P(('fsdp', 'seq')), may hold values from -0.00024414062 to 0.00024414062
- first_vectors: float32 [11, 768], P(None, ('fsdp', 'seq')), may hold values from -0.0008544922 to 0.0008544922
- first_kv_bias: float32 [128], P('seq'), may hold values from -0.0008544922 to 0.0008544922
- second_query: float32 [768, 768], P(('fsdp', 'seq')), may hold values from 8.3262286e-11 to 1.3321966e-09
- second_keyval: float32 [768, 128], P(('fsdp', 'seq')), may hold values from 8.3262286e-11 to 1.3321966e-09
- second_output: float32 [768, 768], P(('fsdp', 'seq')), may hold values from 9.991474e-12 to 1.4987211e-10
- second_up: float32 [768, 3072], P(('fsdp', 'seq')), may hold values from 9.991474e-12 to 1.4987211e-10
- second_down: float32 [3072, 768], P(('fsdp', 'seq')), may hold values from 8.3262286e-11 to 1.3321966e-09
- second_vectors: float32 [11, 768], P(None, ('fsdp', 'seq')), may hold values from 7.493605e-10 to 1.1989768e-08
- second_kv_bias: float32 [128], P('seq'), may hold values from 7.493605e-10 to 1.1989768e-08
Outputs:
- block_output: bfloat16 [8192, 768], P(('fsdp', 'seq'))
- input_grad: float32 [8192, 768], P(('fsdp', 'seq'))
- grad_norm: float32 [], replicated
- new_query_weight: float32 [768, 768], P(('fsdp', 'seq'))
- new_keyval_weight: float32 [768, 128], P(('fsdp', 'seq'))
- new_output_weight: float32 [768, 768], P(('fsdp', 'seq'))
- new_up_weight: float32 [768, 3072], P(('fsdp', 'seq'))
- new_down_weight: float32 [3072, 768], P(('fsdp', 'seq'))
- new_vectors: float32 [11, 768], P(None, ('fsdp', 'seq'))
- new_kv_bias: float32 [128], P('seq')
- next_first_query: float32 [768, 768], P(('fsdp', 'seq'))
- next_first_keyval: float32 [768, 128], P(('fsdp', 'seq'))
- next_first_output: float32 [768, 768], P(('fsdp', 'seq'))
- next_first_up: float32 [768, 3072], P(('fsdp', 'seq'))
- next_first_down: float32 [3072, 768], P(('fsdp', 'seq'))
- next_first_vectors: float32 [11, 768], P(None, ('fsdp', 'seq'))
- next_first_kv_bias: float32 [128], P('seq')
- next_second_query: float32 [768, 768], P(('fsdp', 'seq'))
- next_second_keyval: float32 [768, 128], P(('fsdp', 'seq'))
- next_second_output: float32 [768, 768], P(('fsdp', 'seq'))
- next_second_up: float32 [768, 3072], P(('fsdp', 'seq'))
- next_second_down: float32 [3072, 768], P(('fsdp', 'seq'))
- next_second_vectors: float32 [11, 768], P(None, ('fsdp', 'seq'))
- next_second_kv_bias: float32 [128], P('seq')
- residual_bias_grads: float32 [2, 768], P(None, ('fsdp', 'seq'))
The draws below stay inside these ranges and needn't reach their ends.
Inputs may be any that keep to these rules, and one draw needn't show every extreme that they name: `span_order`: each row holds every block index of one sequence exactly once. `vectors`: rows 0 and 2 are positive gains; the other rows are biases.
All inputs are finite; a program needn't handle non-finite values.
Results may differ from the reference program's by a relative error of at most 0.018.
The reference program's roundings to bfloat16 on the way count: a program that leaves them out, or rounds other values in their place, can miss the bound.
Values may be sent and summed in bfloat16 or wider, within the bound.
A program may use at most 128 MiB of HBM per device.

```python
import math
import jax
import jax.numpy as jnp
from jax import lax

D = 768
HQ = 12
HD = 64
ROT_DIMS = 16
FF = 3072
TOK_DEV = 256
KEY_BLOCK = 512
STEP = 10
LENGTH = 2048
SEQS = 4
TOKENS = 8192
PARAMS = 6005120
N_SEQ = 8


def draw_vectors(key, part):
    key = jax.random.fold_in(key, 7)
    noise_key, bias_key = jax.random.split(key, 2)
    across = jnp.arange(D, dtype=jnp.float32) / (D - 1)
    ramp = 0.6 + 1.2 * across
    noise = jax.random.uniform(noise_key, (2, D), jnp.float32, 0.8, 1.2)
    biases = jnp.clip(0.1 * jax.random.normal(bias_key, (9, D), jnp.float32), -0.3, 0.3)
    gains = ramp[None, :] * noise
    return jnp.concatenate([gains[0:1], biases[0:1], gains[1:2], biases[1:9]], 0)


def levels(stream_key, dims, shards, low, high):
    loudness, own = 1.0, jax.random.fold_in(stream_key, 6)
    for dim, blocks in shards:
        steps = jnp.exp(jax.random.uniform(jax.random.fold_in(own, dim), (blocks,), jnp.float32, low / len(shards), high / len(shards)))
        loudness = loudness * jnp.repeat(steps, dims[dim] // blocks).reshape([-1 if axis == dim else 1 for axis in range(len(dims))])
    return loudness


def scatter_about(key, extent, deviation, reach, pieces=(), kind=jnp.bfloat16):
    loudness = levels(key, extent, pieces, -0.22, 0.18) if pieces else 1.0
    result = jax.random.normal(key, extent, jnp.float32) * deviation * loudness
    return jnp.minimum(jnp.maximum(result, -reach), reach).astype(kind)


def setup_inputs(seed: int = 0) -> dict:
    arg_keys = jax.random.split(jax.random.key(seed), 25)
    return {
        "inputs": scatter_about(arg_keys[0], (TOKENS, D), 1.0, 6.0, ((0, 32),)),
        "cotangent": scatter_about(arg_keys[1], (TOKENS, D), 1.0, 6.0, ((0, 32),)),
        "span_order": jax.vmap(lambda own: jax.random.permutation(own, N_SEQ))(jax.random.split(arg_keys[2], SEQS)).reshape((SEQS, N_SEQ)).astype(jnp.int32),
        "query_weight": scatter_about(arg_keys[3], (D, HQ * HD), (D // 2) ** -0.5, 0.3125, ((0, 32),), jnp.float32),
        "keyval_weight": scatter_about(arg_keys[4], (D, 2 * HD), D ** -0.5, 0.21875, ((0, 32),), jnp.float32),
        "output_weight": scatter_about(arg_keys[5], (HQ * HD, D), (HQ * HD // 64) ** -0.5, 1.75, ((0, 32),), jnp.float32),
        "up_weight": scatter_about(arg_keys[6], (D, FF), D ** -0.5, 0.21875, ((0, 32),), jnp.float32),
        "down_weight": scatter_about(arg_keys[7], (FF, D), FF ** -0.5, 0.109375, ((0, 32),), jnp.float32),
        "vectors": draw_vectors(jax.random.fold_in(arg_keys[24], 71), 0),
        "kv_bias": scatter_about(arg_keys[9], (2 * HD,), 0.3, 1.8, ((0, 8),), jnp.float32),
        "first_query": scatter_about(arg_keys[10], (D, HQ * HD), (0.11 * PARAMS ** -0.5), 0.00024414062, ((0, 32),), jnp.float32),
        "first_keyval": scatter_about(arg_keys[11], (D, 2 * HD), (0.11 * PARAMS ** -0.5), 0.00024414062, ((0, 32),), jnp.float32),
        "first_output": scatter_about(arg_keys[12], (HQ * HD, D), (0.033 * PARAMS ** -0.5), 7.62939453125e-05, ((0, 32),), jnp.float32),
        "first_up": scatter_about(arg_keys[13], (D, FF), (0.033 * PARAMS ** -0.5), 7.62939453125e-05, ((0, 32),), jnp.float32),
        "first_down": scatter_about(arg_keys[14], (FF, D), (0.11 * PARAMS ** -0.5), 0.00024414062, ((0, 32),), jnp.float32),
        "first_vectors": scatter_about(arg_keys[15], (11, D), (0.33 * PARAMS ** -0.5), 0.0008544922, ((1, 32),), jnp.float32),
        "first_kv_bias": scatter_about(arg_keys[16], (2 * HD,), (0.33 * PARAMS ** -0.5), 0.0008544922, ((0, 8),), jnp.float32),
        "second_query": jnp.clip(jnp.exp(math.log(1.3321965752766118e-09) - 2.7725887 * jax.random.uniform(arg_keys[17], (D, HQ * HD), jnp.float32) ** levels(arg_keys[17], (D, HQ * HD), ((0, 32),), -0.2, 0.2)), 8.326228595478824e-11, 1.3321965752766118e-09),
        "second_keyval": jnp.clip(jnp.exp(math.log(1.3321965752766118e-09) - 2.7725887 * jax.random.uniform(arg_keys[18], (D, 2 * HD), jnp.float32) ** levels(arg_keys[18], (D, 2 * HD), ((0, 32),), -0.2, 0.2)), 8.326228595478824e-11, 1.3321965752766118e-09),
        "second_output": jnp.clip(jnp.exp(math.log(1.4987211471861883e-10) - 2.7080503 * jax.random.uniform(arg_keys[19], (HQ * HD, D), jnp.float32) ** levels(arg_keys[19], (HQ * HD, D), ((0, 32),), -0.2, 0.2)), 9.991473794157546e-12, 1.4987211471861883e-10),
        "second_up": jnp.clip(jnp.exp(math.log(1.4987211471861883e-10) - 2.7080503 * jax.random.uniform(arg_keys[20], (D, FF), jnp.float32) ** levels(arg_keys[20], (D, FF), ((0, 32),), -0.2, 0.2)), 9.991473794157546e-12, 1.4987211471861883e-10),
        "second_down": jnp.clip(jnp.exp(math.log(1.3321965752766118e-09) - 2.7725887 * jax.random.uniform(arg_keys[21], (FF, D), jnp.float32) ** levels(arg_keys[21], (FF, D), ((0, 32),), -0.2, 0.2)), 8.326228595478824e-11, 1.3321965752766118e-09),
        "second_vectors": jnp.clip(jnp.exp(math.log(1.1989768289311087e-08) - 2.7725887 * jax.random.uniform(arg_keys[22], (11, D), jnp.float32) ** levels(arg_keys[22], (11, D), ((1, 32),), -0.2, 0.2)), 7.493605180819429e-10, 1.1989768289311087e-08),
        "second_kv_bias": jnp.clip(jnp.exp(math.log(1.1989768289311087e-08) - 2.7725887 * jax.random.uniform(arg_keys[23], (2 * HD,), jnp.float32) ** levels(arg_keys[23], (2 * HD,), ((0, 8),), -0.2, 0.2)), 7.493605180819429e-10, 1.1989768289311087e-08),
    }


NORM_EPS = 1e-05
MASKED = -1e+30
CLIP_NORM = 1.0
BETA_ONE = 0.9
BETA_TWO = 0.999
ADAM_EPS = 1e-08
MATRIX_DECAY = 0.1
MATRIX_RATE = 0.1
VECTOR_RATE = 0.3
PRECISE = lax.Precision.HIGHEST

@jax.custom_vjp
def low(v):
    return lax.optimization_barrier(v.astype(jnp.bfloat16)).astype(jnp.float32)

@jax.custom_vjp
def low_back(v):
    return v

def low_keep(v):
    return (low(v), None)

def low_pass(kept, grad):
    return (grad,)

def back_keep(v):
    return (v, None)

def back_low(kept, grad):
    return (low(grad),)
low.defvjp(low_keep, low_pass)
low_back.defvjp(back_keep, back_low)

def layer_norm(tensor, gain_row, shift_row):
    centre = tensor - lax.optimization_barrier(jnp.mean(tensor, -1, keepdims=True))
    spread = lax.optimization_barrier(jnp.mean(centre * centre, -1, keepdims=True))
    return centre * lax.rsqrt(spread + NORM_EPS) * gain_row + shift_row

def rotary_tables(places):
    half_steps = jnp.arange(ROT_DIMS // 2, dtype=jnp.float32)
    inverse = jnp.exp(half_steps * (-2.0 * math.log(10000.0) / ROT_DIMS))
    angles = places.astype(jnp.float32)[:, None] * (0.25 * inverse)[None, :]
    angles = jnp.concatenate([angles, angles], 1)
    return (jnp.cos(angles), jnp.sin(angles))

def rotate(tensor, cosine, sine_table):
    rotary_part = tensor[..., :ROT_DIMS]
    lower_half = rotary_part[..., :ROT_DIMS // 2]
    upper_half = rotary_part[..., ROT_DIMS // 2:]
    turned = jnp.concatenate([-upper_half, lower_half], -1)
    return jnp.concatenate([rotary_part * cosine + turned * sine_table, tensor[..., ROT_DIMS:]], -1)

def adamw(master, clipped, first_old, second_old, step_rate, decay_rate):
    first_new = BETA_ONE * first_old + (1.0 - BETA_ONE) * clipped
    second_new = BETA_TWO * second_old + (1.0 - BETA_TWO) * clipped * clipped
    ascent = first_new / (1.0 - BETA_ONE ** STEP) / (jnp.sqrt(second_new / (1.0 - BETA_TWO ** STEP)) + ADAM_EPS)
    return (master - step_rate * (ascent + decay_rate * master), first_new, second_new)

def block_forward(hidden, places, query_weight, keyval_weight, output_weight, up_weight, down_weight, vectors, kv_bias):
    query_low = low(query_weight)
    keyval_low = low(keyval_weight)
    output_low = low(output_weight)
    up_low = low(up_weight)
    down_low = low(down_weight)
    gains = low(vectors)
    kv_shift = low(kv_bias)
    up_bias = gains[7:].reshape(FF)
    score_scale = HD ** (-0.5)

    def one_sequence(sequence_pair):
        seq_rows, seq_places = sequence_pair
        normed_one = low(layer_norm(seq_rows, gains[0], gains[1]))
        queries = low_back(jnp.dot(normed_one, query_low, precision=PRECISE) + gains[4])
        keyvals = low_back(jnp.dot(normed_one, keyval_low, precision=PRECISE) + kv_shift)
        cosine, sine_table = rotary_tables(seq_places)
        turned_queries = low(rotate(queries.reshape(LENGTH, HQ, HD), cosine[:, None, :], sine_table[:, None, :]))
        key_rows = low(rotate(keyvals[:, :HD], cosine, sine_table))
        value_rows = low(keyvals[:, HD:])

        def attend(query_pair):
            query_block, query_places = query_pair
            scores = low_back(jnp.einsum('qhd,kd->qhk', query_block, key_rows, precision=PRECISE) * score_scale)
            allowed = seq_places[None, None, :] <= query_places[:, None, None]
            probs = low(jax.nn.softmax(jnp.where(allowed, scores, MASKED), -1))
            return jnp.einsum('qhk,kd->qhd', probs, value_rows, precision=PRECISE)
        mixed = lax.map(jax.checkpoint(attend), (turned_queries.reshape(LENGTH // KEY_BLOCK, KEY_BLOCK, HQ, HD), seq_places.reshape(LENGTH // KEY_BLOCK, KEY_BLOCK)))
        mixed = low_back(low(mixed.reshape(LENGTH, D)))
        attention_out = jnp.dot(mixed, output_low, precision=PRECISE) + gains[5]
        normed_two = low(layer_norm(seq_rows, gains[2], gains[3]))
        lifted = low_back(jnp.dot(normed_two, up_low, precision=PRECISE) + up_bias)
        active = low(jax.nn.gelu(lifted, approximate=False))
        return seq_rows + attention_out + jnp.dot(active, down_low, precision=PRECISE) + gains[6]
    return lax.map(jax.checkpoint(one_sequence), (hidden, places))

def reference(inputs, cotangent, span_order, query_weight, keyval_weight, output_weight, up_weight, down_weight, vectors, kv_bias, first_query, first_keyval, first_output, first_up, first_down, first_vectors, first_kv_bias, second_query, second_keyval, second_output, second_up, second_down, second_vectors, second_kv_bias):
    token_index = jnp.arange(LENGTH, dtype=jnp.int32)
    places = span_order[:, token_index // TOK_DEV] * TOK_DEV + (token_index % TOK_DEV)[None, :]
    hidden = inputs.astype(jnp.float32).reshape(SEQS, LENGTH, D)
    masters = (query_weight, keyval_weight, output_weight, up_weight, down_weight, vectors, kv_bias)

    def forward_run(states, *params):
        return block_forward(states, places, *params)
    output, pullback = jax.vjp(forward_run, hidden, *masters)
    gradients = pullback(cotangent.astype(jnp.float32).reshape(SEQS, LENGTH, D))
    weight_grads = gradients[1:]
    squares = sum((jnp.sum(gradient * gradient) for gradient in weight_grads))
    grad_norm = jnp.sqrt(squares)
    factor = jnp.minimum(1.0, CLIP_NORM / (grad_norm + 1e-06))
    firsts = (first_query, first_keyval, first_output, first_up, first_down, first_vectors, first_kv_bias)
    seconds = (second_query, second_keyval, second_output, second_up, second_down, second_vectors, second_kv_bias)
    step_rates = (MATRIX_RATE,) * 5 + (VECTOR_RATE, VECTOR_RATE)
    decays = (MATRIX_DECAY,) * 5 + (0.0, 0.0)
    updated = [adamw(master, gradient * factor, first_old, second_old, step_rate, decay_rate) for master, gradient, first_old, second_old, step_rate, decay_rate in zip(masters, weight_grads, firsts, seconds, step_rates, decays)]
    residual_bias_grads = (weight_grads[5] * factor)[5:7]
    return (output.reshape(TOKENS, D).astype(jnp.bfloat16), gradients[0].reshape(TOKENS, D), grad_norm, updated[0][0], updated[1][0], updated[2][0], updated[3][0], updated[4][0], updated[5][0], updated[6][0], updated[0][1], updated[1][1], updated[2][1], updated[3][1], updated[4][1], updated[5][1], updated[6][1], updated[0][2], updated[1][2], updated[2][2], updated[3][2], updated[4][2], updated[5][2], updated[6][2], residual_bias_grads)
```

```python
import math

import jax
import jax.numpy as jnp
from jax import lax
from jax.experimental import pallas as pl
from jax.experimental.pallas import tpu as pltpu
from jax.sharding import PartitionSpec as P

D = 768
HQ = 12
HD = 64
ROT_DIMS = 16
FF = 3072
KEY_BLOCK = 512
STEP = 10
F32 = jnp.float32
BF16 = jnp.bfloat16


NORM_EPS = 1e-05
MASKED = -1e30
CLIP_NORM = 1.0
BETA_ONE = 0.9
BETA_TWO = 0.999
ADAM_EPS = 1e-08
MATRIX_DECAY = 0.1
MATRIX_RATE = 0.1
VECTOR_RATE = 0.3


def layer_norm(tensor, gain_row, shift_row):
    centre = tensor - jnp.mean(tensor, -1, keepdims=True)
    spread = jnp.mean(centre * centre, -1, keepdims=True)
    return centre * lax.rsqrt(spread + NORM_EPS) * gain_row + shift_row


def rotary_tables(places):
    half_steps = jnp.arange(ROT_DIMS // 2, dtype=jnp.float32)
    inverse = jnp.exp(half_steps * (-2.0 * math.log(10000.0) / ROT_DIMS))
    angles = places.astype(jnp.float32)[:, None] * (0.25 * inverse)[None, :]
    angles = jnp.concatenate([angles, angles], 1)
    return (jnp.cos(angles), jnp.sin(angles))


def rotate(tensor, cosine, sine_table):
    rotary_part = tensor[..., :ROT_DIMS]
    lower_half = rotary_part[..., : ROT_DIMS // 2]
    upper_half = rotary_part[..., ROT_DIMS // 2 :]
    turned = jnp.concatenate([-upper_half, lower_half], -1)
    return jnp.concatenate([rotary_part * cosine + turned * sine_table, tensor[..., ROT_DIMS:]], -1)


def adamw(master, clipped, first_old, second_old, step_rate, decay_rate):
    first_new = BETA_ONE * first_old + (1.0 - BETA_ONE) * clipped
    second_new = BETA_TWO * second_old + (1.0 - BETA_TWO) * clipped * clipped
    ascent = (
        first_new
        / (1.0 - BETA_ONE**STEP)
        / (jnp.sqrt(second_new / (1.0 - BETA_TWO**STEP)) + ADAM_EPS)
    )
    return (master - step_rate * (ascent + decay_rate * master), first_new, second_new)


def gelu_exact(tensor):
    return jax.nn.gelu(tensor, approximate=False)


def across_tokens(left_side, right_side):
    return lax.dot_general(
        left_side, right_side, (((0,), (0,)), ((), ())), preferred_element_type=jnp.float32
    )


def against(left_side, right_side):
    return lax.dot_general(
        left_side, right_side, (((1,), (1,)), ((), ())), preferred_element_type=jnp.float32
    )


def masked_scores(query_rows, row_places, key_block, key_places):
    scores = against(query_rows, key_block) * HD ** (-0.5)
    return jnp.where(key_places[None, :] <= row_places[:, None], scores, MASKED)


def body(
    inputs,
    cotangent,
    span_order,
    query_weight,
    keyval_weight,
    output_weight,
    up_weight,
    down_weight,
    vectors,
    kv_bias,
    first_query,
    first_keyval,
    first_output,
    first_up,
    first_down,
    first_vectors,
    first_kv_bias,
    second_query,
    second_keyval,
    second_output,
    second_up,
    second_down,
    second_vectors,
    second_kv_bias,
):
    tok_rows = inputs.shape[0]
    seq_count = lax.axis_size("seq")
    seq_rank = lax.axis_index("seq")
    order_row = span_order[0]
    token_steps = jnp.arange(tok_rows, dtype=jnp.int32)
    all_places = (order_row[:, None] * tok_rows + token_steps[None, :]).reshape(
        seq_count * tok_rows
    )
    own_span = jnp.sum(jnp.where(jnp.arange(seq_count, dtype=jnp.int32) == seq_rank, order_row, 0))
    own_places = own_span * tok_rows + token_steps
    query_rows_count = tok_rows * HQ
    query_full, keyval_full, output_full, up_full, down_full, vector_full = (
        lax.all_gather(query_weight.astype(jnp.bfloat16), ("fsdp", "seq"), axis=0, tiled=True),
        lax.all_gather(keyval_weight.astype(jnp.bfloat16), ("fsdp", "seq"), axis=0, tiled=True),
        lax.all_gather(output_weight.astype(jnp.bfloat16), ("fsdp", "seq"), axis=0, tiled=True),
        lax.all_gather(up_weight.astype(jnp.bfloat16), ("fsdp", "seq"), axis=0, tiled=True),
        lax.all_gather(down_weight.astype(jnp.bfloat16), ("fsdp", "seq"), axis=0, tiled=True),
        lax.all_gather(vectors.astype(jnp.bfloat16), ("fsdp", "seq"), axis=1, tiled=True),
    )
    kv_shift = lax.all_gather(kv_bias.astype(jnp.bfloat16), "seq", axis=0, tiled=True).astype(
        jnp.float32
    )
    gains = vector_full.astype(jnp.float32)
    states = inputs.astype(jnp.float32)
    normed_one = layer_norm(states, gains[0], gains[1])
    normed_low = normed_one.astype(jnp.bfloat16)
    query_pre = jnp.dot(normed_low, query_full, preferred_element_type=jnp.float32) + gains[4]
    keyval_pre = jnp.dot(normed_low, keyval_full, preferred_element_type=jnp.float32) + kv_shift
    cosine, sine_table = rotary_tables(own_places)

    def turn_queries(tensor):
        return rotate(tensor.reshape(tok_rows, HQ, HD), cosine[:, None, :], sine_table[:, None, :])

    def turn_keys(tensor):
        return jnp.concatenate([rotate(tensor[:, :HD], cosine, sine_table), tensor[:, HD:]], 1)

    query_rows = turn_queries(query_pre).astype(jnp.bfloat16).reshape(query_rows_count, HD)
    local_pairs = turn_keys(keyval_pre).astype(jnp.bfloat16)
    row_places = jnp.broadcast_to(own_places[:, None], (tok_rows, HQ)).reshape(query_rows_count)
    all_pairs = lax.all_gather(local_pairs, "seq", axis=0, tiled=True)
    block_count = all_pairs.shape[0] // KEY_BLOCK
    place_blocks = all_places.reshape(block_count, KEY_BLOCK)

    def lse_step(carry_pair, block_pair):
        running_top, running_total = carry_pair
        pair_block, key_places = block_pair
        scores = masked_scores(query_rows, row_places, pair_block[:, :HD], key_places)
        new_top = jnp.maximum(running_top, jnp.max(scores, 1, keepdims=True))
        running_total = running_total * jnp.exp(running_top - new_top) + jnp.sum(
            jnp.exp(scores - new_top), 1, keepdims=True
        )
        return ((new_top, running_total), None)

    start_carry = (
        jnp.full((query_rows_count, 1), MASKED, jnp.float32),
        jnp.zeros((query_rows_count, 1), jnp.float32),
    )
    (row_top, row_total), _ = lax.scan(
        lse_step, start_carry, (all_pairs.reshape(block_count, KEY_BLOCK, 2 * HD), place_blocks)
    )
    log_total = row_top + jnp.log(row_total)

    def mix_step(mixed_acc, block_pair):
        pair_block, key_places = block_pair
        probs_low = jnp.exp(
            masked_scores(query_rows, row_places, pair_block[:, :HD], key_places) - log_total
        ).astype(jnp.bfloat16)
        return (
            mixed_acc + jnp.dot(probs_low, pair_block[:, HD:], preferred_element_type=jnp.float32),
            None,
        )

    mixed, _ = lax.scan(
        mix_step,
        jnp.zeros((query_rows_count, HD), jnp.float32),
        (all_pairs.reshape(block_count, KEY_BLOCK, 2 * HD), place_blocks),
    )
    mixed_low = mixed.reshape(tok_rows, D).astype(jnp.bfloat16)
    attention_out = jnp.dot(mixed_low, output_full, preferred_element_type=jnp.float32) + gains[5]
    normed_two = layer_norm(states, gains[2], gains[3])
    normed_two_low = normed_two.astype(jnp.bfloat16)
    lifted = jnp.dot(normed_two_low, up_full, preferred_element_type=jnp.float32) + gains[
        7:
    ].reshape(FF)
    active_low = gelu_exact(lifted).astype(jnp.bfloat16)
    block_output = (
        states
        + attention_out
        + jnp.dot(active_low, down_full, preferred_element_type=jnp.float32)
        + gains[6]
    ).astype(jnp.bfloat16)
    back_rows = cotangent.astype(jnp.float32)
    query_back, keyval_back, output_back, up_back, down_back = (
        lax.all_gather(query_weight.astype(jnp.bfloat16), ("fsdp", "seq"), axis=0, tiled=True),
        lax.all_gather(keyval_weight.astype(jnp.bfloat16), ("fsdp", "seq"), axis=0, tiled=True),
        lax.all_gather(output_weight.astype(jnp.bfloat16), ("fsdp", "seq"), axis=0, tiled=True),
        lax.all_gather(up_weight.astype(jnp.bfloat16), ("fsdp", "seq"), axis=0, tiled=True),
        lax.all_gather(down_weight.astype(jnp.bfloat16), ("fsdp", "seq"), axis=0, tiled=True),
    )
    grad_down = across_tokens(active_low, cotangent)
    grad_output = across_tokens(mixed_low, cotangent)
    out_bias_grad = jnp.sum(back_rows, 0)
    active_grad = against(cotangent, down_back)
    _, gelu_pull = jax.vjp(gelu_exact, lifted)
    (lifted_grad,) = gelu_pull(active_grad)
    lifted_low = lifted_grad.astype(jnp.bfloat16)
    grad_up = across_tokens(normed_two_low, lifted_low)
    normed_two_grad = against(lifted_low, up_back)
    mixed_grad = against(cotangent, output_back).astype(jnp.bfloat16).reshape(query_rows_count, HD)
    row_delta = jnp.sum(mixed_grad.astype(jnp.float32) * mixed, 1, keepdims=True)
    pairs_back = lax.all_gather(local_pairs, "seq", axis=0, tiled=True)

    def grad_step(query_acc, block_pair):
        pair_block, key_places = block_pair
        key_block = pair_block[:, :HD]
        probs = jnp.exp(masked_scores(query_rows, row_places, key_block, key_places) - log_total)
        prob_grad = against(mixed_grad, pair_block[:, HD:])
        score_low = (probs * (prob_grad - row_delta)).astype(jnp.bfloat16)
        query_acc = query_acc + jnp.dot(score_low, key_block, preferred_element_type=jnp.float32)
        key_grad = across_tokens(score_low, query_rows) * HD ** (-0.5)
        value_grad = across_tokens(probs.astype(jnp.bfloat16), mixed_grad)
        return (query_acc, jnp.concatenate([key_grad, value_grad], 1))

    query_sum, pair_grads = lax.scan(
        grad_step,
        jnp.zeros((query_rows_count, HD), jnp.float32),
        (pairs_back.reshape(block_count, KEY_BLOCK, 2 * HD), place_blocks),
    )
    query_rot_grad = (query_sum * HD ** (-0.5)).reshape(tok_rows, HQ, HD)
    own_pair_grad = lax.psum_scatter(
        pair_grads.reshape(block_count * KEY_BLOCK, 2 * HD).astype(jnp.bfloat16),
        "seq",
        scatter_dimension=0,
        tiled=True,
    ).astype(jnp.float32)
    _, key_pull = jax.vjp(turn_keys, keyval_pre)
    (keyval_grad,) = key_pull(own_pair_grad)
    keyval_low = keyval_grad.astype(jnp.bfloat16)
    _, query_pull = jax.vjp(turn_queries, query_pre)
    (query_pre_grad,) = query_pull(query_rot_grad)
    query_low = query_pre_grad.astype(jnp.bfloat16)
    grad_query = across_tokens(normed_low, query_low)
    grad_keyval = across_tokens(normed_low, keyval_low)
    kv_bias_part = jnp.sum(keyval_low.astype(jnp.float32), 0)
    normed_one_grad = against(query_low, query_back) + against(keyval_low, keyval_back)
    _, first_pull = jax.vjp(layer_norm, states, gains[0], gains[1])
    input_one, gain_one_grad, shift_one_grad = first_pull(normed_one_grad)
    _, second_pull = jax.vjp(layer_norm, states, gains[2], gains[3])
    input_two, gain_two_grad, shift_two_grad = second_pull(normed_two_grad)
    input_grad = back_rows + input_one + input_two
    vector_grad = jnp.concatenate(
        [
            jnp.stack(
                [
                    gain_one_grad,
                    shift_one_grad,
                    gain_two_grad,
                    shift_two_grad,
                    jnp.sum(query_low.astype(jnp.float32), 0),
                    out_bias_grad,
                    out_bias_grad,
                ]
            ),
            jnp.sum(lifted_low.astype(jnp.float32), 0).reshape(FF // D, D),
        ],
        0,
    )
    reduced = (
        lax.psum_scatter(grad_query, ("fsdp", "seq"), scatter_dimension=0, tiled=True),
        lax.psum_scatter(grad_keyval, ("fsdp", "seq"), scatter_dimension=0, tiled=True),
        lax.psum_scatter(grad_output, ("fsdp", "seq"), scatter_dimension=0, tiled=True),
        lax.psum_scatter(grad_up, ("fsdp", "seq"), scatter_dimension=0, tiled=True),
        lax.psum_scatter(grad_down, ("fsdp", "seq"), scatter_dimension=0, tiled=True),
        lax.psum_scatter(vector_grad, ("fsdp", "seq"), scatter_dimension=1, tiled=True),
    )
    reduced = tuple(reduced)
    local_squares = sum((jnp.sum(gradient * gradient) for gradient in reduced))
    global_squares, kv_bias_total = lax.psum((local_squares, kv_bias_part), ("fsdp", "seq"))
    grad_norm = jnp.sqrt(global_squares + jnp.sum(kv_bias_total * kv_bias_total))
    piece_width = kv_bias.shape[0]
    kv_bias_grad = lax.dynamic_slice_in_dim(kv_bias_total, seq_rank * piece_width, piece_width)
    factor = jnp.minimum(1.0, CLIP_NORM / (grad_norm + 1e-06))
    masters = (query_weight, keyval_weight, output_weight, up_weight, down_weight, vectors, kv_bias)
    all_grads = reduced + (kv_bias_grad,)
    firsts = (
        first_query,
        first_keyval,
        first_output,
        first_up,
        first_down,
        first_vectors,
        first_kv_bias,
    )
    seconds = (
        second_query,
        second_keyval,
        second_output,
        second_up,
        second_down,
        second_vectors,
        second_kv_bias,
    )
    step_rates = (MATRIX_RATE,) * 5 + (VECTOR_RATE, VECTOR_RATE)
    decays = (MATRIX_DECAY,) * 5 + (0.0, 0.0)
    updated = [
        adamw(master, gradient * factor, first_old, second_old, step_rate, decay_rate)
        for master, gradient, first_old, second_old, step_rate, decay_rate in zip(
            masters, all_grads, firsts, seconds, step_rates, decays
        )
    ]
    residual_bias_grads = (reduced[5] * factor)[5:7]
    return (
        block_output,
        input_grad,
        grad_norm,
        updated[0][0],
        updated[1][0],
        updated[2][0],
        updated[3][0],
        updated[4][0],
        updated[5][0],
        updated[6][0],
        updated[0][1],
        updated[1][1],
        updated[2][1],
        updated[3][1],
        updated[4][1],
        updated[5][1],
        updated[6][1],
        updated[0][2],
        updated[1][2],
        updated[2][2],
        updated[3][2],
        updated[4][2],
        updated[5][2],
        updated[6][2],
        residual_bias_grads,
    )


def dot_nn(left, right):
    return lax.dot_general(left, right, (((1,), (0,)), ((), ())), preferred_element_type=F32)


def dot_nt(left, right):
    return lax.dot_general(left, right, (((1,), (1,)), ((), ())), preferred_element_type=F32)


def dot_tn(left, right):
    return lax.dot_general(left, right, (((0,), (0,)), ((), ())), preferred_element_type=F32)


def normalise(rows):
    centre = rows - jnp.mean(rows, -1, keepdims=True)
    scale = lax.rsqrt(jnp.mean(centre * centre, -1, keepdims=True) + NORM_EPS)
    return centre * scale, scale


def norm_back(grad, hat, scale, gain):
    inner = grad * gain
    return scale * (
        inner
        - jnp.mean(inner, -1, keepdims=True)
        - hat * jnp.mean(inner * hat, -1, keepdims=True)
    )


class Copies:
    def __init__(self, send_sems, recv_sems):
        self.send_sems, self.recv_sems, self.all = send_sems, recv_sems, []

    def make(self, source, target, device):
        index = len(self.all)
        copy = pltpu.make_async_remote_copy(
            src_ref=source,
            dst_ref=target,
            send_sem=self.send_sems.at[index],
            recv_sem=self.recv_sems.at[index],
            device_id=device,
            device_id_type=pl.DeviceIdType.MESH,
        )
        self.all.append(copy)
        return copy


def slab_rows(block, index):
    return pl.ds(pl.multiple_of((block * 8 + index) * 24, 8), 24)


class Panels:
    def __init__(self, ref, height):
        self.ref, self.height, self.count = ref, height, ref.shape[0] // height

    def rows(self, panel, block, index):
        return pl.ds(pl.multiple_of(panel * self.height + (block * 8 + index) * 24, 8), 24)

    def get(self, block, index):
        parts = [self.ref[self.rows(p, block, index), :] for p in range(self.count)]
        return parts[0] if self.count == 1 else jnp.concatenate(parts, 1)

    def put(self, block, index, value):
        for p in range(self.count):
            self.ref[self.rows(p, block, index), :] = value[:, p * 256 : p * 256 + 256]


N_COPIES = 130
QO = 1536
AW = 1664


def layer_kernel(
    span, x, cot, qw, kw, ow, uw, dw, vec, kvb,
    bo, ig, g_qo, g_vp, g_up, g_dn, g_small,
    A, U, Dn, VT, X, C, KV, ub, WA, WU, gains, vsq,
    n1, hat1, scale1, N2, act, dl, OP, NP,
    qz, doz, doT, kvT, bias, sbuf, mixT, dqT, dkv,
    GP, GU, GD, vg,
    SK1, RK1, SK2, RK2,
    RO1, SO2, RO2, RN1, SN2, RN2,
    SQ1, RQ1, SQ2, RQ2, SQ3, RQ3, SQ4, RQ4,
    SP1, RP1, SP2, RP2, SP3, RP3, SP4, RP4,
    SU1, RU1, SU2, RU2, SU3, RU3,
    SD1, RD1, SD2, RD2,
    NS1, NS2,
    send_sems, recv_sems,
):
    tok = x.shape[0]
    f = lax.axis_index("fsdp")
    s = lax.axis_index("seq")
    z = lax.div(s, 2)
    y = lax.rem(s, 2)
    yo = 1 - y
    fc = f + 1 - 2 * lax.rem(f, 2)
    fx = lax.rem(f + 2, 4)
    fd = 3 - f
    zk = (z, z + 1 - 2 * lax.rem(z, 2), lax.rem(z + 2, 4), 3 - z)
    dev_c, dev_x, dev_d = (fc, s), (fx, s), (fd, s)
    dev_y = (f, z * 2 + yo)
    dev_z = tuple((f, zz * 2 + y) for zz in zk)
    dev_zy = tuple((f, zz * 2 + yo) for zz in zk)
    fsdp_devs = (dev_c, dev_x, dev_d)
    seq_devs = dev_z[1:] + dev_zy

    copies = Copies(send_sems, recv_sems)
    make = copies.make

    def seq_gather(ref):
        to_z = [None] + [make(ref(z, y), ref(z, y), dev_z[k]) for k in (1, 2, 3)]
        to_y = [make(ref(zk[k], y), ref(zk[k], y), dev_y) for k in range(4)]
        return to_z, to_y

    a_z, a_y = seq_gather(lambda i, j: A.at[f, i, j])
    v_z, v_y = seq_gather(lambda i, j: VT.at[f, i, j])
    u_z, u_y = seq_gather(lambda i, j: U.at[i, j])
    d_z, d_y = seq_gather(lambda i, j: Dn.at[i, j])
    k_z, k_y = seq_gather(lambda i, j: KV.at[i, j])

    def fsdp_gather(ref):
        to_x = [make(ref(f, j), ref(f, j), dev_x) for j in (y, yo)]
        to_c = [make(ref(f, j), ref(f, j), dev_c) for j in (y, yo)]
        on_c = [make(ref(fx, j), ref(fx, j), dev_c) for j in (y, yo)]
        return to_x, to_c, on_c

    a_x, a_c, a_xc = fsdp_gather(lambda i, j: A.at[i, :, j])
    v_x, v_c, v_xc = fsdp_gather(lambda i, j: VT.at[i, :, j])

    def token_gather(ref):
        return (
            make(ref.at[f], ref.at[f], dev_x),
            make(ref.at[f], ref.at[f], dev_c),
            make(ref.at[fx], ref.at[fx], dev_c),
        )

    x_x, x_c, x_xc = token_gather(X)
    c_x, c_c, c_xc = token_gather(C)
    u_f = [make(ub.at[g], U.at[z, y, f], dev) for g, dev in zip((fc, fx, fd), fsdp_devs)]

    rk1 = make(SK1, RK1, dev_y)
    rk2 = [make(SK2.at[k], RK2.at[k], dev_z[k + 1]) for k in range(3)]
    out_c = [make(OP.at[g], RO1.at[i], dev_c) for i, g in enumerate((fc, fd))]
    out_x = make(SO2, RO2, dev_x)
    nrm_c = [make(NP.at[g], RN1.at[i], dev_c) for i, g in enumerate((fc, fd))]
    nrm_x = make(SN2, RN2, dev_x)

    def full_scatter(S1, R1, S2, R2, S3, R3, S4, R4):
        return (
            make(S1, R1, dev_c),
            make(S2, R2, dev_x),
            make(S3, R3, dev_y),
            [make(S4.at[k], R4.at[k], dev_z[k + 1]) for k in range(3)],
        )

    q_sc = full_scatter(SQ1, RQ1, SQ2, RQ2, SQ3, RQ3, SQ4, RQ4)
    p_sc = full_scatter(SP1, RP1, SP2, RP2, SP3, RP3, SP4, RP4)
    su_y = [make(SU1.at[zz], RU1.at[zz], dev_y) for zz in zk]
    su_z = [make(SU2.at[k], RU2.at[k], dev_z[k + 1]) for k in range(3)]
    su_f = [make(SU3.at[g], RU3.at[i], dev) for i, (g, dev) in enumerate(zip((fc, fx, fd), fsdp_devs))]
    sd_y = [make(SD1.at[zz], RD1.at[zz], dev_y) for zz in zk]
    sd_z = [make(SD2.at[k], RD2.at[k], dev_z[k + 1]) for k in range(3)]
    n_f = [make(NS1.at[f], NS1.at[f], dev) for dev in fsdp_devs]
    n_s = [make(NS2.at[s], NS2.at[s], dev) for dev in seq_devs]

    barrier = pltpu.get_barrier_semaphore()
    for dev in fsdp_devs + seq_devs:
        pl.semaphore_signal(barrier, inc=1, device_id=dev, device_id_type=pl.DeviceIdType.MESH)

    for j in range(4):
        ub[j] = uw[:, j * D : (j + 1) * D].astype(BF16)
    U[z, y, f] = ub[f]
    Dn[z, y] = dw[...].astype(BF16)
    A[f, z, y, :, :D] = qw[...].astype(BF16)
    A[f, z, y, :, D : D + 128] = kw[...].astype(BF16)
    A[f, z, y, :, D + 128 :] = ow[...].astype(BF16)
    vsq[...] = jnp.zeros((128, 128), F32)
    vsq[0:11, 0:24] = vec[...]
    vsq[11:12, 0:16] = kvb[...]
    VT[f, z, y] = vsq[...].astype(BF16).astype(F32).T[:24, :]
    X[f] = x[...]
    C[f] = cot[...]

    pl.semaphore_wait(barrier, 10)

    for copy in u_f:
        copy.start()
    for k in (1, 2, 3):
        v_z[k].start()
    v_y[0].start()
    for copy in (x_x, c_x, x_c, c_c):
        copy.start()
    for k in (1, 2, 3):
        d_z[k].start()
    d_y[0].start()
    for copy in u_f:
        copy.wait_recv()
    for k in (1, 2, 3):
        u_z[k].start()
    u_y[0].start()
    for k in (1, 2, 3):
        v_z[k].wait_recv()
        v_y[k].start()
    v_x[0].start()
    v_c[0].start()
    for k in (1, 2, 3):
        a_z[k].start()
    a_y[0].start()
    for k in range(4):
        v_y[k].wait_recv()
    v_x[1].start()
    v_c[1].start()
    for j in range(2):
        v_x[j].wait_recv()
        v_xc[j].start()
    for k in (1, 2, 3):
        d_z[k].wait_recv()
        d_y[k].start()
    x_x.wait_recv()
    x_xc.start()
    for k in (1, 2, 3):
        u_z[k].wait_recv()
        u_y[k].start()
    c_x.wait_recv()
    c_xc.start()
    for k in (1, 2, 3):
        a_z[k].wait_recv()
        a_y[k].start()
    a_x[0].start()
    a_c[0].start()
    for j in range(2):
        v_c[j].wait_recv()
        v_xc[j].wait_recv()

    gains[...] = VT.reshape(D, 128)[...].T
    vsq[...] = jnp.concatenate([VT[0, i // 2, i % 2][:16] for i in range(8)], 0).T
    kv_shift = vsq[11:12, :]
    hat, scale = normalise(x[...].astype(F32))
    hat1[...] = hat
    scale1[...] = jnp.broadcast_to(scale, (tok, 128))
    n1[...] = (hat * gains[0:1, :] + gains[1:2, :]).astype(BF16)
    vg[...] = jnp.zeros((128, D), F32)
    csum = jnp.sum(cot[...].astype(F32), 0, keepdims=True)
    vg[5:6, :] = csum
    vg[6:7, :] = csum

    for k in range(4):
        d_y[k].wait_recv()
    for k in range(4):
        u_y[k].wait_recv()
    for copy in (x_c, x_xc, c_c, c_xc):
        copy.wait_recv()

    for g in range(4):
        for i in range(4):
            pair = jnp.concatenate([U[i, j, g].astype(F32) for j in range(2)], 0)
            WU[(g * 4 + i) * 48 : (g * 4 + i + 1) * 48, :] = pair.astype(BF16)
    WD = Dn.reshape(D, D)
    up_bias = gains[pl.ds(7 + f, 1), :]
    vg[pl.ds(7 + f, 1), :] = jnp.zeros((1, D), F32)

    def token_block(t, carry):
        two_gain, two_shift, up_sum = carry
        rows = pl.ds(pl.multiple_of(t * tok, tok), tok)
        hat2, _ = normalise(X[t].astype(F32))
        low2 = (hat2 * gains[2:3, :] + gains[3:4, :]).astype(BF16)
        N2[rows, :] = low2
        back = C[t]
        sums = []
        for c in range(3):
            units = slice(c * 256, c * 256 + 256)
            lifted = dot_nn(low2, WU[:, units]) + up_bias[:, units]
            active_grad = dot_nt(back, WD[units, :])
            half = 0.5 + 0.5 * lax.erf(lifted * (0.5**0.5))
            act[rows, units] = (lifted * half).astype(BF16)
            bell = jnp.exp(lifted * lifted * -0.5) * (1.0 / math.sqrt(2.0 * math.pi))
            low = ((half + lifted * bell) * active_grad).astype(BF16)
            dl[rows, units] = low
            sums.append(jnp.sum(low.astype(F32), 0, keepdims=True))
        OP[t] = dot_nn(act[rows, :], WD[...]).astype(BF16)
        grad2 = dot_nt(dl[rows, :], WU[...])
        NP[t] = grad2.astype(BF16)
        return (
            two_gain + jnp.sum(grad2 * hat2, 0, keepdims=True),
            two_shift + jnp.sum(grad2, 0, keepdims=True),
            up_sum + jnp.concatenate(sums, 1),
        )

    zero_row = jnp.zeros((1, D), F32)
    two_gain, two_shift, up_sum = lax.fori_loop(0, 4, token_block, (zero_row,) * 3)
    vg[2:3, :] = two_gain
    vg[3:4, :] = two_shift
    vg[pl.ds(7 + f, 1), :] = up_sum
    for copy in out_c + nrm_c:
        copy.start()

    for k in range(4):
        a_y[k].wait_recv()
    a_x[1].start()
    a_c[1].start()

    CF = C.reshape(4 * tok, D)
    for c in range(3):
        units = slice(c * 256, c * 256 + 256)
        GD[units, :] = dot_tn(act[:, units], CF[...])
    for k in (1, 2, 3, 0):
        for i in range(1):
            SD1[zk[k]] = GD[pl.ds(pl.multiple_of((zk[k] * 2 + yo) * 96, 8), 96), :].astype(BF16)
        sd_y[k].start()
    a_x[0].wait_recv()
    a_xc[0].start()
    for c in range(3):
        units = slice(c * 256, c * 256 + 256)
        GU[units, :] = dot_tn(N2[:, units], dl[...])
    for k in (1, 2, 3, 0):
        for g in range(4):
            SU1[zk[k], g] = GU[slab_rows(g, zk[k] * 2 + yo), :].astype(BF16)
        su_y[k].start()
    a_x[1].wait_recv()
    a_xc[1].start()
    for j in range(2):
        a_c[j].wait_recv()
        a_xc[j].wait_recv()

    def join(i, carry):
        g = lax.div(i, 4)
        zz = lax.rem(i, 4)
        pair = jnp.concatenate([A[g, zz, 0].astype(F32), A[g, zz, 1].astype(F32)], 0)
        WA[pl.ds(pl.multiple_of(i * 48, 16), 48), :] = pair.astype(BF16)
        return carry

    lax.fori_loop(0, 16, join, 0)
    own_span = span[0, s]
    lane = lax.broadcasted_iota(jnp.int32, (tok, 128), 1)
    spot = lax.broadcasted_iota(jnp.int32, (tok, 128), 0) + own_span * tok
    in_head = lax.rem(lane, 64)
    step = lax.rem(in_head, ROT_DIMS // 2).astype(F32)
    inverse = jnp.exp(step * (-2.0 * math.log(10000.0) / ROT_DIMS))
    angle = spot.astype(F32) * (0.25 * inverse)
    sine = jnp.sin(angle)
    cosine = jnp.where(in_head < ROT_DIMS, jnp.cos(angle), 1.0)
    sine_low = jnp.where(in_head < ROT_DIMS // 2, sine, 0.0)
    sine_high = jnp.where((in_head >= ROT_DIMS // 2) & (in_head < ROT_DIMS), sine, 0.0)
    key_lane = lane < 64
    key_cos = jnp.where(key_lane, cosine, 1.0)
    key_low = jnp.where(key_lane, sine_low, 0.0)
    key_high = jnp.where(key_lane, sine_high, 0.0)

    def turn(block, cos_t, low_t, high_t):
        up = pltpu.roll(block, 120, 1)
        down = pltpu.roll(block, 8, 1)
        return block * cos_t - up * low_t + down * high_t

    def turn_back(block, cos_t, low_t, high_t):
        up = pltpu.roll(block, 120, 1)
        down = pltpu.roll(block, 8, 1)
        return block * cos_t + up * low_t - down * high_t

    kv_pre = dot_nn(n1[...], WA[:, D : D + 128]) + kv_shift
    KV[z, y] = turn(kv_pre, key_cos, key_low, key_high).astype(BF16)
    for k in (1, 2, 3):
        k_z[k].start()
    k_y[0].start()

    q_pre = dot_nn(n1[...], WA[:, :D]) + gains[4:5, :]
    gap = jnp.zeros((tok, 64), BF16)
    for j in range(6):
        cols = slice(j * 128, j * 128 + 128)
        turned = turn(q_pre[:, cols], cosine, sine_low, sine_high).astype(BF16).astype(F32)
        turned = (turned * HD ** (-0.5)).astype(BF16)
        qz[2 * j] = jnp.concatenate([turned[:, :64], gap], 1)
        qz[2 * j + 1] = jnp.concatenate([turned[:, 64:], gap], 1)
    for k in (1, 2, 3):
        k_z[k].wait_recv()
        k_y[k].start()
    mixed_back = dot_nt(cot[...], WA[:, D + 128 :]).astype(BF16)
    for j in range(6):
        pair = mixed_back[:, j * 128 : j * 128 + 128]
        doz[2 * j] = jnp.concatenate([gap, pair[:, :64]], 1)
        doz[2 * j + 1] = jnp.concatenate([gap, pair[:, 64:]], 1)
    doT[...] = mixed_back.astype(F32).T.astype(BF16).reshape(HQ, HD, tok)
    key_iota = lax.broadcasted_iota(jnp.int32, (tok, tok), 0)
    row_iota = lax.broadcasted_iota(jnp.int32, (tok, tok), 1) + own_span * tok
    for i in range(8):
        bias[i * tok : (i + 1) * tok, :] = jnp.where(
            key_iota + span[0, i] * tok <= row_iota, 0.0, MASKED
        ).astype(F32)
    dkv[...] = jnp.zeros((8 * tok, 128), F32)
    for k in range(4):
        k_y[k].wait_recv()
    KVF = KV.reshape(8 * tok, 128)
    kvT[...] = KVF[...].astype(F32).T.astype(BF16)

    def scatter_step(k):
        su_y[k].wait_recv()
        sd_y[k].wait_recv()
        own = zk[k]
        rows = pl.ds(pl.multiple_of((own * 2 + y) * 96, 8), 96)
        total = GD[rows, :] + RD1[own].astype(F32)
        if k:
            SD2[k - 1] = total.astype(BF16)
            sd_z[k - 1].start()
        else:
            GD[rows, :] = total
        for g in range(4):
            rows = slab_rows(g, own * 2 + y)
            total = GU[rows, :] + RU1[own, g].astype(F32)
            if k:
                SU2[k - 1, g] = total.astype(BF16)
            else:
                GU[rows, :] = total
        if k:
            su_z[k - 1].start()

    def tokens_to_x():
        for copy in out_c + nrm_c:
            copy.wait_recv()
        SO2[...] = (OP[fx].astype(F32) + RO1[1].astype(F32)).astype(BF16)
        out_x.start()
        SN2[...] = (NP[fx].astype(F32) + RN1[1].astype(F32)).astype(BF16)
        nrm_x.start()

    def attend(step_index, carry):
        @pl.when(step_index == 0)
        def _():
            tokens_to_x()

        for k, at in ((1, 1), (2, 2), (3, 3), (0, 4)):

            @pl.when(step_index == at)
            def _():
                scatter_step(k)

        heads = [step_index * 2, step_index * 2 + 1]
        tops, shares, deltas = [], [], []
        for j, h in enumerate(heads):
            top = jnp.full((8, tok), MASKED, F32)
            for i in range(8):
                rows = pl.ds(i * tok, tok)
                held = pl.ds((j * 8 + i) * tok, tok)
                scores = dot_nt(KVF[rows, :], qz[h]) + bias[rows, :]
                sbuf[held, :] = scores
                top = jnp.maximum(top, jnp.max(scores.reshape(tok // 8, 8, tok), axis=0))
            tops.append(jnp.max(top, axis=0, keepdims=True))
        for j, h in enumerate(heads):
            total = jnp.zeros((8, tok), F32)
            for i in range(8):
                held = pl.ds((j * 8 + i) * tok, tok)
                weights = jnp.exp(sbuf[held, :] - tops[j])
                sbuf[held, :] = weights
                total = total + jnp.sum(weights.reshape(tok // 8, 8, tok), axis=0)
            shares.append(1.0 / jnp.sum(total, axis=0, keepdims=True))
        for j, h in enumerate(heads):
            acc = jnp.zeros((128, tok), F32)
            for i in range(8):
                rows = pl.ds(i * tok, tok)
                held = pl.ds((j * 8 + i) * tok, tok)
                probs = sbuf[held, :] * shares[j]
                probs_low = probs.astype(BF16)
                sbuf[held, :] = probs
                acc = acc + dot_nn(kvT[:, rows], probs_low)
                dkv[rows, :] += dot_nn(probs_low, doz[h])
            mixed = acc[64:, :]
            mixT[h] = mixed.astype(BF16)
            deltas.append(jnp.sum(mixed * doT[h].astype(F32), axis=0, keepdims=True))
        for j, h in enumerate(heads):
            acc = jnp.zeros((128, tok), F32)
            for i in range(8):
                rows = pl.ds(i * tok, tok)
                held = pl.ds((j * 8 + i) * tok, tok)
                prob_grad = dot_nt(KVF[rows, :], doz[h])
                score_low = (sbuf[held, :] * (prob_grad - deltas[j])).astype(BF16)
                acc = acc + dot_nn(kvT[:, rows], score_low)
                dkv[rows, :] += dot_nn(score_low, qz[h])
            dqT[h] = acc[:64, :] * HD ** (-0.5)
        return carry

    lax.fori_loop(0, HQ // 2, attend, 0)

    for zz in range(4):
        SK1[zz] = dkv[pl.ds(pl.multiple_of((2 * zz + yo) * tok, 8), tok), :].astype(BF16)
    rk1.start()
    mix_low = mixT.reshape(D, tok)[...]
    for c in range(3):
        sbuf[(3 + c) * D : (4 + c) * D, :] = dot_nn(mix_low, cot[:, c * 256 : c * 256 + 256])
    q_back = dqT.reshape(D, tok)[...].T
    parts = []
    for j in range(6):
        parts.append(
            turn_back(q_back[:, j * 128 : j * 128 + 128], cosine, sine_low, sine_high).astype(BF16)
        )
    q_low = jnp.concatenate(parts, 1)
    vg[4:5, :] = jnp.sum(q_low.astype(F32), 0, keepdims=True)
    for c in range(3):
        sbuf[c * D : (c + 1) * D, :] = dot_tn(n1[...], q_low[:, c * 256 : c * 256 + 256])
    GQ = Panels(sbuf, D)
    GPP = Panels(GP, D)

    def scatter_c(G, S1, copy):
        def put(i, carry):
            for j, g in enumerate((fc, fd)):
                S1[j, i] = G.get(g, i).astype(S1.dtype)
            return carry

        lax.fori_loop(0, 8, put, 0)
        copy.start()

    def scatter_x(G, R1, S2, copies_):
        copies_[0].wait_recv()

        def put(i, carry):
            S2[i] = (G.get(fx, i) + R1[1, i].astype(F32)).astype(S2.dtype)
            G.put(f, i, G.get(f, i) + R1[0, i].astype(F32))
            return carry

        lax.fori_loop(0, 8, put, 0)
        copies_[1].start()

    def scatter_y(G, R2, S3, copies_):
        copies_[1].wait_recv()

        def put(i, carry):
            S3[i] = (G.get(f, 2 * i + yo) + R2[2 * i + yo].astype(F32)).astype(S3.dtype)
            G.put(f, 2 * i + y, G.get(f, 2 * i + y) + R2[2 * i + y].astype(F32))
            return carry

        lax.fori_loop(0, 4, put, 0)
        copies_[2].start()

    def scatter_z(G, R3, S4, copies_):
        copies_[2].wait_recv()
        for k in (1, 2, 3):
            total = G.get(f, 2 * zk[k] + y) + R3[zk[k]].astype(F32)
            S4[k - 1] = total.astype(S4.dtype)
            copies_[3][k - 1].start()

    def scatter_end(G, R3, R4, copies_):
        total = G.get(f, 2 * z + y) + R3[z].astype(F32)
        for k in range(3):
            copies_[3][k].wait_recv()
            total = total + R4[k].astype(F32)
        return total

    scatter_c(GQ, SQ1, q_sc[0])
    rk1.wait_recv()
    for k in (1, 2, 3):
        rows = pl.ds(pl.multiple_of((2 * zk[k] + y) * tok, 8), tok)
        SK2[k - 1] = (dkv[rows, :] + RK1[zk[k]].astype(F32)).astype(BF16)
        rk2[k - 1].start()
    grad1 = dot_nt(q_low, WA[:, :D])
    scatter_x(GQ, RQ1, SQ2, q_sc)
    kv_back = dkv[pl.ds(pl.multiple_of((2 * z + y) * tok, 8), tok), :] + RK1[z].astype(F32)
    for k in range(3):
        rk2[k].wait_recv()
        kv_back = kv_back + RK2[k].astype(F32)
    kv_low = turn_back(kv_back, key_cos, key_low, key_high).astype(BF16)
    grad1 = grad1 + dot_nt(kv_low, WA[:, D : D + 128])
    vg[0:1, :] = jnp.sum(grad1 * hat1[...], 0, keepdims=True)
    vg[1:2, :] = jnp.sum(grad1, 0, keepdims=True)
    kv_sum = jnp.sum(kv_low.astype(F32), 0, keepdims=True)
    short = jnp.zeros((1, 8), F32)
    spread = jnp.concatenate(
        [part for i in range(8) for part in (kv_sum[:, i * 16 : i * 16 + 16], short)], 1
    )
    vg[11:12, :] = jnp.concatenate([spread] * 4, 1)
    GP[:, :128] = dot_tn(n1[...], kv_low)
    GP[:, 128:] = vg[...].T
    scatter_c(GPP, SP1, p_sc[0])

    rows = pl.ds(pl.multiple_of(s * 96, 8), 96)
    down_grad = GD[rows, :]
    for k in range(3):
        sd_z[k].wait_recv()
        down_grad = down_grad + RD2[k].astype(F32)
    g_dn[...] = down_grad
    for k in range(3):
        su_z[k].wait_recv()
    for g in range(4):
        total = GU[slab_rows(g, s), :]
        for k in range(3):
            total = total + RU2[k, g].astype(F32)
        g_up[g] = total
        SU3[g] = total.astype(BF16)
    for copy in su_f:
        copy.start()
    scatter_x(GPP, RP1, SP2, p_sc)
    scatter_y(GQ, RQ2, SQ3, q_sc)

    mixed_rows = mix_low.astype(F32).T.astype(BF16)
    out_x.wait_recv()
    bo[...] = (
        x[...].astype(F32)
        + (dot_nn(mixed_rows, WA[:, D + 128 :]) + gains[5:6, :])
        + (OP[f].astype(F32) + RO1[0].astype(F32) + RO2[...].astype(F32) + gains[6:7, :])
    ).astype(BF16)
    scatter_y(GPP, RP2, SP3, p_sc)
    scatter_z(GQ, RQ3, SQ4, q_sc)
    nrm_x.wait_recv()
    grad2 = NP[f].astype(F32) + RN1[0].astype(F32) + RN2[...].astype(F32)
    hat_rows = hat1[...]
    scale_rows = scale1[:, 0:1]
    ig[...] = (
        cot[...].astype(F32)
        + norm_back(grad1, hat_rows, scale_rows, gains[0:1, :])
        + norm_back(grad2, hat_rows, scale_rows, gains[2:3, :])
    )
    scatter_z(GPP, RP3, SP4, p_sc)
    for i, g in enumerate((fc, fx, fd)):
        su_f[i].wait_recv()
        g_up[g] = RU3[i].astype(F32)
    qo_grad = scatter_end(GQ, RQ3, RQ4, q_sc)
    g_qo[...] = qo_grad
    vp_grad = scatter_end(GPP, RP3, RP4, p_sc)
    g_vp[...] = vp_grad

    def fold(values):
        return jnp.sum(jnp.sum(values * values, 0, keepdims=True), 1, keepdims=True)

    lanes = lax.broadcasted_iota(jnp.int32, (24, 256), 1)
    squares = fold(qo_grad) + fold(jnp.where(lanes == 128 + 11, 0.0, vp_grad)) + fold(g_dn[...])
    for g in range(4):
        squares = squares + fold(g_up[g])
    kv_rows = jnp.concatenate([vp_grad[:, 128:], jnp.zeros((104, 128), F32)], 0).T
    line = lax.broadcasted_iota(jnp.int32, (8, 128), 0)
    column = lax.broadcasted_iota(jnp.int32, (8, 128), 1)
    kv_line = jnp.where(column < 16, jnp.broadcast_to(kv_rows[11:12, :], (8, 128)), 0.0)
    NS1[f] = jnp.where(line == 0, squares, kv_line)
    for copy in n_f:
        copy.start()
    for copy in n_f:
        copy.wait_recv()
    kv_piece = NS1[0][1:2, :]
    chip = NS1[0] + NS1[1] + NS1[2] + NS1[3]
    part = chip[0:1, 0:1] + jnp.sum(kv_piece * kv_piece, 1, keepdims=True)
    NS2[s] = jnp.broadcast_to(part, (8, 128))
    for copy in n_s:
        copy.start()
    for copy in n_s:
        copy.wait_recv()
    everything = NS2[0]
    for i in range(1, 8):
        everything = everything + NS2[i]
    g_small[...] = jnp.where(line == 0, everything, jnp.broadcast_to(kv_piece, (8, 128)))
    for copy in copies.all:
        copy.wait_send()


def update_kernel(
    small, g_qo, g_vp, g_up, g_dn, bo_in, ig_in,
    mq, mk, mo, mu, md, mv, mb,
    fq, fk, fo, fu, fdn, fv, fb,
    sq, sk, so, su, sd, sv, sb,
    bo, ig, norm,
    nmq, nmk, nmo, nmu, nmd, nmv, nmb,
    nfq, nfk, nfo, nfu, nfd, nfv, nfb,
    nsq, nsk, nso, nsu, nsd, nsv, nsb,
    residual,
):
    bo[...] = bo_in[...]
    ig[...] = ig_in[...]
    size = jnp.sqrt(small[0:1, 0:1])
    norm[...] = size
    factor = jnp.minimum(1.0, CLIP_NORM / (size + 1e-06))

    def update(grad, master, first, second, new_master, new_first, new_second, rate, decay):
        clipped = grad * factor
        values = adamw(master, clipped, first, second, rate, decay)
        for ref, value in zip((new_master, new_first, new_second), values):
            ref[...] = value

    rates = (MATRIX_RATE, MATRIX_DECAY)
    update(g_qo[:, :D], mq[...], fq[...], sq[...], nmq, nfq, nsq, *rates)
    update(g_qo[:, D:], mo[...], fo[...], so[...], nmo, nfo, nso, *rates)
    update(g_vp[:, :128], mk[...], fk[...], sk[...], nmk, nfk, nsk, *rates)
    for g in range(4):
        cols = slice(g * D, (g + 1) * D)
        update(
            g_up[g], mu[:, cols], fu[:, cols], su[:, cols],
            nmu.at[:, cols], nfu.at[:, cols], nsu.at[:, cols], *rates,
        )
    update(g_dn[...], md[...], fdn[...], sd[...], nmd, nfd, nsd, *rates)
    flipped = jnp.concatenate([g_vp[:, 128:], jnp.zeros((104, 128), F32)], 0).T
    vector_grad = flipped[:11, :24]
    update(vector_grad, mv[...], fv[...], sv[...], nmv, nfv, nsv, VECTOR_RATE, 0.0)
    residual[...] = flipped[5:7, :24] * factor
    update(small[1:2, :16], mb[...], fb[...], sb[...], nmb, nfb, nsb, VECTOR_RATE, 0.0)


def fast_body(
    inputs, cotangent, span_order,
    query_weight, keyval_weight, output_weight, up_weight, down_weight, vectors, kv_bias,
    *moments,
):
    tok = inputs.shape[0]
    vmem = pl.BlockSpec(memory_space=pltpu.VMEM)
    smem = pl.BlockSpec(memory_space=pltpu.SMEM)
    shape = jax.ShapeDtypeStruct
    V = pltpu.VMEM
    scratch = [
        V((4, 4, 2, 24, AW), BF16),
        V((4, 2, 4, 24, D), BF16),
        V((4, 2, 96, D), BF16),
        V((4, 4, 2, 24, 128), F32),
        V((4, tok, D), BF16),
        V((4, tok, D), BF16),
        V((4, 2, tok, 128), BF16),
        V((4, 24, D), BF16),
        V((D, AW), BF16),
        V((D, D), BF16),
        V((128, D), F32),
        V((128, 128), F32),
        V((tok, D), BF16),
        V((tok, D), F32),
        V((tok, 128), F32),
        V((4 * tok, D), BF16),
        V((4 * tok, D), BF16),
        V((4 * tok, D), BF16),
        V((4, tok, D), BF16),
        V((4, tok, D), BF16),
        V((HQ, tok, 128), BF16),
        V((HQ, tok, 128), BF16),
        V((HQ, HD, tok), BF16),
        V((128, 8 * tok), BF16),
        V((8 * tok, tok), F32),
        V((QO // 256 * D, 256), F32),
        V((HQ, HD, tok), BF16),
        V((HQ, HD, tok), F32),
        V((8 * tok, 128), F32),
        V((D, 256), F32),
        V((D, D), F32),
        V((D, D), F32),
        V((128, D), F32),
        V((4, tok, 128), BF16), V((4, tok, 128), BF16),
        V((3, tok, 128), BF16), V((3, tok, 128), BF16),
        V((2, tok, D), BF16), V((tok, D), BF16), V((tok, D), BF16),
        V((2, tok, D), BF16), V((tok, D), BF16), V((tok, D), BF16),
    ]
    for width, kind in ((QO, BF16), (256, F32)):
        for lead in ((2, 8), (8,), (4,), (3,)):
            scratch += [V(lead + (24, width), kind)] * 2
    scratch += [V((4, 4, 24, D), BF16)] * 2 + [V((3, 4, 24, D), BF16)] * 2
    scratch += [V((4, 24, D), BF16), V((3, 24, D), BF16)]
    scratch += [V((4, 96, D), BF16)] * 2 + [V((3, 96, D), BF16)] * 2
    scratch += [V((4, 8, 128), F32), V((8, 8, 128), F32)]
    scratch += [pltpu.SemaphoreType.DMA((N_COPIES,))] * 2
    kv_row = kv_bias.reshape(1, -1)
    bo, ig, g_qo, g_vp, g_up, g_dn, small = pl.pallas_call(
        layer_kernel,
        name="layer",
        out_shape=(
            shape((tok, D), BF16),
            shape((tok, D), F32),
            shape((24, QO), F32),
            shape((24, 256), F32),
            shape((4, 24, D), F32),
            shape((96, D), F32),
            shape((8, 128), F32),
        ),
        in_specs=[smem] + [vmem] * 9,
        out_specs=(vmem,) * 7,
        scratch_shapes=scratch,
        compiler_params=pltpu.CompilerParams(
            collective_id=0, has_side_effects=True, vmem_limit_bytes=62 * 2**20
        ),
    )(
        span_order, inputs, cotangent,
        query_weight, keyval_weight, output_weight, up_weight, down_weight, vectors, kv_row,
    )
    masters = (query_weight, keyval_weight, output_weight, up_weight, down_weight, vectors, kv_row)
    firsts = tuple(moments[:6]) + (moments[6].reshape(1, -1),)
    seconds = tuple(moments[7:13]) + (moments[13].reshape(1, -1),)
    state = [shape(a.shape, F32) for a in masters]
    results = pl.pallas_call(
        update_kernel,
        name="update",
        out_shape=[shape((tok, D), BF16), shape((tok, D), F32), shape((1, 1), F32)]
        + state * 3
        + [shape((2, vectors.shape[1]), F32)],
        in_specs=[vmem] * 28,
        out_specs=[vmem] * 25,
        compiler_params=pltpu.CompilerParams(vmem_limit_bytes=48 * 2**20),
    )(small, g_qo, g_vp, g_up, g_dn, bo, ig, *masters, *firsts, *seconds)
    results = list(results)
    results[2] = results[2].reshape(())
    for i in (9, 16, 23):
        results[i] = results[i].reshape(-1)
    return tuple(results)


def solution(mesh):
    grid = (mesh.shape["fsdp"], mesh.shape["seq"])
    return jax.shard_map(
        fast_body if grid == (4, 8) else body,
        mesh=mesh,
        in_specs=(
            P(("fsdp", "seq"), None),
            P(("fsdp", "seq"), None),
            P("fsdp", None),
            P(("fsdp", "seq"), None),
            P(("fsdp", "seq"), None),
            P(("fsdp", "seq"), None),
            P(("fsdp", "seq"), None),
            P(("fsdp", "seq"), None),
            P(None, ("fsdp", "seq")),
            P("seq"),
            P(("fsdp", "seq"), None),
            P(("fsdp", "seq"), None),
            P(("fsdp", "seq"), None),
            P(("fsdp", "seq"), None),
            P(("fsdp", "seq"), None),
            P(None, ("fsdp", "seq")),
            P("seq"),
            P(("fsdp", "seq"), None),
            P(("fsdp", "seq"), None),
            P(("fsdp", "seq"), None),
            P(("fsdp", "seq"), None),
            P(("fsdp", "seq"), None),
            P(None, ("fsdp", "seq")),
            P("seq"),
        ),
        out_specs=(
            P(("fsdp", "seq"), None),
            P(("fsdp", "seq"), None),
            P(),
            P(("fsdp", "seq"), None),
            P(("fsdp", "seq"), None),
            P(("fsdp", "seq"), None),
            P(("fsdp", "seq"), None),
            P(("fsdp", "seq"), None),
            P(None, ("fsdp", "seq")),
            P("seq"),
            P(("fsdp", "seq"), None),
            P(("fsdp", "seq"), None),
            P(("fsdp", "seq"), None),
            P(("fsdp", "seq"), None),
            P(("fsdp", "seq"), None),
            P(None, ("fsdp", "seq")),
            P("seq"),
            P(("fsdp", "seq"), None),
            P(("fsdp", "seq"), None),
            P(("fsdp", "seq"), None),
            P(("fsdp", "seq"), None),
            P(("fsdp", "seq"), None),
            P(None, ("fsdp", "seq")),
            P("seq"),
            P(None, ("fsdp", "seq")),
        ),
        check_vma=False,
    )
```

```python
import math

import jax
import jax.numpy as jnp
from jax import lax
from jax.experimental import pallas as pl
from jax.experimental.pallas import tpu as pltpu
from jax.sharding import PartitionSpec as P

D = 768
HQ = 12
HD = 64
ROT_DIMS = 16
FF = 3072
KEY_BLOCK = 512
STEP = 10
F32 = jnp.float32
BF16 = jnp.bfloat16


NORM_EPS = 1e-05
MASKED = -1e30
CLIP_NORM = 1.0
BETA_ONE = 0.9
BETA_TWO = 0.999
ADAM_EPS = 1e-08
MATRIX_DECAY = 0.1
MATRIX_RATE = 0.1
VECTOR_RATE = 0.3


def layer_norm(tensor, gain_row, shift_row):
    centre = tensor - jnp.mean(tensor, -1, keepdims=True)
    spread = jnp.mean(centre * centre, -1, keepdims=True)
    return centre * lax.rsqrt(spread + NORM_EPS) * gain_row + shift_row


def rotary_tables(places):
    half_steps = jnp.arange(ROT_DIMS // 2, dtype=jnp.float32)
    inverse = jnp.exp(half_steps * (-2.0 * math.log(10000.0) / ROT_DIMS))
    angles = places.astype(jnp.float32)[:, None] * (0.25 * inverse)[None, :]
    angles = jnp.concatenate([angles, angles], 1)
    return (jnp.cos(angles), jnp.sin(angles))


def rotate(tensor, cosine, sine_table):
    rotary_part = tensor[..., :ROT_DIMS]
    lower_half = rotary_part[..., : ROT_DIMS // 2]
    upper_half = rotary_part[..., ROT_DIMS // 2 :]
    turned = jnp.concatenate([-upper_half, lower_half], -1)
    return jnp.concatenate([rotary_part * cosine + turned * sine_table, tensor[..., ROT_DIMS:]], -1)


def adamw(master, clipped, first_old, second_old, step_rate, decay_rate):
    first_new = BETA_ONE * first_old + (1.0 - BETA_ONE) * clipped
    second_new = BETA_TWO * second_old + (1.0 - BETA_TWO) * clipped * clipped
    ascent = (
        first_new
        / (1.0 - BETA_ONE**STEP)
        / (jnp.sqrt(second_new / (1.0 - BETA_TWO**STEP)) + ADAM_EPS)
    )
    return (master - step_rate * (ascent + decay_rate * master), first_new, second_new)


def gelu_exact(tensor):
    return jax.nn.gelu(tensor, approximate=False)


def across_tokens(left_side, right_side):
    return lax.dot_general(
        left_side, right_side, (((0,), (0,)), ((), ())), preferred_element_type=jnp.float32
    )


def against(left_side, right_side):
    return lax.dot_general(
        left_side, right_side, (((1,), (1,)), ((), ())), preferred_element_type=jnp.float32
    )


def masked_scores(query_rows, row_places, key_block, key_places):
    scores = against(query_rows, key_block) * HD ** (-0.5)
    return jnp.where(key_places[None, :] <= row_places[:, None], scores, MASKED)


def body(
    inputs,
    cotangent,
    span_order,
    query_weight,
    keyval_weight,
    output_weight,
    up_weight,
    down_weight,
    vectors,
    kv_bias,
    first_query,
    first_keyval,
    first_output,
    first_up,
    first_down,
    first_vectors,
    first_kv_bias,
    second_query,
    second_keyval,
    second_output,
    second_up,
    second_down,
    second_vectors,
    second_kv_bias,
):
    tok_rows = inputs.shape[0]
    seq_count = lax.axis_size("seq")
    seq_rank = lax.axis_index("seq")
    order_row = span_order[0]
    token_steps = jnp.arange(tok_rows, dtype=jnp.int32)
    all_places = (order_row[:, None] * tok_rows + token_steps[None, :]).reshape(
        seq_count * tok_rows
    )
    own_span = jnp.sum(jnp.where(jnp.arange(seq_count, dtype=jnp.int32) == seq_rank, order_row, 0))
    own_places = own_span * tok_rows + token_steps
    query_rows_count = tok_rows * HQ
    query_full, keyval_full, output_full, up_full, down_full, vector_full = (
        lax.all_gather(query_weight.astype(jnp.bfloat16), ("fsdp", "seq"), axis=0, tiled=True),
        lax.all_gather(keyval_weight.astype(jnp.bfloat16), ("fsdp", "seq"), axis=0, tiled=True),
        lax.all_gather(output_weight.astype(jnp.bfloat16), ("fsdp", "seq"), axis=0, tiled=True),
        lax.all_gather(up_weight.astype(jnp.bfloat16), ("fsdp", "seq"), axis=0, tiled=True),
        lax.all_gather(down_weight.astype(jnp.bfloat16), ("fsdp", "seq"), axis=0, tiled=True),
        lax.all_gather(vectors.astype(jnp.bfloat16), ("fsdp", "seq"), axis=1, tiled=True),
    )
    kv_shift = lax.all_gather(kv_bias.astype(jnp.bfloat16), "seq", axis=0, tiled=True).astype(
        jnp.float32
    )
    gains = vector_full.astype(jnp.float32)
    states = inputs.astype(jnp.float32)
    normed_one = layer_norm(states, gains[0], gains[1])
    normed_low = normed_one.astype(jnp.bfloat16)
    query_pre = jnp.dot(normed_low, query_full, preferred_element_type=jnp.float32) + gains[4]
    keyval_pre = jnp.dot(normed_low, keyval_full, preferred_element_type=jnp.float32) + kv_shift
    cosine, sine_table = rotary_tables(own_places)

    def turn_queries(tensor):
        return rotate(tensor.reshape(tok_rows, HQ, HD), cosine[:, None, :], sine_table[:, None, :])

    def turn_keys(tensor):
        return jnp.concatenate([rotate(tensor[:, :HD], cosine, sine_table), tensor[:, HD:]], 1)

    query_rows = turn_queries(query_pre).astype(jnp.bfloat16).reshape(query_rows_count, HD)
    local_pairs = turn_keys(keyval_pre).astype(jnp.bfloat16)
    row_places = jnp.broadcast_to(own_places[:, None], (tok_rows, HQ)).reshape(query_rows_count)
    all_pairs = lax.all_gather(local_pairs, "seq", axis=0, tiled=True)
    block_count = all_pairs.shape[0] // KEY_BLOCK
    place_blocks = all_places.reshape(block_count, KEY_BLOCK)

    def lse_step(carry_pair, block_pair):
        running_top, running_total = carry_pair
        pair_block, key_places = block_pair
        scores = masked_scores(query_rows, row_places, pair_block[:, :HD], key_places)
        new_top = jnp.maximum(running_top, jnp.max(scores, 1, keepdims=True))
        running_total = running_total * jnp.exp(running_top - new_top) + jnp.sum(
            jnp.exp(scores - new_top), 1, keepdims=True
        )
        return ((new_top, running_total), None)

    start_carry = (
        jnp.full((query_rows_count, 1), MASKED, jnp.float32),
        jnp.zeros((query_rows_count, 1), jnp.float32),
    )
    (row_top, row_total), _ = lax.scan(
        lse_step, start_carry, (all_pairs.reshape(block_count, KEY_BLOCK, 2 * HD), place_blocks)
    )
    log_total = row_top + jnp.log(row_total)

    def mix_step(mixed_acc, block_pair):
        pair_block, key_places = block_pair
        probs_low = jnp.exp(
            masked_scores(query_rows, row_places, pair_block[:, :HD], key_places) - log_total
        ).astype(jnp.bfloat16)
        return (
            mixed_acc + jnp.dot(probs_low, pair_block[:, HD:], preferred_element_type=jnp.float32),
            None,
        )

    mixed, _ = lax.scan(
        mix_step,
        jnp.zeros((query_rows_count, HD), jnp.float32),
        (all_pairs.reshape(block_count, KEY_BLOCK, 2 * HD), place_blocks),
    )
    mixed_low = mixed.reshape(tok_rows, D).astype(jnp.bfloat16)
    attention_out = jnp.dot(mixed_low, output_full, preferred_element_type=jnp.float32) + gains[5]
    normed_two = layer_norm(states, gains[2], gains[3])
    normed_two_low = normed_two.astype(jnp.bfloat16)
    lifted = jnp.dot(normed_two_low, up_full, preferred_element_type=jnp.float32) + gains[
        7:
    ].reshape(FF)
    active_low = gelu_exact(lifted).astype(jnp.bfloat16)
    block_output = (
        states
        + attention_out
        + jnp.dot(active_low, down_full, preferred_element_type=jnp.float32)
        + gains[6]
    ).astype(jnp.bfloat16)
    back_rows = cotangent.astype(jnp.float32)
    query_back, keyval_back, output_back, up_back, down_back = (
        lax.all_gather(query_weight.astype(jnp.bfloat16), ("fsdp", "seq"), axis=0, tiled=True),
        lax.all_gather(keyval_weight.astype(jnp.bfloat16), ("fsdp", "seq"), axis=0, tiled=True),
        lax.all_gather(output_weight.astype(jnp.bfloat16), ("fsdp", "seq"), axis=0, tiled=True),
        lax.all_gather(up_weight.astype(jnp.bfloat16), ("fsdp", "seq"), axis=0, tiled=True),
        lax.all_gather(down_weight.astype(jnp.bfloat16), ("fsdp", "seq"), axis=0, tiled=True),
    )
    grad_down = across_tokens(active_low, cotangent)
    grad_output = across_tokens(mixed_low, cotangent)
    out_bias_grad = jnp.sum(back_rows, 0)
    active_grad = against(cotangent, down_back)
    _, gelu_pull = jax.vjp(gelu_exact, lifted)
    (lifted_grad,) = gelu_pull(active_grad)
    lifted_low = lifted_grad.astype(jnp.bfloat16)
    grad_up = across_tokens(normed_two_low, lifted_low)
    normed_two_grad = against(lifted_low, up_back)
    mixed_grad = against(cotangent, output_back).astype(jnp.bfloat16).reshape(query_rows_count, HD)
    row_delta = jnp.sum(mixed_grad.astype(jnp.float32) * mixed, 1, keepdims=True)
    pairs_back = lax.all_gather(local_pairs, "seq", axis=0, tiled=True)

    def grad_step(query_acc, block_pair):
        pair_block, key_places = block_pair
        key_block = pair_block[:, :HD]
        probs = jnp.exp(masked_scores(query_rows, row_places, key_block, key_places) - log_total)
        prob_grad = against(mixed_grad, pair_block[:, HD:])
        score_low = (probs * (prob_grad - row_delta)).astype(jnp.bfloat16)
        query_acc = query_acc + jnp.dot(score_low, key_block, preferred_element_type=jnp.float32)
        key_grad = across_tokens(score_low, query_rows) * HD ** (-0.5)
        value_grad = across_tokens(probs.astype(jnp.bfloat16), mixed_grad)
        return (query_acc, jnp.concatenate([key_grad, value_grad], 1))

    query_sum, pair_grads = lax.scan(
        grad_step,
        jnp.zeros((query_rows_count, HD), jnp.float32),
        (pairs_back.reshape(block_count, KEY_BLOCK, 2 * HD), place_blocks),
    )
    query_rot_grad = (query_sum * HD ** (-0.5)).reshape(tok_rows, HQ, HD)
    own_pair_grad = lax.psum_scatter(
        pair_grads.reshape(block_count * KEY_BLOCK, 2 * HD).astype(jnp.bfloat16),
        "seq",
        scatter_dimension=0,
        tiled=True,
    ).astype(jnp.float32)
    _, key_pull = jax.vjp(turn_keys, keyval_pre)
    (keyval_grad,) = key_pull(own_pair_grad)
    keyval_low = keyval_grad.astype(jnp.bfloat16)
    _, query_pull = jax.vjp(turn_queries, query_pre)
    (query_pre_grad,) = query_pull(query_rot_grad)
    query_low = query_pre_grad.astype(jnp.bfloat16)
    grad_query = across_tokens(normed_low, query_low)
    grad_keyval = across_tokens(normed_low, keyval_low)
    kv_bias_part = jnp.sum(keyval_low.astype(jnp.float32), 0)
    normed_one_grad = against(query_low, query_back) + against(keyval_low, keyval_back)
    _, first_pull = jax.vjp(layer_norm, states, gains[0], gains[1])
    input_one, gain_one_grad, shift_one_grad = first_pull(normed_one_grad)
    _, second_pull = jax.vjp(layer_norm, states, gains[2], gains[3])
    input_two, gain_two_grad, shift_two_grad = second_pull(normed_two_grad)
    input_grad = back_rows + input_one + input_two
    vector_grad = jnp.concatenate(
        [
            jnp.stack(
                [
                    gain_one_grad,
                    shift_one_grad,
                    gain_two_grad,
                    shift_two_grad,
                    jnp.sum(query_low.astype(jnp.float32), 0),
                    out_bias_grad,
                    out_bias_grad,
                ]
            ),
            jnp.sum(lifted_low.astype(jnp.float32), 0).reshape(FF // D, D),
        ],
        0,
    )
    reduced = (
        lax.psum_scatter(grad_query, ("fsdp", "seq"), scatter_dimension=0, tiled=True),
        lax.psum_scatter(grad_keyval, ("fsdp", "seq"), scatter_dimension=0, tiled=True),
        lax.psum_scatter(grad_output, ("fsdp", "seq"), scatter_dimension=0, tiled=True),
        lax.psum_scatter(grad_up, ("fsdp", "seq"), scatter_dimension=0, tiled=True),
        lax.psum_scatter(grad_down, ("fsdp", "seq"), scatter_dimension=0, tiled=True),
        lax.psum_scatter(vector_grad, ("fsdp", "seq"), scatter_dimension=1, tiled=True),
    )
    reduced = tuple(reduced)
    local_squares = sum((jnp.sum(gradient * gradient) for gradient in reduced))
    global_squares, kv_bias_total = lax.psum((local_squares, kv_bias_part), ("fsdp", "seq"))
    grad_norm = jnp.sqrt(global_squares + jnp.sum(kv_bias_total * kv_bias_total))
    piece_width = kv_bias.shape[0]
    kv_bias_grad = lax.dynamic_slice_in_dim(kv_bias_total, seq_rank * piece_width, piece_width)
    factor = jnp.minimum(1.0, CLIP_NORM / (grad_norm + 1e-06))
    masters = (query_weight, keyval_weight, output_weight, up_weight, down_weight, vectors, kv_bias)
    all_grads = reduced + (kv_bias_grad,)
    firsts = (
        first_query,
        first_keyval,
        first_output,
        first_up,
        first_down,
        first_vectors,
        first_kv_bias,
    )
    seconds = (
        second_query,
        second_keyval,
        second_output,
        second_up,
        second_down,
        second_vectors,
        second_kv_bias,
    )
    step_rates = (MATRIX_RATE,) * 5 + (VECTOR_RATE, VECTOR_RATE)
    decays = (MATRIX_DECAY,) * 5 + (0.0, 0.0)
    updated = [
        adamw(master, gradient * factor, first_old, second_old, step_rate, decay_rate)
        for master, gradient, first_old, second_old, step_rate, decay_rate in zip(
            masters, all_grads, firsts, seconds, step_rates, decays
        )
    ]
    residual_bias_grads = (reduced[5] * factor)[5:7]
    return (
        block_output,
        input_grad,
        grad_norm,
        updated[0][0],
        updated[1][0],
        updated[2][0],
        updated[3][0],
        updated[4][0],
        updated[5][0],
        updated[6][0],
        updated[0][1],
        updated[1][1],
        updated[2][1],
        updated[3][1],
        updated[4][1],
        updated[5][1],
        updated[6][1],
        updated[0][2],
        updated[1][2],
        updated[2][2],
        updated[3][2],
        updated[4][2],
        updated[5][2],
        updated[6][2],
        residual_bias_grads,
    )


def dot_nn(left, right):
    return lax.dot_general(left, right, (((1,), (0,)), ((), ())), preferred_element_type=F32)


def dot_nt(left, right):
    return lax.dot_general(left, right, (((1,), (1,)), ((), ())), preferred_element_type=F32)


def dot_tn(left, right):
    return lax.dot_general(left, right, (((0,), (0,)), ((), ())), preferred_element_type=F32)


def normalise(rows):
    centre = rows - jnp.mean(rows, -1, keepdims=True)
    scale = lax.rsqrt(jnp.mean(centre * centre, -1, keepdims=True) + NORM_EPS)
    return centre * scale, scale


def norm_back(grad, hat, scale, gain):
    inner = grad * gain
    return scale * (
        inner
        - jnp.mean(inner, -1, keepdims=True)
        - hat * jnp.mean(inner * hat, -1, keepdims=True)
    )


class Copy:
    def __init__(self, copy):
        self.copy, self.started, self.received = copy, False, False

    def start(self):
        self.started = True
        self.copy.start()

    def wait_recv(self):
        self.received = True
        self.copy.wait_recv()

    def wait_send(self):
        self.copy.wait_send()


class Copies:
    def __init__(self, send_sems, recv_sems):
        self.send_sems, self.recv_sems, self.all = send_sems, recv_sems, []

    def make(self, source, target, device):
        index = len(self.all)
        copy = Copy(pltpu.make_async_remote_copy(
            src_ref=source,
            dst_ref=target,
            send_sem=self.send_sems.at[index],
            recv_sem=self.recv_sems.at[index],
            device_id=device,
            device_id_type=pl.DeviceIdType.MESH,
        ))
        self.all.append(copy)
        return copy

    def finish(self):
        for copy in self.all:
            if copy.started:
                if not copy.received:
                    copy.wait_recv()
                copy.wait_send()


def slab_rows(block, index):
    return pl.ds(pl.multiple_of((block * 8 + index) * 24, 8), 24)


class Panels:
    def __init__(self, ref, height):
        self.ref, self.height, self.count = ref, height, ref.shape[0] // height

    def rows(self, panel, block, index):
        return pl.ds(pl.multiple_of(panel * self.height + (block * 8 + index) * 24, 8), 24)

    def get(self, block, index):
        parts = [self.ref[self.rows(p, block, index), :] for p in range(self.count)]
        return parts[0] if self.count == 1 else jnp.concatenate(parts, 1)

    def put(self, block, index, value):
        for p in range(self.count):
            self.ref[self.rows(p, block, index), :] = value[:, p * 256 : p * 256 + 256]


N_COPIES = 150
QO = 1536


def layer_kernel(
    span, x, cot, qw, kw, ow, uw, dw, vec, kvb,
    bo, ig, g_qo, g_vp, g_up, g_dn, g_small,
    KW, Q, O, U, Dn, X, C, KV, ub, WQ, WKV, WO, WU, gains, vsq,
    n1, hat1, scale1, N2, act, dl, OP, NP,
    qz, doz, doT, kvT, bias, sbuf, mixT, dqT, dkv,
    GP, GU, GD, vg,
    SK1, RK1, SK2, RK2,
    RO1, SO2, RO2, RN1, SN2, RN2,
    SQ1, RQ1, SQ2, RQ2, SQ3, RQ3, SQ4, RQ4,
    SP1, RP1, SP2, RP2, SP3, RP3, SP4, RP4,
    SU1, RU1, SU2, RU2, SU3, RU3,
    SD1, RD1, SD2, RD2,
    NS1, NS2,
    send_sems, recv_sems,
):
    tok = x.shape[0]
    f = lax.axis_index("fsdp")
    s = lax.axis_index("seq")
    z = lax.div(s, 2)
    y = lax.rem(s, 2)
    yo = 1 - y
    fc = f + 1 - 2 * lax.rem(f, 2)
    fx = lax.rem(f + 2, 4)
    fd = 3 - f
    zk = (z, z + 1 - 2 * lax.rem(z, 2), lax.rem(z + 2, 4), 3 - z)
    dev_c, dev_x, dev_d = (fc, s), (fx, s), (fd, s)
    dev_y = (f, z * 2 + yo)
    dev_z = tuple((f, zz * 2 + y) for zz in zk)
    dev_zy = tuple((f, zz * 2 + yo) for zz in zk)
    fsdp_devs = (dev_c, dev_x, dev_d)
    seq_devs = dev_z[1:] + dev_zy
    far = (1, 2, 3)

    copies = Copies(send_sems, recv_sems)
    make = copies.make

    def start(*wanted):
        for copy in wanted:
            copy.start()

    def arrive(*wanted):
        for copy in wanted:
            copy.wait_recv()

    def seq_gather(ref):
        to_z = [None] + [make(ref(z, y), ref(z, y), dev_z[k]) for k in far]
        to_y = [make(ref(zk[k], y), ref(zk[k], y), dev_y) for k in range(4)]
        return to_z, to_y

    w_z, w_y = seq_gather(lambda i, j: KW.at[f, i, j])
    q_z, q_y = seq_gather(lambda i, j: Q.at[f, i, j])
    o_z, o_y = seq_gather(lambda i, j: O.at[f, i, j])
    p_z, p_y = seq_gather(lambda i, j: O.at[fx, i, j])
    u_z, u_y = seq_gather(lambda i, j: U.at[i, j])
    d_z, d_y = seq_gather(lambda i, j: Dn.at[i, j])
    k_z, k_y = seq_gather(lambda i, j: KV.at[i, j])

    def fsdp_gather(ref):
        to_x = [make(ref(f, j), ref(f, j), dev_x) for j in (y, yo)]
        to_c = [make(ref(f, j), ref(f, j), dev_c) for j in (y, yo)]
        on_c = [make(ref(fx, j), ref(fx, j), dev_c) for j in (y, yo)]
        return to_x, to_c, on_c

    w_x, w_c, w_xc = fsdp_gather(lambda i, j: KW.at[i, :, j])
    q_x, q_c, q_xc = fsdp_gather(lambda i, j: Q.at[i, :, j])
    o_x = make(O.at[f, z, y], O.at[f, z, y], dev_x)
    o_c = [make(O.at[f, :, j], O.at[f, :, j], dev_c) for j in (y, yo)]
    p_c = [make(O.at[fx, :, j], O.at[fx, :, j], dev_c) for j in (y, yo)]

    def token_gather(ref):
        return (
            make(ref.at[f], ref.at[f], dev_x),
            make(ref.at[f], ref.at[f], dev_c),
            make(ref.at[fx], ref.at[fx], dev_c),
        )

    x_x, x_c, x_xc = token_gather(X)
    c_x, c_c, c_xc = token_gather(C)
    u_f = [make(ub.at[g], U.at[z, y, f], dev) for g, dev in zip((fc, fx, fd), fsdp_devs)]

    rk1 = make(SK1, RK1, dev_y)
    rk2 = [make(SK2.at[k], RK2.at[k], dev_z[k + 1]) for k in range(3)]
    out_c = [make(OP.at[g], RO1.at[i], dev_c) for i, g in enumerate((fc, fd))]
    out_x = make(SO2, RO2, dev_x)
    nrm_c = [make(NP.at[g], RN1.at[i], dev_c) for i, g in enumerate((fc, fd))]
    nrm_x = make(SN2, RN2, dev_x)

    def full_scatter(S1, R1, S2, R2, S3, R3, S4, R4):
        return (
            make(S1, R1, dev_c),
            make(S2, R2, dev_x),
            make(S3, R3, dev_y),
            [make(S4.at[k], R4.at[k], dev_z[k + 1]) for k in range(3)],
        )

    q_sc = full_scatter(SQ1, RQ1, SQ2, RQ2, SQ3, RQ3, SQ4, RQ4)
    p_sc = full_scatter(SP1, RP1, SP2, RP2, SP3, RP3, SP4, RP4)
    su_y = [make(SU1.at[zz], RU1.at[zz], dev_y) for zz in zk]
    su_z = [make(SU2.at[k], RU2.at[k], dev_z[k + 1]) for k in range(3)]
    su_f = [make(SU3.at[g], RU3.at[i], dev) for i, (g, dev) in enumerate(zip((fc, fx, fd), fsdp_devs))]
    sd_y = [make(SD1.at[zz], RD1.at[zz], dev_y) for zz in zk]
    sd_z = [make(SD2.at[k], RD2.at[k], dev_z[k + 1]) for k in range(3)]
    n_f = [make(NS1.at[f], NS1.at[f], dev) for dev in fsdp_devs]
    n_s = [make(NS2.at[s], NS2.at[s], dev) for dev in seq_devs]

    barrier = pltpu.get_barrier_semaphore()
    for dev in fsdp_devs + seq_devs:
        pl.semaphore_signal(barrier, inc=1, device_id=dev, device_id_type=pl.DeviceIdType.MESH)

    vsq[...] = jnp.zeros((128, 128), F32)
    vsq[0:11, 0:24] = vec[...]
    vsq[11:12, 0:16] = kvb[...]
    KW[f, z, y, :, :128] = kw[...].astype(BF16)
    KW[f, z, y, :, 128:] = vsq[...].T[:24, :].astype(BF16)
    Q[f, z, y] = qw[...].astype(BF16)
    O[f, z, y] = ow[...].astype(BF16)
    for j in range(4):
        ub[j] = uw[:, j * D : (j + 1) * D].astype(BF16)
    U[z, y, f] = ub[f]
    Dn[z, y] = dw[...].astype(BF16)
    X[f] = x[...]
    C[f] = cot[...]

    pl.semaphore_wait(barrier, 10)
    start(w_z[1], w_z[2], w_z[3], w_y[0])
    start(o_x, q_z[1], q_z[2], q_z[3], q_y[0])
    start(o_z[1], o_z[2], o_z[3], o_y[0])
    start(*u_f)

    hat, scale = normalise(x[...].astype(F32))
    hat1[...] = hat
    scale1[...] = jnp.broadcast_to(scale, (tok, 128))
    own_span = span[0, s]
    lane = lax.broadcasted_iota(jnp.int32, (tok, 128), 1)
    spot = lax.broadcasted_iota(jnp.int32, (tok, 128), 0) + own_span * tok
    in_head = lax.rem(lane, 64)
    step = lax.rem(in_head, ROT_DIMS // 2).astype(F32)
    inverse = jnp.exp(step * (-2.0 * math.log(10000.0) / ROT_DIMS))
    angle = spot.astype(F32) * (0.25 * inverse)
    sine = jnp.sin(angle)
    cosine = jnp.where(in_head < ROT_DIMS, jnp.cos(angle), 1.0)
    sine_low = jnp.where(in_head < ROT_DIMS // 2, sine, 0.0)
    sine_high = jnp.where((in_head >= ROT_DIMS // 2) & (in_head < ROT_DIMS), sine, 0.0)
    key_lane = lane < 64
    key_cos = jnp.where(key_lane, cosine, 1.0)
    key_low = jnp.where(key_lane, sine_low, 0.0)
    key_high = jnp.where(key_lane, sine_high, 0.0)

    def turn(block, cos_t, low_t, high_t):
        up = pltpu.roll(block, 120, 1)
        down = pltpu.roll(block, 8, 1)
        return block * cos_t - up * low_t + down * high_t

    def turn_back(block, cos_t, low_t, high_t):
        up = pltpu.roll(block, 120, 1)
        down = pltpu.roll(block, 8, 1)
        return block * cos_t + up * low_t - down * high_t

    for k in far:
        arrive(w_z[k])
        start(w_y[k])
    start(w_x[0], w_c[0])
    arrive(o_x)
    start(p_z[1], p_z[2], p_z[3], p_y[0])
    for k in far:
        arrive(q_z[k])
        start(q_y[k])
    start(q_x[0], q_c[0])
    arrive(*w_y)
    start(w_x[1], w_c[1])
    for k in far:
        arrive(o_z[k])
        start(o_y[k])
    start(o_c[0])
    arrive(w_x[0])
    start(w_xc[0])
    arrive(w_x[1])
    start(w_xc[1])
    for k in far:
        arrive(p_z[k])
        start(p_y[k])
    start(p_c[0])
    arrive(*q_y)
    start(q_x[1], q_c[1])
    arrive(*w_c, *w_xc)

    slabs = [KW[g, i, j].astype(F32) for g in range(4) for i in range(4) for j in range(2)]
    for i in range(16):
        pair = jnp.concatenate([slabs[2 * i][:, :128], slabs[2 * i + 1][:, :128]], 0)
        WKV[i * 48 : (i + 1) * 48, :] = pair.astype(BF16)
    gains[...] = jnp.concatenate([slab[:, 128:] for slab in slabs], 0).T
    vsq[...] = jnp.concatenate([slab[:16, 128:] for slab in slabs[:8]], 0).T
    kv_shift = vsq[11:12, :]
    n1[...] = (hat * gains[0:1, :] + gains[1:2, :]).astype(BF16)
    kv_pre = dot_nn(n1[...], WKV[...]) + kv_shift
    KV[z, y] = turn(kv_pre, key_cos, key_low, key_high).astype(BF16)
    start(k_z[1], k_z[2], k_z[3], k_y[0])
    arrive(q_x[0])
    start(q_xc[0])
    arrive(*u_f)
    start(d_z[1], d_z[2], d_z[3], d_y[0])
    vg[...] = jnp.zeros((128, D), F32)
    csum = jnp.sum(cot[...].astype(F32), 0, keepdims=True)
    vg[5:6, :] = csum
    vg[6:7, :] = csum
    key_iota = lax.broadcasted_iota(jnp.int32, (tok, tok), 0)
    row_iota = lax.broadcasted_iota(jnp.int32, (tok, tok), 1) + own_span * tok
    for i in range(8):
        bias[i * tok : (i + 1) * tok, :] = jnp.where(
            key_iota + span[0, i] * tok <= row_iota, 0.0, MASKED
        ).astype(F32)
    dkv[...] = jnp.zeros((8 * tok, 128), F32)
    arrive(*o_y)
    start(o_c[1])
    arrive(*p_y)
    start(p_c[1])
    for k in far:
        arrive(k_z[k])
        start(k_y[k])
    arrive(q_x[1])
    start(q_xc[1])
    start(x_x, c_x, x_c, c_c)
    start(u_z[1], u_z[2], u_z[3], u_y[0])
    arrive(*q_c, *q_xc)

    def join(ref, whole):
        def put(i, carry):
            g = lax.div(i, 4)
            zz = lax.rem(i, 4)
            pair = jnp.concatenate([ref[g, zz, 0].astype(F32), ref[g, zz, 1].astype(F32)], 0)
            whole[pl.ds(pl.multiple_of(i * 48, 16), 48), :] = pair.astype(BF16)
            return carry

        lax.fori_loop(0, 16, put, 0)

    join(Q, WQ)
    q_pre = dot_nn(n1[...], WQ[...]) + gains[4:5, :]
    gap = jnp.zeros((tok, 64), BF16)
    for j in range(6):
        cols = slice(j * 128, j * 128 + 128)
        turned = turn(q_pre[:, cols], cosine, sine_low, sine_high).astype(BF16).astype(F32)
        turned = (turned * HD ** (-0.5)).astype(BF16)
        qz[2 * j] = jnp.concatenate([turned[:, :64], gap], 1)
        qz[2 * j + 1] = jnp.concatenate([turned[:, 64:], gap], 1)
    arrive(*o_c, *p_c)
    join(O, WO)
    mixed_back = dot_nt(cot[...], WO[...]).astype(BF16)
    for j in range(6):
        pair = mixed_back[:, j * 128 : j * 128 + 128]
        doz[2 * j] = jnp.concatenate([gap, pair[:, :64]], 1)
        doz[2 * j + 1] = jnp.concatenate([gap, pair[:, 64:]], 1)
    doT[...] = mixed_back.astype(F32).T.astype(BF16).reshape(HQ, HD, tok)
    arrive(*k_y)
    KVF = KV.reshape(8 * tok, 128)
    kvT[...] = KVF[...].astype(F32).T.astype(BF16)

    def attend(step_index):
        heads = [step_index * 2, step_index * 2 + 1]
        tops, shares, deltas = [], [], []
        for j, h in enumerate(heads):
            top = jnp.full((8, tok), MASKED, F32)
            for i in range(8):
                rows = pl.ds(i * tok, tok)
                held = pl.ds((j * 8 + i) * tok, tok)
                scores = dot_nt(KVF[rows, :], qz[h]) + bias[rows, :]
                sbuf[held, :] = scores
                top = jnp.maximum(top, jnp.max(scores.reshape(tok // 8, 8, tok), axis=0))
            tops.append(jnp.max(top, axis=0, keepdims=True))
        for j, h in enumerate(heads):
            total = jnp.zeros((8, tok), F32)
            for i in range(8):
                held = pl.ds((j * 8 + i) * tok, tok)
                weights = jnp.exp(sbuf[held, :] - tops[j])
                sbuf[held, :] = weights
                total = total + jnp.sum(weights.reshape(tok // 8, 8, tok), axis=0)
            shares.append(1.0 / jnp.sum(total, axis=0, keepdims=True))
        for j, h in enumerate(heads):
            acc = jnp.zeros((128, tok), F32)
            for i in range(8):
                rows = pl.ds(i * tok, tok)
                held = pl.ds((j * 8 + i) * tok, tok)
                probs = sbuf[held, :] * shares[j]
                probs_low = probs.astype(BF16)
                sbuf[held, :] = probs
                acc = acc + dot_nn(kvT[:, rows], probs_low)
                dkv[rows, :] += dot_nn(probs_low, doz[h])
            mixed = acc[64:, :]
            mixT[h] = mixed.astype(BF16)
            deltas.append(jnp.sum(mixed * doT[h].astype(F32), axis=0, keepdims=True))
        for j, h in enumerate(heads):
            acc = jnp.zeros((128, tok), F32)
            for i in range(8):
                rows = pl.ds(i * tok, tok)
                held = pl.ds((j * 8 + i) * tok, tok)
                prob_grad = dot_nt(KVF[rows, :], doz[h])
                score_low = (sbuf[held, :] * (prob_grad - deltas[j])).astype(BF16)
                acc = acc + dot_nn(kvT[:, rows], score_low)
                dkv[rows, :] += dot_nn(score_low, qz[h])
            dqT[h] = acc[:64, :] * HD ** (-0.5)

    def attend_all(first, last, meanwhile):
        def body_step(step_index, carry):
            for at, action in meanwhile:
                pl.when(step_index == at)(action)
            attend(step_index)
            return carry

        lax.fori_loop(first, last, body_step, 0)

    def down_on():
        for k in far:
            arrive(d_z[k])
            start(d_y[k])

    def up_on():
        for k in far:
            arrive(u_z[k])
            start(u_y[k])
        arrive(x_x)
        start(x_xc)

    def back_on():
        arrive(c_x)
        start(c_xc)

    attend_all(0, 3, ((0, down_on), (1, up_on), (2, back_on)))
    arrive(*d_y, *u_y, x_c, x_xc, c_c, c_xc)

    for g in range(4):
        for i in range(4):
            pair = jnp.concatenate([U[i, j, g].astype(F32) for j in range(2)], 0)
            WU[(g * 4 + i) * 48 : (g * 4 + i + 1) * 48, :] = pair.astype(BF16)
    WD = Dn.reshape(D, D)
    up_bias = gains[pl.ds(7 + f, 1), :]

    def token_block(t, carry):
        two_gain, two_shift, up_sum = carry
        rows = pl.ds(pl.multiple_of(t * tok, tok), tok)
        hat2, _ = normalise(X[t].astype(F32))
        low2 = (hat2 * gains[2:3, :] + gains[3:4, :]).astype(BF16)
        N2[rows, :] = low2
        back = C[t]
        sums = []
        for c in range(3):
            units = slice(c * 256, c * 256 + 256)
            lifted = dot_nn(low2, WU[:, units]) + up_bias[:, units]
            active_grad = dot_nt(back, WD[units, :])
            half = 0.5 + 0.5 * lax.erf(lifted * (0.5**0.5))
            act[rows, units] = (lifted * half).astype(BF16)
            bell = jnp.exp(lifted * lifted * -0.5) * (1.0 / math.sqrt(2.0 * math.pi))
            low = ((half + lifted * bell) * active_grad).astype(BF16)
            dl[rows, units] = low
            sums.append(jnp.sum(low.astype(F32), 0, keepdims=True))
        OP[t] = dot_nn(act[rows, :], WD[...]).astype(BF16)
        grad2 = dot_nt(dl[rows, :], WU[...])
        NP[t] = grad2.astype(BF16)
        return (
            two_gain + jnp.sum(grad2 * hat2, 0, keepdims=True),
            two_shift + jnp.sum(grad2, 0, keepdims=True),
            up_sum + jnp.concatenate(sums, 1),
        )

    zero_row = jnp.zeros((1, D), F32)
    two_gain, two_shift, up_sum = lax.fori_loop(0, 4, token_block, (zero_row,) * 3)
    vg[2:3, :] = two_gain
    vg[3:4, :] = two_shift
    vg[pl.ds(7 + f, 1), :] = up_sum
    start(*out_c, *nrm_c)
    CF = C.reshape(4 * tok, D)
    for c in range(3):
        units = slice(c * 256, c * 256 + 256)
        GD[units, :] = dot_tn(act[:, units], CF[...])
    for k in (1, 2, 3, 0):
        SD1[zk[k]] = GD[pl.ds(pl.multiple_of((zk[k] * 2 + yo) * 96, 8), 96), :].astype(BF16)
        start(sd_y[k])

    def tokens_to_x():
        arrive(*out_c, *nrm_c)
        SO2[...] = (OP[fx].astype(F32) + RO1[1].astype(F32)).astype(BF16)
        start(out_x)
        SN2[...] = (NP[fx].astype(F32) + RN1[1].astype(F32)).astype(BF16)
        start(nrm_x)

    def down_step(k):
        arrive(sd_y[k])
        rows = pl.ds(pl.multiple_of((zk[k] * 2 + y) * 96, 8), 96)
        total = GD[rows, :] + RD1[zk[k]].astype(F32)
        if k:
            SD2[k - 1] = total.astype(BF16)
            start(sd_z[k - 1])
        else:
            GD[rows, :] = total

    def up_step(k):
        arrive(su_y[k])
        for g in range(4):
            rows = slab_rows(g, zk[k] * 2 + y)
            total = GU[rows, :] + RU1[zk[k], g].astype(F32)
            if k:
                SU2[k - 1, g] = total.astype(BF16)
            else:
                GU[rows, :] = total
        if k:
            start(su_z[k - 1])

    def down_rest():
        down_step(3)
        down_step(0)

    attend_all(
        3, HQ // 2,
        ((3, tokens_to_x), (4, lambda: down_step(1)), (4, lambda: down_step(2)), (5, down_rest)),
    )

    for zz in range(4):
        SK1[zz] = dkv[pl.ds(pl.multiple_of((2 * zz + yo) * tok, 8), tok), :].astype(BF16)
    start(rk1)
    mix_low = mixT.reshape(D, tok)[...]
    for c in range(3):
        sbuf[(3 + c) * D : (4 + c) * D, :] = dot_nn(mix_low, cot[:, c * 256 : c * 256 + 256])
    q_back = dqT.reshape(D, tok)[...].T
    parts = []
    for j in range(6):
        parts.append(
            turn_back(q_back[:, j * 128 : j * 128 + 128], cosine, sine_low, sine_high).astype(BF16)
        )
    q_low = jnp.concatenate(parts, 1)
    vg[4:5, :] = jnp.sum(q_low.astype(F32), 0, keepdims=True)
    for c in range(3):
        sbuf[c * D : (c + 1) * D, :] = dot_tn(n1[...], q_low[:, c * 256 : c * 256 + 256])
    GQ = Panels(sbuf, D)
    GPP = Panels(GP, D)

    def scatter_c(G, S1, copy):
        def put(i, carry):
            for j, g in enumerate((fc, fd)):
                S1[j, i] = G.get(g, i).astype(S1.dtype)
            return carry

        lax.fori_loop(0, 8, put, 0)
        start(copy)

    def scatter_x(G, R1, S2, copies_):
        arrive(copies_[0])

        def put(i, carry):
            S2[i] = (G.get(fx, i) + R1[1, i].astype(F32)).astype(S2.dtype)
            G.put(f, i, G.get(f, i) + R1[0, i].astype(F32))
            return carry

        lax.fori_loop(0, 8, put, 0)
        start(copies_[1])

    def scatter_y(G, R2, S3, copies_):
        arrive(copies_[1])

        def put(i, carry):
            S3[i] = (G.get(f, 2 * i + yo) + R2[2 * i + yo].astype(F32)).astype(S3.dtype)
            G.put(f, 2 * i + y, G.get(f, 2 * i + y) + R2[2 * i + y].astype(F32))
            return carry

        lax.fori_loop(0, 4, put, 0)
        start(copies_[2])

    def scatter_z(G, R3, S4, copies_):
        arrive(copies_[2])
        for k in far:
            total = G.get(f, 2 * zk[k] + y) + R3[zk[k]].astype(F32)
            S4[k - 1] = total.astype(S4.dtype)
            start(copies_[3][k - 1])

    def scatter_end(G, R3, R4, copies_):
        total = G.get(f, 2 * z + y) + R3[z].astype(F32)
        for k in range(3):
            arrive(copies_[3][k])
            total = total + R4[k].astype(F32)
        return total

    scatter_c(GQ, SQ1, q_sc[0])
    arrive(rk1)
    for k in far:
        rows = pl.ds(pl.multiple_of((2 * zk[k] + y) * tok, 8), tok)
        SK2[k - 1] = (dkv[rows, :] + RK1[zk[k]].astype(F32)).astype(BF16)
        start(rk2[k - 1])
    for c in range(3):
        units = slice(c * 256, c * 256 + 256)
        GU[units, :] = dot_tn(N2[:, units], dl[...])
    for k in (1, 2, 3, 0):
        for g in range(4):
            SU1[zk[k], g] = GU[slab_rows(g, zk[k] * 2 + yo), :].astype(BF16)
        start(su_y[k])
    scatter_x(GQ, RQ1, SQ2, q_sc)
    grad1 = dot_nt(q_low, WQ[...])
    kv_back = dkv[pl.ds(pl.multiple_of((2 * z + y) * tok, 8), tok), :] + RK1[z].astype(F32)
    for k in range(3):
        arrive(rk2[k])
        kv_back = kv_back + RK2[k].astype(F32)
    kv_low = turn_back(kv_back, key_cos, key_low, key_high).astype(BF16)
    grad1 = grad1 + dot_nt(kv_low, WKV[...])
    vg[0:1, :] = jnp.sum(grad1 * hat1[...], 0, keepdims=True)
    vg[1:2, :] = jnp.sum(grad1, 0, keepdims=True)
    kv_sum = jnp.sum(kv_low.astype(F32), 0, keepdims=True)
    short = jnp.zeros((1, 8), F32)
    spread = jnp.concatenate(
        [part for i in range(8) for part in (kv_sum[:, i * 16 : i * 16 + 16], short)], 1
    )
    vg[11:12, :] = jnp.concatenate([spread] * 4, 1)
    GP[:, :128] = dot_tn(n1[...], kv_low)
    GP[:, 128:] = vg[...].T
    scatter_c(GPP, SP1, p_sc[0])
    up_step(1)

    rows = pl.ds(pl.multiple_of(s * 96, 8), 96)
    down_grad = GD[rows, :]
    for k in range(3):
        arrive(sd_z[k])
        down_grad = down_grad + RD2[k].astype(F32)
    g_dn[...] = down_grad
    scatter_x(GPP, RP1, SP2, p_sc)
    up_step(2)
    scatter_y(GQ, RQ2, SQ3, q_sc)
    up_step(3)

    mixed_rows = mix_low.astype(F32).T.astype(BF16)
    arrive(out_x)
    bo[...] = (
        x[...].astype(F32)
        + (dot_nn(mixed_rows, WO[...]) + gains[5:6, :])
        + (OP[f].astype(F32) + RO1[0].astype(F32) + RO2[...].astype(F32) + gains[6:7, :])
    ).astype(BF16)
    scatter_y(GPP, RP2, SP3, p_sc)
    up_step(0)
    scatter_z(GQ, RQ3, SQ4, q_sc)
    arrive(nrm_x)
    grad2 = NP[f].astype(F32) + RN1[0].astype(F32) + RN2[...].astype(F32)
    hat_rows = hat1[...]
    scale_rows = scale1[:, 0:1]
    ig[...] = (
        cot[...].astype(F32)
        + norm_back(grad1, hat_rows, scale_rows, gains[0:1, :])
        + norm_back(grad2, hat_rows, scale_rows, gains[2:3, :])
    )
    scatter_z(GPP, RP3, SP4, p_sc)
    arrive(*su_z)
    for g in range(4):
        total = GU[slab_rows(g, s), :]
        for k in range(3):
            total = total + RU2[k, g].astype(F32)
        g_up[g] = total
        SU3[g] = total.astype(BF16)
    start(*su_f)
    qo_grad = scatter_end(GQ, RQ3, RQ4, q_sc)
    g_qo[...] = qo_grad
    vp_grad = scatter_end(GPP, RP3, RP4, p_sc)
    g_vp[...] = vp_grad
    for i, g in enumerate((fc, fx, fd)):
        arrive(su_f[i])
        g_up[g] = RU3[i].astype(F32)

    def fold(values):
        return jnp.sum(jnp.sum(values * values, 0, keepdims=True), 1, keepdims=True)

    lanes = lax.broadcasted_iota(jnp.int32, (24, 256), 1)
    squares = fold(qo_grad) + fold(jnp.where(lanes == 128 + 11, 0.0, vp_grad)) + fold(g_dn[...])
    for g in range(4):
        squares = squares + fold(g_up[g])
    kv_rows = jnp.concatenate([vp_grad[:, 128:], jnp.zeros((104, 128), F32)], 0).T
    line = lax.broadcasted_iota(jnp.int32, (8, 128), 0)
    column = lax.broadcasted_iota(jnp.int32, (8, 128), 1)
    kv_line = jnp.where(column < 16, jnp.broadcast_to(kv_rows[11:12, :], (8, 128)), 0.0)
    NS1[f] = jnp.where(line == 0, squares, kv_line)
    start(*n_f)
    arrive(*n_f)
    kv_piece = NS1[0][1:2, :]
    chip = NS1[0] + NS1[1] + NS1[2] + NS1[3]
    part = chip[0:1, 0:1] + jnp.sum(kv_piece * kv_piece, 1, keepdims=True)
    NS2[s] = jnp.broadcast_to(part, (8, 128))
    start(*n_s)
    arrive(*n_s)
    everything = NS2[0]
    for i in range(1, 8):
        everything = everything + NS2[i]
    g_small[...] = jnp.where(line == 0, everything, jnp.broadcast_to(kv_piece, (8, 128)))
    copies.finish()


def update_kernel(
    small, g_qo, g_vp, g_up, g_dn, bo_in, ig_in,
    mq, mk, mo, mu, md, mv, mb,
    fq, fk, fo, fu, fdn, fv, fb,
    sq, sk, so, su, sd, sv, sb,
    bo, ig, norm,
    nmq, nmk, nmo, nmu, nmd, nmv, nmb,
    nfq, nfk, nfo, nfu, nfd, nfv, nfb,
    nsq, nsk, nso, nsu, nsd, nsv, nsb,
    residual,
):
    bo[...] = bo_in[...]
    ig[...] = ig_in[...]
    size = jnp.sqrt(small[0:1, 0:1])
    norm[...] = size
    factor = jnp.minimum(1.0, CLIP_NORM / (size + 1e-06))

    def update(grad, master, first, second, new_master, new_first, new_second, rate, decay):
        clipped = grad * factor
        values = adamw(master, clipped, first, second, rate, decay)
        for ref, value in zip((new_master, new_first, new_second), values):
            ref[...] = value

    rates = (MATRIX_RATE, MATRIX_DECAY)
    update(g_qo[:, :D], mq[...], fq[...], sq[...], nmq, nfq, nsq, *rates)
    update(g_qo[:, D:], mo[...], fo[...], so[...], nmo, nfo, nso, *rates)
    update(g_vp[:, :128], mk[...], fk[...], sk[...], nmk, nfk, nsk, *rates)
    for g in range(4):
        cols = slice(g * D, (g + 1) * D)
        update(
            g_up[g], mu[:, cols], fu[:, cols], su[:, cols],
            nmu.at[:, cols], nfu.at[:, cols], nsu.at[:, cols], *rates,
        )
    update(g_dn[...], md[...], fdn[...], sd[...], nmd, nfd, nsd, *rates)
    flipped = jnp.concatenate([g_vp[:, 128:], jnp.zeros((104, 128), F32)], 0).T
    vector_grad = flipped[:11, :24]
    update(vector_grad, mv[...], fv[...], sv[...], nmv, nfv, nsv, VECTOR_RATE, 0.0)
    residual[...] = flipped[5:7, :24] * factor
    update(small[1:2, :16], mb[...], fb[...], sb[...], nmb, nfb, nsb, VECTOR_RATE, 0.0)


def fast_body(
    inputs, cotangent, span_order,
    query_weight, keyval_weight, output_weight, up_weight, down_weight, vectors, kv_bias,
    *moments,
):
    tok = inputs.shape[0]
    vmem = pl.BlockSpec(memory_space=pltpu.VMEM)
    smem = pl.BlockSpec(memory_space=pltpu.SMEM)
    shape = jax.ShapeDtypeStruct
    V = pltpu.VMEM
    scratch = [
        V((4, 4, 2, 24, 256), BF16),
        V((4, 4, 2, 24, D), BF16),
        V((4, 4, 2, 24, D), BF16),
        V((4, 2, 4, 24, D), BF16),
        V((4, 2, 96, D), BF16),
        V((4, tok, D), BF16),
        V((4, tok, D), BF16),
        V((4, 2, tok, 128), BF16),
        V((4, 24, D), BF16),
        V((D, D), BF16),
        V((D, 128), BF16),
        V((D, D), BF16),
        V((D, D), BF16),
        V((128, D), F32),
        V((128, 128), F32),
        V((tok, D), BF16),
        V((tok, D), F32),
        V((tok, 128), F32),
        V((4 * tok, D), BF16),
        V((4 * tok, D), BF16),
        V((4 * tok, D), BF16),
        V((4, tok, D), BF16),
        V((4, tok, D), BF16),
        V((HQ, tok, 128), BF16),
        V((HQ, tok, 128), BF16),
        V((HQ, HD, tok), BF16),
        V((128, 8 * tok), BF16),
        V((8 * tok, tok), F32),
        V((QO // 256 * D, 256), F32),
        V((HQ, HD, tok), BF16),
        V((HQ, HD, tok), F32),
        V((8 * tok, 128), F32),
        V((D, 256), F32),
        V((D, D), F32),
        V((D, D), F32),
        V((128, D), F32),
        V((4, tok, 128), BF16), V((4, tok, 128), BF16),
        V((3, tok, 128), BF16), V((3, tok, 128), BF16),
        V((2, tok, D), BF16), V((tok, D), BF16), V((tok, D), BF16),
        V((2, tok, D), BF16), V((tok, D), BF16), V((tok, D), BF16),
    ]
    for width, kind in ((QO, BF16), (256, BF16)):
        for lead in ((2, 8), (8,), (4,), (3,)):
            scratch += [V(lead + (24, width), kind)] * 2
    scratch += [V((4, 4, 24, D), BF16)] * 2 + [V((3, 4, 24, D), BF16)] * 2
    scratch += [V((4, 24, D), BF16), V((3, 24, D), BF16)]
    scratch += [V((4, 96, D), BF16)] * 2 + [V((3, 96, D), BF16)] * 2
    scratch += [V((4, 8, 128), F32), V((8, 8, 128), F32)]
    scratch += [pltpu.SemaphoreType.DMA((N_COPIES,))] * 2
    kv_row = kv_bias.reshape(1, -1)
    bo, ig, g_qo, g_vp, g_up, g_dn, small = pl.pallas_call(
        layer_kernel,
        name="layer",
        out_shape=(
            shape((tok, D), BF16),
            shape((tok, D), F32),
            shape((24, QO), F32),
            shape((24, 256), F32),
            shape((4, 24, D), F32),
            shape((96, D), F32),
            shape((8, 128), F32),
        ),
        in_specs=[smem] + [vmem] * 9,
        out_specs=(vmem,) * 7,
        scratch_shapes=scratch,
        compiler_params=pltpu.CompilerParams(
            collective_id=0, has_side_effects=True, vmem_limit_bytes=62 * 2**20
        ),
    )(
        span_order, inputs, cotangent,
        query_weight, keyval_weight, output_weight, up_weight, down_weight, vectors, kv_row,
    )
    masters = (query_weight, keyval_weight, output_weight, up_weight, down_weight, vectors, kv_row)
    firsts = tuple(moments[:6]) + (moments[6].reshape(1, -1),)
    seconds = tuple(moments[7:13]) + (moments[13].reshape(1, -1),)
    state = [shape(a.shape, F32) for a in masters]
    operands = (small, g_qo, g_vp, g_up, g_dn, bo, ig) + masters + firsts + seconds
    outcomes = [shape((tok, D), BF16), shape((tok, D), F32), shape((1, 1), F32)]
    outcomes += state * 3 + [shape((2, vectors.shape[1]), F32)]

    def whole(a):
        return pl.BlockSpec(a.shape, lambda i: (0,) * len(a.shape))

    results = pl.pallas_call(
        update_kernel,
        name="update",
        grid=(1,),
        out_shape=outcomes,
        in_specs=[whole(a) for a in operands],
        out_specs=[whole(a) for a in outcomes],
        compiler_params=pltpu.CompilerParams(vmem_limit_bytes=62 * 2**20),
    )(*operands)
    results = list(results)
    results[2] = results[2].reshape(())
    for i in (9, 16, 23):
        results[i] = results[i].reshape(-1)
    return tuple(results)


def solution(mesh):
    grid = (mesh.shape["fsdp"], mesh.shape["seq"])
    return jax.shard_map(
        fast_body if grid == (4, 8) else body,
        mesh=mesh,
        in_specs=(
            P(("fsdp", "seq"), None),
            P(("fsdp", "seq"), None),
            P("fsdp", None),
            P(("fsdp", "seq"), None),
            P(("fsdp", "seq"), None),
            P(("fsdp", "seq"), None),
            P(("fsdp", "seq"), None),
            P(("fsdp", "seq"), None),
            P(None, ("fsdp", "seq")),
            P("seq"),
            P(("fsdp", "seq"), None),
            P(("fsdp", "seq"), None),
            P(("fsdp", "seq"), None),
            P(("fsdp", "seq"), None),
            P(("fsdp", "seq"), None),
            P(None, ("fsdp", "seq")),
            P("seq"),
            P(("fsdp", "seq"), None),
            P(("fsdp", "seq"), None),
            P(("fsdp", "seq"), None),
            P(("fsdp", "seq"), None),
            P(("fsdp", "seq"), None),
            P(None, ("fsdp", "seq")),
            P("seq"),
        ),
        out_specs=(
            P(("fsdp", "seq"), None),
            P(("fsdp", "seq"), None),
            P(),
            P(("fsdp", "seq"), None),
            P(("fsdp", "seq"), None),
            P(("fsdp", "seq"), None),
            P(("fsdp", "seq"), None),
            P(("fsdp", "seq"), None),
            P(None, ("fsdp", "seq")),
            P("seq"),
            P(("fsdp", "seq"), None),
            P(("fsdp", "seq"), None),
            P(("fsdp", "seq"), None),
            P(("fsdp", "seq"), None),
            P(("fsdp", "seq"), None),
            P(None, ("fsdp", "seq")),
            P("seq"),
            P(("fsdp", "seq"), None),
            P(("fsdp", "seq"), None),
            P(("fsdp", "seq"), None),
            P(("fsdp", "seq"), None),
            P(("fsdp", "seq"), None),
            P(None, ("fsdp", "seq")),
            P("seq"),
            P(None, ("fsdp", "seq")),
        ),
        check_vma=False,
    )
```

```python
import math

import jax
import jax.numpy as jnp
from jax import lax
from jax.experimental import pallas as pl
from jax.experimental.pallas import tpu as pltpu
from jax.sharding import PartitionSpec as P

D = 768
HQ = 12
HD = 64
ROT_DIMS = 16
FF = 3072
KEY_BLOCK = 512
STEP = 10
F32 = jnp.float32
BF16 = jnp.bfloat16


NORM_EPS = 1e-05
MASKED = -1e30
CLIP_NORM = 1.0
BETA_ONE = 0.9
BETA_TWO = 0.999
ADAM_EPS = 1e-08
MATRIX_DECAY = 0.1
MATRIX_RATE = 0.1
VECTOR_RATE = 0.3


def layer_norm(tensor, gain_row, shift_row):
    centre = tensor - jnp.mean(tensor, -1, keepdims=True)
    spread = jnp.mean(centre * centre, -1, keepdims=True)
    return centre * lax.rsqrt(spread + NORM_EPS) * gain_row + shift_row


def rotary_tables(places):
    half_steps = jnp.arange(ROT_DIMS // 2, dtype=jnp.float32)
    inverse = jnp.exp(half_steps * (-2.0 * math.log(10000.0) / ROT_DIMS))
    angles = places.astype(jnp.float32)[:, None] * (0.25 * inverse)[None, :]
    angles = jnp.concatenate([angles, angles], 1)
    return (jnp.cos(angles), jnp.sin(angles))


def rotate(tensor, cosine, sine_table):
    rotary_part = tensor[..., :ROT_DIMS]
    lower_half = rotary_part[..., : ROT_DIMS // 2]
    upper_half = rotary_part[..., ROT_DIMS // 2 :]
    turned = jnp.concatenate([-upper_half, lower_half], -1)
    return jnp.concatenate([rotary_part * cosine + turned * sine_table, tensor[..., ROT_DIMS:]], -1)


def adamw(master, clipped, first_old, second_old, step_rate, decay_rate):
    first_new = BETA_ONE * first_old + (1.0 - BETA_ONE) * clipped
    second_new = BETA_TWO * second_old + (1.0 - BETA_TWO) * clipped * clipped
    ascent = (
        first_new
        / (1.0 - BETA_ONE**STEP)
        / (jnp.sqrt(second_new / (1.0 - BETA_TWO**STEP)) + ADAM_EPS)
    )
    return (master - step_rate * (ascent + decay_rate * master), first_new, second_new)


def gelu_exact(tensor):
    return jax.nn.gelu(tensor, approximate=False)


def across_tokens(left_side, right_side):
    return lax.dot_general(
        left_side, right_side, (((0,), (0,)), ((), ())), preferred_element_type=jnp.float32
    )


def against(left_side, right_side):
    return lax.dot_general(
        left_side, right_side, (((1,), (1,)), ((), ())), preferred_element_type=jnp.float32
    )


def masked_scores(query_rows, row_places, key_block, key_places):
    scores = against(query_rows, key_block) * HD ** (-0.5)
    return jnp.where(key_places[None, :] <= row_places[:, None], scores, MASKED)


def body(
    inputs,
    cotangent,
    span_order,
    query_weight,
    keyval_weight,
    output_weight,
    up_weight,
    down_weight,
    vectors,
    kv_bias,
    first_query,
    first_keyval,
    first_output,
    first_up,
    first_down,
    first_vectors,
    first_kv_bias,
    second_query,
    second_keyval,
    second_output,
    second_up,
    second_down,
    second_vectors,
    second_kv_bias,
):
    tok_rows = inputs.shape[0]
    seq_count = lax.axis_size("seq")
    seq_rank = lax.axis_index("seq")
    order_row = span_order[0]
    token_steps = jnp.arange(tok_rows, dtype=jnp.int32)
    all_places = (order_row[:, None] * tok_rows + token_steps[None, :]).reshape(
        seq_count * tok_rows
    )
    own_span = jnp.sum(jnp.where(jnp.arange(seq_count, dtype=jnp.int32) == seq_rank, order_row, 0))
    own_places = own_span * tok_rows + token_steps
    query_rows_count = tok_rows * HQ
    query_full, keyval_full, output_full, up_full, down_full, vector_full = (
        lax.all_gather(query_weight.astype(jnp.bfloat16), ("fsdp", "seq"), axis=0, tiled=True),
        lax.all_gather(keyval_weight.astype(jnp.bfloat16), ("fsdp", "seq"), axis=0, tiled=True),
        lax.all_gather(output_weight.astype(jnp.bfloat16), ("fsdp", "seq"), axis=0, tiled=True),
        lax.all_gather(up_weight.astype(jnp.bfloat16), ("fsdp", "seq"), axis=0, tiled=True),
        lax.all_gather(down_weight.astype(jnp.bfloat16), ("fsdp", "seq"), axis=0, tiled=True),
        lax.all_gather(vectors.astype(jnp.bfloat16), ("fsdp", "seq"), axis=1, tiled=True),
    )
    kv_shift = lax.all_gather(kv_bias.astype(jnp.bfloat16), "seq", axis=0, tiled=True).astype(
        jnp.float32
    )
    gains = vector_full.astype(jnp.float32)
    states = inputs.astype(jnp.float32)
    normed_one = layer_norm(states, gains[0], gains[1])
    normed_low = normed_one.astype(jnp.bfloat16)
    query_pre = jnp.dot(normed_low, query_full, preferred_element_type=jnp.float32) + gains[4]
    keyval_pre = jnp.dot(normed_low, keyval_full, preferred_element_type=jnp.float32) + kv_shift
    cosine, sine_table = rotary_tables(own_places)

    def turn_queries(tensor):
        return rotate(tensor.reshape(tok_rows, HQ, HD), cosine[:, None, :], sine_table[:, None, :])

    def turn_keys(tensor):
        return jnp.concatenate([rotate(tensor[:, :HD], cosine, sine_table), tensor[:, HD:]], 1)

    query_rows = turn_queries(query_pre).astype(jnp.bfloat16).reshape(query_rows_count, HD)
    local_pairs = turn_keys(keyval_pre).astype(jnp.bfloat16)
    row_places = jnp.broadcast_to(own_places[:, None], (tok_rows, HQ)).reshape(query_rows_count)
    all_pairs = lax.all_gather(local_pairs, "seq", axis=0, tiled=True)
    block_count = all_pairs.shape[0] // KEY_BLOCK
    place_blocks = all_places.reshape(block_count, KEY_BLOCK)

    def lse_step(carry_pair, block_pair):
        running_top, running_total = carry_pair
        pair_block, key_places = block_pair
        scores = masked_scores(query_rows, row_places, pair_block[:, :HD], key_places)
        new_top = jnp.maximum(running_top, jnp.max(scores, 1, keepdims=True))
        running_total = running_total * jnp.exp(running_top - new_top) + jnp.sum(
            jnp.exp(scores - new_top), 1, keepdims=True
        )
        return ((new_top, running_total), None)

    start_carry = (
        jnp.full((query_rows_count, 1), MASKED, jnp.float32),
        jnp.zeros((query_rows_count, 1), jnp.float32),
    )
    (row_top, row_total), _ = lax.scan(
        lse_step, start_carry, (all_pairs.reshape(block_count, KEY_BLOCK, 2 * HD), place_blocks)
    )
    log_total = row_top + jnp.log(row_total)

    def mix_step(mixed_acc, block_pair):
        pair_block, key_places = block_pair
        probs_low = jnp.exp(
            masked_scores(query_rows, row_places, pair_block[:, :HD], key_places) - log_total
        ).astype(jnp.bfloat16)
        return (
            mixed_acc + jnp.dot(probs_low, pair_block[:, HD:], preferred_element_type=jnp.float32),
            None,
        )

    mixed, _ = lax.scan(
        mix_step,
        jnp.zeros((query_rows_count, HD), jnp.float32),
        (all_pairs.reshape(block_count, KEY_BLOCK, 2 * HD), place_blocks),
    )
    mixed_low = mixed.reshape(tok_rows, D).astype(jnp.bfloat16)
    attention_out = jnp.dot(mixed_low, output_full, preferred_element_type=jnp.float32) + gains[5]
    normed_two = layer_norm(states, gains[2], gains[3])
    normed_two_low = normed_two.astype(jnp.bfloat16)
    lifted = jnp.dot(normed_two_low, up_full, preferred_element_type=jnp.float32) + gains[
        7:
    ].reshape(FF)
    active_low = gelu_exact(lifted).astype(jnp.bfloat16)
    block_output = (
        states
        + attention_out
        + jnp.dot(active_low, down_full, preferred_element_type=jnp.float32)
        + gains[6]
    ).astype(jnp.bfloat16)
    back_rows = cotangent.astype(jnp.float32)
    query_back, keyval_back, output_back, up_back, down_back = (
        lax.all_gather(query_weight.astype(jnp.bfloat16), ("fsdp", "seq"), axis=0, tiled=True),
        lax.all_gather(keyval_weight.astype(jnp.bfloat16), ("fsdp", "seq"), axis=0, tiled=True),
        lax.all_gather(output_weight.astype(jnp.bfloat16), ("fsdp", "seq"), axis=0, tiled=True),
        lax.all_gather(up_weight.astype(jnp.bfloat16), ("fsdp", "seq"), axis=0, tiled=True),
        lax.all_gather(down_weight.astype(jnp.bfloat16), ("fsdp", "seq"), axis=0, tiled=True),
    )
    grad_down = across_tokens(active_low, cotangent)
    grad_output = across_tokens(mixed_low, cotangent)
    out_bias_grad = jnp.sum(back_rows, 0)
    active_grad = against(cotangent, down_back)
    _, gelu_pull = jax.vjp(gelu_exact, lifted)
    (lifted_grad,) = gelu_pull(active_grad)
    lifted_low = lifted_grad.astype(jnp.bfloat16)
    grad_up = across_tokens(normed_two_low, lifted_low)
    normed_two_grad = against(lifted_low, up_back)
    mixed_grad = against(cotangent, output_back).astype(jnp.bfloat16).reshape(query_rows_count, HD)
    row_delta = jnp.sum(mixed_grad.astype(jnp.float32) * mixed, 1, keepdims=True)
    pairs_back = lax.all_gather(local_pairs, "seq", axis=0, tiled=True)

    def grad_step(query_acc, block_pair):
        pair_block, key_places = block_pair
        key_block = pair_block[:, :HD]
        probs = jnp.exp(masked_scores(query_rows, row_places, key_block, key_places) - log_total)
        prob_grad = against(mixed_grad, pair_block[:, HD:])
        score_low = (probs * (prob_grad - row_delta)).astype(jnp.bfloat16)
        query_acc = query_acc + jnp.dot(score_low, key_block, preferred_element_type=jnp.float32)
        key_grad = across_tokens(score_low, query_rows) * HD ** (-0.5)
        value_grad = across_tokens(probs.astype(jnp.bfloat16), mixed_grad)
        return (query_acc, jnp.concatenate([key_grad, value_grad], 1))

    query_sum, pair_grads = lax.scan(
        grad_step,
        jnp.zeros((query_rows_count, HD), jnp.float32),
        (pairs_back.reshape(block_count, KEY_BLOCK, 2 * HD), place_blocks),
    )
    query_rot_grad = (query_sum * HD ** (-0.5)).reshape(tok_rows, HQ, HD)
    own_pair_grad = lax.psum_scatter(
        pair_grads.reshape(block_count * KEY_BLOCK, 2 * HD).astype(jnp.bfloat16),
        "seq",
        scatter_dimension=0,
        tiled=True,
    ).astype(jnp.float32)
    _, key_pull = jax.vjp(turn_keys, keyval_pre)
    (keyval_grad,) = key_pull(own_pair_grad)
    keyval_low = keyval_grad.astype(jnp.bfloat16)
    _, query_pull = jax.vjp(turn_queries, query_pre)
    (query_pre_grad,) = query_pull(query_rot_grad)
    query_low = query_pre_grad.astype(jnp.bfloat16)
    grad_query = across_tokens(normed_low, query_low)
    grad_keyval = across_tokens(normed_low, keyval_low)
    kv_bias_part = jnp.sum(keyval_low.astype(jnp.float32), 0)
    normed_one_grad = against(query_low, query_back) + against(keyval_low, keyval_back)
    _, first_pull = jax.vjp(layer_norm, states, gains[0], gains[1])
    input_one, gain_one_grad, shift_one_grad = first_pull(normed_one_grad)
    _, second_pull = jax.vjp(layer_norm, states, gains[2], gains[3])
    input_two, gain_two_grad, shift_two_grad = second_pull(normed_two_grad)
    input_grad = back_rows + input_one + input_two
    vector_grad = jnp.concatenate(
        [
            jnp.stack(
                [
                    gain_one_grad,
                    shift_one_grad,
                    gain_two_grad,
                    shift_two_grad,
                    jnp.sum(query_low.astype(jnp.float32), 0),
                    out_bias_grad,
                    out_bias_grad,
                ]
            ),
            jnp.sum(lifted_low.astype(jnp.float32), 0).reshape(FF // D, D),
        ],
        0,
    )
    reduced = (
        lax.psum_scatter(grad_query, ("fsdp", "seq"), scatter_dimension=0, tiled=True),
        lax.psum_scatter(grad_keyval, ("fsdp", "seq"), scatter_dimension=0, tiled=True),
        lax.psum_scatter(grad_output, ("fsdp", "seq"), scatter_dimension=0, tiled=True),
        lax.psum_scatter(grad_up, ("fsdp", "seq"), scatter_dimension=0, tiled=True),
        lax.psum_scatter(grad_down, ("fsdp", "seq"), scatter_dimension=0, tiled=True),
        lax.psum_scatter(vector_grad, ("fsdp", "seq"), scatter_dimension=1, tiled=True),
    )
    reduced = tuple(reduced)
    local_squares = sum((jnp.sum(gradient * gradient) for gradient in reduced))
    global_squares, kv_bias_total = lax.psum((local_squares, kv_bias_part), ("fsdp", "seq"))
    grad_norm = jnp.sqrt(global_squares + jnp.sum(kv_bias_total * kv_bias_total))
    piece_width = kv_bias.shape[0]
    kv_bias_grad = lax.dynamic_slice_in_dim(kv_bias_total, seq_rank * piece_width, piece_width)
    factor = jnp.minimum(1.0, CLIP_NORM / (grad_norm + 1e-06))
    masters = (query_weight, keyval_weight, output_weight, up_weight, down_weight, vectors, kv_bias)
    all_grads = reduced + (kv_bias_grad,)
    firsts = (
        first_query,
        first_keyval,
        first_output,
        first_up,
        first_down,
        first_vectors,
        first_kv_bias,
    )
    seconds = (
        second_query,
        second_keyval,
        second_output,
        second_up,
        second_down,
        second_vectors,
        second_kv_bias,
    )
    step_rates = (MATRIX_RATE,) * 5 + (VECTOR_RATE, VECTOR_RATE)
    decays = (MATRIX_DECAY,) * 5 + (0.0, 0.0)
    updated = [
        adamw(master, gradient * factor, first_old, second_old, step_rate, decay_rate)
        for master, gradient, first_old, second_old, step_rate, decay_rate in zip(
            masters, all_grads, firsts, seconds, step_rates, decays
        )
    ]
    residual_bias_grads = (reduced[5] * factor)[5:7]
    return (
        block_output,
        input_grad,
        grad_norm,
        updated[0][0],
        updated[1][0],
        updated[2][0],
        updated[3][0],
        updated[4][0],
        updated[5][0],
        updated[6][0],
        updated[0][1],
        updated[1][1],
        updated[2][1],
        updated[3][1],
        updated[4][1],
        updated[5][1],
        updated[6][1],
        updated[0][2],
        updated[1][2],
        updated[2][2],
        updated[3][2],
        updated[4][2],
        updated[5][2],
        updated[6][2],
        residual_bias_grads,
    )


def dot_nn(left, right):
    return lax.dot_general(left, right, (((1,), (0,)), ((), ())), preferred_element_type=F32)


def dot_nt(left, right):
    return lax.dot_general(left, right, (((1,), (1,)), ((), ())), preferred_element_type=F32)


def dot_tn(left, right):
    return lax.dot_general(left, right, (((0,), (0,)), ((), ())), preferred_element_type=F32)


def normalise(rows):
    centre = rows - jnp.mean(rows, -1, keepdims=True)
    scale = lax.rsqrt(jnp.mean(centre * centre, -1, keepdims=True) + NORM_EPS)
    return centre * scale, scale


def norm_back(grad, hat, scale, gain):
    inner = grad * gain
    return scale * (
        inner
        - jnp.mean(inner, -1, keepdims=True)
        - hat * jnp.mean(inner * hat, -1, keepdims=True)
    )


class Copy:
    def __init__(self, copy):
        self.copy, self.started, self.received, self.sent = copy, False, False, False

    def start(self):
        self.started = True
        self.copy.start()

    def wait_recv(self):
        self.received = True
        self.copy.wait_recv()

    def wait_send(self):
        self.sent = True
        self.copy.wait_send()


class Copies:
    def __init__(self, send_sems, recv_sems):
        self.send_sems, self.recv_sems, self.all = send_sems, recv_sems, []

    def make(self, source, target, device):
        index = len(self.all)
        copy = Copy(pltpu.make_async_remote_copy(
            src_ref=source,
            dst_ref=target,
            send_sem=self.send_sems.at[index],
            recv_sem=self.recv_sems.at[index],
            device_id=device,
            device_id_type=pl.DeviceIdType.MESH,
        ))
        self.all.append(copy)
        return copy

    def settle(self):
        for copy in self.all:
            if copy.started and not copy.sent:
                copy.wait_send()

    def finish(self):
        for copy in self.all:
            if copy.started and not copy.received:
                copy.wait_recv()
        self.settle()


def slab_rows(block, index):
    return pl.ds(pl.multiple_of((block * 8 + index) * 24, 8), 24)


class Panels:
    def __init__(self, ref, height, first, count):
        self.ref, self.height, self.first, self.count = ref, height, first, count

    def rows(self, panel, block, index):
        return pl.ds(pl.multiple_of((self.first + panel) * self.height + (block * 8 + index) * 24, 8), 24)

    def get(self, block, index):
        parts = [self.ref[self.rows(p, block, index), :] for p in range(self.count)]
        return parts[0] if self.count == 1 else jnp.concatenate(parts, 1)

    def put(self, block, index, value):
        for p in range(self.count):
            self.ref[self.rows(p, block, index), :] = value[:, p * 256 : p * 256 + 256]


N_COPIES = 151


def layer_kernel(
    span, x_in, cot_in, qw_in, kw_in, ow_in, uw_in, dw_in, vec_in, kvb_in,
    to_bo, to_ig, to_q, to_o, to_kv, to_vec, to_up, to_dn, to_small,
    x, cot, qw, kw, ow, uw, dw, vec, kvb,
    bo, ig, g_q, g_o, g_kv, g_vec, g_up, g_dn, g_small,
    KW, Q, O, U, Dn, X, C, KV, ub, WQ, WKV, WO, WU, gains, vsq,
    n1, hat1, scale1, N2, act, dl, OP, NP,
    qz, doz, doT, kvT, bias, sbuf, mixT, dqT, dkv,
    GP, GV, GU, GD, vg,
    SK1, RK1, SK2, RK2,
    RO1, SO2, RO2, RN1, SN2, RN2,
    SQ1, RQ1, SQ2, RQ2, SQ3, RQ3, SQ4, RQ4,
    SO1, QO1, SO2b, RO2b, SO3, RO3, SO4, RO4,
    SP1, RP1, SP2, RP2, SP3, RP3,
    SV1, RV1, SV2, RV2, SV3, RV3,
    SU1, RU1, SU2, RU2, SU3, RU3,
    SD1, RD1, SD2, RD2,
    NS1, NS2,
    send_sems, recv_sems, save_sems, load_sems,
):
    tok = x.shape[0]
    f = lax.axis_index("fsdp")
    s = lax.axis_index("seq")
    z = lax.div(s, 2)
    y = lax.rem(s, 2)
    yo = 1 - y
    fc = f + 1 - 2 * lax.rem(f, 2)
    fx = lax.rem(f + 2, 4)
    fd = 3 - f
    zk = (z, z + 1 - 2 * lax.rem(z, 2), lax.rem(z + 2, 4), 3 - z)
    dev_c, dev_x, dev_d = (fc, s), (fx, s), (fd, s)
    dev_y = (f, z * 2 + yo)
    dev_z = tuple((f, zz * 2 + y) for zz in zk)
    dev_zy = tuple((f, zz * 2 + yo) for zz in zk)
    fsdp_devs = (dev_c, dev_x, dev_d)
    seq_devs = dev_z[1:] + dev_zy
    far = (3, 2, 1)

    copies = Copies(send_sems, recv_sems)
    make = copies.make

    def start(*wanted):
        for copy in wanted:
            copy.start()

    def arrive(*wanted):
        for copy in wanted:
            copy.wait_recv()

    saved = []

    def save(source, target):
        copy = pltpu.make_async_copy(source, target, save_sems.at[len(saved)])
        copy.start()
        saved.append(copy)

    def seq_gather(ref):
        to_z = [None] + [make(ref(z, y), ref(z, y), dev_z[k]) for k in (1, 2, 3)]
        to_y = [make(ref(zk[k], y), ref(zk[k], y), dev_y) for k in range(4)]
        return to_z, to_y

    w_z, w_y = seq_gather(lambda i, j: KW.at[f, i, j])
    q_z, q_y = seq_gather(lambda i, j: Q.at[f, i, j])
    o_z, o_y = seq_gather(lambda i, j: O.at[f, i, j])
    p_z, p_y = seq_gather(lambda i, j: O.at[fx, i, j])
    u_z, u_y = seq_gather(lambda i, j: U.at[i, j])
    d_z, d_y = seq_gather(lambda i, j: Dn.at[i, j])
    k_z, k_y = seq_gather(lambda i, j: KV.at[i, j])

    def fsdp_gather(ref):
        to_x = [make(ref(f, j), ref(f, j), dev_x) for j in (y, yo)]
        to_c = [make(ref(f, j), ref(f, j), dev_c) for j in (y, yo)]
        on_c = [make(ref(fx, j), ref(fx, j), dev_c) for j in (y, yo)]
        return to_x, to_c, on_c

    w_x, w_c, w_xc = fsdp_gather(lambda i, j: KW.at[i, :, j])
    q_x, q_c, q_xc = fsdp_gather(lambda i, j: Q.at[i, :, j])
    q_xs = [make(Q.at[f, zz, yo], Q.at[f, zz, yo], dev_x) for zz in zk]
    o_x = make(O.at[f, z, y], O.at[f, z, y], dev_x)
    o_c = [make(O.at[f, :, j], O.at[f, :, j], dev_c) for j in (y, yo)]
    op_c = [make(O.at[fx, :, j], O.at[fx, :, j], dev_c) for j in (y, yo)]

    def token_gather(ref):
        return (
            make(ref.at[f], ref.at[f], dev_x),
            make(ref.at[f], ref.at[f], dev_c),
            make(ref.at[fx], ref.at[fx], dev_c),
        )

    x_x, x_c, x_xc = token_gather(X)
    c_x, c_c, c_xc = token_gather(C)
    u_f = [make(ub.at[g], U.at[z, y, f], dev) for g, dev in zip((fc, fx, fd), fsdp_devs)]

    rk1 = [make(SK1.at[zz], RK1.at[zz], dev_y) for zz in zk]
    rk2 = [make(SK2.at[k], RK2.at[k], dev_z[k + 1]) for k in range(3)]
    out_c = [make(OP.at[g], RO1.at[i], dev_c) for i, g in enumerate((fc, fd))]
    out_x = make(SO2, RO2, dev_x)
    nrm_c = [make(NP.at[g], RN1.at[i], dev_c) for i, g in enumerate((fc, fd))]
    nrm_x = make(SN2, RN2, dev_x)

    def full_scatter(S1, R1, S2, R2, S3, R3, S4, R4):
        return (
            make(S1, R1, dev_c),
            [make(S2.at[i], R2.at[i], dev_x) for i in range(2)],
            make(S3, R3, dev_y),
            [make(S4.at[k], R4.at[k], dev_z[k + 1]) for k in range(3)],
        )

    q_sc = full_scatter(SQ1, RQ1, SQ2, RQ2, SQ3, RQ3, SQ4, RQ4)
    p_c = make(SP1, RP1, dev_c)
    p_x = make(SP2, RP2, dev_x)
    p_s = [make(SP3.at[i], RP3.at[i], dev) for i, dev in enumerate(seq_devs)]
    v_c = make(SV1, RV1, dev_c)
    v_x = make(SV2, RV2, dev_x)
    v_s = [make(SV3, RV3.at[i], dev) for i, dev in enumerate(seq_devs)]
    o_sc = full_scatter(SO1, QO1, SO2b, RO2b, SO3, RO3, SO4, RO4)
    su_y = [make(SU1.at[zz], RU1.at[zz], dev_y) for zz in zk]
    su_z = [make(SU2.at[k], RU2.at[k], dev_z[k + 1]) for k in range(3)]
    su_f = [make(SU3.at[g], RU3.at[i], dev) for i, (g, dev) in enumerate(zip((fc, fx, fd), fsdp_devs))]
    sd_y = [make(SD1.at[zz], RD1.at[zz], dev_y) for zz in zk]
    sd_z = [make(SD2.at[k], RD2.at[k], dev_z[k + 1]) for k in range(3)]
    n_f = [make(NS1.at[f], NS1.at[f], dev) for dev in fsdp_devs]
    n_s = [make(NS2.at[s], NS2.at[s], dev) for dev in seq_devs]

    barrier = pltpu.get_barrier_semaphore()
    for dev in fsdp_devs + seq_devs:
        pl.semaphore_signal(barrier, inc=1, device_id=dev, device_id_type=pl.DeviceIdType.MESH)

    loads = []
    pairs = (
        (vec_in, vec), (kvb_in, kvb), (kw_in, kw), (qw_in, qw), (ow_in, ow),
        (x_in, x), (cot_in, cot), (uw_in, uw), (dw_in, dw),
    )
    for i, (source, target) in enumerate(pairs):
        copy = pltpu.make_async_copy(source, target, load_sems.at[i])
        copy.start()
        loads.append(copy)
    for copy in loads:
        copy.wait()

    vsq[...] = jnp.zeros((128, 128), F32)
    vsq[0:11, 0:24] = vec[...]
    vsq[11:12, 0:16] = kvb[...]
    KW[f, z, y, :, :128] = kw[...].astype(BF16)
    KW[f, z, y, :, 128:] = vsq[...].T[:24, :].astype(BF16)
    Q[f, z, y] = qw[...].astype(BF16)
    O[f, z, y] = ow[...].astype(BF16)
    for j in range(4):
        ub[j] = uw[:, j * D : (j + 1) * D].astype(BF16)
    U[z, y, f] = ub[f]
    Dn[z, y] = dw[...].astype(BF16)
    X[f] = x[...]
    C[f] = cot[...]

    pl.semaphore_wait(barrier, 10)
    start(w_z[3], w_z[2], w_z[1], w_y[0])
    start(o_x, q_z[3], q_z[2], q_z[1], q_y[0])
    start(o_z[3], o_z[2], o_z[1], o_y[0])

    hat, scale = normalise(x[...].astype(F32))
    hat1[...] = hat
    scale1[...] = jnp.broadcast_to(scale, (tok, 128))
    own_span = span[0, s]
    lane = lax.broadcasted_iota(jnp.int32, (tok, 128), 1)
    spot = lax.broadcasted_iota(jnp.int32, (tok, 128), 0) + own_span * tok
    in_head = lax.rem(lane, 64)
    step = lax.rem(in_head, ROT_DIMS // 2).astype(F32)
    inverse = jnp.exp(step * (-2.0 * math.log(10000.0) / ROT_DIMS))
    angle = spot.astype(F32) * (0.25 * inverse)
    sine = jnp.sin(angle)
    cosine = jnp.where(in_head < ROT_DIMS, jnp.cos(angle), 1.0)
    sine_low = jnp.where(in_head < ROT_DIMS // 2, sine, 0.0)
    sine_high = jnp.where((in_head >= ROT_DIMS // 2) & (in_head < ROT_DIMS), sine, 0.0)
    key_lane = lane < 64
    key_cos = jnp.where(key_lane, cosine, 1.0)
    key_low = jnp.where(key_lane, sine_low, 0.0)
    key_high = jnp.where(key_lane, sine_high, 0.0)

    def turn(block, cos_t, low_t, high_t):
        up = pltpu.roll(block, 120, 1)
        down = pltpu.roll(block, 8, 1)
        return block * cos_t - up * low_t + down * high_t

    def turn_back(block, cos_t, low_t, high_t):
        up = pltpu.roll(block, 120, 1)
        down = pltpu.roll(block, 8, 1)
        return block * cos_t + up * low_t - down * high_t

    def forward(to_z, to_y, *which):
        for k in which:
            arrive(to_z[k])
            start(to_y[k])

    forward(w_z, w_y, *far)
    start(w_x[0], w_c[0])
    arrive(o_x)
    start(p_z[3], p_z[2], p_z[1], p_y[0])
    arrive(*w_y)
    start(w_x[1], w_c[1])
    forward(q_z, q_y, *far)
    start(q_x[0], q_c[0])
    arrive(w_x[0])
    start(w_xc[0])
    arrive(w_x[1])
    start(w_xc[1])
    arrive(*w_c, *w_xc)
    slabs = [KW[g, i, j].astype(F32) for g in range(4) for i in range(4) for j in range(2)]
    for i in range(16):
        pair = jnp.concatenate([slabs[2 * i][:, :128], slabs[2 * i + 1][:, :128]], 0)
        WKV[i * 48 : (i + 1) * 48, :] = pair.astype(BF16)
    gains[...] = jnp.concatenate([slab[:, 128:] for slab in slabs], 0).T
    vsq[...] = jnp.concatenate([slab[:16, 128:] for slab in slabs[:8]], 0).T
    kv_shift = vsq[11:12, :]
    n1[...] = (hat * gains[0:1, :] + gains[1:2, :]).astype(BF16)
    kv_pre = dot_nn(n1[...], WKV[...]) + kv_shift
    KV[z, y] = turn(kv_pre, key_cos, key_low, key_high).astype(BF16)
    start(k_z[3], k_z[2], k_z[1], k_y[0])
    for k in range(4):
        arrive(q_y[k])
        start(q_xs[k])
    start(q_c[1])
    forward(o_z, o_y, *far)
    start(o_c[0])
    forward(p_z, p_y, *far)
    start(op_c[0])
    arrive(q_x[0])
    start(q_xc[0])
    vg[...] = jnp.zeros((128, D), F32)
    csum = jnp.sum(cot[...].astype(F32), 0, keepdims=True)
    vg[5:6, :] = csum
    vg[6:7, :] = csum
    key_iota = lax.broadcasted_iota(jnp.int32, (tok, tok), 0)
    row_iota = lax.broadcasted_iota(jnp.int32, (tok, tok), 1) + own_span * tok
    for i in range(8):
        bias[i * tok : (i + 1) * tok, :] = jnp.where(
            key_iota + span[0, i] * tok <= row_iota, 0.0, MASKED
        ).astype(F32)
    dkv[...] = jnp.zeros((8 * tok, 128), F32)
    start(*u_f)
    forward(k_z, k_y, *far)
    arrive(*q_xs)
    start(q_xc[1])
    arrive(*o_y)
    start(o_c[1])
    arrive(*p_y)
    start(op_c[1])
    arrive(*u_f)
    start(x_x, c_x, x_c, c_c)
    start(u_z[3], u_z[2], u_z[1], u_y[0])
    arrive(*q_c, *q_xc)

    def join(ref, whole):
        def put(i, carry):
            g = lax.div(i, 4)
            zz = lax.rem(i, 4)
            pair = jnp.concatenate([ref[g, zz, 0].astype(F32), ref[g, zz, 1].astype(F32)], 0)
            whole[pl.ds(pl.multiple_of(i * 48, 16), 48), :] = pair.astype(BF16)
            return carry

        lax.fori_loop(0, 16, put, 0)

    join(Q, WQ)
    q_pre = dot_nn(n1[...], WQ[...]) + gains[4:5, :]
    gap = jnp.zeros((tok, 64), BF16)
    for j in range(6):
        cols = slice(j * 128, j * 128 + 128)
        turned = turn(q_pre[:, cols], cosine, sine_low, sine_high).astype(BF16).astype(F32)
        turned = (turned * HD ** (-0.5)).astype(BF16)
        qz[2 * j] = jnp.concatenate([turned[:, :64], gap], 1)
        qz[2 * j + 1] = jnp.concatenate([turned[:, 64:], gap], 1)
    arrive(*o_c, *op_c)
    join(O, WO)
    mixed_back = dot_nt(cot[...], WO[...]).astype(BF16)
    for j in range(6):
        pair = mixed_back[:, j * 128 : j * 128 + 128]
        doz[2 * j] = jnp.concatenate([gap, pair[:, :64]], 1)
        doz[2 * j + 1] = jnp.concatenate([gap, pair[:, 64:]], 1)
    doT[...] = mixed_back.astype(F32).T.astype(BF16).reshape(HQ, HD, tok)
    arrive(*k_y)
    KVF = KV.reshape(8 * tok, 128)
    kvT[...] = KVF[...].astype(F32).T.astype(BF16)

    span_rows = 2 * tok
    chunks = 8 * tok // span_rows

    def fold(values, reduce):
        return reduce(values.reshape(span_rows // 8, 8, tok), axis=0)

    def attend(step_index):
        heads = [step_index * 2, step_index * 2 + 1]
        top, total, share, delta, acc = {}, {}, {}, {}, {}

        def rows_of(i):
            return pl.ds(i * span_rows, span_rows)

        def held_of(j, i):
            return pl.ds((j * chunks + i) * span_rows, span_rows)

        def score(j, i):
            scores = dot_nt(KVF[rows_of(i), :], qz[heads[j]]) + bias[rows_of(i), :]
            sbuf[held_of(j, i), :] = scores
            here = fold(scores, jnp.max)
            top[j] = here if i == 0 else jnp.maximum(top[j], here)
            if i == chunks - 1:
                top[j] = jnp.max(top[j], axis=0, keepdims=True)

        def weigh(j, i):
            weights = jnp.exp(sbuf[held_of(j, i), :] - top[j])
            sbuf[held_of(j, i), :] = weights
            here = fold(weights, jnp.sum)
            total[j] = here if i == 0 else total[j] + here
            if i == chunks - 1:
                share[j] = 1.0 / jnp.sum(total[j], axis=0, keepdims=True)

        def mix(j, i):
            rows = rows_of(i)
            probs = sbuf[held_of(j, i), :] * share[j]
            probs_low = probs.astype(BF16)
            sbuf[held_of(j, i), :] = probs
            here = dot_nn(kvT[:, rows], probs_low)
            acc[j] = here if i == 0 else acc[j] + here
            dkv[rows, :] += dot_nn(probs_low, doz[heads[j]])
            if i == chunks - 1:
                mixed = acc[j][64:, :]
                mixT[heads[j]] = mixed.astype(BF16)
                delta[j] = jnp.sum(mixed * doT[heads[j]].astype(F32), axis=0, keepdims=True)

        def back(j, i):
            rows = rows_of(i)
            prob_grad = dot_nt(KVF[rows, :], doz[heads[j]])
            score_low = (sbuf[held_of(j, i), :] * (prob_grad - delta[j])).astype(BF16)
            here = dot_nn(kvT[:, rows], score_low)
            acc[j] = here if i == 0 else acc[j] + here
            dkv[rows, :] += dot_nn(score_low, qz[heads[j]])
            if i == chunks - 1:
                dqT[heads[j]] = acc[j][:64, :] * HD ** (-0.5)

        for stage in (
            ((score, 0),),
            ((weigh, 0), (score, 1)),
            ((mix, 0), (weigh, 1)),
            ((back, 0), (mix, 1)),
            ((back, 1),),
        ):
            for i in range(chunks):
                for part, j in stage:
                    part(j, i)

    def attend_all(first, last, meanwhile):
        def body_step(step_index, carry):
            for at, action in meanwhile:
                pl.when(step_index == at)(action)
            attend(step_index)
            return carry

        lax.fori_loop(first, last, body_step, 0)


    def pump_one():
        start(d_z[3], d_z[2], d_z[1], d_y[0])

    def pump_two():
        forward(u_z, u_y, 3)
        arrive(x_x)
        start(x_xc)

    def pump_three():
        forward(u_z, u_y, 2, 1)

    def pump_four():
        forward(d_z, d_y, 3)
        arrive(c_x)
        start(c_xc)

    def pump_five():
        forward(d_z, d_y, 2)

    attend_all(
        0, HQ // 2,
        ((0, pump_one), (2, pump_two), (3, pump_three), (4, pump_four), (5, pump_five)),
    )

    for k in (3, 2, 1, 0):
        rows = pl.ds(pl.multiple_of((2 * zk[k] + yo) * tok, 8), tok)
        SK1[zk[k]] = dkv[rows, :].astype(BF16)
        start(rk1[k])
    mix_low = mixT.reshape(D, tok)[...]
    for c in range(3):
        sbuf[(3 + c) * D : (4 + c) * D, :] = dot_nn(mix_low, cot[:, c * 256 : c * 256 + 256])
    GQ = Panels(sbuf, D, 0, 3)
    GO = Panels(sbuf, D, 3, 3)

    def scatter_c(G, S1, copy):
        def put(i, carry):
            for j, g in enumerate((fc, fd)):
                S1[j, i] = G.get(g, i).astype(S1.dtype)
            return carry

        lax.fori_loop(0, 8, put, 0)
        start(copy)

    def scatter_x(G, R1, S2, copies_):
        arrive(copies_[0])
        for j, yy in enumerate((yo, y)):
            for i in range(4):
                slab = 2 * i + yy
                S2[j, i] = (G.get(fx, slab) + R1[1, slab].astype(F32)).astype(S2.dtype)
                G.put(f, slab, G.get(f, slab) + R1[0, slab].astype(F32))
            start(copies_[1][j])

    def scatter_y(G, R2, S3, copies_):
        arrive(copies_[1][0])
        for i in range(4):
            S3[i] = (G.get(f, 2 * i + yo) + R2[0, i].astype(F32)).astype(S3.dtype)
        start(copies_[2])

    def scatter_z(G, R2, R3, S4, copies_):
        arrive(copies_[1][1], copies_[2])
        for k in far:
            total = G.get(f, 2 * zk[k] + y) + R2[1, zk[k]].astype(F32) + R3[zk[k]].astype(F32)
            S4[k - 1] = total.astype(S4.dtype)
            start(copies_[3][k - 1])

    def scatter_end(G, R2, R3, R4, copies_):
        total = G.get(f, 2 * z + y) + R2[1, z].astype(F32) + R3[z].astype(F32)
        for k in range(3):
            arrive(copies_[3][k])
            total = total + R4[k].astype(F32)
        return total

    scatter_c(GO, SO1, o_sc[0])
    q_back = dqT.reshape(D, tok)[...].T
    parts = []
    for j in range(6):
        parts.append(
            turn_back(q_back[:, j * 128 : j * 128 + 128], cosine, sine_low, sine_high).astype(BF16)
        )
    q_low = jnp.concatenate(parts, 1)
    vg[4:5, :] = jnp.sum(q_low.astype(F32), 0, keepdims=True)
    for c in range(3):
        sbuf[c * D : (c + 1) * D, :] = dot_tn(n1[...], q_low[:, c * 256 : c * 256 + 256])
    scatter_c(GQ, SQ1, q_sc[0])
    forward(d_z, d_y, 1)
    arrive(*u_y, x_c, x_xc)

    def pair_step(k):
        arrive(rk1[k])
        rows = pl.ds(pl.multiple_of((2 * zk[k] + y) * tok, 8), tok)
        SK2[k - 1] = (dkv[rows, :] + RK1[zk[k]].astype(F32)).astype(BF16)
        start(rk2[k - 1])

    def lift_one():
        pair_step(3)

    def lift_two():
        pair_step(2)
        scatter_x(GO, QO1, SO2b, o_sc)

    def lift_three():
        pair_step(1)
        scatter_x(GQ, RQ1, SQ2, q_sc)

    def tokens_to_x():
        arrive(*out_c, *nrm_c)
        SO2[...] = (OP[fx].astype(F32) + RO1[1].astype(F32)).astype(BF16)
        start(out_x)
        SN2[...] = (NP[fx].astype(F32) + RN1[1].astype(F32)).astype(BF16)
        start(nrm_x)

    def down_step(k):
        arrive(sd_y[k])
        rows = pl.ds(pl.multiple_of((zk[k] * 2 + y) * 96, 8), 96)
        total = GD[rows, :] + RD1[zk[k]].astype(F32)
        if k:
            SD2[k - 1] = total.astype(BF16)
            start(sd_z[k - 1])
        else:
            GD[rows, :] = total

    def up_step(k):
        arrive(su_y[k])
        for g in range(4):
            rows = slab_rows(g, zk[k] * 2 + y)
            total = GU[rows, :] + RU1[zk[k], g].astype(F32)
            if k:
                SU2[k - 1, g] = total.astype(BF16)
            else:
                GU[rows, :] = total
        if k:
            start(su_z[k - 1])

    up_totals = []

    def up_end():
        arrive(*su_z)
        for g in range(4):
            total = GU[slab_rows(g, s), :]
            for k in range(3):
                total = total + RU2[k, g].astype(F32)
            up_totals.append(total)
            g_up[g] = total
            SU3[g] = total.astype(BF16)
        start(*su_f)

    for g in range(4):
        for i in range(4):
            pair = jnp.concatenate([U[i, j, g].astype(F32) for j in range(2)], 0)
            WU[(g * 4 + i) * 48 : (g * 4 + i + 1) * 48, :] = pair.astype(BF16)
    WD = Dn.reshape(D, D)
    up_bias = gains[pl.ds(7 + f, 1), :]

    def slope_rows(c, t):
        return pl.ds(pl.multiple_of(c * 4 * tok + t * tok, tok), tok)

    def lift_block(t, carry):
        for at, action in ((1, lift_one), (2, lift_two), (3, lift_three)):
            pl.when(t == at)(action)
        rows = pl.ds(pl.multiple_of(t * tok, tok), tok)
        hat2, _ = normalise(X[t].astype(F32))
        low2 = (hat2 * gains[2:3, :] + gains[3:4, :]).astype(BF16)
        N2[rows, :] = low2
        for c in range(3):
            units = slice(c * 256, c * 256 + 256)
            lifted = dot_nn(low2, WU[:, units]) + up_bias[:, units]
            half = 0.5 + 0.5 * lax.erf(lifted * (0.5**0.5))
            act[rows, units] = (lifted * half).astype(BF16)
            bell = jnp.exp(lifted * lifted * -0.5) * (1.0 / math.sqrt(2.0 * math.pi))
            bias[slope_rows(c, t), :] = half + lifted * bell
        return carry

    lax.fori_loop(0, 4, lift_block, 0)
    arrive(c_c, c_xc)
    CF = C.reshape(4 * tok, D)
    for c in range(3):
        units = slice(c * 256, c * 256 + 256)
        GD[units, :] = dot_tn(act[:, units], CF[...])
    for k in (3, 2, 1, 0):
        SD1[zk[k]] = GD[pl.ds(pl.multiple_of((zk[k] * 2 + yo) * 96, 8), 96), :].astype(BF16)
        start(sd_y[k])
    arrive(*d_y)

    def back_one():
        scatter_y(GO, RO2b, SO3, o_sc)

    def back_two():
        down_step(3)

    def back_three():
        scatter_y(GQ, RQ2, SQ3, q_sc)

    def back_block(t, carry):
        for at, action in ((1, back_one), (2, back_two), (3, back_three)):
            pl.when(t == at)(action)
        two_gain, two_shift, up_sum = carry
        rows = pl.ds(pl.multiple_of(t * tok, tok), tok)
        back = C[t]
        sums = []
        for c in range(3):
            units = slice(c * 256, c * 256 + 256)
            low = (bias[slope_rows(c, t), :] * dot_nt(back, WD[units, :])).astype(BF16)
            dl[rows, units] = low
            sums.append(jnp.sum(low.astype(F32), 0, keepdims=True))
        OP[t] = dot_nn(act[rows, :], WD[...]).astype(BF16)
        grad2 = dot_nt(dl[rows, :], WU[...])
        NP[t] = grad2.astype(BF16)
        hat2, _ = normalise(X[t].astype(F32))
        return (
            two_gain + jnp.sum(grad2 * hat2, 0, keepdims=True),
            two_shift + jnp.sum(grad2, 0, keepdims=True),
            up_sum + jnp.concatenate(sums, 1),
        )

    zero_row = jnp.zeros((1, D), F32)
    two_gain, two_shift, up_sum = lax.fori_loop(0, 4, back_block, (zero_row,) * 3)
    vg[2:3, :] = two_gain
    vg[3:4, :] = two_shift
    vg[pl.ds(7 + f, 1), :] = up_sum
    start(*out_c, *nrm_c)
    down_step(2)
    for c in range(3):
        units = slice(c * 256, c * 256 + 256)
        GU[units, :] = dot_tn(N2[:, units], dl[...])
    for k in (3, 2, 1, 0):
        for g in range(4):
            SU1[zk[k], g] = GU[slab_rows(g, zk[k] * 2 + yo), :].astype(BF16)
        start(su_y[k])
    down_step(1)
    grad1 = dot_nt(q_low, WQ[...])
    arrive(rk1[0])
    kv_back = dkv[pl.ds(pl.multiple_of((2 * z + y) * tok, 8), tok), :] + RK1[z].astype(F32)
    for k in range(3):
        arrive(rk2[k])
        kv_back = kv_back + RK2[k].astype(F32)
    kv_low = turn_back(kv_back, key_cos, key_low, key_high).astype(BF16)
    grad1 = grad1 + dot_nt(kv_low, WKV[...])
    vg[0:1, :] = jnp.sum(grad1 * hat1[...], 0, keepdims=True)
    vg[1:2, :] = jnp.sum(grad1, 0, keepdims=True)
    kv_sum = jnp.sum(kv_low.astype(F32), 0, keepdims=True)
    short = jnp.zeros((1, 8), F32)
    spread = jnp.concatenate(
        [part for i in range(8) for part in (kv_sum[:, i * 16 : i * 16 + 16], short)], 1
    )
    vg[11:12, :] = jnp.concatenate([spread] * 4, 1)
    GP[...] = dot_tn(n1[...], kv_low)
    flipped = vg[...].T

    def packed(g):
        parts = [flipped[(g * 8 + i) * 24 : (g * 8 + i + 1) * 24, :16] for i in range(8)]
        return jnp.concatenate(parts, 1)

    for g in range(4):
        GV[g] = packed(g)
    for i in range(8):
        for j, g in enumerate((fc, fd)):
            SP1[j, i] = GP[slab_rows(g, i), :].astype(BF16)
    for j, g in enumerate((fc, fd)):
        SV1[j] = GV[g]
    start(p_c, v_c)
    down_step(0)
    arrive(p_c, v_c)
    for i in range(8):
        SP2[i] = (GP[slab_rows(fx, i), :] + RP1[1, i].astype(F32)).astype(BF16)
    SV2[...] = GV[fx] + RV1[1]
    start(p_x, v_x)
    tokens_to_x()
    scatter_z(GO, RO2b, RO3, SO4, o_sc)
    arrive(p_x, v_x)

    def kv_sum_of(slab):
        return GP[slab_rows(f, slab), :] + RP1[0, slab].astype(F32) + RP2[slab].astype(F32)

    seq_slabs = [2 * zk[k] + y for k in (1, 2, 3)] + [2 * zk[k] + yo for k in range(4)]
    for i, slab in enumerate(seq_slabs):
        SP3[i] = kv_sum_of(slab).astype(BF16)
    SV3[...] = GV[f] + RV1[0] + RV2[...]
    start(*p_s, *v_s)
    up_step(3)
    scatter_z(GQ, RQ2, RQ3, SQ4, q_sc)
    up_step(2)
    up_step(1)
    up_step(0)
    mixed_rows = mix_low.astype(F32).T.astype(BF16)
    arrive(out_x)
    bo[...] = (
        x[...].astype(F32)
        + (dot_nn(mixed_rows, WO[...]) + gains[5:6, :])
        + (OP[f].astype(F32) + RO1[0].astype(F32) + RO2[...].astype(F32) + gains[6:7, :])
    ).astype(BF16)
    save(bo, to_bo)
    arrive(nrm_x)
    grad2 = NP[f].astype(F32) + RN1[0].astype(F32) + RN2[...].astype(F32)
    hat_rows = hat1[...]
    scale_rows = scale1[:, 0:1]
    ig[...] = (
        cot[...].astype(F32)
        + norm_back(grad1, hat_rows, scale_rows, gains[0:1, :])
        + norm_back(grad2, hat_rows, scale_rows, gains[2:3, :])
    )
    save(ig, to_ig)
    copies.settle()
    q_grad = scatter_end(GQ, RQ2, RQ3, RQ4, q_sc)
    g_q[...] = q_grad
    save(g_q, to_q)
    o_grad = scatter_end(GO, RO2b, RO3, RO4, o_sc)
    g_o[...] = o_grad
    save(g_o, to_o)
    kv_grad = kv_sum_of(s)
    vec_sum = SV3[...]
    for i in range(7):
        arrive(p_s[i], v_s[i])
        kv_grad = kv_grad + RP3[i].astype(F32)
        vec_sum = vec_sum + RV3[i]
    vec_own = jnp.zeros((24, 16), F32)
    for i in range(8):
        vec_own = vec_own + jnp.where(s == i, vec_sum[:, i * 16 : i * 16 + 16], 0.0)
    vec_grad = jnp.concatenate([vec_own, jnp.zeros((24, 112), F32)], 1)
    g_kv[...] = kv_grad
    g_vec[...] = vec_grad
    save(g_kv, to_kv)
    save(g_vec, to_vec)
    rows = pl.ds(pl.multiple_of(s * 96, 8), 96)
    down_grad = GD[rows, :]
    for k in range(3):
        arrive(sd_z[k])
        down_grad = down_grad + RD2[k].astype(F32)
    g_dn[...] = down_grad
    save(g_dn, to_dn)
    up_end()
    save(g_up.at[f], to_up.at[f])

    def energy(values):
        return jnp.sum(jnp.sum(values * values, 0, keepdims=True), 1, keepdims=True)

    lanes = lax.broadcasted_iota(jnp.int32, (24, 128), 1)
    squares = energy(q_grad) + energy(o_grad) + energy(kv_grad) + energy(jnp.where(lanes == 11, 0.0, vec_grad)) + energy(g_dn[...])
    for total in up_totals:
        squares = squares + energy(total)
    kv_rows = jnp.concatenate([vec_grad, jnp.zeros((104, 128), F32)], 0).T
    line = lax.broadcasted_iota(jnp.int32, (8, 128), 0)
    column = lax.broadcasted_iota(jnp.int32, (8, 128), 1)
    kv_line = jnp.where(column < 16, jnp.broadcast_to(kv_rows[11:12, :], (8, 128)), 0.0)
    NS1[f] = jnp.where(line == 0, squares, kv_line)
    start(*n_f)
    arrive(*n_f)
    kv_piece = NS1[0][1:2, :]
    chip = NS1[0] + NS1[1] + NS1[2] + NS1[3]
    part = chip[0:1, 0:1] + jnp.sum(kv_piece * kv_piece, 1, keepdims=True)
    NS2[s] = jnp.broadcast_to(part, (8, 128))
    start(*n_s)
    for i, g in enumerate((fc, fx, fd)):
        arrive(su_f[i])
        g_up[g] = RU3[i].astype(F32)
        save(g_up.at[g], to_up.at[g])
    arrive(*n_s)
    everything = NS2[0]
    for i in range(1, 8):
        everything = everything + NS2[i]
    g_small[...] = jnp.where(line == 0, everything, jnp.broadcast_to(kv_piece, (8, 128)))
    save(g_small, to_small)
    copies.finish()
    assert len(copies.all) == N_COPIES, len(copies.all)
    for copy in saved:
        copy.wait()


def update_kernel(
    small, g_q, g_o, g_kv, g_vec, g_up, g_dn, bo_in, ig_in,
    mq, mk, mo, mu, md, mv, mb,
    fq, fk, fo, fu, fdn, fv, fb,
    sq, sk, so, su, sd, sv, sb,
    bo, ig, norm,
    nmq, nmk, nmo, nmu, nmd, nmv, nmb,
    nfq, nfk, nfo, nfu, nfd, nfv, nfb,
    nsq, nsk, nso, nsu, nsd, nsv, nsb,
    residual,
):
    bo[...] = bo_in[...]
    ig[...] = ig_in[...]
    size = jnp.sqrt(small[0:1, 0:1])
    norm[...] = size
    factor = jnp.minimum(1.0, CLIP_NORM / (size + 1e-06))

    def update(grad, master, first, second, new_master, new_first, new_second, rate, decay):
        clipped = grad * factor
        values = adamw(master, clipped, first, second, rate, decay)
        for ref, value in zip((new_master, new_first, new_second), values):
            ref[...] = value

    rates = (MATRIX_RATE, MATRIX_DECAY)
    update(g_q[...], mq[...], fq[...], sq[...], nmq, nfq, nsq, *rates)
    update(g_o[...], mo[...], fo[...], so[...], nmo, nfo, nso, *rates)
    update(g_kv[...], mk[...], fk[...], sk[...], nmk, nfk, nsk, *rates)
    for g in range(4):
        cols = slice(g * D, (g + 1) * D)
        update(
            g_up[g], mu[:, cols], fu[:, cols], su[:, cols],
            nmu.at[:, cols], nfu.at[:, cols], nsu.at[:, cols], *rates,
        )
    update(g_dn[...], md[...], fdn[...], sd[...], nmd, nfd, nsd, *rates)
    flipped = jnp.concatenate([g_vec[...], jnp.zeros((104, 128), F32)], 0).T
    vector_grad = flipped[:11, :24]
    update(vector_grad, mv[...], fv[...], sv[...], nmv, nfv, nsv, VECTOR_RATE, 0.0)
    residual[...] = flipped[5:7, :24] * factor
    update(small[1:2, :16], mb[...], fb[...], sb[...], nmb, nfb, nsb, VECTOR_RATE, 0.0)


def fast_body(
    inputs, cotangent, span_order,
    query_weight, keyval_weight, output_weight, up_weight, down_weight, vectors, kv_bias,
    *moments,
):
    tok = inputs.shape[0]
    smem = pl.BlockSpec(memory_space=pltpu.SMEM)
    shape = jax.ShapeDtypeStruct
    V = pltpu.VMEM
    results_here = (
        shape((tok, D), BF16),
        shape((tok, D), F32),
        shape((24, D), F32),
        shape((24, D), F32),
        shape((24, 128), F32),
        shape((24, 128), F32),
        shape((4, 24, D), F32),
        shape((96, D), F32),
        shape((8, 128), F32),
    )
    operands_here = (
        inputs, cotangent, query_weight, keyval_weight, output_weight, up_weight, down_weight,
        vectors, kv_bias.reshape(1, -1),
    )
    scratch = [V(a.shape, a.dtype) for a in operands_here + results_here]
    scratch += [
        V((4, 4, 2, 24, 256), BF16),
        V((4, 4, 2, 24, D), BF16),
        V((4, 4, 2, 24, D), BF16),
        V((4, 2, 4, 24, D), BF16),
        V((4, 2, 96, D), BF16),
        V((4, tok, D), BF16),
        V((4, tok, D), BF16),
        V((4, 2, tok, 128), BF16),
        V((4, 24, D), BF16),
        V((D, D), BF16),
        V((D, 128), BF16),
        V((D, D), BF16),
        V((D, D), BF16),
        V((128, D), F32),
        V((128, 128), F32),
        V((tok, D), BF16),
        V((tok, D), F32),
        V((tok, 128), F32),
        V((4 * tok, D), BF16),
        V((4 * tok, D), BF16),
        V((4 * tok, D), BF16),
        V((4, tok, D), BF16),
        V((4, tok, D), BF16),
        V((HQ, tok, 128), BF16),
        V((HQ, tok, 128), BF16),
        V((HQ, HD, tok), BF16),
        V((128, 8 * tok), BF16),
        V((12 * tok, tok), F32),
        V((6 * D, 256), F32),
        V((HQ, HD, tok), BF16),
        V((HQ, HD, tok), F32),
        V((8 * tok, 128), F32),
        V((D, 128), F32),
        V((4, 24, 128), F32),
        V((D, D), F32),
        V((D, D), F32),
        V((128, D), F32),
        V((4, tok, 128), BF16), V((4, tok, 128), BF16),
        V((3, tok, 128), BF16), V((3, tok, 128), BF16),
        V((2, tok, D), BF16), V((tok, D), BF16), V((tok, D), BF16),
        V((2, tok, D), BF16), V((tok, D), BF16), V((tok, D), BF16),
    ]
    def scatter_buffers(width):
        found = []
        for lead in ((2, 8), (2, 4), (4,), (3,)):
            found += [V(lead + (24, width), BF16)] * 2
        return found

    scratch += scatter_buffers(D)
    scratch += scatter_buffers(D)
    for lead in ((2, 8), (8,), (7,)):
        scratch += [V(lead + (24, 128), BF16)] * 2
    scratch += [V((2, 24, 128), F32)] * 2 + [V((24, 128), F32)] * 3 + [V((7, 24, 128), F32)]
    scratch += [V((4, 4, 24, D), BF16)] * 2 + [V((3, 4, 24, D), BF16)] * 2
    scratch += [V((4, 24, D), BF16), V((3, 24, D), BF16)]
    scratch += [V((4, 96, D), BF16)] * 2 + [V((3, 96, D), BF16)] * 2
    scratch += [V((4, 8, 128), F32), V((8, 8, 128), F32)]
    scratch += [pltpu.SemaphoreType.DMA((N_COPIES,))] * 2 + [pltpu.SemaphoreType.DMA((12,)), pltpu.SemaphoreType.DMA((9,))]
    kv_row = kv_bias.reshape(1, -1)
    bo, ig, g_q, g_o, g_kv, g_vec, g_up, g_dn, small = pl.pallas_call(
        layer_kernel,
        name="layer",
        out_shape=results_here,
        in_specs=[smem] + [pl.BlockSpec(memory_space=pl.ANY)] * 9,
        out_specs=(pl.BlockSpec(memory_space=pl.ANY),) * 9,
        scratch_shapes=scratch,
        compiler_params=pltpu.CompilerParams(
            collective_id=0, has_side_effects=True, vmem_limit_bytes=62 * 2**20
        ),
    )(
        span_order, inputs, cotangent,
        query_weight, keyval_weight, output_weight, up_weight, down_weight, vectors, kv_row,
    )
    masters = (query_weight, keyval_weight, output_weight, up_weight, down_weight, vectors, kv_row)
    firsts = tuple(moments[:6]) + (moments[6].reshape(1, -1),)
    seconds = tuple(moments[7:13]) + (moments[13].reshape(1, -1),)
    state = [shape(a.shape, F32) for a in masters]
    operands = (small, g_q, g_o, g_kv, g_vec, g_up, g_dn, bo, ig) + masters + firsts + seconds
    outcomes = [shape((tok, D), BF16), shape((tok, D), F32), shape((1, 1), F32)]
    outcomes += state * 3 + [shape((2, vectors.shape[1]), F32)]

    def whole(a):
        return pl.BlockSpec(a.shape, lambda i: (0,) * len(a.shape))

    results = pl.pallas_call(
        update_kernel,
        name="update",
        grid=(1,),
        out_shape=outcomes,
        in_specs=[whole(a) for a in operands],
        out_specs=[whole(a) for a in outcomes],
        compiler_params=pltpu.CompilerParams(vmem_limit_bytes=62 * 2**20),
    )(*operands)
    results = list(results)
    results[2] = results[2].reshape(())
    for i in (9, 16, 23):
        results[i] = results[i].reshape(-1)
    return tuple(results)


def solution(mesh):
    grid = (mesh.shape["fsdp"], mesh.shape["seq"])
    return jax.shard_map(
        fast_body if grid == (4, 8) else body,
        mesh=mesh,
        in_specs=(
            P(("fsdp", "seq"), None),
            P(("fsdp", "seq"), None),
            P("fsdp", None),
            P(("fsdp", "seq"), None),
            P(("fsdp", "seq"), None),
            P(("fsdp", "seq"), None),
            P(("fsdp", "seq"), None),
            P(("fsdp", "seq"), None),
            P(None, ("fsdp", "seq")),
            P("seq"),
            P(("fsdp", "seq"), None),
            P(("fsdp", "seq"), None),
            P(("fsdp", "seq"), None),
            P(("fsdp", "seq"), None),
            P(("fsdp", "seq"), None),
            P(None, ("fsdp", "seq")),
            P("seq"),
            P(("fsdp", "seq"), None),
            P(("fsdp", "seq"), None),
            P(("fsdp", "seq"), None),
            P(("fsdp", "seq"), None),
            P(("fsdp", "seq"), None),
            P(None, ("fsdp", "seq")),
            P("seq"),
        ),
        out_specs=(
            P(("fsdp", "seq"), None),
            P(("fsdp", "seq"), None),
            P(),
            P(("fsdp", "seq"), None),
            P(("fsdp", "seq"), None),
            P(("fsdp", "seq"), None),
            P(("fsdp", "seq"), None),
            P(("fsdp", "seq"), None),
            P(None, ("fsdp", "seq")),
            P("seq"),
            P(("fsdp", "seq"), None),
            P(("fsdp", "seq"), None),
            P(("fsdp", "seq"), None),
            P(("fsdp", "seq"), None),
            P(("fsdp", "seq"), None),
            P(None, ("fsdp", "seq")),
            P("seq"),
            P(("fsdp", "seq"), None),
            P(("fsdp", "seq"), None),
            P(("fsdp", "seq"), None),
            P(("fsdp", "seq"), None),
            P(("fsdp", "seq"), None),
            P(None, ("fsdp", "seq")),
            P("seq"),
            P(None, ("fsdp", "seq")),
        ),
        check_vma=False,
    )
```

```python
import math

import jax
import jax.numpy as jnp
from jax import lax
from jax.experimental import pallas as pl
from jax.experimental.pallas import tpu as pltpu
from jax.sharding import PartitionSpec as P

D = 768
HQ = 12
HD = 64
ROT_DIMS = 16
FF = 3072
KEY_BLOCK = 512
STEP = 10
F32 = jnp.float32
BF16 = jnp.bfloat16


NORM_EPS = 1e-05
MASKED = -1e30
CLIP_NORM = 1.0
BETA_ONE = 0.9
BETA_TWO = 0.999
ADAM_EPS = 1e-08
MATRIX_DECAY = 0.1
MATRIX_RATE = 0.1
VECTOR_RATE = 0.3


def layer_norm(tensor, gain_row, shift_row):
    centre = tensor - jnp.mean(tensor, -1, keepdims=True)
    spread = jnp.mean(centre * centre, -1, keepdims=True)
    return centre * lax.rsqrt(spread + NORM_EPS) * gain_row + shift_row


def rotary_tables(places):
    half_steps = jnp.arange(ROT_DIMS // 2, dtype=jnp.float32)
    inverse = jnp.exp(half_steps * (-2.0 * math.log(10000.0) / ROT_DIMS))
    angles = places.astype(jnp.float32)[:, None] * (0.25 * inverse)[None, :]
    angles = jnp.concatenate([angles, angles], 1)
    return (jnp.cos(angles), jnp.sin(angles))


def rotate(tensor, cosine, sine_table):
    rotary_part = tensor[..., :ROT_DIMS]
    lower_half = rotary_part[..., : ROT_DIMS // 2]
    upper_half = rotary_part[..., ROT_DIMS // 2 :]
    turned = jnp.concatenate([-upper_half, lower_half], -1)
    return jnp.concatenate([rotary_part * cosine + turned * sine_table, tensor[..., ROT_DIMS:]], -1)


def adamw(master, clipped, first_old, second_old, step_rate, decay_rate):
    first_new = BETA_ONE * first_old + (1.0 - BETA_ONE) * clipped
    second_new = BETA_TWO * second_old + (1.0 - BETA_TWO) * clipped * clipped
    ascent = (
        first_new
        / (1.0 - BETA_ONE**STEP)
        / (jnp.sqrt(second_new / (1.0 - BETA_TWO**STEP)) + ADAM_EPS)
    )
    return (master - step_rate * (ascent + decay_rate * master), first_new, second_new)


def gelu_exact(tensor):
    return jax.nn.gelu(tensor, approximate=False)


def across_tokens(left_side, right_side):
    return lax.dot_general(
        left_side, right_side, (((0,), (0,)), ((), ())), preferred_element_type=jnp.float32
    )


def against(left_side, right_side):
    return lax.dot_general(
        left_side, right_side, (((1,), (1,)), ((), ())), preferred_element_type=jnp.float32
    )


def masked_scores(query_rows, row_places, key_block, key_places):
    scores = against(query_rows, key_block) * HD ** (-0.5)
    return jnp.where(key_places[None, :] <= row_places[:, None], scores, MASKED)


def body(
    inputs,
    cotangent,
    span_order,
    query_weight,
    keyval_weight,
    output_weight,
    up_weight,
    down_weight,
    vectors,
    kv_bias,
    first_query,
    first_keyval,
    first_output,
    first_up,
    first_down,
    first_vectors,
    first_kv_bias,
    second_query,
    second_keyval,
    second_output,
    second_up,
    second_down,
    second_vectors,
    second_kv_bias,
):
    tok_rows = inputs.shape[0]
    seq_count = lax.axis_size("seq")
    seq_rank = lax.axis_index("seq")
    order_row = span_order[0]
    token_steps = jnp.arange(tok_rows, dtype=jnp.int32)
    all_places = (order_row[:, None] * tok_rows + token_steps[None, :]).reshape(
        seq_count * tok_rows
    )
    own_span = jnp.sum(jnp.where(jnp.arange(seq_count, dtype=jnp.int32) == seq_rank, order_row, 0))
    own_places = own_span * tok_rows + token_steps
    query_rows_count = tok_rows * HQ
    query_full, keyval_full, output_full, up_full, down_full, vector_full = (
        lax.all_gather(query_weight.astype(jnp.bfloat16), ("fsdp", "seq"), axis=0, tiled=True),
        lax.all_gather(keyval_weight.astype(jnp.bfloat16), ("fsdp", "seq"), axis=0, tiled=True),
        lax.all_gather(output_weight.astype(jnp.bfloat16), ("fsdp", "seq"), axis=0, tiled=True),
        lax.all_gather(up_weight.astype(jnp.bfloat16), ("fsdp", "seq"), axis=0, tiled=True),
        lax.all_gather(down_weight.astype(jnp.bfloat16), ("fsdp", "seq"), axis=0, tiled=True),
        lax.all_gather(vectors.astype(jnp.bfloat16), ("fsdp", "seq"), axis=1, tiled=True),
    )
    kv_shift = lax.all_gather(kv_bias.astype(jnp.bfloat16), "seq", axis=0, tiled=True).astype(
        jnp.float32
    )
    gains = vector_full.astype(jnp.float32)
    states = inputs.astype(jnp.float32)
    normed_one = layer_norm(states, gains[0], gains[1])
    normed_low = normed_one.astype(jnp.bfloat16)
    query_pre = jnp.dot(normed_low, query_full, preferred_element_type=jnp.float32) + gains[4]
    keyval_pre = jnp.dot(normed_low, keyval_full, preferred_element_type=jnp.float32) + kv_shift
    cosine, sine_table = rotary_tables(own_places)

    def turn_queries(tensor):
        return rotate(tensor.reshape(tok_rows, HQ, HD), cosine[:, None, :], sine_table[:, None, :])

    def turn_keys(tensor):
        return jnp.concatenate([rotate(tensor[:, :HD], cosine, sine_table), tensor[:, HD:]], 1)

    query_rows = turn_queries(query_pre).astype(jnp.bfloat16).reshape(query_rows_count, HD)
    local_pairs = turn_keys(keyval_pre).astype(jnp.bfloat16)
    row_places = jnp.broadcast_to(own_places[:, None], (tok_rows, HQ)).reshape(query_rows_count)
    all_pairs = lax.all_gather(local_pairs, "seq", axis=0, tiled=True)
    block_count = all_pairs.shape[0] // KEY_BLOCK
    place_blocks = all_places.reshape(block_count, KEY_BLOCK)

    def lse_step(carry_pair, block_pair):
        running_top, running_total = carry_pair
        pair_block, key_places = block_pair
        scores = masked_scores(query_rows, row_places, pair_block[:, :HD], key_places)
        new_top = jnp.maximum(running_top, jnp.max(scores, 1, keepdims=True))
        running_total = running_total * jnp.exp(running_top - new_top) + jnp.sum(
            jnp.exp(scores - new_top), 1, keepdims=True
        )
        return ((new_top, running_total), None)

    start_carry = (
        jnp.full((query_rows_count, 1), MASKED, jnp.float32),
        jnp.zeros((query_rows_count, 1), jnp.float32),
    )
    (row_top, row_total), _ = lax.scan(
        lse_step, start_carry, (all_pairs.reshape(block_count, KEY_BLOCK, 2 * HD), place_blocks)
    )
    log_total = row_top + jnp.log(row_total)

    def mix_step(mixed_acc, block_pair):
        pair_block, key_places = block_pair
        probs_low = jnp.exp(
            masked_scores(query_rows, row_places, pair_block[:, :HD], key_places) - log_total
        ).astype(jnp.bfloat16)
        return (
            mixed_acc + jnp.dot(probs_low, pair_block[:, HD:], preferred_element_type=jnp.float32),
            None,
        )

    mixed, _ = lax.scan(
        mix_step,
        jnp.zeros((query_rows_count, HD), jnp.float32),
        (all_pairs.reshape(block_count, KEY_BLOCK, 2 * HD), place_blocks),
    )
    mixed_low = mixed.reshape(tok_rows, D).astype(jnp.bfloat16)
    attention_out = jnp.dot(mixed_low, output_full, preferred_element_type=jnp.float32) + gains[5]
    normed_two = layer_norm(states, gains[2], gains[3])
    normed_two_low = normed_two.astype(jnp.bfloat16)
    lifted = jnp.dot(normed_two_low, up_full, preferred_element_type=jnp.float32) + gains[
        7:
    ].reshape(FF)
    active_low = gelu_exact(lifted).astype(jnp.bfloat16)
    block_output = (
        states
        + attention_out
        + jnp.dot(active_low, down_full, preferred_element_type=jnp.float32)
        + gains[6]
    ).astype(jnp.bfloat16)
    back_rows = cotangent.astype(jnp.float32)
    query_back, keyval_back, output_back, up_back, down_back = (
        lax.all_gather(query_weight.astype(jnp.bfloat16), ("fsdp", "seq"), axis=0, tiled=True),
        lax.all_gather(keyval_weight.astype(jnp.bfloat16), ("fsdp", "seq"), axis=0, tiled=True),
        lax.all_gather(output_weight.astype(jnp.bfloat16), ("fsdp", "seq"), axis=0, tiled=True),
        lax.all_gather(up_weight.astype(jnp.bfloat16), ("fsdp", "seq"), axis=0, tiled=True),
        lax.all_gather(down_weight.astype(jnp.bfloat16), ("fsdp", "seq"), axis=0, tiled=True),
    )
    grad_down = across_tokens(active_low, cotangent)
    grad_output = across_tokens(mixed_low, cotangent)
    out_bias_grad = jnp.sum(back_rows, 0)
    active_grad = against(cotangent, down_back)
    _, gelu_pull = jax.vjp(gelu_exact, lifted)
    (lifted_grad,) = gelu_pull(active_grad)
    lifted_low = lifted_grad.astype(jnp.bfloat16)
    grad_up = across_tokens(normed_two_low, lifted_low)
    normed_two_grad = against(lifted_low, up_back)
    mixed_grad = against(cotangent, output_back).astype(jnp.bfloat16).reshape(query_rows_count, HD)
    row_delta = jnp.sum(mixed_grad.astype(jnp.float32) * mixed, 1, keepdims=True)
    pairs_back = lax.all_gather(local_pairs, "seq", axis=0, tiled=True)

    def grad_step(query_acc, block_pair):
        pair_block, key_places = block_pair
        key_block = pair_block[:, :HD]
        probs = jnp.exp(masked_scores(query_rows, row_places, key_block, key_places) - log_total)
        prob_grad = against(mixed_grad, pair_block[:, HD:])
        score_low = (probs * (prob_grad - row_delta)).astype(jnp.bfloat16)
        query_acc = query_acc + jnp.dot(score_low, key_block, preferred_element_type=jnp.float32)
        key_grad = across_tokens(score_low, query_rows) * HD ** (-0.5)
        value_grad = across_tokens(probs.astype(jnp.bfloat16), mixed_grad)
        return (query_acc, jnp.concatenate([key_grad, value_grad], 1))

    query_sum, pair_grads = lax.scan(
        grad_step,
        jnp.zeros((query_rows_count, HD), jnp.float32),
        (pairs_back.reshape(block_count, KEY_BLOCK, 2 * HD), place_blocks),
    )
    query_rot_grad = (query_sum * HD ** (-0.5)).reshape(tok_rows, HQ, HD)
    own_pair_grad = lax.psum_scatter(
        pair_grads.reshape(block_count * KEY_BLOCK, 2 * HD).astype(jnp.bfloat16),
        "seq",
        scatter_dimension=0,
        tiled=True,
    ).astype(jnp.float32)
    _, key_pull = jax.vjp(turn_keys, keyval_pre)
    (keyval_grad,) = key_pull(own_pair_grad)
    keyval_low = keyval_grad.astype(jnp.bfloat16)
    _, query_pull = jax.vjp(turn_queries, query_pre)
    (query_pre_grad,) = query_pull(query_rot_grad)
    query_low = query_pre_grad.astype(jnp.bfloat16)
    grad_query = across_tokens(normed_low, query_low)
    grad_keyval = across_tokens(normed_low, keyval_low)
    kv_bias_part = jnp.sum(keyval_low.astype(jnp.float32), 0)
    normed_one_grad = against(query_low, query_back) + against(keyval_low, keyval_back)
    _, first_pull = jax.vjp(layer_norm, states, gains[0], gains[1])
    input_one, gain_one_grad, shift_one_grad = first_pull(normed_one_grad)
    _, second_pull = jax.vjp(layer_norm, states, gains[2], gains[3])
    input_two, gain_two_grad, shift_two_grad = second_pull(normed_two_grad)
    input_grad = back_rows + input_one + input_two
    vector_grad = jnp.concatenate(
        [
            jnp.stack(
                [
                    gain_one_grad,
                    shift_one_grad,
                    gain_two_grad,
                    shift_two_grad,
                    jnp.sum(query_low.astype(jnp.float32), 0),
                    out_bias_grad,
                    out_bias_grad,
                ]
            ),
            jnp.sum(lifted_low.astype(jnp.float32), 0).reshape(FF // D, D),
        ],
        0,
    )
    reduced = (
        lax.psum_scatter(grad_query, ("fsdp", "seq"), scatter_dimension=0, tiled=True),
        lax.psum_scatter(grad_keyval, ("fsdp", "seq"), scatter_dimension=0, tiled=True),
        lax.psum_scatter(grad_output, ("fsdp", "seq"), scatter_dimension=0, tiled=True),
        lax.psum_scatter(grad_up, ("fsdp", "seq"), scatter_dimension=0, tiled=True),
        lax.psum_scatter(grad_down, ("fsdp", "seq"), scatter_dimension=0, tiled=True),
        lax.psum_scatter(vector_grad, ("fsdp", "seq"), scatter_dimension=1, tiled=True),
    )
    reduced = tuple(reduced)
    local_squares = sum((jnp.sum(gradient * gradient) for gradient in reduced))
    global_squares, kv_bias_total = lax.psum((local_squares, kv_bias_part), ("fsdp", "seq"))
    grad_norm = jnp.sqrt(global_squares + jnp.sum(kv_bias_total * kv_bias_total))
    piece_width = kv_bias.shape[0]
    kv_bias_grad = lax.dynamic_slice_in_dim(kv_bias_total, seq_rank * piece_width, piece_width)
    factor = jnp.minimum(1.0, CLIP_NORM / (grad_norm + 1e-06))
    masters = (query_weight, keyval_weight, output_weight, up_weight, down_weight, vectors, kv_bias)
    all_grads = reduced + (kv_bias_grad,)
    firsts = (
        first_query,
        first_keyval,
        first_output,
        first_up,
        first_down,
        first_vectors,
        first_kv_bias,
    )
    seconds = (
        second_query,
        second_keyval,
        second_output,
        second_up,
        second_down,
        second_vectors,
        second_kv_bias,
    )
    step_rates = (MATRIX_RATE,) * 5 + (VECTOR_RATE, VECTOR_RATE)
    decays = (MATRIX_DECAY,) * 5 + (0.0, 0.0)
    updated = [
        adamw(master, gradient * factor, first_old, second_old, step_rate, decay_rate)
        for master, gradient, first_old, second_old, step_rate, decay_rate in zip(
            masters, all_grads, firsts, seconds, step_rates, decays
        )
    ]
    residual_bias_grads = (reduced[5] * factor)[5:7]
    return (
        block_output,
        input_grad,
        grad_norm,
        updated[0][0],
        updated[1][0],
        updated[2][0],
        updated[3][0],
        updated[4][0],
        updated[5][0],
        updated[6][0],
        updated[0][1],
        updated[1][1],
        updated[2][1],
        updated[3][1],
        updated[4][1],
        updated[5][1],
        updated[6][1],
        updated[0][2],
        updated[1][2],
        updated[2][2],
        updated[3][2],
        updated[4][2],
        updated[5][2],
        updated[6][2],
        residual_bias_grads,
    )


def dot_nn(left, right):
    return lax.dot_general(left, right, (((1,), (0,)), ((), ())), preferred_element_type=F32)


def dot_nt(left, right):
    return lax.dot_general(left, right, (((1,), (1,)), ((), ())), preferred_element_type=F32)


def dot_tn(left, right):
    return lax.dot_general(left, right, (((0,), (0,)), ((), ())), preferred_element_type=F32)


def normalise(rows):
    centre = rows - jnp.mean(rows, -1, keepdims=True)
    scale = lax.rsqrt(jnp.mean(centre * centre, -1, keepdims=True) + NORM_EPS)
    return centre * scale, scale


def norm_back(grad, hat, scale, gain):
    inner = grad * gain
    return scale * (
        inner
        - jnp.mean(inner, -1, keepdims=True)
        - hat * jnp.mean(inner * hat, -1, keepdims=True)
    )


def where(condition, action):
    if condition is None:
        action()
    else:
        pl.when(condition)(lambda: action())


class Copy:
    def __init__(self, copy, send_if, recv_if):
        self.copy, self.send_if, self.recv_if = copy, send_if, recv_if
        self.started = self.received = self.sent = False

    def start(self):
        self.started = True
        where(self.send_if, self.copy.start)

    def wait_recv(self):
        self.received = True
        where(self.recv_if, self.copy.wait_recv)

    def wait_send(self):
        self.sent = True
        where(self.send_if, self.copy.wait_send)


class Copies:
    def __init__(self, send_sems, recv_sems):
        self.send_sems, self.recv_sems, self.all = send_sems, recv_sems, []

    def make(self, source, target, device, send_if=None, recv_if=None):
        index = len(self.all)
        copy = Copy(pltpu.make_async_remote_copy(
            src_ref=source,
            dst_ref=target,
            send_sem=self.send_sems.at[index],
            recv_sem=self.recv_sems.at[index],
            device_id=device,
            device_id_type=pl.DeviceIdType.MESH,
        ), send_if, recv_if)
        self.all.append(copy)
        return copy

    def settle(self):
        for copy in self.all:
            if copy.started and not copy.sent:
                copy.wait_send()

    def finish(self):
        for copy in self.all:
            if copy.started and not copy.received:
                copy.wait_recv()
        self.settle()


def slab_rows(block, index):
    return pl.ds(pl.multiple_of((block * 8 + index) * 24, 8), 24)


class Panels:
    def __init__(self, ref, height, first, count):
        self.ref, self.height, self.first, self.count = ref, height, first, count

    def rows(self, panel, block, index):
        return pl.ds(pl.multiple_of((self.first + panel) * self.height + (block * 8 + index) * 24, 8), 24)

    def get(self, block, index):
        parts = [self.ref[self.rows(p, block, index), :] for p in range(self.count)]
        return parts[0] if self.count == 1 else jnp.concatenate(parts, 1)

    def put(self, block, index, value):
        for p in range(self.count):
            self.ref[self.rows(p, block, index), :] = value[:, p * 256 : p * 256 + 256]


N_COPIES = 153


def layer_kernel(
    span, x_in, cot_in, qw_in, kw_in, ow_in, uw_in, dw_in, vec_in, kvb_in,
    to_bo, to_ig, to_q, to_o, to_kv, to_vec, to_up, to_dn, to_small,
    x, cot, qw, kw, ow, uw, dw, vec, kvb,
    bo, ig, g_q, g_o, g_kv, g_vec, g_up, g_dn, g_small,
    KW, Q, O, U, Dn, X, C, KV, ub, WQ, WKV, WO, WU, gains, vsq,
    n1, hat1, scale1, N2, act, dl, OP, NP,
    qz, doz, doT, kvT, bias, sbuf, mixT, dqT, dkv,
    GP, GV, GU, GD, vg,
    SK1, RK1, SK2, RK2,
    RO1, SO2, RO2, RN1, SN2, RN2,
    SQ1, RQ1, SQ2, RQ2, SQ3, RQ3, SQ4, RQ4,
    SO1, QO1, SO2b, RO2b, SO3, RO3, SO4, RO4,
    SP1, RP1, SP2, RP2, SP3, RP3,
    SV1, RV1, SV2, RV2, SV3, RV3,
    SU1, RU1, SU2, RU2, SU3, RU3, RXU,
    SD1, RD1, SD2, RD2, RXD,
    NS1, NS2,
    send_sems, recv_sems, save_sems, load_sems,
):
    tok = x.shape[0]
    f = lax.axis_index("fsdp")
    s = lax.axis_index("seq")
    z = lax.div(s, 2)
    y = lax.rem(s, 2)
    yo = 1 - y
    fc = f + 1 - 2 * lax.rem(f, 2)
    fx = lax.rem(f + 2, 4)
    fd = 3 - f
    zk = (z, z + 1 - 2 * lax.rem(z, 2), lax.rem(z + 2, 4), 3 - z)
    dev_c, dev_x, dev_d = (fc, s), (fx, s), (fd, s)
    dev_y = (f, z * 2 + yo)
    dev_z = tuple((f, zz * 2 + y) for zz in zk)
    dev_zy = tuple((f, zz * 2 + yo) for zz in zk)
    fsdp_devs = (dev_c, dev_x, dev_d)
    seq_devs = dev_z[1:] + dev_zy
    far = (3, 2, 1)

    copies = Copies(send_sems, recv_sems)
    make = copies.make

    def start(*wanted):
        for copy in wanted:
            copy.start()

    def arrive(*wanted):
        for copy in wanted:
            copy.wait_recv()

    saved = []

    def save(source, target):
        copy = pltpu.make_async_copy(source, target, save_sems.at[len(saved)])
        copy.start()
        saved.append(copy)

    def seq_gather(ref):
        to_z = [None] + [make(ref(z, y), ref(z, y), dev_z[k]) for k in (1, 2, 3)]
        to_y = [make(ref(zk[k], y), ref(zk[k], y), dev_y) for k in range(4)]
        return to_z, to_y

    w_z, w_y = seq_gather(lambda i, j: KW.at[f, i, j])
    q_z, q_y = seq_gather(lambda i, j: Q.at[f, i, j])
    o_z, o_y = seq_gather(lambda i, j: O.at[f, i, j])
    p_z, p_y = seq_gather(lambda i, j: O.at[fx, i, j])
    u_z, u_y = seq_gather(lambda i, j: U.at[i, j])
    d_z, d_y = seq_gather(lambda i, j: Dn.at[i, j])
    k_z, k_y = seq_gather(lambda i, j: KV.at[i, j])

    def fsdp_gather(ref):
        to_x = [make(ref(f, j), ref(f, j), dev_x) for j in (y, yo)]
        to_c = [make(ref(f, j), ref(f, j), dev_c) for j in (y, yo)]
        on_c = [make(ref(fx, j), ref(fx, j), dev_c) for j in (y, yo)]
        return to_x, to_c, on_c

    w_x, w_c, w_xc = fsdp_gather(lambda i, j: KW.at[i, :, j])
    q_x, q_c, q_xc = fsdp_gather(lambda i, j: Q.at[i, :, j])
    q_xs = [make(Q.at[f, zz, yo], Q.at[f, zz, yo], dev_x) for zz in zk]
    o_x = make(O.at[f, z, y], O.at[f, z, y], dev_x)
    o_c = [make(O.at[f, :, j], O.at[f, :, j], dev_c) for j in (y, yo)]
    op_c = [make(O.at[fx, :, j], O.at[fx, :, j], dev_c) for j in (y, yo)]

    def token_gather(ref):
        return (
            make(ref.at[f], ref.at[f], dev_x),
            make(ref.at[f], ref.at[f], dev_c),
            make(ref.at[fx], ref.at[fx], dev_c),
        )

    x_x, x_c, x_xc = token_gather(X)
    c_x, c_c, c_xc = token_gather(C)
    u_f = [make(ub.at[g], U.at[z, y, f], dev) for g, dev in zip((fc, fx, fd), fsdp_devs)]

    rk1 = [make(SK1.at[zz], RK1.at[zz], dev_y) for zz in zk]
    rk2 = [make(SK2.at[k], RK2.at[k], dev_z[k + 1]) for k in range(3)]
    out_c = [make(OP.at[g], RO1.at[i], dev_c) for i, g in enumerate((fc, fd))]
    out_x = make(SO2, RO2, dev_x)
    nrm_c = [make(NP.at[g], RN1.at[i], dev_c) for i, g in enumerate((fc, fd))]
    nrm_x = make(SN2, RN2, dev_x)

    def full_scatter(S1, R1, S2, R2, S3, R3, S4, R4):
        return (
            make(S1, R1, dev_c),
            [make(S2.at[i], R2.at[i], dev_x) for i in range(2)],
            make(S3, R3, dev_y),
            [make(S4.at[k], R4.at[k], dev_z[k + 1]) for k in range(3)],
        )

    q_sc = full_scatter(SQ1, RQ1, SQ2, RQ2, SQ3, RQ3, SQ4, RQ4)
    p_c = make(SP1, RP1, dev_c)
    p_x = make(SP2, RP2, dev_x)
    p_s = [make(SP3.at[i], RP3.at[i], dev) for i, dev in enumerate(seq_devs)]
    v_c = make(SV1, RV1, dev_c)
    v_x = make(SV2, RV2, dev_x)
    v_s = [make(SV3, RV3.at[i], dev) for i, dev in enumerate(seq_devs)]
    o_sc = full_scatter(SO1, QO1, SO2b, RO2b, SO3, RO3, SO4, RO4)
    su_y = [make(SU1.at[zz], RU1.at[zz], dev_y) for zz in zk]
    inner = lax.div(z + 1, 2) == 1
    outer = lax.div(z + 1, 2) != 1

    def relayed(S2, R2, RX):
        to_z = [make(S2.at[k], R2.at[k], dev_z[k + 1]) for k in range(2)]
        to_z.append(make(S2.at[2], R2.at[2], dev_z[3], inner, inner))
        return to_z, make(S2.at[2], RX, dev_z[1], outer, inner)

    su_z, su_r = relayed(SU2, RU2, RXU)
    su_f = [make(SU3.at[g], RU3.at[i], dev) for i, (g, dev) in enumerate(zip((fc, fx, fd), fsdp_devs))]
    sd_y = [make(SD1.at[zz], RD1.at[zz], dev_y) for zz in zk]
    sd_z, sd_r = relayed(SD2, RD2, RXD)
    n_f = [make(NS1.at[f], NS1.at[f], dev) for dev in fsdp_devs]
    n_s = [make(NS2.at[s], NS2.at[s], dev) for dev in seq_devs]

    barrier = pltpu.get_barrier_semaphore()
    for dev in fsdp_devs + seq_devs:
        pl.semaphore_signal(barrier, inc=1, device_id=dev, device_id_type=pl.DeviceIdType.MESH)

    loads = []
    pairs = (
        (vec_in, vec), (kvb_in, kvb), (kw_in, kw), (qw_in, qw), (ow_in, ow),
        (x_in, x), (cot_in, cot), (uw_in, uw), (dw_in, dw),
    )
    for i, (source, target) in enumerate(pairs):
        copy = pltpu.make_async_copy(source, target, load_sems.at[i])
        copy.start()
        loads.append(copy)
    for copy in loads:
        copy.wait()

    vsq[...] = jnp.zeros((128, 128), F32)
    vsq[0:11, 0:24] = vec[...]
    vsq[11:12, 0:16] = kvb[...]
    KW[f, z, y, :, :128] = kw[...].astype(BF16)
    KW[f, z, y, :, 128:] = vsq[...].T[:24, :].astype(BF16)
    Q[f, z, y] = qw[...].astype(BF16)
    O[f, z, y] = ow[...].astype(BF16)
    for j in range(4):
        ub[j] = uw[:, j * D : (j + 1) * D].astype(BF16)
    U[z, y, f] = ub[f]
    Dn[z, y] = dw[...].astype(BF16)
    X[f] = x[...]
    C[f] = cot[...]

    @pl.when(outer)
    def _():
        RU2[2] = jnp.zeros((4, 24, D), BF16)
        RD2[2] = jnp.zeros((96, D), BF16)

    pl.semaphore_wait(barrier, 10)
    start(w_z[3], w_z[2], w_z[1], w_y[0])
    start(o_x, q_z[3], q_z[2], q_z[1], q_y[0])
    start(o_z[3], o_z[2], o_z[1], o_y[0])

    hat, scale = normalise(x[...].astype(F32))
    hat1[...] = hat
    scale1[...] = jnp.broadcast_to(scale, (tok, 128))
    own_span = span[0, s]
    lane = lax.broadcasted_iota(jnp.int32, (tok, 128), 1)
    spot = lax.broadcasted_iota(jnp.int32, (tok, 128), 0) + own_span * tok
    in_head = lax.rem(lane, 64)
    step = lax.rem(in_head, ROT_DIMS // 2).astype(F32)
    inverse = jnp.exp(step * (-2.0 * math.log(10000.0) / ROT_DIMS))
    angle = spot.astype(F32) * (0.25 * inverse)
    sine = jnp.sin(angle)
    cosine = jnp.where(in_head < ROT_DIMS, jnp.cos(angle), 1.0)
    sine_low = jnp.where(in_head < ROT_DIMS // 2, sine, 0.0)
    sine_high = jnp.where((in_head >= ROT_DIMS // 2) & (in_head < ROT_DIMS), sine, 0.0)
    key_lane = lane < 64
    key_cos = jnp.where(key_lane, cosine, 1.0)
    key_low = jnp.where(key_lane, sine_low, 0.0)
    key_high = jnp.where(key_lane, sine_high, 0.0)

    def turn(block, cos_t, low_t, high_t):
        up = pltpu.roll(block, 120, 1)
        down = pltpu.roll(block, 8, 1)
        return block * cos_t - up * low_t + down * high_t

    def turn_back(block, cos_t, low_t, high_t):
        up = pltpu.roll(block, 120, 1)
        down = pltpu.roll(block, 8, 1)
        return block * cos_t + up * low_t - down * high_t

    def forward(to_z, to_y, *which):
        for k in which:
            arrive(to_z[k])
            start(to_y[k])

    forward(w_z, w_y, *far)
    start(w_x[0], w_c[0])
    arrive(o_x)
    start(p_z[3], p_z[2], p_z[1], p_y[0])
    arrive(*w_y)
    start(w_x[1], w_c[1])
    forward(q_z, q_y, *far)
    start(q_x[0], q_c[0])
    arrive(w_x[0])
    start(w_xc[0])
    arrive(w_x[1])
    start(w_xc[1])
    arrive(*w_c, *w_xc)
    slabs = [KW[g, i, j].astype(F32) for g in range(4) for i in range(4) for j in range(2)]
    for i in range(16):
        pair = jnp.concatenate([slabs[2 * i][:, :128], slabs[2 * i + 1][:, :128]], 0)
        WKV[i * 48 : (i + 1) * 48, :] = pair.astype(BF16)
    gains[...] = jnp.concatenate([slab[:, 128:] for slab in slabs], 0).T
    vsq[...] = jnp.concatenate([slab[:16, 128:] for slab in slabs[:8]], 0).T
    kv_shift = vsq[11:12, :]
    n1[...] = (hat * gains[0:1, :] + gains[1:2, :]).astype(BF16)
    kv_pre = dot_nn(n1[...], WKV[...]) + kv_shift
    KV[z, y] = turn(kv_pre, key_cos, key_low, key_high).astype(BF16)
    start(k_z[3], k_z[2], k_z[1], k_y[0])
    for k in range(4):
        arrive(q_y[k])
        start(q_xs[k])
    start(q_c[1])
    forward(o_z, o_y, *far)
    start(o_c[0])
    forward(p_z, p_y, *far)
    start(op_c[0])
    arrive(q_x[0])
    start(q_xc[0])
    vg[...] = jnp.zeros((128, D), F32)
    csum = jnp.sum(cot[...].astype(F32), 0, keepdims=True)
    vg[5:6, :] = csum
    vg[6:7, :] = csum
    key_iota = lax.broadcasted_iota(jnp.int32, (tok, tok), 0)
    row_iota = lax.broadcasted_iota(jnp.int32, (tok, tok), 1) + own_span * tok
    for i in range(8):
        bias[i * tok : (i + 1) * tok, :] = jnp.where(
            key_iota + span[0, i] * tok <= row_iota, 0.0, MASKED
        ).astype(F32)
    dkv[...] = jnp.zeros((8 * tok, 128), F32)
    start(*u_f)
    forward(k_z, k_y, *far)
    arrive(*q_xs)
    start(q_xc[1])
    arrive(*o_y)
    start(o_c[1])
    arrive(*p_y)
    start(op_c[1])
    arrive(*u_f)
    start(u_z[3], u_z[2], u_z[1], u_y[0])
    start(x_x, c_x, x_c, c_c)
    arrive(*q_c, *q_xc)

    def join(ref, whole):
        def put(i, carry):
            g = lax.div(i, 4)
            zz = lax.rem(i, 4)
            pair = jnp.concatenate([ref[g, zz, 0].astype(F32), ref[g, zz, 1].astype(F32)], 0)
            whole[pl.ds(pl.multiple_of(i * 48, 16), 48), :] = pair.astype(BF16)
            return carry

        lax.fori_loop(0, 16, put, 0)

    join(Q, WQ)
    q_pre = dot_nn(n1[...], WQ[...]) + gains[4:5, :]
    gap = jnp.zeros((tok, 64), BF16)
    for j in range(6):
        cols = slice(j * 128, j * 128 + 128)
        turned = turn(q_pre[:, cols], cosine, sine_low, sine_high).astype(BF16).astype(F32)
        turned = (turned * HD ** (-0.5)).astype(BF16)
        qz[2 * j] = jnp.concatenate([turned[:, :64], gap], 1)
        qz[2 * j + 1] = jnp.concatenate([turned[:, 64:], gap], 1)
    arrive(*o_c, *op_c)
    join(O, WO)
    mixed_back = dot_nt(cot[...], WO[...]).astype(BF16)
    for j in range(6):
        pair = mixed_back[:, j * 128 : j * 128 + 128]
        doz[2 * j] = jnp.concatenate([gap, pair[:, :64]], 1)
        doz[2 * j + 1] = jnp.concatenate([gap, pair[:, 64:]], 1)
    doT[...] = mixed_back.astype(F32).T.astype(BF16).reshape(HQ, HD, tok)
    arrive(*k_y)
    KVF = KV.reshape(8 * tok, 128)
    kvT[...] = KVF[...].astype(F32).T.astype(BF16)

    span_rows = 2 * tok
    chunks = 8 * tok // span_rows

    def fold(values, reduce):
        return reduce(values.reshape(span_rows // 8, 8, tok), axis=0)

    def attend(step_index):
        heads = [step_index * 2, step_index * 2 + 1]
        top, total, share, delta, acc = {}, {}, {}, {}, {}

        def rows_of(i):
            return pl.ds(i * span_rows, span_rows)

        def held_of(j, i):
            return pl.ds((j * chunks + i) * span_rows, span_rows)

        def score(j, i):
            scores = dot_nt(KVF[rows_of(i), :], qz[heads[j]]) + bias[rows_of(i), :]
            sbuf[held_of(j, i), :] = scores
            here = fold(scores, jnp.max)
            top[j] = here if i == 0 else jnp.maximum(top[j], here)
            if i == chunks - 1:
                top[j] = jnp.max(top[j], axis=0, keepdims=True)

        def weigh(j, i):
            weights = jnp.exp(sbuf[held_of(j, i), :] - top[j])
            sbuf[held_of(j, i), :] = weights
            here = fold(weights, jnp.sum)
            total[j] = here if i == 0 else total[j] + here
            if i == chunks - 1:
                share[j] = 1.0 / jnp.sum(total[j], axis=0, keepdims=True)

        def mix(j, i):
            rows = rows_of(i)
            probs = sbuf[held_of(j, i), :] * share[j]
            probs_low = probs.astype(BF16)
            sbuf[held_of(j, i), :] = probs
            here = dot_nn(kvT[:, rows], probs_low)
            acc[j] = here if i == 0 else acc[j] + here
            dkv[rows, :] += dot_nn(probs_low, doz[heads[j]])
            if i == chunks - 1:
                mixed = acc[j][64:, :]
                mixT[heads[j]] = mixed.astype(BF16)
                delta[j] = jnp.sum(mixed * doT[heads[j]].astype(F32), axis=0, keepdims=True)

        def back(j, i):
            rows = rows_of(i)
            prob_grad = dot_nt(KVF[rows, :], doz[heads[j]])
            score_low = (sbuf[held_of(j, i), :] * (prob_grad - delta[j])).astype(BF16)
            here = dot_nn(kvT[:, rows], score_low)
            acc[j] = here if i == 0 else acc[j] + here
            dkv[rows, :] += dot_nn(score_low, qz[heads[j]])
            if i == chunks - 1:
                dqT[heads[j]] = acc[j][:64, :] * HD ** (-0.5)

        for stage in (
            ((score, 0),),
            ((weigh, 0), (score, 1)),
            ((mix, 0), (weigh, 1)),
            ((back, 0), (mix, 1)),
            ((back, 1),),
        ):
            for i in range(chunks):
                for part, j in stage:
                    part(j, i)

    def attend_all(first, last, meanwhile):
        def body_step(step_index, carry):
            for at, action in meanwhile:
                pl.when(step_index == at)(action)
            attend(step_index)
            return carry

        lax.fori_loop(first, last, body_step, 0)


    def pump_two():
        forward(u_z, u_y, 1)

    def pump_three():
        forward(u_z, u_y, 3, 2)

    def pump_four():
        forward(d_z, d_y, 1)
        arrive(x_x, c_x)
        start(x_xc, c_xc)

    def pump_five():
        forward(d_z, d_y, 3)

    attend_all(
        0, HQ // 2,
        (
            (1, lambda: start(d_z[3], d_z[2], d_z[1], d_y[0])),
            (2, pump_two), (3, pump_three), (4, pump_four), (5, pump_five),
        ),
    )

    for k in (3, 2, 1, 0):
        rows = pl.ds(pl.multiple_of((2 * zk[k] + yo) * tok, 8), tok)
        SK1[zk[k]] = dkv[rows, :].astype(BF16)
        start(rk1[k])
    mix_low = mixT.reshape(D, tok)[...]
    for c in range(3):
        sbuf[(3 + c) * D : (4 + c) * D, :] = dot_nn(mix_low, cot[:, c * 256 : c * 256 + 256])
    GQ = Panels(sbuf, D, 0, 3)
    GO = Panels(sbuf, D, 3, 3)

    def scatter_c(G, S1, copy):
        def put(i, carry):
            for j, g in enumerate((fc, fd)):
                S1[j, i] = G.get(g, i).astype(S1.dtype)
            return carry

        lax.fori_loop(0, 8, put, 0)
        start(copy)

    def scatter_x(G, R1, S2, copies_):
        arrive(copies_[0])
        for j, yy in enumerate((yo, y)):
            for i in range(4):
                slab = 2 * i + yy
                S2[j, i] = (G.get(fx, slab) + R1[1, slab].astype(F32)).astype(S2.dtype)
                G.put(f, slab, G.get(f, slab) + R1[0, slab].astype(F32))
            start(copies_[1][j])

    def scatter_y(G, R2, S3, copies_):
        arrive(copies_[1][0])
        for i in range(4):
            S3[i] = (G.get(f, 2 * i + yo) + R2[0, i].astype(F32)).astype(S3.dtype)
        start(copies_[2])

    def scatter_z(G, R2, R3, S4, copies_):
        arrive(copies_[1][1], copies_[2])
        for k in far:
            total = G.get(f, 2 * zk[k] + y) + R2[1, zk[k]].astype(F32) + R3[zk[k]].astype(F32)
            S4[k - 1] = total.astype(S4.dtype)
            start(copies_[3][k - 1])

    def scatter_end(G, R2, R3, R4, copies_):
        total = G.get(f, 2 * z + y) + R2[1, z].astype(F32) + R3[z].astype(F32)
        for k in range(3):
            arrive(copies_[3][k])
            total = total + R4[k].astype(F32)
        return total

    scatter_c(GO, SO1, o_sc[0])
    q_back = dqT.reshape(D, tok)[...].T
    parts = []
    for j in range(6):
        parts.append(
            turn_back(q_back[:, j * 128 : j * 128 + 128], cosine, sine_low, sine_high).astype(BF16)
        )
    q_low = jnp.concatenate(parts, 1)
    vg[4:5, :] = jnp.sum(q_low.astype(F32), 0, keepdims=True)
    for c in range(3):
        sbuf[c * D : (c + 1) * D, :] = dot_tn(n1[...], q_low[:, c * 256 : c * 256 + 256])
    scatter_c(GQ, SQ1, q_sc[0])
    forward(d_z, d_y, 2)
    arrive(*u_y, x_c, x_xc)

    def pair_step(k):
        arrive(rk1[k])
        rows = pl.ds(pl.multiple_of((2 * zk[k] + y) * tok, 8), tok)
        SK2[k - 1] = (dkv[rows, :] + RK1[zk[k]].astype(F32)).astype(BF16)
        start(rk2[k - 1])

    def lift_one():
        pair_step(3)

    def lift_two():
        pair_step(2)
        scatter_x(GO, QO1, SO2b, o_sc)

    def lift_three():
        pair_step(1)
        scatter_x(GQ, RQ1, SQ2, q_sc)

    def tokens_to_x():
        arrive(*out_c, *nrm_c)
        SO2[...] = (OP[fx].astype(F32) + RO1[1].astype(F32)).astype(BF16)
        start(out_x)
        SN2[...] = (NP[fx].astype(F32) + RN1[1].astype(F32)).astype(BF16)
        start(nrm_x)

    def down_rows(k):
        return pl.ds(pl.multiple_of((zk[k] * 2 + y) * 96, 8), 96)

    def down_step(k):
        arrive(sd_y[k])
        total = GD[down_rows(k), :] + RD1[zk[k]].astype(F32)
        if k in (0, 2):
            GD[down_rows(k), :] = total
        if k:
            SD2[k - 1] = total.astype(BF16)
        if k == 2:
            pl.when(outer)(lambda: start(sd_z[1]))
        elif k:
            start(sd_z[k - 1])
        if k == 3:
            start(sd_r)

    def down_relay():
        arrive(sd_r)

        @pl.when(inner)
        def _():
            SD2[1] = (GD[down_rows(2), :] + RXD[...].astype(F32)).astype(BF16)
            start(sd_z[1])

    def up_step(k):
        arrive(su_y[k])
        for g in range(4):
            rows = slab_rows(g, zk[k] * 2 + y)
            total = GU[rows, :] + RU1[zk[k], g].astype(F32)
            if k in (0, 2):
                GU[rows, :] = total
            if k:
                SU2[k - 1, g] = total.astype(BF16)
        if k == 2:
            pl.when(outer)(lambda: start(su_z[1]))
        elif k:
            start(su_z[k - 1])
        if k == 3:
            start(su_r)

    def up_relay():
        arrive(su_r)

        @pl.when(inner)
        def _():
            for g in range(4):
                total = GU[slab_rows(g, zk[2] * 2 + y), :] + RXU[g].astype(F32)
                SU2[1, g] = total.astype(BF16)
            start(su_z[1])

    up_totals = []

    def up_end():
        arrive(*su_z)
        for g in range(4):
            total = GU[slab_rows(g, s), :]
            for k in range(3):
                total = total + RU2[k, g].astype(F32)
            up_totals.append(total)
            g_up[g] = total
            SU3[g] = total.astype(BF16)
        start(*su_f)

    for g in range(4):
        for i in range(4):
            pair = jnp.concatenate([U[i, j, g].astype(F32) for j in range(2)], 0)
            WU[(g * 4 + i) * 48 : (g * 4 + i + 1) * 48, :] = pair.astype(BF16)
    WD = Dn.reshape(D, D)
    up_bias = gains[pl.ds(7 + f, 1), :]

    def slope_rows(c, t):
        return pl.ds(pl.multiple_of(c * 4 * tok + t * tok, tok), tok)

    def lift_block(t, carry):
        for at, action in ((1, lift_one), (2, lift_two), (3, lift_three)):
            pl.when(t == at)(action)
        rows = pl.ds(pl.multiple_of(t * tok, tok), tok)
        hat2, _ = normalise(X[t].astype(F32))
        low2 = (hat2 * gains[2:3, :] + gains[3:4, :]).astype(BF16)
        N2[rows, :] = low2
        for c in range(3):
            units = slice(c * 256, c * 256 + 256)
            lifted = dot_nn(low2, WU[:, units]) + up_bias[:, units]
            half = 0.5 + 0.5 * lax.erf(lifted * (0.5**0.5))
            act[rows, units] = (lifted * half).astype(BF16)
            bell = jnp.exp(lifted * lifted * -0.5) * (1.0 / math.sqrt(2.0 * math.pi))
            bias[slope_rows(c, t), :] = half + lifted * bell
        return carry

    lax.fori_loop(0, 4, lift_block, 0)
    arrive(c_c, c_xc)
    CF = C.reshape(4 * tok, D)
    for c in range(3):
        units = slice(c * 256, c * 256 + 256)
        GD[units, :] = dot_tn(act[:, units], CF[...])
    for k in (3, 2, 1, 0):
        SD1[zk[k]] = GD[pl.ds(pl.multiple_of((zk[k] * 2 + yo) * 96, 8), 96), :].astype(BF16)
        start(sd_y[k])
    arrive(*d_y)

    def back_one():
        scatter_y(GO, RO2b, SO3, o_sc)

    def back_two():
        down_step(3)

    def back_three():
        scatter_y(GQ, RQ2, SQ3, q_sc)

    def back_block(t, carry):
        for at, action in ((1, back_one), (2, back_two), (3, back_three)):
            pl.when(t == at)(action)
        two_gain, two_shift, up_sum = carry
        rows = pl.ds(pl.multiple_of(t * tok, tok), tok)
        back = C[t]
        sums = []
        for c in range(3):
            units = slice(c * 256, c * 256 + 256)
            low = (bias[slope_rows(c, t), :] * dot_nt(back, WD[units, :])).astype(BF16)
            dl[rows, units] = low
            sums.append(jnp.sum(low.astype(F32), 0, keepdims=True))
        OP[t] = dot_nn(act[rows, :], WD[...]).astype(BF16)
        grad2 = dot_nt(dl[rows, :], WU[...])
        NP[t] = grad2.astype(BF16)
        hat2, _ = normalise(X[t].astype(F32))
        return (
            two_gain + jnp.sum(grad2 * hat2, 0, keepdims=True),
            two_shift + jnp.sum(grad2, 0, keepdims=True),
            up_sum + jnp.concatenate(sums, 1),
        )

    zero_row = jnp.zeros((1, D), F32)
    two_gain, two_shift, up_sum = lax.fori_loop(0, 4, back_block, (zero_row,) * 3)
    vg[2:3, :] = two_gain
    vg[3:4, :] = two_shift
    vg[pl.ds(7 + f, 1), :] = up_sum
    start(*out_c, *nrm_c)
    down_step(2)
    for c in range(3):
        units = slice(c * 256, c * 256 + 256)
        GU[units, :] = dot_tn(N2[:, units], dl[...])
    for k in (3, 2, 1, 0):
        for g in range(4):
            SU1[zk[k], g] = GU[slab_rows(g, zk[k] * 2 + yo), :].astype(BF16)
        start(su_y[k])
    down_step(1)
    grad1 = dot_nt(q_low, WQ[...])
    arrive(rk1[0])
    kv_back = dkv[pl.ds(pl.multiple_of((2 * z + y) * tok, 8), tok), :] + RK1[z].astype(F32)
    for k in range(3):
        arrive(rk2[k])
        kv_back = kv_back + RK2[k].astype(F32)
    kv_low = turn_back(kv_back, key_cos, key_low, key_high).astype(BF16)
    grad1 = grad1 + dot_nt(kv_low, WKV[...])
    vg[0:1, :] = jnp.sum(grad1 * hat1[...], 0, keepdims=True)
    vg[1:2, :] = jnp.sum(grad1, 0, keepdims=True)
    kv_sum = jnp.sum(kv_low.astype(F32), 0, keepdims=True)
    short = jnp.zeros((1, 8), F32)
    spread = jnp.concatenate(
        [part for i in range(8) for part in (kv_sum[:, i * 16 : i * 16 + 16], short)], 1
    )
    vg[11:12, :] = jnp.concatenate([spread] * 4, 1)
    GP[...] = dot_tn(n1[...], kv_low)
    flipped = vg[...].T

    def packed(g):
        parts = [flipped[(g * 8 + i) * 24 : (g * 8 + i + 1) * 24, :16] for i in range(8)]
        return jnp.concatenate(parts, 1)

    for g in range(4):
        GV[g] = packed(g)
    for i in range(8):
        for j, g in enumerate((fc, fd)):
            SP1[j, i] = GP[slab_rows(g, i), :].astype(BF16)
    for j, g in enumerate((fc, fd)):
        SV1[j] = GV[g]
    start(p_c, v_c)
    down_relay()
    down_step(0)
    arrive(p_c, v_c)
    for i in range(8):
        SP2[i] = (GP[slab_rows(fx, i), :] + RP1[1, i].astype(F32)).astype(BF16)
    SV2[...] = GV[fx] + RV1[1]
    start(p_x, v_x)
    tokens_to_x()
    scatter_z(GO, RO2b, RO3, SO4, o_sc)
    arrive(p_x, v_x)

    def kv_sum_of(slab):
        return GP[slab_rows(f, slab), :] + RP1[0, slab].astype(F32) + RP2[slab].astype(F32)

    seq_slabs = [2 * zk[k] + y for k in (1, 2, 3)] + [2 * zk[k] + yo for k in range(4)]
    for i, slab in enumerate(seq_slabs):
        SP3[i] = kv_sum_of(slab).astype(BF16)
    SV3[...] = GV[f] + RV1[0] + RV2[...]
    start(*p_s, *v_s)
    up_step(3)
    scatter_z(GQ, RQ2, RQ3, SQ4, q_sc)
    up_step(2)
    up_step(1)
    up_relay()
    up_step(0)
    mixed_rows = mix_low.astype(F32).T.astype(BF16)
    arrive(out_x)
    bo[...] = (
        x[...].astype(F32)
        + (dot_nn(mixed_rows, WO[...]) + gains[5:6, :])
        + (OP[f].astype(F32) + RO1[0].astype(F32) + RO2[...].astype(F32) + gains[6:7, :])
    ).astype(BF16)
    save(bo, to_bo)
    arrive(nrm_x)
    grad2 = NP[f].astype(F32) + RN1[0].astype(F32) + RN2[...].astype(F32)
    hat_rows = hat1[...]
    scale_rows = scale1[:, 0:1]
    ig[...] = (
        cot[...].astype(F32)
        + norm_back(grad1, hat_rows, scale_rows, gains[0:1, :])
        + norm_back(grad2, hat_rows, scale_rows, gains[2:3, :])
    )
    save(ig, to_ig)
    copies.settle()
    q_grad = scatter_end(GQ, RQ2, RQ3, RQ4, q_sc)
    g_q[...] = q_grad
    save(g_q, to_q)
    o_grad = scatter_end(GO, RO2b, RO3, RO4, o_sc)
    g_o[...] = o_grad
    save(g_o, to_o)
    kv_grad = kv_sum_of(s)
    vec_sum = SV3[...]
    for i in range(7):
        arrive(p_s[i], v_s[i])
        kv_grad = kv_grad + RP3[i].astype(F32)
        vec_sum = vec_sum + RV3[i]
    vec_own = jnp.zeros((24, 16), F32)
    for i in range(8):
        vec_own = vec_own + jnp.where(s == i, vec_sum[:, i * 16 : i * 16 + 16], 0.0)
    vec_grad = jnp.concatenate([vec_own, jnp.zeros((24, 112), F32)], 1)
    g_kv[...] = kv_grad
    g_vec[...] = vec_grad
    save(g_kv, to_kv)
    save(g_vec, to_vec)
    rows = pl.ds(pl.multiple_of(s * 96, 8), 96)
    down_grad = GD[rows, :]
    for k in range(3):
        arrive(sd_z[k])
        down_grad = down_grad + RD2[k].astype(F32)
    g_dn[...] = down_grad
    save(g_dn, to_dn)
    up_end()
    save(g_up.at[f], to_up.at[f])

    def energy(values):
        return jnp.sum(jnp.sum(values * values, 0, keepdims=True), 1, keepdims=True)

    lanes = lax.broadcasted_iota(jnp.int32, (24, 128), 1)
    squares = energy(q_grad) + energy(o_grad) + energy(kv_grad) + energy(jnp.where(lanes == 11, 0.0, vec_grad)) + energy(g_dn[...])
    for total in up_totals:
        squares = squares + energy(total)
    kv_rows = jnp.concatenate([vec_grad, jnp.zeros((104, 128), F32)], 0).T
    line = lax.broadcasted_iota(jnp.int32, (8, 128), 0)
    column = lax.broadcasted_iota(jnp.int32, (8, 128), 1)
    kv_line = jnp.where(column < 16, jnp.broadcast_to(kv_rows[11:12, :], (8, 128)), 0.0)
    NS1[f] = jnp.where(line == 0, squares, kv_line)
    start(*n_f)
    arrive(*n_f)
    kv_piece = NS1[0][1:2, :]
    chip = NS1[0] + NS1[1] + NS1[2] + NS1[3]
    part = chip[0:1, 0:1] + jnp.sum(kv_piece * kv_piece, 1, keepdims=True)
    NS2[s] = jnp.broadcast_to(part, (8, 128))
    start(*n_s)
    for i, g in enumerate((fc, fx, fd)):
        arrive(su_f[i])
        g_up[g] = RU3[i].astype(F32)
        save(g_up.at[g], to_up.at[g])
    arrive(*n_s)
    everything = NS2[0]
    for i in range(1, 8):
        everything = everything + NS2[i]
    g_small[...] = jnp.where(line == 0, everything, jnp.broadcast_to(kv_piece, (8, 128)))
    save(g_small, to_small)
    copies.finish()
    assert len(copies.all) == N_COPIES, len(copies.all)
    for copy in saved:
        copy.wait()


def update_kernel(
    small, g_q, g_o, g_kv, g_vec, g_up, g_dn, bo_in, ig_in,
    mq, mk, mo, mu, md, mv, mb,
    fq, fk, fo, fu, fdn, fv, fb,
    sq, sk, so, su, sd, sv, sb,
    bo, ig, norm,
    nmq, nmk, nmo, nmu, nmd, nmv, nmb,
    nfq, nfk, nfo, nfu, nfd, nfv, nfb,
    nsq, nsk, nso, nsu, nsd, nsv, nsb,
    residual,
):
    bo[...] = bo_in[...]
    ig[...] = ig_in[...]
    size = jnp.sqrt(small[0:1, 0:1])
    norm[...] = size
    factor = jnp.minimum(1.0, CLIP_NORM / (size + 1e-06))

    def update(grad, master, first, second, new_master, new_first, new_second, rate, decay):
        clipped = grad * factor
        values = adamw(master, clipped, first, second, rate, decay)
        for ref, value in zip((new_master, new_first, new_second), values):
            ref[...] = value

    rates = (MATRIX_RATE, MATRIX_DECAY)
    update(g_q[...], mq[...], fq[...], sq[...], nmq, nfq, nsq, *rates)
    update(g_o[...], mo[...], fo[...], so[...], nmo, nfo, nso, *rates)
    update(g_kv[...], mk[...], fk[...], sk[...], nmk, nfk, nsk, *rates)
    for g in range(4):
        cols = slice(g * D, (g + 1) * D)
        update(
            g_up[g], mu[:, cols], fu[:, cols], su[:, cols],
            nmu.at[:, cols], nfu.at[:, cols], nsu.at[:, cols], *rates,
        )
    update(g_dn[...], md[...], fdn[...], sd[...], nmd, nfd, nsd, *rates)
    flipped = jnp.concatenate([g_vec[...], jnp.zeros((104, 128), F32)], 0).T
    vector_grad = flipped[:11, :24]
    update(vector_grad, mv[...], fv[...], sv[...], nmv, nfv, nsv, VECTOR_RATE, 0.0)
    residual[...] = flipped[5:7, :24] * factor
    update(small[1:2, :16], mb[...], fb[...], sb[...], nmb, nfb, nsb, VECTOR_RATE, 0.0)


def fast_body(
    inputs, cotangent, span_order,
    query_weight, keyval_weight, output_weight, up_weight, down_weight, vectors, kv_bias,
    *moments,
):
    tok = inputs.shape[0]
    smem = pl.BlockSpec(memory_space=pltpu.SMEM)
    shape = jax.ShapeDtypeStruct
    V = pltpu.VMEM
    results_here = (
        shape((tok, D), BF16),
        shape((tok, D), F32),
        shape((24, D), F32),
        shape((24, D), F32),
        shape((24, 128), F32),
        shape((24, 128), F32),
        shape((4, 24, D), F32),
        shape((96, D), F32),
        shape((8, 128), F32),
    )
    operands_here = (
        inputs, cotangent, query_weight, keyval_weight, output_weight, up_weight, down_weight,
        vectors, kv_bias.reshape(1, -1),
    )
    scratch = [V(a.shape, a.dtype) for a in operands_here + results_here]
    scratch += [
        V((4, 4, 2, 24, 256), BF16),
        V((4, 4, 2, 24, D), BF16),
        V((4, 4, 2, 24, D), BF16),
        V((4, 2, 4, 24, D), BF16),
        V((4, 2, 96, D), BF16),
        V((4, tok, D), BF16),
        V((4, tok, D), BF16),
        V((4, 2, tok, 128), BF16),
        V((4, 24, D), BF16),
        V((D, D), BF16),
        V((D, 128), BF16),
        V((D, D), BF16),
        V((D, D), BF16),
        V((128, D), F32),
        V((128, 128), F32),
        V((tok, D), BF16),
        V((tok, D), F32),
        V((tok, 128), F32),
        V((4 * tok, D), BF16),
        V((4 * tok, D), BF16),
        V((4 * tok, D), BF16),
        V((4, tok, D), BF16),
        V((4, tok, D), BF16),
        V((HQ, tok, 128), BF16),
        V((HQ, tok, 128), BF16),
        V((HQ, HD, tok), BF16),
        V((128, 8 * tok), BF16),
        V((12 * tok, tok), F32),
        V((6 * D, 256), F32),
        V((HQ, HD, tok), BF16),
        V((HQ, HD, tok), F32),
        V((8 * tok, 128), F32),
        V((D, 128), F32),
        V((4, 24, 128), F32),
        V((D, D), F32),
        V((D, D), F32),
        V((128, D), F32),
        V((4, tok, 128), BF16), V((4, tok, 128), BF16),
        V((3, tok, 128), BF16), V((3, tok, 128), BF16),
        V((2, tok, D), BF16), V((tok, D), BF16), V((tok, D), BF16),
        V((2, tok, D), BF16), V((tok, D), BF16), V((tok, D), BF16),
    ]
    def scatter_buffers(width):
        found = []
        for lead in ((2, 8), (2, 4), (4,), (3,)):
            found += [V(lead + (24, width), BF16)] * 2
        return found

    scratch += scatter_buffers(D)
    scratch += scatter_buffers(D)
    for lead in ((2, 8), (8,), (7,)):
        scratch += [V(lead + (24, 128), BF16)] * 2
    scratch += [V((2, 24, 128), F32)] * 2 + [V((24, 128), F32)] * 3 + [V((7, 24, 128), F32)]
    scratch += [V((4, 4, 24, D), BF16)] * 2 + [V((3, 4, 24, D), BF16)] * 2
    scratch += [V((4, 24, D), BF16), V((3, 24, D), BF16), V((4, 24, D), BF16)]
    scratch += [V((4, 96, D), BF16)] * 2 + [V((3, 96, D), BF16)] * 2 + [V((96, D), BF16)]
    scratch += [V((4, 8, 128), F32), V((8, 8, 128), F32)]
    scratch += [pltpu.SemaphoreType.DMA((N_COPIES,))] * 2 + [pltpu.SemaphoreType.DMA((12,)), pltpu.SemaphoreType.DMA((9,))]
    kv_row = kv_bias.reshape(1, -1)
    bo, ig, g_q, g_o, g_kv, g_vec, g_up, g_dn, small = pl.pallas_call(
        layer_kernel,
        name="layer",
        out_shape=results_here,
        in_specs=[smem] + [pl.BlockSpec(memory_space=pl.ANY)] * 9,
        out_specs=(pl.BlockSpec(memory_space=pl.ANY),) * 9,
        scratch_shapes=scratch,
        compiler_params=pltpu.CompilerParams(
            collective_id=0, has_side_effects=True, vmem_limit_bytes=62 * 2**20
        ),
    )(
        span_order, inputs, cotangent,
        query_weight, keyval_weight, output_weight, up_weight, down_weight, vectors, kv_row,
    )
    masters = (query_weight, keyval_weight, output_weight, up_weight, down_weight, vectors, kv_row)
    firsts = tuple(moments[:6]) + (moments[6].reshape(1, -1),)
    seconds = tuple(moments[7:13]) + (moments[13].reshape(1, -1),)
    state = [shape(a.shape, F32) for a in masters]
    operands = (small, g_q, g_o, g_kv, g_vec, g_up, g_dn, bo, ig) + masters + firsts + seconds
    outcomes = [shape((tok, D), BF16), shape((tok, D), F32), shape((1, 1), F32)]
    outcomes += state * 3 + [shape((2, vectors.shape[1]), F32)]

    def whole(a):
        return pl.BlockSpec(a.shape, lambda i: (0,) * len(a.shape))

    results = pl.pallas_call(
        update_kernel,
        name="update",
        grid=(1,),
        out_shape=outcomes,
        in_specs=[whole(a) for a in operands],
        out_specs=[whole(a) for a in outcomes],
        compiler_params=pltpu.CompilerParams(vmem_limit_bytes=62 * 2**20),
    )(*operands)
    results = list(results)
    results[2] = results[2].reshape(())
    for i in (9, 16, 23):
        results[i] = results[i].reshape(-1)
    return tuple(results)


def solution(mesh):
    grid = (mesh.shape["fsdp"], mesh.shape["seq"])
    return jax.shard_map(
        fast_body if grid == (4, 8) else body,
        mesh=mesh,
        in_specs=(
            P(("fsdp", "seq"), None),
            P(("fsdp", "seq"), None),
            P("fsdp", None),
            P(("fsdp", "seq"), None),
            P(("fsdp", "seq"), None),
            P(("fsdp", "seq"), None),
            P(("fsdp", "seq"), None),
            P(("fsdp", "seq"), None),
            P(None, ("fsdp", "seq")),
            P("seq"),
            P(("fsdp", "seq"), None),
            P(("fsdp", "seq"), None),
            P(("fsdp", "seq"), None),
            P(("fsdp", "seq"), None),
            P(("fsdp", "seq"), None),
            P(None, ("fsdp", "seq")),
            P("seq"),
            P(("fsdp", "seq"), None),
            P(("fsdp", "seq"), None),
            P(("fsdp", "seq"), None),
            P(("fsdp", "seq"), None),
            P(("fsdp", "seq"), None),
            P(None, ("fsdp", "seq")),
            P("seq"),
        ),
        out_specs=(
            P(("fsdp", "seq"), None),
            P(("fsdp", "seq"), None),
            P(),
            P(("fsdp", "seq"), None),
            P(("fsdp", "seq"), None),
            P(("fsdp", "seq"), None),
            P(("fsdp", "seq"), None),
            P(("fsdp", "seq"), None),
            P(None, ("fsdp", "seq")),
            P("seq"),
            P(("fsdp", "seq"), None),
            P(("fsdp", "seq"), None),
            P(("fsdp", "seq"), None),
            P(("fsdp", "seq"), None),
            P(("fsdp", "seq"), None),
            P(None, ("fsdp", "seq")),
            P("seq"),
            P(("fsdp", "seq"), None),
            P(("fsdp", "seq"), None),
            P(("fsdp", "seq"), None),
            P(("fsdp", "seq"), None),
            P(("fsdp", "seq"), None),
            P(None, ("fsdp", "seq")),
            P("seq"),
            P(None, ("fsdp", "seq")),
        ),
        check_vma=False,
    )
```

```python
import math

import jax
import jax.numpy as jnp
from jax import lax
from jax.experimental import pallas as pl
from jax.experimental.pallas import tpu as pltpu
from jax.sharding import PartitionSpec as P

D = 768
HQ = 12
HD = 64
ROT_DIMS = 16
FF = 3072
KEY_BLOCK = 512
STEP = 10
F32 = jnp.float32
BF16 = jnp.bfloat16


NORM_EPS = 1e-05
MASKED = -1e30
CLIP_NORM = 1.0
BETA_ONE = 0.9
BETA_TWO = 0.999
ADAM_EPS = 1e-08
MATRIX_DECAY = 0.1
MATRIX_RATE = 0.1
VECTOR_RATE = 0.3


def layer_norm(tensor, gain_row, shift_row):
    centre = tensor - jnp.mean(tensor, -1, keepdims=True)
    spread = jnp.mean(centre * centre, -1, keepdims=True)
    return centre * lax.rsqrt(spread + NORM_EPS) * gain_row + shift_row


def rotary_tables(places):
    half_steps = jnp.arange(ROT_DIMS // 2, dtype=jnp.float32)
    inverse = jnp.exp(half_steps * (-2.0 * math.log(10000.0) / ROT_DIMS))
    angles = places.astype(jnp.float32)[:, None] * (0.25 * inverse)[None, :]
    angles = jnp.concatenate([angles, angles], 1)
    return (jnp.cos(angles), jnp.sin(angles))


def rotate(tensor, cosine, sine_table):
    rotary_part = tensor[..., :ROT_DIMS]
    lower_half = rotary_part[..., : ROT_DIMS // 2]
    upper_half = rotary_part[..., ROT_DIMS // 2 :]
    turned = jnp.concatenate([-upper_half, lower_half], -1)
    return jnp.concatenate([rotary_part * cosine + turned * sine_table, tensor[..., ROT_DIMS:]], -1)


def adamw(master, clipped, first_old, second_old, step_rate, decay_rate):
    first_new = BETA_ONE * first_old + (1.0 - BETA_ONE) * clipped
    second_new = BETA_TWO * second_old + (1.0 - BETA_TWO) * clipped * clipped
    ascent = (
        first_new
        / (1.0 - BETA_ONE**STEP)
        / (jnp.sqrt(second_new / (1.0 - BETA_TWO**STEP)) + ADAM_EPS)
    )
    return (master - step_rate * (ascent + decay_rate * master), first_new, second_new)


def gelu_exact(tensor):
    return jax.nn.gelu(tensor, approximate=False)


def across_tokens(left_side, right_side):
    return lax.dot_general(
        left_side, right_side, (((0,), (0,)), ((), ())), preferred_element_type=jnp.float32
    )


def against(left_side, right_side):
    return lax.dot_general(
        left_side, right_side, (((1,), (1,)), ((), ())), preferred_element_type=jnp.float32
    )


def masked_scores(query_rows, row_places, key_block, key_places):
    scores = against(query_rows, key_block) * HD ** (-0.5)
    return jnp.where(key_places[None, :] <= row_places[:, None], scores, MASKED)


def body(
    inputs,
    cotangent,
    span_order,
    query_weight,
    keyval_weight,
    output_weight,
    up_weight,
    down_weight,
    vectors,
    kv_bias,
    first_query,
    first_keyval,
    first_output,
    first_up,
    first_down,
    first_vectors,
    first_kv_bias,
    second_query,
    second_keyval,
    second_output,
    second_up,
    second_down,
    second_vectors,
    second_kv_bias,
):
    tok_rows = inputs.shape[0]
    seq_count = lax.axis_size("seq")
    seq_rank = lax.axis_index("seq")
    order_row = span_order[0]
    token_steps = jnp.arange(tok_rows, dtype=jnp.int32)
    all_places = (order_row[:, None] * tok_rows + token_steps[None, :]).reshape(
        seq_count * tok_rows
    )
    own_span = jnp.sum(jnp.where(jnp.arange(seq_count, dtype=jnp.int32) == seq_rank, order_row, 0))
    own_places = own_span * tok_rows + token_steps
    query_rows_count = tok_rows * HQ
    query_full, keyval_full, output_full, up_full, down_full, vector_full = (
        lax.all_gather(query_weight.astype(jnp.bfloat16), ("fsdp", "seq"), axis=0, tiled=True),
        lax.all_gather(keyval_weight.astype(jnp.bfloat16), ("fsdp", "seq"), axis=0, tiled=True),
        lax.all_gather(output_weight.astype(jnp.bfloat16), ("fsdp", "seq"), axis=0, tiled=True),
        lax.all_gather(up_weight.astype(jnp.bfloat16), ("fsdp", "seq"), axis=0, tiled=True),
        lax.all_gather(down_weight.astype(jnp.bfloat16), ("fsdp", "seq"), axis=0, tiled=True),
        lax.all_gather(vectors.astype(jnp.bfloat16), ("fsdp", "seq"), axis=1, tiled=True),
    )
    kv_shift = lax.all_gather(kv_bias.astype(jnp.bfloat16), "seq", axis=0, tiled=True).astype(
        jnp.float32
    )
    gains = vector_full.astype(jnp.float32)
    states = inputs.astype(jnp.float32)
    normed_one = layer_norm(states, gains[0], gains[1])
    normed_low = normed_one.astype(jnp.bfloat16)
    query_pre = jnp.dot(normed_low, query_full, preferred_element_type=jnp.float32) + gains[4]
    keyval_pre = jnp.dot(normed_low, keyval_full, preferred_element_type=jnp.float32) + kv_shift
    cosine, sine_table = rotary_tables(own_places)

    def turn_queries(tensor):
        return rotate(tensor.reshape(tok_rows, HQ, HD), cosine[:, None, :], sine_table[:, None, :])

    def turn_keys(tensor):
        return jnp.concatenate([rotate(tensor[:, :HD], cosine, sine_table), tensor[:, HD:]], 1)

    query_rows = turn_queries(query_pre).astype(jnp.bfloat16).reshape(query_rows_count, HD)
    local_pairs = turn_keys(keyval_pre).astype(jnp.bfloat16)
    row_places = jnp.broadcast_to(own_places[:, None], (tok_rows, HQ)).reshape(query_rows_count)
    all_pairs = lax.all_gather(local_pairs, "seq", axis=0, tiled=True)
    block_count = all_pairs.shape[0] // KEY_BLOCK
    place_blocks = all_places.reshape(block_count, KEY_BLOCK)

    def lse_step(carry_pair, block_pair):
        running_top, running_total = carry_pair
        pair_block, key_places = block_pair
        scores = masked_scores(query_rows, row_places, pair_block[:, :HD], key_places)
        new_top = jnp.maximum(running_top, jnp.max(scores, 1, keepdims=True))
        running_total = running_total * jnp.exp(running_top - new_top) + jnp.sum(
            jnp.exp(scores - new_top), 1, keepdims=True
        )
        return ((new_top, running_total), None)

    start_carry = (
        jnp.full((query_rows_count, 1), MASKED, jnp.float32),
        jnp.zeros((query_rows_count, 1), jnp.float32),
    )
    (row_top, row_total), _ = lax.scan(
        lse_step, start_carry, (all_pairs.reshape(block_count, KEY_BLOCK, 2 * HD), place_blocks)
    )
    log_total = row_top + jnp.log(row_total)

    def mix_step(mixed_acc, block_pair):
        pair_block, key_places = block_pair
        probs_low = jnp.exp(
            masked_scores(query_rows, row_places, pair_block[:, :HD], key_places) - log_total
        ).astype(jnp.bfloat16)
        return (
            mixed_acc + jnp.dot(probs_low, pair_block[:, HD:], preferred_element_type=jnp.float32),
            None,
        )

    mixed, _ = lax.scan(
        mix_step,
        jnp.zeros((query_rows_count, HD), jnp.float32),
        (all_pairs.reshape(block_count, KEY_BLOCK, 2 * HD), place_blocks),
    )
    mixed_low = mixed.reshape(tok_rows, D).astype(jnp.bfloat16)
    attention_out = jnp.dot(mixed_low, output_full, preferred_element_type=jnp.float32) + gains[5]
    normed_two = layer_norm(states, gains[2], gains[3])
    normed_two_low = normed_two.astype(jnp.bfloat16)
    lifted = jnp.dot(normed_two_low, up_full, preferred_element_type=jnp.float32) + gains[
        7:
    ].reshape(FF)
    active_low = gelu_exact(lifted).astype(jnp.bfloat16)
    block_output = (
        states
        + attention_out
        + jnp.dot(active_low, down_full, preferred_element_type=jnp.float32)
        + gains[6]
    ).astype(jnp.bfloat16)
    back_rows = cotangent.astype(jnp.float32)
    query_back, keyval_back, output_back, up_back, down_back = (
        lax.all_gather(query_weight.astype(jnp.bfloat16), ("fsdp", "seq"), axis=0, tiled=True),
        lax.all_gather(keyval_weight.astype(jnp.bfloat16), ("fsdp", "seq"), axis=0, tiled=True),
        lax.all_gather(output_weight.astype(jnp.bfloat16), ("fsdp", "seq"), axis=0, tiled=True),
        lax.all_gather(up_weight.astype(jnp.bfloat16), ("fsdp", "seq"), axis=0, tiled=True),
        lax.all_gather(down_weight.astype(jnp.bfloat16), ("fsdp", "seq"), axis=0, tiled=True),
    )
    grad_down = across_tokens(active_low, cotangent)
    grad_output = across_tokens(mixed_low, cotangent)
    out_bias_grad = jnp.sum(back_rows, 0)
    active_grad = against(cotangent, down_back)
    _, gelu_pull = jax.vjp(gelu_exact, lifted)
    (lifted_grad,) = gelu_pull(active_grad)
    lifted_low = lifted_grad.astype(jnp.bfloat16)
    grad_up = across_tokens(normed_two_low, lifted_low)
    normed_two_grad = against(lifted_low, up_back)
    mixed_grad = against(cotangent, output_back).astype(jnp.bfloat16).reshape(query_rows_count, HD)
    row_delta = jnp.sum(mixed_grad.astype(jnp.float32) * mixed, 1, keepdims=True)
    pairs_back = lax.all_gather(local_pairs, "seq", axis=0, tiled=True)

    def grad_step(query_acc, block_pair):
        pair_block, key_places = block_pair
        key_block = pair_block[:, :HD]
        probs = jnp.exp(masked_scores(query_rows, row_places, key_block, key_places) - log_total)
        prob_grad = against(mixed_grad, pair_block[:, HD:])
        score_low = (probs * (prob_grad - row_delta)).astype(jnp.bfloat16)
        query_acc = query_acc + jnp.dot(score_low, key_block, preferred_element_type=jnp.float32)
        key_grad = across_tokens(score_low, query_rows) * HD ** (-0.5)
        value_grad = across_tokens(probs.astype(jnp.bfloat16), mixed_grad)
        return (query_acc, jnp.concatenate([key_grad, value_grad], 1))

    query_sum, pair_grads = lax.scan(
        grad_step,
        jnp.zeros((query_rows_count, HD), jnp.float32),
        (pairs_back.reshape(block_count, KEY_BLOCK, 2 * HD), place_blocks),
    )
    query_rot_grad = (query_sum * HD ** (-0.5)).reshape(tok_rows, HQ, HD)
    own_pair_grad = lax.psum_scatter(
        pair_grads.reshape(block_count * KEY_BLOCK, 2 * HD).astype(jnp.bfloat16),
        "seq",
        scatter_dimension=0,
        tiled=True,
    ).astype(jnp.float32)
    _, key_pull = jax.vjp(turn_keys, keyval_pre)
    (keyval_grad,) = key_pull(own_pair_grad)
    keyval_low = keyval_grad.astype(jnp.bfloat16)
    _, query_pull = jax.vjp(turn_queries, query_pre)
    (query_pre_grad,) = query_pull(query_rot_grad)
    query_low = query_pre_grad.astype(jnp.bfloat16)
    grad_query = across_tokens(normed_low, query_low)
    grad_keyval = across_tokens(normed_low, keyval_low)
    kv_bias_part = jnp.sum(keyval_low.astype(jnp.float32), 0)
    normed_one_grad = against(query_low, query_back) + against(keyval_low, keyval_back)
    _, first_pull = jax.vjp(layer_norm, states, gains[0], gains[1])
    input_one, gain_one_grad, shift_one_grad = first_pull(normed_one_grad)
    _, second_pull = jax.vjp(layer_norm, states, gains[2], gains[3])
    input_two, gain_two_grad, shift_two_grad = second_pull(normed_two_grad)
    input_grad = back_rows + input_one + input_two
    vector_grad = jnp.concatenate(
        [
            jnp.stack(
                [
                    gain_one_grad,
                    shift_one_grad,
                    gain_two_grad,
                    shift_two_grad,
                    jnp.sum(query_low.astype(jnp.float32), 0),
                    out_bias_grad,
                    out_bias_grad,
                ]
            ),
            jnp.sum(lifted_low.astype(jnp.float32), 0).reshape(FF // D, D),
        ],
        0,
    )
    reduced = (
        lax.psum_scatter(grad_query, ("fsdp", "seq"), scatter_dimension=0, tiled=True),
        lax.psum_scatter(grad_keyval, ("fsdp", "seq"), scatter_dimension=0, tiled=True),
        lax.psum_scatter(grad_output, ("fsdp", "seq"), scatter_dimension=0, tiled=True),
        lax.psum_scatter(grad_up, ("fsdp", "seq"), scatter_dimension=0, tiled=True),
        lax.psum_scatter(grad_down, ("fsdp", "seq"), scatter_dimension=0, tiled=True),
        lax.psum_scatter(vector_grad, ("fsdp", "seq"), scatter_dimension=1, tiled=True),
    )
    reduced = tuple(reduced)
    local_squares = sum((jnp.sum(gradient * gradient) for gradient in reduced))
    global_squares, kv_bias_total = lax.psum((local_squares, kv_bias_part), ("fsdp", "seq"))
    grad_norm = jnp.sqrt(global_squares + jnp.sum(kv_bias_total * kv_bias_total))
    piece_width = kv_bias.shape[0]
    kv_bias_grad = lax.dynamic_slice_in_dim(kv_bias_total, seq_rank * piece_width, piece_width)
    factor = jnp.minimum(1.0, CLIP_NORM / (grad_norm + 1e-06))
    masters = (query_weight, keyval_weight, output_weight, up_weight, down_weight, vectors, kv_bias)
    all_grads = reduced + (kv_bias_grad,)
    firsts = (
        first_query,
        first_keyval,
        first_output,
        first_up,
        first_down,
        first_vectors,
        first_kv_bias,
    )
    seconds = (
        second_query,
        second_keyval,
        second_output,
        second_up,
        second_down,
        second_vectors,
        second_kv_bias,
    )
    step_rates = (MATRIX_RATE,) * 5 + (VECTOR_RATE, VECTOR_RATE)
    decays = (MATRIX_DECAY,) * 5 + (0.0, 0.0)
    updated = [
        adamw(master, gradient * factor, first_old, second_old, step_rate, decay_rate)
        for master, gradient, first_old, second_old, step_rate, decay_rate in zip(
            masters, all_grads, firsts, seconds, step_rates, decays
        )
    ]
    residual_bias_grads = (reduced[5] * factor)[5:7]
    return (
        block_output,
        input_grad,
        grad_norm,
        updated[0][0],
        updated[1][0],
        updated[2][0],
        updated[3][0],
        updated[4][0],
        updated[5][0],
        updated[6][0],
        updated[0][1],
        updated[1][1],
        updated[2][1],
        updated[3][1],
        updated[4][1],
        updated[5][1],
        updated[6][1],
        updated[0][2],
        updated[1][2],
        updated[2][2],
        updated[3][2],
        updated[4][2],
        updated[5][2],
        updated[6][2],
        residual_bias_grads,
    )


def dot_nn(left, right):
    return lax.dot_general(left, right, (((1,), (0,)), ((), ())), preferred_element_type=F32)


def dot_nt(left, right):
    return lax.dot_general(left, right, (((1,), (1,)), ((), ())), preferred_element_type=F32)


def dot_tn(left, right):
    return lax.dot_general(left, right, (((0,), (0,)), ((), ())), preferred_element_type=F32)


def normalise(rows):
    centre = rows - jnp.mean(rows, -1, keepdims=True)
    scale = lax.rsqrt(jnp.mean(centre * centre, -1, keepdims=True) + NORM_EPS)
    return centre * scale, scale


def norm_back(grad, hat, scale, gain):
    inner = grad * gain
    return scale * (
        inner
        - jnp.mean(inner, -1, keepdims=True)
        - hat * jnp.mean(inner * hat, -1, keepdims=True)
    )


def where(condition, action):
    if condition is None:
        action()
    else:
        pl.when(condition)(lambda: action())


class Copy:
    def __init__(self, copy, send_if, recv_if):
        self.copy, self.send_if, self.recv_if = copy, send_if, recv_if
        self.started = self.received = self.sent = False

    def start(self):
        self.started = True
        where(self.send_if, self.copy.start)

    def wait_recv(self):
        self.received = True
        where(self.recv_if, self.copy.wait_recv)

    def wait_send(self):
        self.sent = True
        where(self.send_if, self.copy.wait_send)


class Group:
    def __init__(self, whole, sem):
        self.whole, self.sem, self.members, self.waited = whole, sem, [], False

    def wait_recv(self):
        self.waited = True
        for copy in self.members:
            copy.received = True
        pltpu.make_async_copy(self.whole, self.whole, self.sem).wait()

    def wait_send(self):
        self.waited = True
        pltpu.make_async_copy(self.whole, self.whole, self.sem).wait()


class Copies:
    def __init__(self, send_sems, recv_sems):
        self.send_sems, self.recv_sems, self.all, self.groups = send_sems, recv_sems, [], []
        self.sends = self.recvs = 0

    def next_send(self):
        self.sends += 1
        return self.send_sems.at[self.sends - 1]

    def next_recv(self):
        self.recvs += 1
        return self.recv_sems.at[self.recvs - 1]

    def leaving(self, whole):
        self.groups.append(Group(whole, self.next_send()))
        return self.groups[-1]

    def arriving(self, whole):
        return Group(whole, self.next_recv())

    def make(self, source, target, device, send_if=None, recv_if=None, out=None, into=None):
        copy = Copy(pltpu.make_async_remote_copy(
            src_ref=source,
            dst_ref=target,
            send_sem=out.sem if out else self.next_send(),
            recv_sem=into.sem if into else self.next_recv(),
            device_id=device,
            device_id_type=pl.DeviceIdType.MESH,
        ), send_if, recv_if)
        copy.sent = out is not None
        for group in (out, into):
            if group:
                group.members.append(copy)
        self.all.append(copy)
        return copy

    def settle(self):
        for copy in self.all:
            if copy.started and not copy.sent:
                copy.wait_send()
        for group in self.groups:
            if not group.waited and all(copy.started for copy in group.members):
                group.wait_send()


def slab_rows(block, index):
    return pl.ds(pl.multiple_of((block * 8 + index) * 24, 8), 24)


class Panels:
    def __init__(self, ref, height, first, count):
        self.ref, self.height, self.first, self.count = ref, height, first, count

    def rows(self, panel, block, index):
        return pl.ds(pl.multiple_of((self.first + panel) * self.height + (block * 8 + index) * 24, 8), 24)

    def get(self, block, index):
        parts = [self.ref[self.rows(p, block, index), :] for p in range(self.count)]
        return parts[0] if self.count == 1 else jnp.concatenate(parts, 1)

    def put(self, block, index, value):
        for p in range(self.count):
            self.ref[self.rows(p, block, index), :] = value[:, p * 256 : p * 256 + 256]


N_SEMS = (54, 93)


def layer_kernel(
    span, x_in, cot_in, qw_in, kw_in, ow_in, uw_in, dw_in, vec_in, kvb_in,
    to_bo, to_ig, to_q, to_o, to_kv, to_vec, to_up, to_dn, to_small,
    x, cot, qw, kw, ow, uw, dw, vec, kvb,
    bo, ig, g_q, g_o, g_kv, g_vec, g_up, g_dn, g_small,
    KW, Q, O, U, Dn, X, C, KV, ub, WQ, WKV, WO, WU, gains, vsq,
    n1, hat1, scale1, N2, act, dl, OP, NP,
    qz, doz, doT, kvT, bias, sbuf, mixT, dqT, dkv,
    GP, GV, GU, GD, vg,
    SK1, RK1, SK2, RK2,
    RO1, SO2, RO2, RN1, SN2, RN2,
    SQ1, RQ1, SQ2, RQ2, SQ3, RQ3, SQ4, RQ4,
    SO1, QO1, SO2b, RO2b, SO3, RO3, SO4, RO4,
    SP1, RP1, SP2, RP2, SP3, RP3,
    SV1, RV1, SV2, RV2, SV3, RV3,
    SU1, RU1, SU2, RU2, SU3, RU3, RXU,
    SD1, RD1, SD2, RD2, RXD,
    NS1, NS2,
    send_sems, recv_sems, save_sems, load_sems,
):
    tok = x.shape[0]
    f = lax.axis_index("fsdp")
    s = lax.axis_index("seq")
    z = lax.div(s, 2)
    y = lax.rem(s, 2)
    yo = 1 - y
    fc = f + 1 - 2 * lax.rem(f, 2)
    fx = lax.rem(f + 2, 4)
    fd = 3 - f
    zk = (z, z + 1 - 2 * lax.rem(z, 2), lax.rem(z + 2, 4), 3 - z)
    dev_c, dev_x, dev_d = (fc, s), (fx, s), (fd, s)
    dev_y = (f, z * 2 + yo)
    dev_z = tuple((f, zz * 2 + y) for zz in zk)
    dev_zy = tuple((f, zz * 2 + yo) for zz in zk)
    fsdp_devs = (dev_c, dev_x, dev_d)
    seq_devs = dev_z[1:] + dev_zy
    far = (3, 2, 1)

    copies = Copies(send_sems, recv_sems)
    make = copies.make

    def start(*wanted):
        for copy in wanted:
            copy.start()

    def arrive(*wanted):
        for copy in wanted:
            copy.wait_recv()

    saved = []

    def save(source, target):
        copy = pltpu.make_async_copy(source, target, save_sems.at[len(saved)])
        copy.start()
        saved.append(copy)

    leaving, arriving = copies.leaving, copies.arriving
    three, four = pl.ds(0, 3), pl.ds(0, 4)

    def seq_gather(ref, some, together=True):
        to_z, to_y = [None], []
        out = leaving(some(three))
        for k in (1, 2, 3):
            to_z.append(make(ref(z, y), ref(z, y), dev_z[k], out=out))
        out, into = leaving(some(four)), arriving(some(four)) if together else None
        for k in range(4):
            to_y.append(make(ref(zk[k], y), ref(zk[k], y), dev_y, out=out, into=into))
        return to_z, to_y, into

    w_z, w_y, w_yin = seq_gather(lambda i, j: KW.at[f, i, j], lambda n: KW.at[0, n, 0])
    q_z, q_y, _ = seq_gather(lambda i, j: Q.at[f, i, j], lambda n: Q.at[0, n, 0], False)
    o_z, o_y, o_yin = seq_gather(lambda i, j: O.at[f, i, j], lambda n: O.at[0, n, 0])
    p_z, p_y, p_yin = seq_gather(lambda i, j: O.at[fx, i, j], lambda n: O.at[0, n, 0])
    u_z, u_y, u_yin = seq_gather(lambda i, j: U.at[i, j], lambda n: U.at[n, 0])
    d_z, d_y, d_yin = seq_gather(lambda i, j: Dn.at[i, j], lambda n: Dn.at[n, 0])
    k_z, k_y, k_yin = seq_gather(lambda i, j: KV.at[i, j], lambda n: KV.at[n, 0])

    def fsdp_gather(ref, some):
        out, into = leaving(some(three)), arriving(some(pl.ds(0, 2)))
        to_x = [make(ref(f, j), ref(f, j), dev_x, out=out) for j in (y, yo)]
        to_c = [make(ref(f, j), ref(f, j), dev_c, out=out, into=into) for j in (y, yo)]
        on_c = [make(ref(fx, j), ref(fx, j), dev_c, out=out, into=into) for j in (y, yo)]
        return to_x, to_c, on_c, into

    w_x, w_c, w_xc, w_in = fsdp_gather(lambda i, j: KW.at[i, :, j], lambda n: KW.at[n])
    q_out, q_in = leaving(Q.at[three]), arriving(Q.at[pl.ds(0, 2)])

    def q_copy(g, j, device, into):
        return make(Q.at[g, :, j], Q.at[g, :, j], device, out=q_out, into=into)

    q_x0 = q_copy(f, y, dev_x, None)
    q_c = [q_copy(f, j, dev_c, q_in) for j in (y, yo)]
    q_xc = [q_copy(fx, j, dev_c, q_in) for j in (y, yo)]
    q_xs = [make(Q.at[f, zz, yo], Q.at[f, zz, yo], dev_x, out=q_out) for zz in zk]
    o_x = make(O.at[f, z, y], O.at[f, z, y], dev_x)
    o_out, o_in = leaving(O.at[pl.ds(0, 2)]), arriving(O.at[pl.ds(0, 2)])

    def o_copy(g, j):
        return make(O.at[g, :, j], O.at[g, :, j], dev_c, out=o_out, into=o_in)

    o_c = [o_copy(f, j) for j in (y, yo)]
    op_c = [o_copy(fx, j) for j in (y, yo)]

    def token_gather(ref):
        out = leaving(ref.at[three])
        return (
            make(ref.at[f], ref.at[f], dev_x, out=out),
            make(ref.at[f], ref.at[f], dev_c, out=out),
            make(ref.at[fx], ref.at[fx], dev_c, out=out),
        )

    x_x, x_c, x_xc = token_gather(X)
    c_x, c_c, c_xc = token_gather(C)
    uf_out, uf_in = leaving(ub.at[three]), arriving(U.at[0, 0, three])
    u_f = [
        make(ub.at[g], U.at[z, y, f], dev, out=uf_out, into=uf_in)
        for g, dev in zip((fc, fx, fd), fsdp_devs)
    ]

    out = leaving(SK1)
    rk1 = [make(SK1.at[zz], RK1.at[zz], dev_y, out=out) for zz in zk]

    def to_z_peers(S, R):
        out, into = leaving(S), arriving(R)
        return [make(S.at[k], R.at[k], dev_z[k + 1], out=out, into=into) for k in range(3)], into

    rk2, rk2_in = to_z_peers(SK2, RK2)

    def to_core(ref, R):
        out, into = leaving(ref.at[pl.ds(0, 2)]), arriving(R)
        found = [
            make(ref.at[g], R.at[i], dev_c, out=out, into=into) for i, g in enumerate((fc, fd))
        ]
        return found, into

    out_c, out_in = to_core(OP, RO1)
    out_x = make(SO2, RO2, dev_x)
    nrm_c, nrm_in = to_core(NP, RN1)
    nrm_x = make(SN2, RN2, dev_x)

    def full_scatter(S1, R1, S2, R2, S3, R3, S4, R4):
        c_copy = make(S1, R1, dev_c)
        out = leaving(S2)
        x_copies = [make(S2.at[i], R2.at[i], dev_x, out=out) for i in range(2)]
        y_copy = make(S3, R3, dev_y)
        return (c_copy, x_copies, y_copy, *to_z_peers(S4, R4))

    q_sc = full_scatter(SQ1, RQ1, SQ2, RQ2, SQ3, RQ3, SQ4, RQ4)
    o_sc = full_scatter(SO1, QO1, SO2b, RO2b, SO3, RO3, SO4, RO4)
    p_c = make(SP1, RP1, dev_c)
    p_x = make(SP2, RP2, dev_x)
    out, p_in = leaving(SP3), arriving(RP3)
    p_s = [
        make(SP3.at[i], RP3.at[i], dev, out=out, into=p_in) for i, dev in enumerate(seq_devs)
    ]
    v_c = make(SV1, RV1, dev_c)
    v_x = make(SV2, RV2, dev_x)
    out, v_in = leaving(RV3), arriving(RV3)
    v_s = [make(SV3, RV3.at[i], dev, out=out, into=v_in) for i, dev in enumerate(seq_devs)]
    out = leaving(SU1)
    su_y = [make(SU1.at[zz], RU1.at[zz], dev_y, out=out) for zz in zk]
    inner = lax.div(z + 1, 2) == 1
    outer = lax.div(z + 1, 2) != 1

    def relayed(S2, R2, RX):
        to_z = [make(S2.at[k], R2.at[k], dev_z[k + 1]) for k in range(2)]
        to_z.append(make(S2.at[2], R2.at[2], dev_z[3], inner, inner))
        return to_z, make(S2.at[2], RX, dev_z[1], outer, inner)

    su_z, su_r = relayed(SU2, RU2, RXU)
    out, su_fin = leaving(SU3.at[three]), arriving(RU3)
    su_f = [
        make(SU3.at[g], RU3.at[i], dev, out=out, into=su_fin)
        for i, (g, dev) in enumerate(zip((fc, fx, fd), fsdp_devs))
    ]
    out = leaving(SD1)
    sd_y = [make(SD1.at[zz], RD1.at[zz], dev_y, out=out) for zz in zk]
    sd_z, sd_r = relayed(SD2, RD2, RXD)
    out, nf_in = leaving(NS1.at[three]), arriving(NS1.at[three])
    n_f = [make(NS1.at[f], NS1.at[f], dev, out=out, into=nf_in) for dev in fsdp_devs]
    seven = pl.ds(0, 7)
    out, ns_in = leaving(NS2.at[seven]), arriving(NS2.at[seven])
    n_s = [make(NS2.at[s], NS2.at[s], dev, out=out, into=ns_in) for dev in seq_devs]

    barrier = pltpu.get_barrier_semaphore()
    for dev in fsdp_devs + seq_devs:
        pl.semaphore_signal(barrier, inc=1, device_id=dev, device_id_type=pl.DeviceIdType.MESH)

    loads = []
    pairs = (
        (vec_in, vec), (kvb_in, kvb), (kw_in, kw), (qw_in, qw), (ow_in, ow),
        (x_in, x), (cot_in, cot), (uw_in, uw), (dw_in, dw),
    )
    for i, (source, target) in enumerate(pairs):
        copy = pltpu.make_async_copy(source, target, load_sems.at[i])
        copy.start()
        loads.append(copy)
    for copy in loads:
        copy.wait()

    vsq[...] = jnp.zeros((128, 128), F32)
    vsq[0:11, 0:24] = vec[...]
    vsq[11:12, 0:16] = kvb[...]
    KW[f, z, y, :, :128] = kw[...].astype(BF16)
    KW[f, z, y, :, 128:] = vsq[...].T[:24, :].astype(BF16)
    Q[f, z, y] = qw[...].astype(BF16)
    O[f, z, y] = ow[...].astype(BF16)
    for j in range(4):
        ub[j] = uw[:, j * D : (j + 1) * D].astype(BF16)
    U[z, y, f] = ub[f]
    Dn[z, y] = dw[...].astype(BF16)
    X[f] = x[...]
    C[f] = cot[...]

    @pl.when(outer)
    def _():
        RU2[2] = jnp.zeros((4, 24, D), BF16)
        RD2[2] = jnp.zeros((96, D), BF16)

    pl.semaphore_wait(barrier, 10)
    start(w_z[3], w_z[2], w_z[1], w_y[0])
    start(o_x, q_z[3], q_z[2], q_z[1], q_y[0])
    start(o_z[3], o_z[2], o_z[1], o_y[0])

    hat, scale = normalise(x[...].astype(F32))
    hat1[...] = hat
    scale1[...] = jnp.broadcast_to(scale, (tok, 128))
    own_span = span[0, s]
    lane = lax.broadcasted_iota(jnp.int32, (tok, 128), 1)
    spot = lax.broadcasted_iota(jnp.int32, (tok, 128), 0) + own_span * tok
    in_head = lax.rem(lane, 64)
    step = lax.rem(in_head, ROT_DIMS // 2).astype(F32)
    inverse = jnp.exp(step * (-2.0 * math.log(10000.0) / ROT_DIMS))
    angle = spot.astype(F32) * (0.25 * inverse)
    sine = jnp.sin(angle)
    cosine = jnp.where(in_head < ROT_DIMS, jnp.cos(angle), 1.0)
    sine_low = jnp.where(in_head < ROT_DIMS // 2, sine, 0.0)
    sine_high = jnp.where((in_head >= ROT_DIMS // 2) & (in_head < ROT_DIMS), sine, 0.0)
    key_lane = lane < 64
    key_cos = jnp.where(key_lane, cosine, 1.0)
    key_low = jnp.where(key_lane, sine_low, 0.0)
    key_high = jnp.where(key_lane, sine_high, 0.0)

    def turn(block, cos_t, low_t, high_t):
        up = pltpu.roll(block, 120, 1)
        down = pltpu.roll(block, 8, 1)
        return block * cos_t - up * low_t + down * high_t

    def turn_back(block, cos_t, low_t, high_t):
        up = pltpu.roll(block, 120, 1)
        down = pltpu.roll(block, 8, 1)
        return block * cos_t + up * low_t - down * high_t

    def forward(to_z, to_y, *which):
        for k in which:
            arrive(to_z[k])
            start(to_y[k])

    forward(w_z, w_y, *far)
    start(w_x[0], w_c[0])
    arrive(o_x)
    start(p_z[3], p_z[2], p_z[1], p_y[0])
    arrive(w_yin)
    start(w_x[1], w_c[1])
    forward(q_z, q_y, *far)
    start(q_x0, q_c[0])
    arrive(w_x[0])
    start(w_xc[0])
    arrive(w_x[1])
    start(w_xc[1])
    arrive(w_in)
    slabs = [KW[g, i, j].astype(F32) for g in range(4) for i in range(4) for j in range(2)]
    for i in range(16):
        pair = jnp.concatenate([slabs[2 * i][:, :128], slabs[2 * i + 1][:, :128]], 0)
        WKV[i * 48 : (i + 1) * 48, :] = pair.astype(BF16)
    gains[...] = jnp.concatenate([slab[:, 128:] for slab in slabs], 0).T
    vsq[...] = jnp.concatenate([slab[:16, 128:] for slab in slabs[:8]], 0).T
    kv_shift = vsq[11:12, :]
    n1[...] = (hat * gains[0:1, :] + gains[1:2, :]).astype(BF16)
    kv_pre = dot_nn(n1[...], WKV[...]) + kv_shift
    KV[z, y] = turn(kv_pre, key_cos, key_low, key_high).astype(BF16)
    start(k_z[3], k_z[2], k_z[1], k_y[0])
    for k in range(4):
        arrive(q_y[k])
        start(q_xs[k])
    start(q_c[1])
    forward(o_z, o_y, *far)
    start(o_c[0])
    forward(p_z, p_y, *far)
    start(op_c[0])
    arrive(q_x0)
    start(q_xc[0])
    vg[...] = jnp.zeros((128, D), F32)
    csum = jnp.sum(cot[...].astype(F32), 0, keepdims=True)
    vg[5:6, :] = csum
    vg[6:7, :] = csum
    key_iota = lax.broadcasted_iota(jnp.int32, (tok, tok), 0)
    row_iota = lax.broadcasted_iota(jnp.int32, (tok, tok), 1) + own_span * tok
    for i in range(8):
        bias[i * tok : (i + 1) * tok, :] = jnp.where(
            key_iota + span[0, i] * tok <= row_iota, 0.0, MASKED
        ).astype(F32)
    dkv[...] = jnp.zeros((8 * tok, 128), F32)
    start(*u_f)
    forward(k_z, k_y, *far)
    arrive(*q_xs)
    start(q_xc[1])
    arrive(o_yin)
    start(o_c[1])
    arrive(p_yin)
    start(op_c[1])
    arrive(uf_in)
    start(u_z[3], u_z[2], u_z[1], u_y[0])
    start(x_x, c_x, x_c, c_c)
    arrive(q_in)

    def join(ref, whole):
        def put(i, carry):
            g = lax.div(i, 4)
            zz = lax.rem(i, 4)
            pair = jnp.concatenate([ref[g, zz, 0].astype(F32), ref[g, zz, 1].astype(F32)], 0)
            whole[pl.ds(pl.multiple_of(i * 48, 16), 48), :] = pair.astype(BF16)
            return carry

        lax.fori_loop(0, 16, put, 0)

    join(Q, WQ)
    q_pre = dot_nn(n1[...], WQ[...]) + gains[4:5, :]
    gap = jnp.zeros((tok, 64), BF16)
    for j in range(6):
        cols = slice(j * 128, j * 128 + 128)
        turned = turn(q_pre[:, cols], cosine, sine_low, sine_high).astype(BF16).astype(F32)
        turned = (turned * HD ** (-0.5)).astype(BF16)
        qz[2 * j] = jnp.concatenate([turned[:, :64], gap], 1)
        qz[2 * j + 1] = jnp.concatenate([turned[:, 64:], gap], 1)
    arrive(o_in)
    join(O, WO)
    mixed_back = dot_nt(cot[...], WO[...]).astype(BF16)
    for j in range(6):
        pair = mixed_back[:, j * 128 : j * 128 + 128]
        doz[2 * j] = jnp.concatenate([gap, pair[:, :64]], 1)
        doz[2 * j + 1] = jnp.concatenate([gap, pair[:, 64:]], 1)
    doT[...] = mixed_back.astype(F32).T.astype(BF16).reshape(HQ, HD, tok)
    arrive(k_yin)
    KVF = KV.reshape(8 * tok, 128)
    kvT[...] = KVF[...].astype(F32).T.astype(BF16)

    span_rows = 2 * tok
    chunks = 8 * tok // span_rows

    def fold(values, reduce):
        return reduce(values.reshape(span_rows // 8, 8, tok), axis=0)

    def attend(step_index):
        heads = [step_index * 2, step_index * 2 + 1]
        top, total, share, delta, acc = {}, {}, {}, {}, {}

        def rows_of(i):
            return pl.ds(i * span_rows, span_rows)

        def held_of(j, i):
            return pl.ds((j * chunks + i) * span_rows, span_rows)

        def score(j, i):
            scores = dot_nt(KVF[rows_of(i), :], qz[heads[j]]) + bias[rows_of(i), :]
            sbuf[held_of(j, i), :] = scores
            here = fold(scores, jnp.max)
            top[j] = here if i == 0 else jnp.maximum(top[j], here)
            if i == chunks - 1:
                top[j] = jnp.max(top[j], axis=0, keepdims=True)

        def weigh(j, i):
            weights = jnp.exp(sbuf[held_of(j, i), :] - top[j])
            sbuf[held_of(j, i), :] = weights
            here = fold(weights, jnp.sum)
            total[j] = here if i == 0 else total[j] + here
            if i == chunks - 1:
                share[j] = 1.0 / jnp.sum(total[j], axis=0, keepdims=True)

        def mix(j, i):
            rows = rows_of(i)
            probs = sbuf[held_of(j, i), :] * share[j]
            probs_low = probs.astype(BF16)
            sbuf[held_of(j, i), :] = probs
            here = dot_nn(kvT[:, rows], probs_low)
            acc[j] = here if i == 0 else acc[j] + here
            dkv[rows, :] += dot_nn(probs_low, doz[heads[j]])
            if i == chunks - 1:
                mixed = acc[j][64:, :]
                mixT[heads[j]] = mixed.astype(BF16)
                delta[j] = jnp.sum(mixed * doT[heads[j]].astype(F32), axis=0, keepdims=True)

        def back(j, i):
            rows = rows_of(i)
            prob_grad = dot_nt(KVF[rows, :], doz[heads[j]])
            score_low = (sbuf[held_of(j, i), :] * (prob_grad - delta[j])).astype(BF16)
            here = dot_nn(kvT[:, rows], score_low)
            acc[j] = here if i == 0 else acc[j] + here
            dkv[rows, :] += dot_nn(score_low, qz[heads[j]])
            if i == chunks - 1:
                dqT[heads[j]] = acc[j][:64, :] * HD ** (-0.5)

        for stage in (
            ((score, 0),),
            ((weigh, 0), (score, 1)),
            ((mix, 0), (weigh, 1)),
            ((back, 0), (mix, 1)),
            ((back, 1),),
        ):
            for i in range(chunks):
                for part, j in stage:
                    part(j, i)

    def attend_all(first, last, meanwhile):
        def body_step(step_index, carry):
            for at, action in meanwhile:
                pl.when(step_index == at)(action)
            attend(step_index)
            return carry

        lax.fori_loop(first, last, body_step, 0)


    def pump_two():
        forward(u_z, u_y, 1)

    def pump_three():
        forward(u_z, u_y, 3, 2)

    def pump_four():
        forward(d_z, d_y, 1)
        arrive(x_x, c_x)
        start(x_xc, c_xc)

    def pump_five():
        forward(d_z, d_y, 3)

    attend_all(
        0, HQ // 2,
        (
            (1, lambda: start(d_z[3], d_z[2], d_z[1], d_y[0])),
            (2, pump_two), (3, pump_three), (4, pump_four), (5, pump_five),
        ),
    )

    for k in (3, 2, 1, 0):
        rows = pl.ds(pl.multiple_of((2 * zk[k] + yo) * tok, 8), tok)
        SK1[zk[k]] = dkv[rows, :].astype(BF16)
        start(rk1[k])
    mix_low = mixT.reshape(D, tok)[...]
    for c in range(3):
        sbuf[(3 + c) * D : (4 + c) * D, :] = dot_nn(mix_low, cot[:, c * 256 : c * 256 + 256])
    GQ = Panels(sbuf, D, 0, 3)
    GO = Panels(sbuf, D, 3, 3)

    def scatter_c(G, S1, copy):
        def put(i, carry):
            for j, g in enumerate((fc, fd)):
                S1[j, i] = G.get(g, i).astype(S1.dtype)
            return carry

        lax.fori_loop(0, 8, put, 0)
        start(copy)

    def scatter_x(G, R1, S2, copies_):
        arrive(copies_[0])
        for j, yy in enumerate((yo, y)):
            for i in range(4):
                slab = 2 * i + yy
                S2[j, i] = (G.get(fx, slab) + R1[1, slab].astype(F32)).astype(S2.dtype)
                G.put(f, slab, G.get(f, slab) + R1[0, slab].astype(F32))
            start(copies_[1][j])

    def scatter_y(G, R2, S3, copies_):
        arrive(copies_[1][0])
        for i in range(4):
            S3[i] = (G.get(f, 2 * i + yo) + R2[0, i].astype(F32)).astype(S3.dtype)
        start(copies_[2])

    def scatter_z(G, R2, R3, S4, copies_):
        arrive(copies_[1][1], copies_[2])
        for k in far:
            total = G.get(f, 2 * zk[k] + y) + R2[1, zk[k]].astype(F32) + R3[zk[k]].astype(F32)
            S4[k - 1] = total.astype(S4.dtype)
            start(copies_[3][k - 1])

    def scatter_end(G, R2, R3, R4, copies_):
        total = G.get(f, 2 * z + y) + R2[1, z].astype(F32) + R3[z].astype(F32)
        arrive(copies_[4])
        for k in range(3):
            total = total + R4[k].astype(F32)
        return total

    scatter_c(GO, SO1, o_sc[0])
    q_back = dqT.reshape(D, tok)[...].T
    parts = []
    for j in range(6):
        parts.append(
            turn_back(q_back[:, j * 128 : j * 128 + 128], cosine, sine_low, sine_high).astype(BF16)
        )
    q_low = jnp.concatenate(parts, 1)
    vg[4:5, :] = jnp.sum(q_low.astype(F32), 0, keepdims=True)
    for c in range(3):
        sbuf[c * D : (c + 1) * D, :] = dot_tn(n1[...], q_low[:, c * 256 : c * 256 + 256])
    scatter_c(GQ, SQ1, q_sc[0])
    forward(d_z, d_y, 2)
    arrive(u_yin, x_c, x_xc)

    def pair_step(k):
        arrive(rk1[k])
        rows = pl.ds(pl.multiple_of((2 * zk[k] + y) * tok, 8), tok)
        SK2[k - 1] = (dkv[rows, :] + RK1[zk[k]].astype(F32)).astype(BF16)
        start(rk2[k - 1])

    def lift_one():
        pair_step(3)

    def lift_two():
        pair_step(2)
        scatter_x(GO, QO1, SO2b, o_sc)

    def lift_three():
        pair_step(1)
        scatter_x(GQ, RQ1, SQ2, q_sc)

    def tokens_to_x():
        arrive(out_in, nrm_in)
        SO2[...] = (OP[fx].astype(F32) + RO1[1].astype(F32)).astype(BF16)
        start(out_x)
        SN2[...] = (NP[fx].astype(F32) + RN1[1].astype(F32)).astype(BF16)
        start(nrm_x)

    def down_rows(k):
        return pl.ds(pl.multiple_of((zk[k] * 2 + y) * 96, 8), 96)

    def down_step(k):
        arrive(sd_y[k])
        total = GD[down_rows(k), :] + RD1[zk[k]].astype(F32)
        if k in (0, 2):
            GD[down_rows(k), :] = total
        if k:
            SD2[k - 1] = total.astype(BF16)
        if k == 2:
            pl.when(outer)(lambda: start(sd_z[1]))
        elif k:
            start(sd_z[k - 1])
        if k == 3:
            start(sd_r)

    def down_relay():
        arrive(sd_r)

        @pl.when(inner)
        def _():
            SD2[1] = (GD[down_rows(2), :] + RXD[...].astype(F32)).astype(BF16)
            start(sd_z[1])

    def up_step(k):
        arrive(su_y[k])
        for g in range(4):
            rows = slab_rows(g, zk[k] * 2 + y)
            total = GU[rows, :] + RU1[zk[k], g].astype(F32)
            if k in (0, 2):
                GU[rows, :] = total
            if k:
                SU2[k - 1, g] = total.astype(BF16)
        if k == 2:
            pl.when(outer)(lambda: start(su_z[1]))
        elif k:
            start(su_z[k - 1])
        if k == 3:
            start(su_r)

    def up_relay():
        arrive(su_r)

        @pl.when(inner)
        def _():
            for g in range(4):
                total = GU[slab_rows(g, zk[2] * 2 + y), :] + RXU[g].astype(F32)
                SU2[1, g] = total.astype(BF16)
            start(su_z[1])

    up_totals = []

    def up_end():
        arrive(*su_z)
        for g in range(4):
            total = GU[slab_rows(g, s), :]
            for k in range(3):
                total = total + RU2[k, g].astype(F32)
            up_totals.append(total)
            g_up[g] = total
            SU3[g] = total.astype(BF16)
        start(*su_f)

    for g in range(4):
        for i in range(4):
            pair = jnp.concatenate([U[i, j, g].astype(F32) for j in range(2)], 0)
            WU[(g * 4 + i) * 48 : (g * 4 + i + 1) * 48, :] = pair.astype(BF16)
    WD = Dn.reshape(D, D)
    up_bias = gains[pl.ds(7 + f, 1), :]

    def slope_rows(c, t):
        return pl.ds(pl.multiple_of(c * 4 * tok + t * tok, tok), tok)

    def lift_block(t, carry):
        for at, action in ((1, lift_one), (2, lift_two), (3, lift_three)):
            pl.when(t == at)(action)
        rows = pl.ds(pl.multiple_of(t * tok, tok), tok)
        hat2, _ = normalise(X[t].astype(F32))
        low2 = (hat2 * gains[2:3, :] + gains[3:4, :]).astype(BF16)
        N2[rows, :] = low2
        for c in range(3):
            units = slice(c * 256, c * 256 + 256)
            lifted = dot_nn(low2, WU[:, units]) + up_bias[:, units]
            half = 0.5 + 0.5 * lax.erf(lifted * (0.5**0.5))
            act[rows, units] = (lifted * half).astype(BF16)
            bell = jnp.exp(lifted * lifted * -0.5) * (1.0 / math.sqrt(2.0 * math.pi))
            bias[slope_rows(c, t), :] = half + lifted * bell
        return carry

    lax.fori_loop(0, 4, lift_block, 0)
    arrive(c_c, c_xc)
    CF = C.reshape(4 * tok, D)
    for c in range(3):
        units = slice(c * 256, c * 256 + 256)
        GD[units, :] = dot_tn(act[:, units], CF[...])
    for k in (3, 2, 1, 0):
        SD1[zk[k]] = GD[pl.ds(pl.multiple_of((zk[k] * 2 + yo) * 96, 8), 96), :].astype(BF16)
        start(sd_y[k])
    arrive(d_yin)

    def back_one():
        scatter_y(GO, RO2b, SO3, o_sc)

    def back_two():
        down_step(3)

    def back_three():
        scatter_y(GQ, RQ2, SQ3, q_sc)

    def back_block(t, carry):
        for at, action in ((1, back_one), (2, back_two), (3, back_three)):
            pl.when(t == at)(action)
        two_gain, two_shift, up_sum = carry
        rows = pl.ds(pl.multiple_of(t * tok, tok), tok)
        back = C[t]
        sums = []
        for c in range(3):
            units = slice(c * 256, c * 256 + 256)
            low = (bias[slope_rows(c, t), :] * dot_nt(back, WD[units, :])).astype(BF16)
            dl[rows, units] = low
            sums.append(jnp.sum(low.astype(F32), 0, keepdims=True))
        OP[t] = dot_nn(act[rows, :], WD[...]).astype(BF16)
        grad2 = dot_nt(dl[rows, :], WU[...])
        NP[t] = grad2.astype(BF16)
        hat2, _ = normalise(X[t].astype(F32))
        return (
            two_gain + jnp.sum(grad2 * hat2, 0, keepdims=True),
            two_shift + jnp.sum(grad2, 0, keepdims=True),
            up_sum + jnp.concatenate(sums, 1),
        )

    zero_row = jnp.zeros((1, D), F32)
    two_gain, two_shift, up_sum = lax.fori_loop(0, 4, back_block, (zero_row,) * 3)
    vg[2:3, :] = two_gain
    vg[3:4, :] = two_shift
    vg[pl.ds(7 + f, 1), :] = up_sum
    start(*out_c, *nrm_c)
    down_step(2)
    for c in range(3):
        units = slice(c * 256, c * 256 + 256)
        GU[units, :] = dot_tn(N2[:, units], dl[...])
    for k in (3, 2, 1, 0):
        for g in range(4):
            SU1[zk[k], g] = GU[slab_rows(g, zk[k] * 2 + yo), :].astype(BF16)
        start(su_y[k])
    down_step(1)
    grad1 = dot_nt(q_low, WQ[...])
    arrive(rk1[0])
    kv_back = dkv[pl.ds(pl.multiple_of((2 * z + y) * tok, 8), tok), :] + RK1[z].astype(F32)
    arrive(rk2_in)
    for k in range(3):
        kv_back = kv_back + RK2[k].astype(F32)
    kv_low = turn_back(kv_back, key_cos, key_low, key_high).astype(BF16)
    grad1 = grad1 + dot_nt(kv_low, WKV[...])
    vg[0:1, :] = jnp.sum(grad1 * hat1[...], 0, keepdims=True)
    vg[1:2, :] = jnp.sum(grad1, 0, keepdims=True)
    kv_sum = jnp.sum(kv_low.astype(F32), 0, keepdims=True)
    short = jnp.zeros((1, 8), F32)
    spread = jnp.concatenate(
        [part for i in range(8) for part in (kv_sum[:, i * 16 : i * 16 + 16], short)], 1
    )
    vg[11:12, :] = jnp.concatenate([spread] * 4, 1)
    GP[...] = dot_tn(n1[...], kv_low)
    flipped = vg[...].T

    def packed(g):
        parts = [flipped[(g * 8 + i) * 24 : (g * 8 + i + 1) * 24, :16] for i in range(8)]
        return jnp.concatenate(parts, 1)

    for g in range(4):
        GV[g] = packed(g)
    for i in range(8):
        for j, g in enumerate((fc, fd)):
            SP1[j, i] = GP[slab_rows(g, i), :].astype(BF16)
    for j, g in enumerate((fc, fd)):
        SV1[j] = GV[g]
    start(p_c, v_c)
    down_relay()
    down_step(0)
    arrive(p_c, v_c)
    for i in range(8):
        SP2[i] = (GP[slab_rows(fx, i), :] + RP1[1, i].astype(F32)).astype(BF16)
    SV2[...] = GV[fx] + RV1[1]
    start(p_x, v_x)
    tokens_to_x()
    scatter_z(GO, RO2b, RO3, SO4, o_sc)
    arrive(p_x, v_x)

    def kv_sum_of(slab):
        return GP[slab_rows(f, slab), :] + RP1[0, slab].astype(F32) + RP2[slab].astype(F32)

    seq_slabs = [2 * zk[k] + y for k in (1, 2, 3)] + [2 * zk[k] + yo for k in range(4)]
    for i, slab in enumerate(seq_slabs):
        SP3[i] = kv_sum_of(slab).astype(BF16)
    SV3[...] = GV[f] + RV1[0] + RV2[...]
    start(*p_s, *v_s)
    up_step(3)
    scatter_z(GQ, RQ2, RQ3, SQ4, q_sc)
    up_step(2)
    up_step(1)
    up_relay()
    up_step(0)
    mixed_rows = mix_low.astype(F32).T.astype(BF16)
    arrive(out_x)
    bo[...] = (
        x[...].astype(F32)
        + (dot_nn(mixed_rows, WO[...]) + gains[5:6, :])
        + (OP[f].astype(F32) + RO1[0].astype(F32) + RO2[...].astype(F32) + gains[6:7, :])
    ).astype(BF16)
    save(bo, to_bo)
    arrive(nrm_x)
    grad2 = NP[f].astype(F32) + RN1[0].astype(F32) + RN2[...].astype(F32)
    hat_rows = hat1[...]
    scale_rows = scale1[:, 0:1]
    ig[...] = (
        cot[...].astype(F32)
        + norm_back(grad1, hat_rows, scale_rows, gains[0:1, :])
        + norm_back(grad2, hat_rows, scale_rows, gains[2:3, :])
    )
    save(ig, to_ig)
    copies.settle()
    q_grad = scatter_end(GQ, RQ2, RQ3, RQ4, q_sc)
    g_q[...] = q_grad
    save(g_q, to_q)
    o_grad = scatter_end(GO, RO2b, RO3, RO4, o_sc)
    g_o[...] = o_grad
    save(g_o, to_o)
    kv_grad = kv_sum_of(s)
    vec_sum = SV3[...]
    arrive(p_in, v_in)
    for i in range(7):
        kv_grad = kv_grad + RP3[i].astype(F32)
        vec_sum = vec_sum + RV3[i]
    vec_own = jnp.zeros((24, 16), F32)
    for i in range(8):
        vec_own = vec_own + jnp.where(s == i, vec_sum[:, i * 16 : i * 16 + 16], 0.0)
    vec_grad = jnp.concatenate([vec_own, jnp.zeros((24, 112), F32)], 1)
    g_kv[...] = kv_grad
    g_vec[...] = vec_grad
    save(g_kv, to_kv)
    save(g_vec, to_vec)
    rows = pl.ds(pl.multiple_of(s * 96, 8), 96)
    down_grad = GD[rows, :]
    for k in range(3):
        arrive(sd_z[k])
        down_grad = down_grad + RD2[k].astype(F32)
    g_dn[...] = down_grad
    save(g_dn, to_dn)
    up_end()
    save(g_up.at[f], to_up.at[f])

    def energy(values):
        return jnp.sum(jnp.sum(values * values, 0, keepdims=True), 1, keepdims=True)

    lanes = lax.broadcasted_iota(jnp.int32, (24, 128), 1)
    squares = energy(q_grad) + energy(o_grad) + energy(kv_grad) + energy(jnp.where(lanes == 11, 0.0, vec_grad)) + energy(g_dn[...])
    for total in up_totals:
        squares = squares + energy(total)
    kv_rows = jnp.concatenate([vec_grad, jnp.zeros((104, 128), F32)], 0).T
    line = lax.broadcasted_iota(jnp.int32, (8, 128), 0)
    column = lax.broadcasted_iota(jnp.int32, (8, 128), 1)
    kv_line = jnp.where(column < 16, jnp.broadcast_to(kv_rows[11:12, :], (8, 128)), 0.0)
    NS1[f] = jnp.where(line == 0, squares, kv_line)
    start(*n_f)
    arrive(nf_in)
    kv_piece = NS1[0][1:2, :]
    chip = NS1[0] + NS1[1] + NS1[2] + NS1[3]
    part = chip[0:1, 0:1] + jnp.sum(kv_piece * kv_piece, 1, keepdims=True)
    NS2[s] = jnp.broadcast_to(part, (8, 128))
    start(*n_s)
    arrive(su_fin)
    for i, g in enumerate((fc, fx, fd)):
        g_up[g] = RU3[i].astype(F32)
        save(g_up.at[g], to_up.at[g])
    arrive(ns_in)
    everything = NS2[0]
    for i in range(1, 8):
        everything = everything + NS2[i]
    g_small[...] = jnp.where(line == 0, everything, jnp.broadcast_to(kv_piece, (8, 128)))
    save(g_small, to_small)
    copies.settle()
    assert (copies.sends, copies.recvs) == N_SEMS, (copies.sends, copies.recvs)
    for copy in saved:
        copy.wait()


def update_kernel(
    small, g_q, g_o, g_kv, g_vec, g_up, g_dn, bo_in, ig_in,
    mq, mk, mo, mu, md, mv, mb,
    fq, fk, fo, fu, fdn, fv, fb,
    sq, sk, so, su, sd, sv, sb,
    bo, ig, norm,
    nmq, nmk, nmo, nmu, nmd, nmv, nmb,
    nfq, nfk, nfo, nfu, nfd, nfv, nfb,
    nsq, nsk, nso, nsu, nsd, nsv, nsb,
    residual,
):
    bo[...] = bo_in[...]
    ig[...] = ig_in[...]
    size = jnp.sqrt(small[0:1, 0:1])
    norm[...] = size
    factor = jnp.minimum(1.0, CLIP_NORM / (size + 1e-06))

    def update(grad, master, first, second, new_master, new_first, new_second, rate, decay):
        clipped = grad * factor
        values = adamw(master, clipped, first, second, rate, decay)
        for ref, value in zip((new_master, new_first, new_second), values):
            ref[...] = value

    rates = (MATRIX_RATE, MATRIX_DECAY)
    update(g_q[...], mq[...], fq[...], sq[...], nmq, nfq, nsq, *rates)
    update(g_o[...], mo[...], fo[...], so[...], nmo, nfo, nso, *rates)
    update(g_kv[...], mk[...], fk[...], sk[...], nmk, nfk, nsk, *rates)
    for g in range(4):
        cols = slice(g * D, (g + 1) * D)
        update(
            g_up[g], mu[:, cols], fu[:, cols], su[:, cols],
            nmu.at[:, cols], nfu.at[:, cols], nsu.at[:, cols], *rates,
        )
    update(g_dn[...], md[...], fdn[...], sd[...], nmd, nfd, nsd, *rates)
    flipped = jnp.concatenate([g_vec[...], jnp.zeros((104, 128), F32)], 0).T
    vector_grad = flipped[:11, :24]
    update(vector_grad, mv[...], fv[...], sv[...], nmv, nfv, nsv, VECTOR_RATE, 0.0)
    residual[...] = flipped[5:7, :24] * factor
    update(small[1:2, :16], mb[...], fb[...], sb[...], nmb, nfb, nsb, VECTOR_RATE, 0.0)


def fast_body(
    inputs, cotangent, span_order,
    query_weight, keyval_weight, output_weight, up_weight, down_weight, vectors, kv_bias,
    *moments,
):
    tok = inputs.shape[0]
    smem = pl.BlockSpec(memory_space=pltpu.SMEM)
    shape = jax.ShapeDtypeStruct
    V = pltpu.VMEM
    results_here = (
        shape((tok, D), BF16),
        shape((tok, D), F32),
        shape((24, D), F32),
        shape((24, D), F32),
        shape((24, 128), F32),
        shape((24, 128), F32),
        shape((4, 24, D), F32),
        shape((96, D), F32),
        shape((8, 128), F32),
    )
    operands_here = (
        inputs, cotangent, query_weight, keyval_weight, output_weight, up_weight, down_weight,
        vectors, kv_bias.reshape(1, -1),
    )
    scratch = [V(a.shape, a.dtype) for a in operands_here + results_here]
    scratch += [
        V((4, 4, 2, 24, 256), BF16),
        V((4, 4, 2, 24, D), BF16),
        V((4, 4, 2, 24, D), BF16),
        V((4, 2, 4, 24, D), BF16),
        V((4, 2, 96, D), BF16),
        V((4, tok, D), BF16),
        V((4, tok, D), BF16),
        V((4, 2, tok, 128), BF16),
        V((4, 24, D), BF16),
        V((D, D), BF16),
        V((D, 128), BF16),
        V((D, D), BF16),
        V((D, D), BF16),
        V((128, D), F32),
        V((128, 128), F32),
        V((tok, D), BF16),
        V((tok, D), F32),
        V((tok, 128), F32),
        V((4 * tok, D), BF16),
        V((4 * tok, D), BF16),
        V((4 * tok, D), BF16),
        V((4, tok, D), BF16),
        V((4, tok, D), BF16),
        V((HQ, tok, 128), BF16),
        V((HQ, tok, 128), BF16),
        V((HQ, HD, tok), BF16),
        V((128, 8 * tok), BF16),
        V((12 * tok, tok), F32),
        V((6 * D, 256), F32),
        V((HQ, HD, tok), BF16),
        V((HQ, HD, tok), F32),
        V((8 * tok, 128), F32),
        V((D, 128), F32),
        V((4, 24, 128), F32),
        V((D, D), F32),
        V((D, D), F32),
        V((128, D), F32),
        V((4, tok, 128), BF16), V((4, tok, 128), BF16),
        V((3, tok, 128), BF16), V((3, tok, 128), BF16),
        V((2, tok, D), BF16), V((tok, D), BF16), V((tok, D), BF16),
        V((2, tok, D), BF16), V((tok, D), BF16), V((tok, D), BF16),
    ]
    def scatter_buffers(width):
        found = []
        for lead in ((2, 8), (2, 4), (4,), (3,)):
            found += [V(lead + (24, width), BF16)] * 2
        return found

    scratch += scatter_buffers(D)
    scratch += scatter_buffers(D)
    for lead in ((2, 8), (8,), (7,)):
        scratch += [V(lead + (24, 128), BF16)] * 2
    scratch += [V((2, 24, 128), F32)] * 2 + [V((24, 128), F32)] * 3 + [V((7, 24, 128), F32)]
    scratch += [V((4, 4, 24, D), BF16)] * 2 + [V((3, 4, 24, D), BF16)] * 2
    scratch += [V((4, 24, D), BF16), V((3, 24, D), BF16), V((4, 24, D), BF16)]
    scratch += [V((4, 96, D), BF16)] * 2 + [V((3, 96, D), BF16)] * 2 + [V((96, D), BF16)]
    scratch += [V((4, 8, 128), F32), V((8, 8, 128), F32)]
    scratch += [pltpu.SemaphoreType.DMA((n,)) for n in N_SEMS] + [pltpu.SemaphoreType.DMA((12,)), pltpu.SemaphoreType.DMA((9,))]
    kv_row = kv_bias.reshape(1, -1)
    bo, ig, g_q, g_o, g_kv, g_vec, g_up, g_dn, small = pl.pallas_call(
        layer_kernel,
        name="layer",
        out_shape=results_here,
        in_specs=[smem] + [pl.BlockSpec(memory_space=pl.ANY)] * 9,
        out_specs=(pl.BlockSpec(memory_space=pl.ANY),) * 9,
        scratch_shapes=scratch,
        compiler_params=pltpu.CompilerParams(
            collective_id=0, has_side_effects=True, vmem_limit_bytes=62 * 2**20
        ),
    )(
        span_order, inputs, cotangent,
        query_weight, keyval_weight, output_weight, up_weight, down_weight, vectors, kv_row,
    )
    masters = (query_weight, keyval_weight, output_weight, up_weight, down_weight, vectors, kv_row)
    firsts = tuple(moments[:6]) + (moments[6].reshape(1, -1),)
    seconds = tuple(moments[7:13]) + (moments[13].reshape(1, -1),)
    state = [shape(a.shape, F32) for a in masters]
    operands = (small, g_q, g_o, g_kv, g_vec, g_up, g_dn, bo, ig) + masters + firsts + seconds
    outcomes = [shape((tok, D), BF16), shape((tok, D), F32), shape((1, 1), F32)]
    outcomes += state * 3 + [shape((2, vectors.shape[1]), F32)]

    def whole(a):
        return pl.BlockSpec(a.shape, lambda i: (0,) * len(a.shape))

    results = pl.pallas_call(
        update_kernel,
        name="update",
        grid=(1,),
        out_shape=outcomes,
        in_specs=[whole(a) for a in operands],
        out_specs=[whole(a) for a in outcomes],
        compiler_params=pltpu.CompilerParams(vmem_limit_bytes=62 * 2**20),
    )(*operands)
    results = list(results)
    results[2] = results[2].reshape(())
    for i in (9, 16, 23):
        results[i] = results[i].reshape(-1)
    return tuple(results)


def solution(mesh):
    grid = (mesh.shape["fsdp"], mesh.shape["seq"])
    return jax.shard_map(
        fast_body if grid == (4, 8) else body,
        mesh=mesh,
        in_specs=(
            P(("fsdp", "seq"), None),
            P(("fsdp", "seq"), None),
            P("fsdp", None),
            P(("fsdp", "seq"), None),
            P(("fsdp", "seq"), None),
            P(("fsdp", "seq"), None),
            P(("fsdp", "seq"), None),
            P(("fsdp", "seq"), None),
            P(None, ("fsdp", "seq")),
            P("seq"),
            P(("fsdp", "seq"), None),
            P(("fsdp", "seq"), None),
            P(("fsdp", "seq"), None),
            P(("fsdp", "seq"), None),
            P(("fsdp", "seq"), None),
            P(None, ("fsdp", "seq")),
            P("seq"),
            P(("fsdp", "seq"), None),
            P(("fsdp", "seq"), None),
            P(("fsdp", "seq"), None),
            P(("fsdp", "seq"), None),
            P(("fsdp", "seq"), None),
            P(None, ("fsdp", "seq")),
            P("seq"),
        ),
        out_specs=(
            P(("fsdp", "seq"), None),
            P(("fsdp", "seq"), None),
            P(),
            P(("fsdp", "seq"), None),
            P(("fsdp", "seq"), None),
            P(("fsdp", "seq"), None),
            P(("fsdp", "seq"), None),
            P(("fsdp", "seq"), None),
            P(None, ("fsdp", "seq")),
            P("seq"),
            P(("fsdp", "seq"), None),
            P(("fsdp", "seq"), None),
            P(("fsdp", "seq"), None),
            P(("fsdp", "seq"), None),
            P(("fsdp", "seq"), None),
            P(None, ("fsdp", "seq")),
            P("seq"),
            P(("fsdp", "seq"), None),
            P(("fsdp", "seq"), None),
            P(("fsdp", "seq"), None),
            P(("fsdp", "seq"), None),
            P(("fsdp", "seq"), None),
            P(None, ("fsdp", "seq")),
            P("seq"),
            P(None, ("fsdp", "seq")),
        ),
        check_vma=False,
    )
```

```python
import math

import jax
import jax.numpy as jnp
from jax import lax
from jax.experimental import pallas as pl
from jax.experimental.pallas import tpu as pltpu
from jax.sharding import PartitionSpec as P

D = 768
HQ = 12
HD = 64
ROT_DIMS = 16
FF = 3072
KEY_BLOCK = 512
STEP = 10
F32 = jnp.float32
BF16 = jnp.bfloat16


NORM_EPS = 1e-05
MASKED = -1e30
CLIP_NORM = 1.0
BETA_ONE = 0.9
BETA_TWO = 0.999
ADAM_EPS = 1e-08
MATRIX_DECAY = 0.1
MATRIX_RATE = 0.1
VECTOR_RATE = 0.3


def layer_norm(tensor, gain_row, shift_row):
    centre = tensor - jnp.mean(tensor, -1, keepdims=True)
    spread = jnp.mean(centre * centre, -1, keepdims=True)
    return centre * lax.rsqrt(spread + NORM_EPS) * gain_row + shift_row


def rotary_tables(places):
    half_steps = jnp.arange(ROT_DIMS // 2, dtype=jnp.float32)
    inverse = jnp.exp(half_steps * (-2.0 * math.log(10000.0) / ROT_DIMS))
    angles = places.astype(jnp.float32)[:, None] * (0.25 * inverse)[None, :]
    angles = jnp.concatenate([angles, angles], 1)
    return (jnp.cos(angles), jnp.sin(angles))


def rotate(tensor, cosine, sine_table):
    rotary_part = tensor[..., :ROT_DIMS]
    lower_half = rotary_part[..., : ROT_DIMS // 2]
    upper_half = rotary_part[..., ROT_DIMS // 2 :]
    turned = jnp.concatenate([-upper_half, lower_half], -1)
    return jnp.concatenate([rotary_part * cosine + turned * sine_table, tensor[..., ROT_DIMS:]], -1)


def adamw(master, clipped, first_old, second_old, step_rate, decay_rate):
    first_new = BETA_ONE * first_old + (1.0 - BETA_ONE) * clipped
    second_new = BETA_TWO * second_old + (1.0 - BETA_TWO) * clipped * clipped
    ascent = (
        first_new
        / (1.0 - BETA_ONE**STEP)
        / (jnp.sqrt(second_new / (1.0 - BETA_TWO**STEP)) + ADAM_EPS)
    )
    return (master - step_rate * (ascent + decay_rate * master), first_new, second_new)


def gelu_exact(tensor):
    return jax.nn.gelu(tensor, approximate=False)


def across_tokens(left_side, right_side):
    return lax.dot_general(
        left_side, right_side, (((0,), (0,)), ((), ())), preferred_element_type=jnp.float32
    )


def against(left_side, right_side):
    return lax.dot_general(
        left_side, right_side, (((1,), (1,)), ((), ())), preferred_element_type=jnp.float32
    )


def masked_scores(query_rows, row_places, key_block, key_places):
    scores = against(query_rows, key_block) * HD ** (-0.5)
    return jnp.where(key_places[None, :] <= row_places[:, None], scores, MASKED)


def body(
    inputs,
    cotangent,
    span_order,
    query_weight,
    keyval_weight,
    output_weight,
    up_weight,
    down_weight,
    vectors,
    kv_bias,
    first_query,
    first_keyval,
    first_output,
    first_up,
    first_down,
    first_vectors,
    first_kv_bias,
    second_query,
    second_keyval,
    second_output,
    second_up,
    second_down,
    second_vectors,
    second_kv_bias,
):
    tok_rows = inputs.shape[0]
    seq_count = lax.axis_size("seq")
    seq_rank = lax.axis_index("seq")
    order_row = span_order[0]
    token_steps = jnp.arange(tok_rows, dtype=jnp.int32)
    all_places = (order_row[:, None] * tok_rows + token_steps[None, :]).reshape(
        seq_count * tok_rows
    )
    own_span = jnp.sum(jnp.where(jnp.arange(seq_count, dtype=jnp.int32) == seq_rank, order_row, 0))
    own_places = own_span * tok_rows + token_steps
    query_rows_count = tok_rows * HQ
    query_full, keyval_full, output_full, up_full, down_full, vector_full = (
        lax.all_gather(query_weight.astype(jnp.bfloat16), ("fsdp", "seq"), axis=0, tiled=True),
        lax.all_gather(keyval_weight.astype(jnp.bfloat16), ("fsdp", "seq"), axis=0, tiled=True),
        lax.all_gather(output_weight.astype(jnp.bfloat16), ("fsdp", "seq"), axis=0, tiled=True),
        lax.all_gather(up_weight.astype(jnp.bfloat16), ("fsdp", "seq"), axis=0, tiled=True),
        lax.all_gather(down_weight.astype(jnp.bfloat16), ("fsdp", "seq"), axis=0, tiled=True),
        lax.all_gather(vectors.astype(jnp.bfloat16), ("fsdp", "seq"), axis=1, tiled=True),
    )
    kv_shift = lax.all_gather(kv_bias.astype(jnp.bfloat16), "seq", axis=0, tiled=True).astype(
        jnp.float32
    )
    gains = vector_full.astype(jnp.float32)
    states = inputs.astype(jnp.float32)
    normed_one = layer_norm(states, gains[0], gains[1])
    normed_low = normed_one.astype(jnp.bfloat16)
    query_pre = jnp.dot(normed_low, query_full, preferred_element_type=jnp.float32) + gains[4]
    keyval_pre = jnp.dot(normed_low, keyval_full, preferred_element_type=jnp.float32) + kv_shift
    cosine, sine_table = rotary_tables(own_places)

    def turn_queries(tensor):
        return rotate(tensor.reshape(tok_rows, HQ, HD), cosine[:, None, :], sine_table[:, None, :])

    def turn_keys(tensor):
        return jnp.concatenate([rotate(tensor[:, :HD], cosine, sine_table), tensor[:, HD:]], 1)

    query_rows = turn_queries(query_pre).astype(jnp.bfloat16).reshape(query_rows_count, HD)
    local_pairs = turn_keys(keyval_pre).astype(jnp.bfloat16)
    row_places = jnp.broadcast_to(own_places[:, None], (tok_rows, HQ)).reshape(query_rows_count)
    all_pairs = lax.all_gather(local_pairs, "seq", axis=0, tiled=True)
    block_count = all_pairs.shape[0] // KEY_BLOCK
    place_blocks = all_places.reshape(block_count, KEY_BLOCK)

    def lse_step(carry_pair, block_pair):
        running_top, running_total = carry_pair
        pair_block, key_places = block_pair
        scores = masked_scores(query_rows, row_places, pair_block[:, :HD], key_places)
        new_top = jnp.maximum(running_top, jnp.max(scores, 1, keepdims=True))
        running_total = running_total * jnp.exp(running_top - new_top) + jnp.sum(
            jnp.exp(scores - new_top), 1, keepdims=True
        )
        return ((new_top, running_total), None)

    start_carry = (
        jnp.full((query_rows_count, 1), MASKED, jnp.float32),
        jnp.zeros((query_rows_count, 1), jnp.float32),
    )
    (row_top, row_total), _ = lax.scan(
        lse_step, start_carry, (all_pairs.reshape(block_count, KEY_BLOCK, 2 * HD), place_blocks)
    )
    log_total = row_top + jnp.log(row_total)

    def mix_step(mixed_acc, block_pair):
        pair_block, key_places = block_pair
        probs_low = jnp.exp(
            masked_scores(query_rows, row_places, pair_block[:, :HD], key_places) - log_total
        ).astype(jnp.bfloat16)
        return (
            mixed_acc + jnp.dot(probs_low, pair_block[:, HD:], preferred_element_type=jnp.float32),
            None,
        )

    mixed, _ = lax.scan(
        mix_step,
        jnp.zeros((query_rows_count, HD), jnp.float32),
        (all_pairs.reshape(block_count, KEY_BLOCK, 2 * HD), place_blocks),
    )
    mixed_low = mixed.reshape(tok_rows, D).astype(jnp.bfloat16)
    attention_out = jnp.dot(mixed_low, output_full, preferred_element_type=jnp.float32) + gains[5]
    normed_two = layer_norm(states, gains[2], gains[3])
    normed_two_low = normed_two.astype(jnp.bfloat16)
    lifted = jnp.dot(normed_two_low, up_full, preferred_element_type=jnp.float32) + gains[
        7:
    ].reshape(FF)
    active_low = gelu_exact(lifted).astype(jnp.bfloat16)
    block_output = (
        states
        + attention_out
        + jnp.dot(active_low, down_full, preferred_element_type=jnp.float32)
        + gains[6]
    ).astype(jnp.bfloat16)
    back_rows = cotangent.astype(jnp.float32)
    query_back, keyval_back, output_back, up_back, down_back = (
        lax.all_gather(query_weight.astype(jnp.bfloat16), ("fsdp", "seq"), axis=0, tiled=True),
        lax.all_gather(keyval_weight.astype(jnp.bfloat16), ("fsdp", "seq"), axis=0, tiled=True),
        lax.all_gather(output_weight.astype(jnp.bfloat16), ("fsdp", "seq"), axis=0, tiled=True),
        lax.all_gather(up_weight.astype(jnp.bfloat16), ("fsdp", "seq"), axis=0, tiled=True),
        lax.all_gather(down_weight.astype(jnp.bfloat16), ("fsdp", "seq"), axis=0, tiled=True),
    )
    grad_down = across_tokens(active_low, cotangent)
    grad_output = across_tokens(mixed_low, cotangent)
    out_bias_grad = jnp.sum(back_rows, 0)
    active_grad = against(cotangent, down_back)
    _, gelu_pull = jax.vjp(gelu_exact, lifted)
    (lifted_grad,) = gelu_pull(active_grad)
    lifted_low = lifted_grad.astype(jnp.bfloat16)
    grad_up = across_tokens(normed_two_low, lifted_low)
    normed_two_grad = against(lifted_low, up_back)
    mixed_grad = against(cotangent, output_back).astype(jnp.bfloat16).reshape(query_rows_count, HD)
    row_delta = jnp.sum(mixed_grad.astype(jnp.float32) * mixed, 1, keepdims=True)
    pairs_back = lax.all_gather(local_pairs, "seq", axis=0, tiled=True)

    def grad_step(query_acc, block_pair):
        pair_block, key_places = block_pair
        key_block = pair_block[:, :HD]
        probs = jnp.exp(masked_scores(query_rows, row_places, key_block, key_places) - log_total)
        prob_grad = against(mixed_grad, pair_block[:, HD:])
        score_low = (probs * (prob_grad - row_delta)).astype(jnp.bfloat16)
        query_acc = query_acc + jnp.dot(score_low, key_block, preferred_element_type=jnp.float32)
        key_grad = across_tokens(score_low, query_rows) * HD ** (-0.5)
        value_grad = across_tokens(probs.astype(jnp.bfloat16), mixed_grad)
        return (query_acc, jnp.concatenate([key_grad, value_grad], 1))

    query_sum, pair_grads = lax.scan(
        grad_step,
        jnp.zeros((query_rows_count, HD), jnp.float32),
        (pairs_back.reshape(block_count, KEY_BLOCK, 2 * HD), place_blocks),
    )
    query_rot_grad = (query_sum * HD ** (-0.5)).reshape(tok_rows, HQ, HD)
    own_pair_grad = lax.psum_scatter(
        pair_grads.reshape(block_count * KEY_BLOCK, 2 * HD).astype(jnp.bfloat16),
        "seq",
        scatter_dimension=0,
        tiled=True,
    ).astype(jnp.float32)
    _, key_pull = jax.vjp(turn_keys, keyval_pre)
    (keyval_grad,) = key_pull(own_pair_grad)
    keyval_low = keyval_grad.astype(jnp.bfloat16)
    _, query_pull = jax.vjp(turn_queries, query_pre)
    (query_pre_grad,) = query_pull(query_rot_grad)
    query_low = query_pre_grad.astype(jnp.bfloat16)
    grad_query = across_tokens(normed_low, query_low)
    grad_keyval = across_tokens(normed_low, keyval_low)
    kv_bias_part = jnp.sum(keyval_low.astype(jnp.float32), 0)
    normed_one_grad = against(query_low, query_back) + against(keyval_low, keyval_back)
    _, first_pull = jax.vjp(layer_norm, states, gains[0], gains[1])
    input_one, gain_one_grad, shift_one_grad = first_pull(normed_one_grad)
    _, second_pull = jax.vjp(layer_norm, states, gains[2], gains[3])
    input_two, gain_two_grad, shift_two_grad = second_pull(normed_two_grad)
    input_grad = back_rows + input_one + input_two
    vector_grad = jnp.concatenate(
        [
            jnp.stack(
                [
                    gain_one_grad,
                    shift_one_grad,
                    gain_two_grad,
                    shift_two_grad,
                    jnp.sum(query_low.astype(jnp.float32), 0),
                    out_bias_grad,
                    out_bias_grad,
                ]
            ),
            jnp.sum(lifted_low.astype(jnp.float32), 0).reshape(FF // D, D),
        ],
        0,
    )
    reduced = (
        lax.psum_scatter(grad_query, ("fsdp", "seq"), scatter_dimension=0, tiled=True),
        lax.psum_scatter(grad_keyval, ("fsdp", "seq"), scatter_dimension=0, tiled=True),
        lax.psum_scatter(grad_output, ("fsdp", "seq"), scatter_dimension=0, tiled=True),
        lax.psum_scatter(grad_up, ("fsdp", "seq"), scatter_dimension=0, tiled=True),
        lax.psum_scatter(grad_down, ("fsdp", "seq"), scatter_dimension=0, tiled=True),
        lax.psum_scatter(vector_grad, ("fsdp", "seq"), scatter_dimension=1, tiled=True),
    )
    reduced = tuple(reduced)
    local_squares = sum((jnp.sum(gradient * gradient) for gradient in reduced))
    global_squares, kv_bias_total = lax.psum((local_squares, kv_bias_part), ("fsdp", "seq"))
    grad_norm = jnp.sqrt(global_squares + jnp.sum(kv_bias_total * kv_bias_total))
    piece_width = kv_bias.shape[0]
    kv_bias_grad = lax.dynamic_slice_in_dim(kv_bias_total, seq_rank * piece_width, piece_width)
    factor = jnp.minimum(1.0, CLIP_NORM / (grad_norm + 1e-06))
    masters = (query_weight, keyval_weight, output_weight, up_weight, down_weight, vectors, kv_bias)
    all_grads = reduced + (kv_bias_grad,)
    firsts = (
        first_query,
        first_keyval,
        first_output,
        first_up,
        first_down,
        first_vectors,
        first_kv_bias,
    )
    seconds = (
        second_query,
        second_keyval,
        second_output,
        second_up,
        second_down,
        second_vectors,
        second_kv_bias,
    )
    step_rates = (MATRIX_RATE,) * 5 + (VECTOR_RATE, VECTOR_RATE)
    decays = (MATRIX_DECAY,) * 5 + (0.0, 0.0)
    updated = [
        adamw(master, gradient * factor, first_old, second_old, step_rate, decay_rate)
        for master, gradient, first_old, second_old, step_rate, decay_rate in zip(
            masters, all_grads, firsts, seconds, step_rates, decays
        )
    ]
    residual_bias_grads = (reduced[5] * factor)[5:7]
    return (
        block_output,
        input_grad,
        grad_norm,
        updated[0][0],
        updated[1][0],
        updated[2][0],
        updated[3][0],
        updated[4][0],
        updated[5][0],
        updated[6][0],
        updated[0][1],
        updated[1][1],
        updated[2][1],
        updated[3][1],
        updated[4][1],
        updated[5][1],
        updated[6][1],
        updated[0][2],
        updated[1][2],
        updated[2][2],
        updated[3][2],
        updated[4][2],
        updated[5][2],
        updated[6][2],
        residual_bias_grads,
    )


def dot_nn(left, right):
    return lax.dot_general(left, right, (((1,), (0,)), ((), ())), preferred_element_type=F32)


def dot_nt(left, right):
    return lax.dot_general(left, right, (((1,), (1,)), ((), ())), preferred_element_type=F32)


def dot_tn(left, right):
    return lax.dot_general(left, right, (((0,), (0,)), ((), ())), preferred_element_type=F32)


def normalise(rows):
    centre = rows - jnp.mean(rows, -1, keepdims=True)
    scale = lax.rsqrt(jnp.mean(centre * centre, -1, keepdims=True) + NORM_EPS)
    return centre * scale, scale


def norm_back(grad, hat, scale, gain):
    inner = grad * gain
    return scale * (
        inner
        - jnp.mean(inner, -1, keepdims=True)
        - hat * jnp.mean(inner * hat, -1, keepdims=True)
    )


def where(condition, action):
    if condition is None:
        action()
    else:
        pl.when(condition)(lambda: action())


class Copy:
    def __init__(self, copy, send_if, recv_if):
        self.copy, self.send_if, self.recv_if = copy, send_if, recv_if
        self.started = self.received = self.sent = False

    def start(self):
        self.started = True
        where(self.send_if, self.copy.start)

    def wait_recv(self):
        self.received = True
        where(self.recv_if, self.copy.wait_recv)

    def wait_send(self):
        self.sent = True
        where(self.send_if, self.copy.wait_send)


class Group:
    def __init__(self, whole, sem):
        self.whole, self.sem, self.members, self.waited = whole, sem, [], False

    def wait_recv(self):
        self.waited = True
        for copy in self.members:
            copy.received = True
        pltpu.make_async_copy(self.whole, self.whole, self.sem).wait()

    def wait_send(self):
        self.waited = True
        pltpu.make_async_copy(self.whole, self.whole, self.sem).wait()


class Copies:
    def __init__(self, send_sems, recv_sems):
        self.send_sems, self.recv_sems, self.all, self.groups = send_sems, recv_sems, [], []
        self.sends = self.recvs = 0

    def next_send(self):
        self.sends += 1
        return self.send_sems.at[self.sends - 1]

    def next_recv(self):
        self.recvs += 1
        return self.recv_sems.at[self.recvs - 1]

    def leaving(self, whole):
        self.groups.append(Group(whole, self.next_send()))
        return self.groups[-1]

    def arriving(self, whole):
        return Group(whole, self.next_recv())

    def make(self, source, target, device, send_if=None, recv_if=None, out=None, into=None):
        copy = Copy(pltpu.make_async_remote_copy(
            src_ref=source,
            dst_ref=target,
            send_sem=out.sem if out else self.next_send(),
            recv_sem=into.sem if into else self.next_recv(),
            device_id=device,
            device_id_type=pl.DeviceIdType.MESH,
        ), send_if, recv_if)
        copy.sent = out is not None
        for group in (out, into):
            if group:
                group.members.append(copy)
        self.all.append(copy)
        return copy

    def settle(self):
        for copy in self.all:
            if copy.started and not copy.sent:
                copy.wait_send()
        for group in self.groups:
            if not group.waited and all(copy.started for copy in group.members):
                group.wait_send()


def slab_rows(block, index):
    return pl.ds(pl.multiple_of((block * 8 + index) * 24, 8), 24)


class Panels:
    def __init__(self, ref, height, first, count):
        self.ref, self.height, self.first, self.count = ref, height, first, count

    def rows(self, panel, block, index):
        return pl.ds(pl.multiple_of((self.first + panel) * self.height + (block * 8 + index) * 24, 8), 24)

    def get(self, block, index):
        parts = [self.ref[self.rows(p, block, index), :] for p in range(self.count)]
        return parts[0] if self.count == 1 else jnp.concatenate(parts, 1)

    def put(self, block, index, value):
        for p in range(self.count):
            self.ref[self.rows(p, block, index), :] = value[:, p * 256 : p * 256 + 256]


N_SEMS = (53, 92)


def layer_kernel(
    span, x_in, cot_in, qw_in, kw_in, ow_in, uw_in, dw_in, vec_in, kvb_in,
    to_bo, to_ig, to_q, to_o, to_kv, to_vec, to_up, to_dn, to_small,
    x, cot, qw, kw, ow, uw, dw, vec, kvb,
    bo, ig, g_q, g_o, g_kv, g_vec, g_up, g_dn, g_small,
    KW, Q, O, U, Dn, X, C, KV, ub, WQ, WKV, WO, WU, gains, vsq,
    n1, hat1, scale1, N2, act, dl, OP, NP,
    qz, doz, doT, kvT, bias, sbuf, mixT, dqT, dkv,
    GP, GV, GU, GD, vg,
    SK1, RK1, SK2, RK2,
    RO1, SO2, RO2, RN1, SN2, RN2,
    SQ1, RQ1, SQ2, RQ2, SQ3, RQ3, SQ4, RQ4,
    SO1, QO1, SO2b, RO2b, SO3, RO3, SO4, RO4,
    SP1, RP1, SP2, RP2, SP3, RP3,
    SV1, RV1, SV2, RV2, SV3, RV3,
    SU1, RU1, SU2, RU2, SU3, RU3, RXU,
    SD1, RD1, SD2, RD2, RXD,
    NS1,
    send_sems, recv_sems, save_sems, load_sems,
):
    tok = x.shape[0]
    f = lax.axis_index("fsdp")
    s = lax.axis_index("seq")
    z = lax.div(s, 2)
    y = lax.rem(s, 2)
    yo = 1 - y
    fc = f + 1 - 2 * lax.rem(f, 2)
    fx = lax.rem(f + 2, 4)
    fd = 3 - f
    zk = (z, z + 1 - 2 * lax.rem(z, 2), lax.rem(z + 2, 4), 3 - z)
    dev_c, dev_x, dev_d = (fc, s), (fx, s), (fd, s)
    dev_y = (f, z * 2 + yo)
    dev_z = tuple((f, zz * 2 + y) for zz in zk)
    dev_zy = tuple((f, zz * 2 + yo) for zz in zk)
    fsdp_devs = (dev_c, dev_x, dev_d)
    seq_devs = dev_z[1:] + dev_zy
    far = (3, 2, 1)

    copies = Copies(send_sems, recv_sems)
    make = copies.make

    def start(*wanted):
        for copy in wanted:
            copy.start()

    def arrive(*wanted):
        for copy in wanted:
            copy.wait_recv()

    saved = []

    def save(source, target):
        copy = pltpu.make_async_copy(source, target, save_sems.at[len(saved)])
        copy.start()
        saved.append(copy)

    leaving, arriving = copies.leaving, copies.arriving
    three, four = pl.ds(0, 3), pl.ds(0, 4)

    def seq_gather(ref, some, together=True):
        to_z, to_y = [None], []
        out = leaving(some(three))
        for k in (1, 2, 3):
            to_z.append(make(ref(z, y), ref(z, y), dev_z[k], out=out))
        out, into = leaving(some(four)), arriving(some(four)) if together else None
        for k in range(4):
            to_y.append(make(ref(zk[k], y), ref(zk[k], y), dev_y, out=out, into=into))
        return to_z, to_y, into

    w_z, w_y, w_yin = seq_gather(lambda i, j: KW.at[f, i, j], lambda n: KW.at[0, n, 0])
    q_z, q_y, _ = seq_gather(lambda i, j: Q.at[f, i, j], lambda n: Q.at[0, n, 0], False)
    o_z, o_y, o_yin = seq_gather(lambda i, j: O.at[f, i, j], lambda n: O.at[0, n, 0])
    p_z, p_y, p_yin = seq_gather(lambda i, j: O.at[fx, i, j], lambda n: O.at[0, n, 0])
    u_z, u_y, u_yin = seq_gather(lambda i, j: U.at[i, j], lambda n: U.at[n, 0])
    d_z, d_y, d_yin = seq_gather(lambda i, j: Dn.at[i, j], lambda n: Dn.at[n, 0])
    k_z, k_y, k_yin = seq_gather(lambda i, j: KV.at[i, j], lambda n: KV.at[n, 0])

    def fsdp_gather(ref, some):
        out, into = leaving(some(three)), arriving(some(pl.ds(0, 2)))
        to_x = [make(ref(f, j), ref(f, j), dev_x, out=out) for j in (y, yo)]
        to_c = [make(ref(f, j), ref(f, j), dev_c, out=out, into=into) for j in (y, yo)]
        on_c = [make(ref(fx, j), ref(fx, j), dev_c, out=out, into=into) for j in (y, yo)]
        return to_x, to_c, on_c, into

    w_x, w_c, w_xc, w_in = fsdp_gather(lambda i, j: KW.at[i, :, j], lambda n: KW.at[n])
    q_out, q_in = leaving(Q.at[three]), arriving(Q.at[pl.ds(0, 2)])

    def q_copy(g, j, device, into):
        return make(Q.at[g, :, j], Q.at[g, :, j], device, out=q_out, into=into)

    q_x0 = q_copy(f, y, dev_x, None)
    q_c = [q_copy(f, j, dev_c, q_in) for j in (y, yo)]
    q_xc = [q_copy(fx, j, dev_c, q_in) for j in (y, yo)]
    q_xs = [make(Q.at[f, zz, yo], Q.at[f, zz, yo], dev_x, out=q_out) for zz in zk]
    o_x = make(O.at[f, z, y], O.at[f, z, y], dev_x)
    o_out, o_in = leaving(O.at[pl.ds(0, 2)]), arriving(O.at[pl.ds(0, 2)])

    def o_copy(g, j):
        return make(O.at[g, :, j], O.at[g, :, j], dev_c, out=o_out, into=o_in)

    o_c = [o_copy(f, j) for j in (y, yo)]
    op_c = [o_copy(fx, j) for j in (y, yo)]

    def token_gather(ref):
        out = leaving(ref.at[three])
        return (
            make(ref.at[f], ref.at[f], dev_x, out=out),
            make(ref.at[f], ref.at[f], dev_c, out=out),
            make(ref.at[fx], ref.at[fx], dev_c, out=out),
        )

    x_x, x_c, x_xc = token_gather(X)
    c_x, c_c, c_xc = token_gather(C)
    uf_out, uf_in = leaving(ub.at[three]), arriving(U.at[0, 0, three])
    u_f = [
        make(ub.at[g], U.at[z, y, f], dev, out=uf_out, into=uf_in)
        for g, dev in zip((fc, fx, fd), fsdp_devs)
    ]

    out = leaving(SK1)
    rk1 = [make(SK1.at[zz], RK1.at[zz], dev_y, out=out) for zz in zk]

    def to_z_peers(S, R):
        out, into = leaving(S), arriving(R)
        return [make(S.at[k], R.at[k], dev_z[k + 1], out=out, into=into) for k in range(3)], into

    rk2, rk2_in = to_z_peers(SK2, RK2)

    def to_core(ref, R):
        out, into = leaving(ref.at[pl.ds(0, 2)]), arriving(R)
        found = [
            make(ref.at[g], R.at[i], dev_c, out=out, into=into) for i, g in enumerate((fc, fd))
        ]
        return found, into

    out_c, out_in = to_core(OP, RO1)
    out_x = make(SO2, RO2, dev_x)
    nrm_c, nrm_in = to_core(NP, RN1)
    nrm_x = make(SN2, RN2, dev_x)

    def full_scatter(S1, R1, S2, R2, S3, R3, S4, R4):
        c_copy = make(S1, R1, dev_c)
        out = leaving(S2)
        x_copies = [make(S2.at[i], R2.at[i], dev_x, out=out) for i in range(2)]
        y_copy = make(S3, R3, dev_y)
        return (c_copy, x_copies, y_copy, *to_z_peers(S4, R4))

    q_sc = full_scatter(SQ1, RQ1, SQ2, RQ2, SQ3, RQ3, SQ4, RQ4)
    o_sc = full_scatter(SO1, QO1, SO2b, RO2b, SO3, RO3, SO4, RO4)
    p_c = make(SP1, RP1, dev_c)
    p_x = make(SP2, RP2, dev_x)
    out, p_in = leaving(SP3), arriving(RP3)
    p_s = [
        make(SP3.at[i], RP3.at[i], dev, out=out, into=p_in) for i, dev in enumerate(seq_devs)
    ]
    v_c = make(SV1, RV1, dev_c)
    v_x = make(SV2, RV2, dev_x)
    out, v_in = leaving(RV3), arriving(RV3)
    v_s = [make(SV3, RV3.at[i], dev, out=out, into=v_in) for i, dev in enumerate(seq_devs)]
    out = leaving(SU1)
    su_y = [make(SU1.at[zz], RU1.at[zz], dev_y, out=out) for zz in zk]
    inner = lax.div(z + 1, 2) == 1
    outer = lax.div(z + 1, 2) != 1

    def relayed(S2, R2, RX):
        to_z = [make(S2.at[k], R2.at[k], dev_z[k + 1]) for k in range(2)]
        to_z.append(make(S2.at[2], R2.at[2], dev_z[3], inner, inner))
        return to_z, make(S2.at[2], RX, dev_z[1], outer, inner)

    su_z, su_r = relayed(SU2, RU2, RXU)
    out, su_fin = leaving(SU3.at[three]), arriving(RU3)
    su_f = [
        make(SU3.at[g], RU3.at[i], dev, out=out, into=su_fin)
        for i, (g, dev) in enumerate(zip((fc, fx, fd), fsdp_devs))
    ]
    out = leaving(SD1)
    sd_y = [make(SD1.at[zz], RD1.at[zz], dev_y, out=out) for zz in zk]
    sd_z, sd_r = relayed(SD2, RD2, RXD)
    me = f * 8 + s
    others = [lax.rem(me + i, 32) for i in range(1, 32)]
    everyone = [(lax.div(i, 8), lax.rem(i, 8)) for i in others]
    most = pl.ds(0, 31)
    out, n_in = leaving(NS1.at[most]), arriving(NS1.at[most])
    n_all = [make(NS1.at[me], NS1.at[me], dev, out=out, into=n_in) for dev in everyone]

    barrier = pltpu.get_barrier_semaphore()
    for dev in everyone:
        pl.semaphore_signal(barrier, inc=1, device_id=dev, device_id_type=pl.DeviceIdType.MESH)

    loads = []
    pairs = (
        (vec_in, vec), (kvb_in, kvb), (kw_in, kw), (qw_in, qw), (ow_in, ow),
        (x_in, x), (cot_in, cot), (uw_in, uw), (dw_in, dw),
    )
    for i, (source, target) in enumerate(pairs):
        copy = pltpu.make_async_copy(source, target, load_sems.at[i])
        copy.start()
        loads.append(copy)
    for copy in loads:
        copy.wait()

    vsq[...] = jnp.zeros((128, 128), F32)
    vsq[0:11, 0:24] = vec[...]
    vsq[11:12, 0:16] = kvb[...]
    KW[f, z, y, :, :128] = kw[...].astype(BF16)
    KW[f, z, y, :, 128:] = vsq[...].T[:24, :].astype(BF16)
    Q[f, z, y] = qw[...].astype(BF16)
    O[f, z, y] = ow[...].astype(BF16)
    for j in range(4):
        ub[j] = uw[:, j * D : (j + 1) * D].astype(BF16)
    U[z, y, f] = ub[f]
    Dn[z, y] = dw[...].astype(BF16)
    X[f] = x[...]
    C[f] = cot[...]

    @pl.when(outer)
    def _():
        RU2[2] = jnp.zeros((4, 24, D), BF16)
        RD2[2] = jnp.zeros((96, D), BF16)

    pl.semaphore_wait(barrier, 31)
    start(w_z[3], w_z[2], w_z[1], w_y[0])
    start(o_x, q_z[3], q_z[2], q_z[1], q_y[0])
    start(o_z[3], o_z[2], o_z[1], o_y[0])

    hat, scale = normalise(x[...].astype(F32))
    hat1[...] = hat
    scale1[...] = jnp.broadcast_to(scale, (tok, 128))
    own_span = span[0, s]
    lane = lax.broadcasted_iota(jnp.int32, (tok, 128), 1)
    spot = lax.broadcasted_iota(jnp.int32, (tok, 128), 0) + own_span * tok
    in_head = lax.rem(lane, 64)
    step = lax.rem(in_head, ROT_DIMS // 2).astype(F32)
    inverse = jnp.exp(step * (-2.0 * math.log(10000.0) / ROT_DIMS))
    angle = spot.astype(F32) * (0.25 * inverse)
    sine = jnp.sin(angle)
    cosine = jnp.where(in_head < ROT_DIMS, jnp.cos(angle), 1.0)
    sine_low = jnp.where(in_head < ROT_DIMS // 2, sine, 0.0)
    sine_high = jnp.where((in_head >= ROT_DIMS // 2) & (in_head < ROT_DIMS), sine, 0.0)
    key_lane = lane < 64
    key_cos = jnp.where(key_lane, cosine, 1.0)
    key_low = jnp.where(key_lane, sine_low, 0.0)
    key_high = jnp.where(key_lane, sine_high, 0.0)

    def turn(block, cos_t, low_t, high_t):
        up = pltpu.roll(block, 120, 1)
        down = pltpu.roll(block, 8, 1)
        return block * cos_t - up * low_t + down * high_t

    def turn_back(block, cos_t, low_t, high_t):
        up = pltpu.roll(block, 120, 1)
        down = pltpu.roll(block, 8, 1)
        return block * cos_t + up * low_t - down * high_t

    def forward(to_z, to_y, *which):
        for k in which:
            arrive(to_z[k])
            start(to_y[k])

    forward(w_z, w_y, *far)
    start(w_x[0], w_c[0])
    arrive(o_x)
    start(p_z[3], p_z[2], p_z[1], p_y[0])
    arrive(w_yin)
    start(w_x[1], w_c[1])
    forward(q_z, q_y, *far)
    start(q_x0, q_c[0])
    arrive(w_x[0])
    start(w_xc[0])
    arrive(w_x[1])
    start(w_xc[1])
    arrive(w_in)
    slabs = [KW[g, i, j].astype(F32) for g in range(4) for i in range(4) for j in range(2)]
    for i in range(16):
        pair = jnp.concatenate([slabs[2 * i][:, :128], slabs[2 * i + 1][:, :128]], 0)
        WKV[i * 48 : (i + 1) * 48, :] = pair.astype(BF16)
    gains[...] = jnp.concatenate([slab[:, 128:] for slab in slabs], 0).T
    vsq[...] = jnp.concatenate([slab[:16, 128:] for slab in slabs[:8]], 0).T
    kv_shift = vsq[11:12, :]
    n1[...] = (hat * gains[0:1, :] + gains[1:2, :]).astype(BF16)
    kv_pre = dot_nn(n1[...], WKV[...]) + kv_shift
    KV[z, y] = turn(kv_pre, key_cos, key_low, key_high).astype(BF16)
    start(k_z[3], k_z[2], k_z[1], k_y[0])
    for k in range(4):
        arrive(q_y[k])
        start(q_xs[k])
    start(q_c[1])
    forward(o_z, o_y, *far)
    start(o_c[0])
    forward(p_z, p_y, *far)
    start(op_c[0])
    arrive(q_x0)
    start(q_xc[0])
    vg[...] = jnp.zeros((128, D), F32)
    csum = jnp.sum(cot[...].astype(F32), 0, keepdims=True)
    vg[5:6, :] = csum
    vg[6:7, :] = csum
    key_iota = lax.broadcasted_iota(jnp.int32, (tok, tok), 0)
    row_iota = lax.broadcasted_iota(jnp.int32, (tok, tok), 1) + own_span * tok
    for i in range(8):
        bias[i * tok : (i + 1) * tok, :] = jnp.where(
            key_iota + span[0, i] * tok <= row_iota, 0.0, MASKED
        ).astype(F32)
    dkv[...] = jnp.zeros((8 * tok, 128), F32)
    start(*u_f)
    forward(k_z, k_y, *far)
    arrive(*q_xs)
    start(q_xc[1])
    arrive(o_yin)
    start(o_c[1])
    arrive(p_yin)
    start(op_c[1])
    arrive(uf_in)
    start(u_z[3], u_z[2], u_z[1], u_y[0])
    start(x_x, c_x, x_c, c_c)
    arrive(q_in)

    def join(ref, whole):
        def put(i, carry):
            g = lax.div(i, 4)
            zz = lax.rem(i, 4)
            pair = jnp.concatenate([ref[g, zz, 0].astype(F32), ref[g, zz, 1].astype(F32)], 0)
            whole[pl.ds(pl.multiple_of(i * 48, 16), 48), :] = pair.astype(BF16)
            return carry

        lax.fori_loop(0, 16, put, 0)

    join(Q, WQ)
    q_pre = dot_nn(n1[...], WQ[...]) + gains[4:5, :]
    gap = jnp.zeros((tok, 64), BF16)
    for j in range(6):
        cols = slice(j * 128, j * 128 + 128)
        turned = turn(q_pre[:, cols], cosine, sine_low, sine_high).astype(BF16).astype(F32)
        turned = (turned * HD ** (-0.5)).astype(BF16)
        qz[2 * j] = jnp.concatenate([turned[:, :64], gap], 1)
        qz[2 * j + 1] = jnp.concatenate([turned[:, 64:], gap], 1)
    arrive(o_in)
    join(O, WO)
    mixed_back = dot_nt(cot[...], WO[...]).astype(BF16)
    for j in range(6):
        pair = mixed_back[:, j * 128 : j * 128 + 128]
        doz[2 * j] = jnp.concatenate([gap, pair[:, :64]], 1)
        doz[2 * j + 1] = jnp.concatenate([gap, pair[:, 64:]], 1)
    doT[...] = mixed_back.astype(F32).T.astype(BF16).reshape(HQ, HD, tok)
    arrive(k_yin)
    KVF = KV.reshape(8 * tok, 128)
    kvT[...] = KVF[...].astype(F32).T.astype(BF16)

    span_rows = 2 * tok
    chunks = 8 * tok // span_rows

    def fold(values, reduce):
        return reduce(values.reshape(span_rows // 8, 8, tok), axis=0)

    def attend(step_index):
        heads = [step_index * 2, step_index * 2 + 1]
        top, total, share, delta, acc = {}, {}, {}, {}, {}

        def rows_of(i):
            return pl.ds(i * span_rows, span_rows)

        def held_of(j, i):
            return pl.ds((j * chunks + i) * span_rows, span_rows)

        def score(j, i):
            scores = dot_nt(KVF[rows_of(i), :], qz[heads[j]]) + bias[rows_of(i), :]
            sbuf[held_of(j, i), :] = scores
            here = fold(scores, jnp.max)
            top[j] = here if i == 0 else jnp.maximum(top[j], here)
            if i == chunks - 1:
                top[j] = jnp.max(top[j], axis=0, keepdims=True)

        def weigh(j, i):
            weights = jnp.exp(sbuf[held_of(j, i), :] - top[j])
            sbuf[held_of(j, i), :] = weights
            here = fold(weights, jnp.sum)
            total[j] = here if i == 0 else total[j] + here
            if i == chunks - 1:
                share[j] = 1.0 / jnp.sum(total[j], axis=0, keepdims=True)

        def mix(j, i):
            rows = rows_of(i)
            probs = sbuf[held_of(j, i), :] * share[j]
            probs_low = probs.astype(BF16)
            sbuf[held_of(j, i), :] = probs
            here = dot_nn(kvT[:, rows], probs_low)
            acc[j] = here if i == 0 else acc[j] + here
            dkv[rows, :] += dot_nn(probs_low, doz[heads[j]])
            if i == chunks - 1:
                mixed = acc[j][64:, :]
                mixT[heads[j]] = mixed.astype(BF16)
                delta[j] = jnp.sum(mixed * doT[heads[j]].astype(F32), axis=0, keepdims=True)

        def back(j, i):
            rows = rows_of(i)
            prob_grad = dot_nt(KVF[rows, :], doz[heads[j]])
            score_low = (sbuf[held_of(j, i), :] * (prob_grad - delta[j])).astype(BF16)
            here = dot_nn(kvT[:, rows], score_low)
            acc[j] = here if i == 0 else acc[j] + here
            dkv[rows, :] += dot_nn(score_low, qz[heads[j]])
            if i == chunks - 1:
                dqT[heads[j]] = acc[j][:64, :] * HD ** (-0.5)

        for stage in (
            ((score, 0),),
            ((weigh, 0), (score, 1)),
            ((mix, 0), (weigh, 1)),
            ((back, 0), (mix, 1)),
            ((back, 1),),
        ):
            for i in range(chunks):
                for part, j in stage:
                    part(j, i)

    def attend_all(first, last, meanwhile):
        def body_step(step_index, carry):
            for at, action in meanwhile:
                pl.when(step_index == at)(action)
            attend(step_index)
            return carry

        lax.fori_loop(first, last, body_step, 0)


    def pump_two():
        forward(u_z, u_y, 1)

    def pump_three():
        forward(u_z, u_y, 3, 2)

    def pump_four():
        forward(d_z, d_y, 1)
        arrive(x_x, c_x)
        start(x_xc, c_xc)

    def pump_five():
        forward(d_z, d_y, 3)

    attend_all(
        0, HQ // 2,
        (
            (1, lambda: start(d_z[3], d_z[2], d_z[1], d_y[0])),
            (2, pump_two), (3, pump_three), (4, pump_four), (5, pump_five),
        ),
    )

    for k in (3, 2, 1, 0):
        rows = pl.ds(pl.multiple_of((2 * zk[k] + yo) * tok, 8), tok)
        SK1[zk[k]] = dkv[rows, :].astype(BF16)
        start(rk1[k])
    mix_low = mixT.reshape(D, tok)[...]
    for c in range(3):
        sbuf[(3 + c) * D : (4 + c) * D, :] = dot_nn(mix_low, cot[:, c * 256 : c * 256 + 256])
    GQ = Panels(sbuf, D, 0, 3)
    GO = Panels(sbuf, D, 3, 3)

    def scatter_c(G, S1, copy):
        def put(i, carry):
            for j, g in enumerate((fc, fd)):
                S1[j, i] = G.get(g, i).astype(S1.dtype)
            return carry

        lax.fori_loop(0, 8, put, 0)
        start(copy)

    def scatter_x(G, R1, S2, copies_):
        arrive(copies_[0])
        for j, yy in enumerate((yo, y)):
            for i in range(4):
                slab = 2 * i + yy
                S2[j, i] = (G.get(fx, slab) + R1[1, slab].astype(F32)).astype(S2.dtype)
                G.put(f, slab, G.get(f, slab) + R1[0, slab].astype(F32))
            start(copies_[1][j])

    def scatter_y(G, R2, S3, copies_):
        arrive(copies_[1][0])
        for i in range(4):
            S3[i] = (G.get(f, 2 * i + yo) + R2[0, i].astype(F32)).astype(S3.dtype)
        start(copies_[2])

    def scatter_z(G, R2, R3, S4, copies_):
        arrive(copies_[1][1], copies_[2])
        for k in far:
            total = G.get(f, 2 * zk[k] + y) + R2[1, zk[k]].astype(F32) + R3[zk[k]].astype(F32)
            S4[k - 1] = total.astype(S4.dtype)
            start(copies_[3][k - 1])

    def scatter_end(G, R2, R3, R4, copies_):
        total = G.get(f, 2 * z + y) + R2[1, z].astype(F32) + R3[z].astype(F32)
        arrive(copies_[4])
        for k in range(3):
            total = total + R4[k].astype(F32)
        return total

    scatter_c(GO, SO1, o_sc[0])
    q_back = dqT.reshape(D, tok)[...].T
    parts = []
    for j in range(6):
        parts.append(
            turn_back(q_back[:, j * 128 : j * 128 + 128], cosine, sine_low, sine_high).astype(BF16)
        )
    q_low = jnp.concatenate(parts, 1)
    vg[4:5, :] = jnp.sum(q_low.astype(F32), 0, keepdims=True)
    for c in range(3):
        sbuf[c * D : (c + 1) * D, :] = dot_tn(n1[...], q_low[:, c * 256 : c * 256 + 256])
    scatter_c(GQ, SQ1, q_sc[0])
    forward(d_z, d_y, 2)
    arrive(u_yin, x_c, x_xc)

    def pair_step(k):
        arrive(rk1[k])
        rows = pl.ds(pl.multiple_of((2 * zk[k] + y) * tok, 8), tok)
        SK2[k - 1] = (dkv[rows, :] + RK1[zk[k]].astype(F32)).astype(BF16)
        start(rk2[k - 1])

    def lift_one():
        pair_step(3)

    def lift_two():
        pair_step(2)
        scatter_x(GO, QO1, SO2b, o_sc)

    def lift_three():
        pair_step(1)
        scatter_x(GQ, RQ1, SQ2, q_sc)

    def tokens_to_x():
        arrive(out_in, nrm_in)
        SO2[...] = (OP[fx].astype(F32) + RO1[1].astype(F32)).astype(BF16)
        start(out_x)
        SN2[...] = (NP[fx].astype(F32) + RN1[1].astype(F32)).astype(BF16)
        start(nrm_x)

    def down_rows(k):
        return pl.ds(pl.multiple_of((zk[k] * 2 + y) * 96, 8), 96)

    def down_step(k):
        arrive(sd_y[k])
        total = GD[down_rows(k), :] + RD1[zk[k]].astype(F32)
        if k in (0, 2):
            GD[down_rows(k), :] = total
        if k:
            SD2[k - 1] = total.astype(BF16)
        if k == 2:
            pl.when(outer)(lambda: start(sd_z[1]))
        elif k:
            start(sd_z[k - 1])
        if k == 3:
            start(sd_r)

    def down_relay():
        arrive(sd_r)

        @pl.when(inner)
        def _():
            SD2[1] = (GD[down_rows(2), :] + RXD[...].astype(F32)).astype(BF16)
            start(sd_z[1])

    def up_step(k):
        arrive(su_y[k])
        for g in range(4):
            rows = slab_rows(g, zk[k] * 2 + y)
            total = GU[rows, :] + RU1[zk[k], g].astype(F32)
            if k in (0, 2):
                GU[rows, :] = total
            if k:
                SU2[k - 1, g] = total.astype(BF16)
        if k == 2:
            pl.when(outer)(lambda: start(su_z[1]))
        elif k:
            start(su_z[k - 1])
        if k == 3:
            start(su_r)

    def up_relay():
        arrive(su_r)

        @pl.when(inner)
        def _():
            for g in range(4):
                total = GU[slab_rows(g, zk[2] * 2 + y), :] + RXU[g].astype(F32)
                SU2[1, g] = total.astype(BF16)
            start(su_z[1])

    up_totals = []

    def up_end():
        arrive(*su_z)
        for g in range(4):
            total = GU[slab_rows(g, s), :]
            for k in range(3):
                total = total + RU2[k, g].astype(F32)
            up_totals.append(total)
            g_up[g] = total
            SU3[g] = total.astype(BF16)
        start(*su_f)

    for g in range(4):
        for i in range(4):
            pair = jnp.concatenate([U[i, j, g].astype(F32) for j in range(2)], 0)
            WU[(g * 4 + i) * 48 : (g * 4 + i + 1) * 48, :] = pair.astype(BF16)
    WD = Dn.reshape(D, D)
    up_bias = gains[pl.ds(7 + f, 1), :]

    def slope_rows(c, t):
        return pl.ds(pl.multiple_of(c * 4 * tok + t * tok, tok), tok)

    def lift_block(t, carry):
        for at, action in ((1, lift_one), (2, lift_two), (3, lift_three)):
            pl.when(t == at)(action)
        rows = pl.ds(pl.multiple_of(t * tok, tok), tok)
        hat2, _ = normalise(X[t].astype(F32))
        low2 = (hat2 * gains[2:3, :] + gains[3:4, :]).astype(BF16)
        N2[rows, :] = low2
        for c in range(3):
            units = slice(c * 256, c * 256 + 256)
            lifted = dot_nn(low2, WU[:, units]) + up_bias[:, units]
            half = 0.5 + 0.5 * lax.erf(lifted * (0.5**0.5))
            act[rows, units] = (lifted * half).astype(BF16)
            bell = jnp.exp(lifted * lifted * -0.5) * (1.0 / math.sqrt(2.0 * math.pi))
            bias[slope_rows(c, t), :] = half + lifted * bell
        return carry

    lax.fori_loop(0, 4, lift_block, 0)
    arrive(c_c, c_xc)
    CF = C.reshape(4 * tok, D)
    for c in range(3):
        units = slice(c * 256, c * 256 + 256)
        GD[units, :] = dot_tn(act[:, units], CF[...])
    for k in (3, 2, 1, 0):
        SD1[zk[k]] = GD[pl.ds(pl.multiple_of((zk[k] * 2 + yo) * 96, 8), 96), :].astype(BF16)
        start(sd_y[k])
    arrive(d_yin)

    def back_one():
        scatter_y(GO, RO2b, SO3, o_sc)

    def back_two():
        down_step(3)

    def back_three():
        scatter_y(GQ, RQ2, SQ3, q_sc)

    def back_block(t, carry):
        for at, action in ((1, back_one), (2, back_two), (3, back_three)):
            pl.when(t == at)(action)
        two_gain, two_shift, up_sum = carry
        rows = pl.ds(pl.multiple_of(t * tok, tok), tok)
        back = C[t]
        sums = []
        for c in range(3):
            units = slice(c * 256, c * 256 + 256)
            low = (bias[slope_rows(c, t), :] * dot_nt(back, WD[units, :])).astype(BF16)
            dl[rows, units] = low
            sums.append(jnp.sum(low.astype(F32), 0, keepdims=True))
        OP[t] = dot_nn(act[rows, :], WD[...]).astype(BF16)
        grad2 = dot_nt(dl[rows, :], WU[...])
        NP[t] = grad2.astype(BF16)
        hat2, _ = normalise(X[t].astype(F32))
        return (
            two_gain + jnp.sum(grad2 * hat2, 0, keepdims=True),
            two_shift + jnp.sum(grad2, 0, keepdims=True),
            up_sum + jnp.concatenate(sums, 1),
        )

    zero_row = jnp.zeros((1, D), F32)
    two_gain, two_shift, up_sum = lax.fori_loop(0, 4, back_block, (zero_row,) * 3)
    vg[2:3, :] = two_gain
    vg[3:4, :] = two_shift
    vg[pl.ds(7 + f, 1), :] = up_sum
    start(*out_c, *nrm_c)
    down_step(2)
    for c in range(3):
        units = slice(c * 256, c * 256 + 256)
        GU[units, :] = dot_tn(N2[:, units], dl[...])
    for k in (3, 2, 1, 0):
        for g in range(4):
            SU1[zk[k], g] = GU[slab_rows(g, zk[k] * 2 + yo), :].astype(BF16)
        start(su_y[k])
    down_step(1)
    grad1 = dot_nt(q_low, WQ[...])
    arrive(rk1[0])
    kv_back = dkv[pl.ds(pl.multiple_of((2 * z + y) * tok, 8), tok), :] + RK1[z].astype(F32)
    arrive(rk2_in)
    for k in range(3):
        kv_back = kv_back + RK2[k].astype(F32)
    kv_low = turn_back(kv_back, key_cos, key_low, key_high).astype(BF16)
    grad1 = grad1 + dot_nt(kv_low, WKV[...])
    vg[0:1, :] = jnp.sum(grad1 * hat1[...], 0, keepdims=True)
    vg[1:2, :] = jnp.sum(grad1, 0, keepdims=True)
    kv_sum = jnp.sum(kv_low.astype(F32), 0, keepdims=True)
    short = jnp.zeros((1, 8), F32)
    spread = jnp.concatenate(
        [part for i in range(8) for part in (kv_sum[:, i * 16 : i * 16 + 16], short)], 1
    )
    vg[11:12, :] = jnp.concatenate([spread] * 4, 1)
    GP[...] = dot_tn(n1[...], kv_low)
    flipped = vg[...].T

    def packed(g):
        parts = [flipped[(g * 8 + i) * 24 : (g * 8 + i + 1) * 24, :16] for i in range(8)]
        return jnp.concatenate(parts, 1)

    for g in range(4):
        GV[g] = packed(g)
    for i in range(8):
        for j, g in enumerate((fc, fd)):
            SP1[j, i] = GP[slab_rows(g, i), :].astype(BF16)
    for j, g in enumerate((fc, fd)):
        SV1[j] = GV[g]
    start(p_c, v_c)
    down_relay()
    down_step(0)
    arrive(p_c, v_c)
    for i in range(8):
        SP2[i] = (GP[slab_rows(fx, i), :] + RP1[1, i].astype(F32)).astype(BF16)
    SV2[...] = GV[fx] + RV1[1]
    start(p_x, v_x)
    tokens_to_x()
    scatter_z(GO, RO2b, RO3, SO4, o_sc)
    arrive(p_x, v_x)

    def kv_sum_of(slab):
        return GP[slab_rows(f, slab), :] + RP1[0, slab].astype(F32) + RP2[slab].astype(F32)

    seq_slabs = [2 * zk[k] + y for k in (1, 2, 3)] + [2 * zk[k] + yo for k in range(4)]
    for i, slab in enumerate(seq_slabs):
        SP3[i] = kv_sum_of(slab).astype(BF16)
    SV3[...] = GV[f] + RV1[0] + RV2[...]
    start(*p_s, *v_s)
    up_step(3)
    scatter_z(GQ, RQ2, RQ3, SQ4, q_sc)
    up_step(2)
    up_step(1)
    up_relay()
    up_step(0)
    mixed_rows = mix_low.astype(F32).T.astype(BF16)
    arrive(out_x)
    bo[...] = (
        x[...].astype(F32)
        + (dot_nn(mixed_rows, WO[...]) + gains[5:6, :])
        + (OP[f].astype(F32) + RO1[0].astype(F32) + RO2[...].astype(F32) + gains[6:7, :])
    ).astype(BF16)
    save(bo, to_bo)
    arrive(nrm_x)
    grad2 = NP[f].astype(F32) + RN1[0].astype(F32) + RN2[...].astype(F32)
    hat_rows = hat1[...]
    scale_rows = scale1[:, 0:1]
    ig[...] = (
        cot[...].astype(F32)
        + norm_back(grad1, hat_rows, scale_rows, gains[0:1, :])
        + norm_back(grad2, hat_rows, scale_rows, gains[2:3, :])
    )
    save(ig, to_ig)
    copies.settle()
    q_grad = scatter_end(GQ, RQ2, RQ3, RQ4, q_sc)
    g_q[...] = q_grad
    save(g_q, to_q)
    o_grad = scatter_end(GO, RO2b, RO3, RO4, o_sc)
    g_o[...] = o_grad
    save(g_o, to_o)
    kv_grad = kv_sum_of(s)
    vec_sum = SV3[...]
    arrive(p_in, v_in)
    for i in range(7):
        kv_grad = kv_grad + RP3[i].astype(F32)
        vec_sum = vec_sum + RV3[i]
    vec_own = jnp.zeros((24, 16), F32)
    for i in range(8):
        vec_own = vec_own + jnp.where(s == i, vec_sum[:, i * 16 : i * 16 + 16], 0.0)
    vec_grad = jnp.concatenate([vec_own, jnp.zeros((24, 112), F32)], 1)
    g_kv[...] = kv_grad
    g_vec[...] = vec_grad
    save(g_kv, to_kv)
    save(g_vec, to_vec)
    rows = pl.ds(pl.multiple_of(s * 96, 8), 96)
    down_grad = GD[rows, :]
    for k in range(3):
        arrive(sd_z[k])
        down_grad = down_grad + RD2[k].astype(F32)
    g_dn[...] = down_grad
    save(g_dn, to_dn)
    up_end()
    save(g_up.at[f], to_up.at[f])

    def energy(values):
        return jnp.sum(jnp.sum(values * values, 0, keepdims=True), 1, keepdims=True)

    lanes = lax.broadcasted_iota(jnp.int32, (24, 128), 1)
    squares = energy(q_grad) + energy(o_grad) + energy(kv_grad) + energy(jnp.where(lanes == 11, 0.0, vec_grad)) + energy(g_dn[...])
    for total in up_totals:
        squares = squares + energy(total)
    kv_rows = jnp.concatenate([vec_grad, jnp.zeros((104, 128), F32)], 0).T
    line = lax.broadcasted_iota(jnp.int32, (8, 128), 0)
    column = lax.broadcasted_iota(jnp.int32, (8, 128), 1)
    kv_line = jnp.where(column < 16, jnp.broadcast_to(kv_rows[11:12, :], (8, 128)), 0.0)
    NS1[me] = jnp.where(line == 0, squares, kv_line)
    start(*n_all)
    arrive(su_fin)
    for i, g in enumerate((fc, fx, fd)):
        g_up[g] = RU3[i].astype(F32)
        save(g_up.at[g], to_up.at[g])
    arrive(n_in)
    everything = NS1[0]
    pieces = jnp.zeros((1, 128), F32)
    for i in range(8):
        kv_piece = NS1[i][1:2, :]
        pieces = pieces + kv_piece * kv_piece
    for i in range(1, 32):
        everything = everything + NS1[i]
    whole = everything[0:1, 0:1] + jnp.sum(pieces, 1, keepdims=True)
    kv_piece = NS1[s][1:2, :]
    g_small[...] = jnp.where(line == 0, whole, jnp.broadcast_to(kv_piece, (8, 128)))
    save(g_small, to_small)
    copies.settle()
    assert (copies.sends, copies.recvs) == N_SEMS, (copies.sends, copies.recvs)
    for copy in saved:
        copy.wait()


def update_kernel(
    small, g_q, g_o, g_kv, g_vec, g_up, g_dn, bo_in, ig_in,
    mq, mk, mo, mu, md, mv, mb,
    fq, fk, fo, fu, fdn, fv, fb,
    sq, sk, so, su, sd, sv, sb,
    bo, ig, norm,
    nmq, nmk, nmo, nmu, nmd, nmv, nmb,
    nfq, nfk, nfo, nfu, nfd, nfv, nfb,
    nsq, nsk, nso, nsu, nsd, nsv, nsb,
    residual,
):
    bo[...] = bo_in[...]
    ig[...] = ig_in[...]
    size = jnp.sqrt(small[0:1, 0:1])
    norm[...] = size
    factor = jnp.minimum(1.0, CLIP_NORM / (size + 1e-06))

    def update(grad, master, first, second, new_master, new_first, new_second, rate, decay):
        clipped = grad * factor
        values = adamw(master, clipped, first, second, rate, decay)
        for ref, value in zip((new_master, new_first, new_second), values):
            ref[...] = value

    rates = (MATRIX_RATE, MATRIX_DECAY)
    update(g_q[...], mq[...], fq[...], sq[...], nmq, nfq, nsq, *rates)
    update(g_o[...], mo[...], fo[...], so[...], nmo, nfo, nso, *rates)
    update(g_kv[...], mk[...], fk[...], sk[...], nmk, nfk, nsk, *rates)
    for g in range(4):
        cols = slice(g * D, (g + 1) * D)
        update(
            g_up[g], mu[:, cols], fu[:, cols], su[:, cols],
            nmu.at[:, cols], nfu.at[:, cols], nsu.at[:, cols], *rates,
        )
    update(g_dn[...], md[...], fdn[...], sd[...], nmd, nfd, nsd, *rates)
    flipped = jnp.concatenate([g_vec[...], jnp.zeros((104, 128), F32)], 0).T
    vector_grad = flipped[:11, :24]
    update(vector_grad, mv[...], fv[...], sv[...], nmv, nfv, nsv, VECTOR_RATE, 0.0)
    residual[...] = flipped[5:7, :24] * factor
    update(small[1:2, :16], mb[...], fb[...], sb[...], nmb, nfb, nsb, VECTOR_RATE, 0.0)


def fast_body(
    inputs, cotangent, span_order,
    query_weight, keyval_weight, output_weight, up_weight, down_weight, vectors, kv_bias,
    *moments,
):
    tok = inputs.shape[0]
    smem = pl.BlockSpec(memory_space=pltpu.SMEM)
    shape = jax.ShapeDtypeStruct
    V = pltpu.VMEM
    results_here = (
        shape((tok, D), BF16),
        shape((tok, D), F32),
        shape((24, D), F32),
        shape((24, D), F32),
        shape((24, 128), F32),
        shape((24, 128), F32),
        shape((4, 24, D), F32),
        shape((96, D), F32),
        shape((8, 128), F32),
    )
    operands_here = (
        inputs, cotangent, query_weight, keyval_weight, output_weight, up_weight, down_weight,
        vectors, kv_bias.reshape(1, -1),
    )
    scratch = [V(a.shape, a.dtype) for a in operands_here + results_here]
    scratch += [
        V((4, 4, 2, 24, 256), BF16),
        V((4, 4, 2, 24, D), BF16),
        V((4, 4, 2, 24, D), BF16),
        V((4, 2, 4, 24, D), BF16),
        V((4, 2, 96, D), BF16),
        V((4, tok, D), BF16),
        V((4, tok, D), BF16),
        V((4, 2, tok, 128), BF16),
        V((4, 24, D), BF16),
        V((D, D), BF16),
        V((D, 128), BF16),
        V((D, D), BF16),
        V((D, D), BF16),
        V((128, D), F32),
        V((128, 128), F32),
        V((tok, D), BF16),
        V((tok, D), F32),
        V((tok, 128), F32),
        V((4 * tok, D), BF16),
        V((4 * tok, D), BF16),
        V((4 * tok, D), BF16),
        V((4, tok, D), BF16),
        V((4, tok, D), BF16),
        V((HQ, tok, 128), BF16),
        V((HQ, tok, 128), BF16),
        V((HQ, HD, tok), BF16),
        V((128, 8 * tok), BF16),
        V((12 * tok, tok), F32),
        V((6 * D, 256), F32),
        V((HQ, HD, tok), BF16),
        V((HQ, HD, tok), F32),
        V((8 * tok, 128), F32),
        V((D, 128), F32),
        V((4, 24, 128), F32),
        V((D, D), F32),
        V((D, D), F32),
        V((128, D), F32),
        V((4, tok, 128), BF16), V((4, tok, 128), BF16),
        V((3, tok, 128), BF16), V((3, tok, 128), BF16),
        V((2, tok, D), BF16), V((tok, D), BF16), V((tok, D), BF16),
        V((2, tok, D), BF16), V((tok, D), BF16), V((tok, D), BF16),
    ]
    def scatter_buffers(width):
        found = []
        for lead in ((2, 8), (2, 4), (4,), (3,)):
            found += [V(lead + (24, width), BF16)] * 2
        return found

    scratch += scatter_buffers(D)
    scratch += scatter_buffers(D)
    for lead in ((2, 8), (8,), (7,)):
        scratch += [V(lead + (24, 128), BF16)] * 2
    scratch += [V((2, 24, 128), F32)] * 2 + [V((24, 128), F32)] * 3 + [V((7, 24, 128), F32)]
    scratch += [V((4, 4, 24, D), BF16)] * 2 + [V((3, 4, 24, D), BF16)] * 2
    scratch += [V((4, 24, D), BF16), V((3, 24, D), BF16), V((4, 24, D), BF16)]
    scratch += [V((4, 96, D), BF16)] * 2 + [V((3, 96, D), BF16)] * 2 + [V((96, D), BF16)]
    scratch += [V((32, 8, 128), F32)]
    scratch += [pltpu.SemaphoreType.DMA((n,)) for n in N_SEMS] + [pltpu.SemaphoreType.DMA((12,)), pltpu.SemaphoreType.DMA((9,))]
    kv_row = kv_bias.reshape(1, -1)
    bo, ig, g_q, g_o, g_kv, g_vec, g_up, g_dn, small = pl.pallas_call(
        layer_kernel,
        name="layer",
        out_shape=results_here,
        in_specs=[smem] + [pl.BlockSpec(memory_space=pl.ANY)] * 9,
        out_specs=(pl.BlockSpec(memory_space=pl.ANY),) * 9,
        scratch_shapes=scratch,
        compiler_params=pltpu.CompilerParams(
            collective_id=0, has_side_effects=True, vmem_limit_bytes=62 * 2**20
        ),
    )(
        span_order, inputs, cotangent,
        query_weight, keyval_weight, output_weight, up_weight, down_weight, vectors, kv_row,
    )
    masters = (query_weight, keyval_weight, output_weight, up_weight, down_weight, vectors, kv_row)
    firsts = tuple(moments[:6]) + (moments[6].reshape(1, -1),)
    seconds = tuple(moments[7:13]) + (moments[13].reshape(1, -1),)
    state = [shape(a.shape, F32) for a in masters]
    operands = (small, g_q, g_o, g_kv, g_vec, g_up, g_dn, bo, ig) + masters + firsts + seconds
    outcomes = [shape((tok, D), BF16), shape((tok, D), F32), shape((1, 1), F32)]
    outcomes += state * 3 + [shape((2, vectors.shape[1]), F32)]

    def whole(a):
        return pl.BlockSpec(a.shape, lambda i: (0,) * len(a.shape))

    results = pl.pallas_call(
        update_kernel,
        name="update",
        grid=(1,),
        out_shape=outcomes,
        in_specs=[whole(a) for a in operands],
        out_specs=[whole(a) for a in outcomes],
        compiler_params=pltpu.CompilerParams(vmem_limit_bytes=62 * 2**20),
    )(*operands)
    results = list(results)
    results[2] = results[2].reshape(())
    for i in (9, 16, 23):
        results[i] = results[i].reshape(-1)
    return tuple(results)


def solution(mesh):
    grid = (mesh.shape["fsdp"], mesh.shape["seq"])
    return jax.shard_map(
        fast_body if grid == (4, 8) else body,
        mesh=mesh,
        in_specs=(
            P(("fsdp", "seq"), None),
            P(("fsdp", "seq"), None),
            P("fsdp", None),
            P(("fsdp", "seq"), None),
            P(("fsdp", "seq"), None),
            P(("fsdp", "seq"), None),
            P(("fsdp", "seq"), None),
            P(("fsdp", "seq"), None),
            P(None, ("fsdp", "seq")),
            P("seq"),
            P(("fsdp", "seq"), None),
            P(("fsdp", "seq"), None),
            P(("fsdp", "seq"), None),
            P(("fsdp", "seq"), None),
            P(("fsdp", "seq"), None),
            P(None, ("fsdp", "seq")),
            P("seq"),
            P(("fsdp", "seq"), None),
            P(("fsdp", "seq"), None),
            P(("fsdp", "seq"), None),
            P(("fsdp", "seq"), None),
            P(("fsdp", "seq"), None),
            P(None, ("fsdp", "seq")),
            P("seq"),
        ),
        out_specs=(
            P(("fsdp", "seq"), None),
            P(("fsdp", "seq"), None),
            P(),
            P(("fsdp", "seq"), None),
            P(("fsdp", "seq"), None),
            P(("fsdp", "seq"), None),
            P(("fsdp", "seq"), None),
            P(("fsdp", "seq"), None),
            P(None, ("fsdp", "seq")),
            P("seq"),
            P(("fsdp", "seq"), None),
            P(("fsdp", "seq"), None),
            P(("fsdp", "seq"), None),
            P(("fsdp", "seq"), None),
            P(("fsdp", "seq"), None),
            P(None, ("fsdp", "seq")),
            P("seq"),
            P(("fsdp", "seq"), None),
            P(("fsdp", "seq"), None),
            P(("fsdp", "seq"), None),
            P(("fsdp", "seq"), None),
            P(("fsdp", "seq"), None),
            P(None, ("fsdp", "seq")),
            P("seq"),
            P(None, ("fsdp", "seq")),
        ),
        check_vma=False,
    )
```

```python
import math

import jax
import jax.numpy as jnp
from jax import lax
from jax.experimental import pallas as pl
from jax.experimental.pallas import tpu as pltpu
from jax.sharding import PartitionSpec as P

D = 768
HQ = 12
HD = 64
ROT_DIMS = 16
FF = 3072
KEY_BLOCK = 512
STEP = 10
F32 = jnp.float32
BF16 = jnp.bfloat16


NORM_EPS = 1e-05
MASKED = -1e30
CLIP_NORM = 1.0
BETA_ONE = 0.9
BETA_TWO = 0.999
ADAM_EPS = 1e-08
MATRIX_DECAY = 0.1
MATRIX_RATE = 0.1
VECTOR_RATE = 0.3


def layer_norm(tensor, gain_row, shift_row):
    centre = tensor - jnp.mean(tensor, -1, keepdims=True)
    spread = jnp.mean(centre * centre, -1, keepdims=True)
    return centre * lax.rsqrt(spread + NORM_EPS) * gain_row + shift_row


def rotary_tables(places):
    half_steps = jnp.arange(ROT_DIMS // 2, dtype=jnp.float32)
    inverse = jnp.exp(half_steps * (-2.0 * math.log(10000.0) / ROT_DIMS))
    angles = places.astype(jnp.float32)[:, None] * (0.25 * inverse)[None, :]
    angles = jnp.concatenate([angles, angles], 1)
    return (jnp.cos(angles), jnp.sin(angles))


def rotate(tensor, cosine, sine_table):
    rotary_part = tensor[..., :ROT_DIMS]
    lower_half = rotary_part[..., : ROT_DIMS // 2]
    upper_half = rotary_part[..., ROT_DIMS // 2 :]
    turned = jnp.concatenate([-upper_half, lower_half], -1)
    return jnp.concatenate([rotary_part * cosine + turned * sine_table, tensor[..., ROT_DIMS:]], -1)


def adamw(master, clipped, first_old, second_old, step_rate, decay_rate):
    first_new = BETA_ONE * first_old + (1.0 - BETA_ONE) * clipped
    second_new = BETA_TWO * second_old + (1.0 - BETA_TWO) * clipped * clipped
    ascent = (
        first_new
        / (1.0 - BETA_ONE**STEP)
        / (jnp.sqrt(second_new / (1.0 - BETA_TWO**STEP)) + ADAM_EPS)
    )
    return (master - step_rate * (ascent + decay_rate * master), first_new, second_new)


def gelu_exact(tensor):
    return jax.nn.gelu(tensor, approximate=False)


def across_tokens(left_side, right_side):
    return lax.dot_general(
        left_side, right_side, (((0,), (0,)), ((), ())), preferred_element_type=jnp.float32
    )


def against(left_side, right_side):
    return lax.dot_general(
        left_side, right_side, (((1,), (1,)), ((), ())), preferred_element_type=jnp.float32
    )


def masked_scores(query_rows, row_places, key_block, key_places):
    scores = against(query_rows, key_block) * HD ** (-0.5)
    return jnp.where(key_places[None, :] <= row_places[:, None], scores, MASKED)


def body(
    inputs,
    cotangent,
    span_order,
    query_weight,
    keyval_weight,
    output_weight,
    up_weight,
    down_weight,
    vectors,
    kv_bias,
    first_query,
    first_keyval,
    first_output,
    first_up,
    first_down,
    first_vectors,
    first_kv_bias,
    second_query,
    second_keyval,
    second_output,
    second_up,
    second_down,
    second_vectors,
    second_kv_bias,
):
    tok_rows = inputs.shape[0]
    seq_count = lax.axis_size("seq")
    seq_rank = lax.axis_index("seq")
    order_row = span_order[0]
    token_steps = jnp.arange(tok_rows, dtype=jnp.int32)
    all_places = (order_row[:, None] * tok_rows + token_steps[None, :]).reshape(
        seq_count * tok_rows
    )
    own_span = jnp.sum(jnp.where(jnp.arange(seq_count, dtype=jnp.int32) == seq_rank, order_row, 0))
    own_places = own_span * tok_rows + token_steps
    query_rows_count = tok_rows * HQ
    query_full, keyval_full, output_full, up_full, down_full, vector_full = (
        lax.all_gather(query_weight.astype(jnp.bfloat16), ("fsdp", "seq"), axis=0, tiled=True),
        lax.all_gather(keyval_weight.astype(jnp.bfloat16), ("fsdp", "seq"), axis=0, tiled=True),
        lax.all_gather(output_weight.astype(jnp.bfloat16), ("fsdp", "seq"), axis=0, tiled=True),
        lax.all_gather(up_weight.astype(jnp.bfloat16), ("fsdp", "seq"), axis=0, tiled=True),
        lax.all_gather(down_weight.astype(jnp.bfloat16), ("fsdp", "seq"), axis=0, tiled=True),
        lax.all_gather(vectors.astype(jnp.bfloat16), ("fsdp", "seq"), axis=1, tiled=True),
    )
    kv_shift = lax.all_gather(kv_bias.astype(jnp.bfloat16), "seq", axis=0, tiled=True).astype(
        jnp.float32
    )
    gains = vector_full.astype(jnp.float32)
    states = inputs.astype(jnp.float32)
    normed_one = layer_norm(states, gains[0], gains[1])
    normed_low = normed_one.astype(jnp.bfloat16)
    query_pre = jnp.dot(normed_low, query_full, preferred_element_type=jnp.float32) + gains[4]
    keyval_pre = jnp.dot(normed_low, keyval_full, preferred_element_type=jnp.float32) + kv_shift
    cosine, sine_table = rotary_tables(own_places)

    def turn_queries(tensor):
        return rotate(tensor.reshape(tok_rows, HQ, HD), cosine[:, None, :], sine_table[:, None, :])

    def turn_keys(tensor):
        return jnp.concatenate([rotate(tensor[:, :HD], cosine, sine_table), tensor[:, HD:]], 1)

    query_rows = turn_queries(query_pre).astype(jnp.bfloat16).reshape(query_rows_count, HD)
    local_pairs = turn_keys(keyval_pre).astype(jnp.bfloat16)
    row_places = jnp.broadcast_to(own_places[:, None], (tok_rows, HQ)).reshape(query_rows_count)
    all_pairs = lax.all_gather(local_pairs, "seq", axis=0, tiled=True)
    block_count = all_pairs.shape[0] // KEY_BLOCK
    place_blocks = all_places.reshape(block_count, KEY_BLOCK)

    def lse_step(carry_pair, block_pair):
        running_top, running_total = carry_pair
        pair_block, key_places = block_pair
        scores = masked_scores(query_rows, row_places, pair_block[:, :HD], key_places)
        new_top = jnp.maximum(running_top, jnp.max(scores, 1, keepdims=True))
        running_total = running_total * jnp.exp(running_top - new_top) + jnp.sum(
            jnp.exp(scores - new_top), 1, keepdims=True
        )
        return ((new_top, running_total), None)

    start_carry = (
        jnp.full((query_rows_count, 1), MASKED, jnp.float32),
        jnp.zeros((query_rows_count, 1), jnp.float32),
    )
    (row_top, row_total), _ = lax.scan(
        lse_step, start_carry, (all_pairs.reshape(block_count, KEY_BLOCK, 2 * HD), place_blocks)
    )
    log_total = row_top + jnp.log(row_total)

    def mix_step(mixed_acc, block_pair):
        pair_block, key_places = block_pair
        probs_low = jnp.exp(
            masked_scores(query_rows, row_places, pair_block[:, :HD], key_places) - log_total
        ).astype(jnp.bfloat16)
        return (
            mixed_acc + jnp.dot(probs_low, pair_block[:, HD:], preferred_element_type=jnp.float32),
            None,
        )

    mixed, _ = lax.scan(
        mix_step,
        jnp.zeros((query_rows_count, HD), jnp.float32),
        (all_pairs.reshape(block_count, KEY_BLOCK, 2 * HD), place_blocks),
    )
    mixed_low = mixed.reshape(tok_rows, D).astype(jnp.bfloat16)
    attention_out = jnp.dot(mixed_low, output_full, preferred_element_type=jnp.float32) + gains[5]
    normed_two = layer_norm(states, gains[2], gains[3])
    normed_two_low = normed_two.astype(jnp.bfloat16)
    lifted = jnp.dot(normed_two_low, up_full, preferred_element_type=jnp.float32) + gains[
        7:
    ].reshape(FF)
    active_low = gelu_exact(lifted).astype(jnp.bfloat16)
    block_output = (
        states
        + attention_out
        + jnp.dot(active_low, down_full, preferred_element_type=jnp.float32)
        + gains[6]
    ).astype(jnp.bfloat16)
    back_rows = cotangent.astype(jnp.float32)
    query_back, keyval_back, output_back, up_back, down_back = (
        lax.all_gather(query_weight.astype(jnp.bfloat16), ("fsdp", "seq"), axis=0, tiled=True),
        lax.all_gather(keyval_weight.astype(jnp.bfloat16), ("fsdp", "seq"), axis=0, tiled=True),
        lax.all_gather(output_weight.astype(jnp.bfloat16), ("fsdp", "seq"), axis=0, tiled=True),
        lax.all_gather(up_weight.astype(jnp.bfloat16), ("fsdp", "seq"), axis=0, tiled=True),
        lax.all_gather(down_weight.astype(jnp.bfloat16), ("fsdp", "seq"), axis=0, tiled=True),
    )
    grad_down = across_tokens(active_low, cotangent)
    grad_output = across_tokens(mixed_low, cotangent)
    out_bias_grad = jnp.sum(back_rows, 0)
    active_grad = against(cotangent, down_back)
    _, gelu_pull = jax.vjp(gelu_exact, lifted)
    (lifted_grad,) = gelu_pull(active_grad)
    lifted_low = lifted_grad.astype(jnp.bfloat16)
    grad_up = across_tokens(normed_two_low, lifted_low)
    normed_two_grad = against(lifted_low, up_back)
    mixed_grad = against(cotangent, output_back).astype(jnp.bfloat16).reshape(query_rows_count, HD)
    row_delta = jnp.sum(mixed_grad.astype(jnp.float32) * mixed, 1, keepdims=True)
    pairs_back = lax.all_gather(local_pairs, "seq", axis=0, tiled=True)

    def grad_step(query_acc, block_pair):
        pair_block, key_places = block_pair
        key_block = pair_block[:, :HD]
        probs = jnp.exp(masked_scores(query_rows, row_places, key_block, key_places) - log_total)
        prob_grad = against(mixed_grad, pair_block[:, HD:])
        score_low = (probs * (prob_grad - row_delta)).astype(jnp.bfloat16)
        query_acc = query_acc + jnp.dot(score_low, key_block, preferred_element_type=jnp.float32)
        key_grad = across_tokens(score_low, query_rows) * HD ** (-0.5)
        value_grad = across_tokens(probs.astype(jnp.bfloat16), mixed_grad)
        return (query_acc, jnp.concatenate([key_grad, value_grad], 1))

    query_sum, pair_grads = lax.scan(
        grad_step,
        jnp.zeros((query_rows_count, HD), jnp.float32),
        (pairs_back.reshape(block_count, KEY_BLOCK, 2 * HD), place_blocks),
    )
    query_rot_grad = (query_sum * HD ** (-0.5)).reshape(tok_rows, HQ, HD)
    own_pair_grad = lax.psum_scatter(
        pair_grads.reshape(block_count * KEY_BLOCK, 2 * HD).astype(jnp.bfloat16),
        "seq",
        scatter_dimension=0,
        tiled=True,
    ).astype(jnp.float32)
    _, key_pull = jax.vjp(turn_keys, keyval_pre)
    (keyval_grad,) = key_pull(own_pair_grad)
    keyval_low = keyval_grad.astype(jnp.bfloat16)
    _, query_pull = jax.vjp(turn_queries, query_pre)
    (query_pre_grad,) = query_pull(query_rot_grad)
    query_low = query_pre_grad.astype(jnp.bfloat16)
    grad_query = across_tokens(normed_low, query_low)
    grad_keyval = across_tokens(normed_low, keyval_low)
    kv_bias_part = jnp.sum(keyval_low.astype(jnp.float32), 0)
    normed_one_grad = against(query_low, query_back) + against(keyval_low, keyval_back)
    _, first_pull = jax.vjp(layer_norm, states, gains[0], gains[1])
    input_one, gain_one_grad, shift_one_grad = first_pull(normed_one_grad)
    _, second_pull = jax.vjp(layer_norm, states, gains[2], gains[3])
    input_two, gain_two_grad, shift_two_grad = second_pull(normed_two_grad)
    input_grad = back_rows + input_one + input_two
    vector_grad = jnp.concatenate(
        [
            jnp.stack(
                [
                    gain_one_grad,
                    shift_one_grad,
                    gain_two_grad,
                    shift_two_grad,
                    jnp.sum(query_low.astype(jnp.float32), 0),
                    out_bias_grad,
                    out_bias_grad,
                ]
            ),
            jnp.sum(lifted_low.astype(jnp.float32), 0).reshape(FF // D, D),
        ],
        0,
    )
    reduced = (
        lax.psum_scatter(grad_query, ("fsdp", "seq"), scatter_dimension=0, tiled=True),
        lax.psum_scatter(grad_keyval, ("fsdp", "seq"), scatter_dimension=0, tiled=True),
        lax.psum_scatter(grad_output, ("fsdp", "seq"), scatter_dimension=0, tiled=True),
        lax.psum_scatter(grad_up, ("fsdp", "seq"), scatter_dimension=0, tiled=True),
        lax.psum_scatter(grad_down, ("fsdp", "seq"), scatter_dimension=0, tiled=True),
        lax.psum_scatter(vector_grad, ("fsdp", "seq"), scatter_dimension=1, tiled=True),
    )
    reduced = tuple(reduced)
    local_squares = sum((jnp.sum(gradient * gradient) for gradient in reduced))
    global_squares, kv_bias_total = lax.psum((local_squares, kv_bias_part), ("fsdp", "seq"))
    grad_norm = jnp.sqrt(global_squares + jnp.sum(kv_bias_total * kv_bias_total))
    piece_width = kv_bias.shape[0]
    kv_bias_grad = lax.dynamic_slice_in_dim(kv_bias_total, seq_rank * piece_width, piece_width)
    factor = jnp.minimum(1.0, CLIP_NORM / (grad_norm + 1e-06))
    masters = (query_weight, keyval_weight, output_weight, up_weight, down_weight, vectors, kv_bias)
    all_grads = reduced + (kv_bias_grad,)
    firsts = (
        first_query,
        first_keyval,
        first_output,
        first_up,
        first_down,
        first_vectors,
        first_kv_bias,
    )
    seconds = (
        second_query,
        second_keyval,
        second_output,
        second_up,
        second_down,
        second_vectors,
        second_kv_bias,
    )
    step_rates = (MATRIX_RATE,) * 5 + (VECTOR_RATE, VECTOR_RATE)
    decays = (MATRIX_DECAY,) * 5 + (0.0, 0.0)
    updated = [
        adamw(master, gradient * factor, first_old, second_old, step_rate, decay_rate)
        for master, gradient, first_old, second_old, step_rate, decay_rate in zip(
            masters, all_grads, firsts, seconds, step_rates, decays
        )
    ]
    residual_bias_grads = (reduced[5] * factor)[5:7]
    return (
        block_output,
        input_grad,
        grad_norm,
        updated[0][0],
        updated[1][0],
        updated[2][0],
        updated[3][0],
        updated[4][0],
        updated[5][0],
        updated[6][0],
        updated[0][1],
        updated[1][1],
        updated[2][1],
        updated[3][1],
        updated[4][1],
        updated[5][1],
        updated[6][1],
        updated[0][2],
        updated[1][2],
        updated[2][2],
        updated[3][2],
        updated[4][2],
        updated[5][2],
        updated[6][2],
        residual_bias_grads,
    )


def dot_nn(left, right):
    return lax.dot_general(left, right, (((1,), (0,)), ((), ())), preferred_element_type=F32)


def dot_nt(left, right):
    return lax.dot_general(left, right, (((1,), (1,)), ((), ())), preferred_element_type=F32)


def dot_tn(left, right):
    return lax.dot_general(left, right, (((0,), (0,)), ((), ())), preferred_element_type=F32)


def normalise(rows):
    centre = rows - jnp.mean(rows, -1, keepdims=True)
    scale = lax.rsqrt(jnp.mean(centre * centre, -1, keepdims=True) + NORM_EPS)
    return centre * scale, scale


def norm_back(grad, hat, scale, gain):
    inner = grad * gain
    return scale * (
        inner
        - jnp.mean(inner, -1, keepdims=True)
        - hat * jnp.mean(inner * hat, -1, keepdims=True)
    )


def where(condition, action):
    if condition is None:
        action()
    else:
        pl.when(condition)(lambda: action())


class Copy:
    def __init__(self, copy, send_if, recv_if):
        self.copy, self.send_if, self.recv_if = copy, send_if, recv_if
        self.started = self.received = self.sent = False

    def start(self):
        self.started = True
        where(self.send_if, self.copy.start)

    def wait_recv(self):
        self.received = True
        where(self.recv_if, self.copy.wait_recv)

    def wait_send(self):
        self.sent = True
        where(self.send_if, self.copy.wait_send)


class Group:
    def __init__(self, whole, sem):
        self.whole, self.sem, self.members, self.waited = whole, sem, [], False

    def wait_recv(self):
        self.waited = True
        for copy in self.members:
            copy.received = True
        pltpu.make_async_copy(self.whole, self.whole, self.sem).wait()

    def wait_send(self):
        self.waited = True
        pltpu.make_async_copy(self.whole, self.whole, self.sem).wait()


class Copies:
    def __init__(self, send_sems, recv_sems):
        self.send_sems, self.recv_sems, self.all, self.groups = send_sems, recv_sems, [], []
        self.sends = self.recvs = 0

    def next_send(self):
        self.sends += 1
        return self.send_sems.at[self.sends - 1]

    def next_recv(self):
        self.recvs += 1
        return self.recv_sems.at[self.recvs - 1]

    def leaving(self, whole):
        self.groups.append(Group(whole, self.next_send()))
        return self.groups[-1]

    def arriving(self, whole):
        return Group(whole, self.next_recv())

    def make(self, source, target, device, send_if=None, recv_if=None, out=None, into=None):
        copy = Copy(pltpu.make_async_remote_copy(
            src_ref=source,
            dst_ref=target,
            send_sem=out.sem if out else self.next_send(),
            recv_sem=into.sem if into else self.next_recv(),
            device_id=device,
            device_id_type=pl.DeviceIdType.MESH,
        ), send_if, recv_if)
        copy.sent = out is not None
        for group in (out, into):
            if group:
                group.members.append(copy)
        self.all.append(copy)
        return copy

    def settle(self):
        for copy in self.all:
            if copy.started and not copy.sent:
                copy.wait_send()
        for group in self.groups:
            if not group.waited and all(copy.started for copy in group.members):
                group.wait_send()


def slab_rows(block, index):
    return pl.ds(pl.multiple_of((block * 8 + index) * 24, 8), 24)


class Panels:
    def __init__(self, ref, height, first, count):
        self.ref, self.height, self.first, self.count = ref, height, first, count

    def rows(self, panel, block, index):
        return pl.ds(pl.multiple_of((self.first + panel) * self.height + (block * 8 + index) * 24, 8), 24)

    def get(self, block, index):
        parts = [self.ref[self.rows(p, block, index), :] for p in range(self.count)]
        return parts[0] if self.count == 1 else jnp.concatenate(parts, 1)

    def put(self, block, index, value):
        for p in range(self.count):
            self.ref[self.rows(p, block, index), :] = value[:, p * 256 : p * 256 + 256]


N_SEMS = (53, 92)


def layer_kernel(
    span, x_in, cot_in, qw_in, kw_in, ow_in, uw_in, dw_in, vec_in, kvb_in,
    to_bo, to_ig, to_q, to_o, to_kv, to_vec, to_up, to_dn, to_small,
    x, cot, qw, kw, ow, uw, dw, vec, kvb,
    bo, ig, g_q, g_o, g_kv, g_vec, g_up, g_dn, g_small,
    KW, Q, O, U, Dn, X, C, KV, ub, WQ, WKV, WO, WU, gains, vsq,
    n1, hat1, scale1, N2, act, dl, OP, NP,
    qz, doz, doT, kvT, bias, sbuf, mixT, dqT, dkv,
    GP, GV, GU, GD, vg,
    SK1, RK1, SK2, RK2,
    RO1, SO2, RO2, RN1, SN2, RN2,
    SQ1, RQ1, SQ2, RQ2, SQ3, RQ3, SQ4, RQ4,
    SO1, QO1, SO2b, RO2b, SO3, RO3, SO4, RO4,
    SP1, RP1, SP2, RP2, SP3, RP3,
    SV1, RV1, SV2, RV2, SV3, RV3,
    SU1, RU1, SU2, RU2, SU3, RU3, RXU,
    SD1, RD1, SD2, RD2, RXD,
    NS1,
    send_sems, recv_sems, save_sems, load_sems,
):
    tok = x.shape[0]
    f = lax.axis_index("fsdp")
    s = lax.axis_index("seq")
    z = lax.div(s, 2)
    y = lax.rem(s, 2)
    yo = 1 - y
    fc = f + 1 - 2 * lax.rem(f, 2)
    fx = lax.rem(f + 2, 4)
    fd = 3 - f
    zk = (z, z + 1 - 2 * lax.rem(z, 2), lax.rem(z + 2, 4), 3 - z)
    dev_c, dev_x, dev_d = (fc, s), (fx, s), (fd, s)
    dev_y = (f, z * 2 + yo)
    dev_z = tuple((f, zz * 2 + y) for zz in zk)
    dev_zy = tuple((f, zz * 2 + yo) for zz in zk)
    fsdp_devs = (dev_c, dev_x, dev_d)
    seq_devs = dev_z[1:] + dev_zy
    far = (3, 2, 1)

    copies = Copies(send_sems, recv_sems)
    make = copies.make

    def start(*wanted):
        for copy in wanted:
            copy.start()

    def arrive(*wanted):
        for copy in wanted:
            copy.wait_recv()

    saved = []

    def save(source, target):
        copy = pltpu.make_async_copy(source, target, save_sems.at[len(saved)])
        copy.start()
        saved.append(copy)

    leaving, arriving = copies.leaving, copies.arriving
    three, four = pl.ds(0, 3), pl.ds(0, 4)

    def seq_gather(ref, some, together=True):
        to_z, to_y = [None], []
        out = leaving(some(three))
        for k in (1, 2, 3):
            to_z.append(make(ref(z, y), ref(z, y), dev_z[k], out=out))
        out, into = leaving(some(four)), arriving(some(four)) if together else None
        for k in range(4):
            to_y.append(make(ref(zk[k], y), ref(zk[k], y), dev_y, out=out, into=into))
        return to_z, to_y, into

    w_z, w_y, w_yin = seq_gather(lambda i, j: KW.at[f, i, j], lambda n: KW.at[0, n, 0])
    q_z, q_y, _ = seq_gather(lambda i, j: Q.at[f, i, j], lambda n: Q.at[0, n, 0], False)
    o_z, o_y, o_yin = seq_gather(lambda i, j: O.at[f, i, j], lambda n: O.at[0, n, 0])
    p_z, p_y, p_yin = seq_gather(lambda i, j: O.at[fx, i, j], lambda n: O.at[0, n, 0])
    u_z, u_y, u_yin = seq_gather(lambda i, j: U.at[i, j], lambda n: U.at[n, 0])
    d_z, d_y, d_yin = seq_gather(lambda i, j: Dn.at[i, j], lambda n: Dn.at[n, 0])
    k_z, k_y, k_yin = seq_gather(lambda i, j: KV.at[i, j], lambda n: KV.at[n, 0])

    def fsdp_gather(ref, some):
        out, into = leaving(some(three)), arriving(some(pl.ds(0, 2)))
        to_x = [make(ref(f, j), ref(f, j), dev_x, out=out) for j in (y, yo)]
        to_c = [make(ref(f, j), ref(f, j), dev_c, out=out, into=into) for j in (y, yo)]
        on_c = [make(ref(fx, j), ref(fx, j), dev_c, out=out, into=into) for j in (y, yo)]
        return to_x, to_c, on_c, into

    w_x, w_c, w_xc, w_in = fsdp_gather(lambda i, j: KW.at[i, :, j], lambda n: KW.at[n])
    q_out, q_in = leaving(Q.at[three]), arriving(Q.at[pl.ds(0, 2)])

    def q_copy(g, j, device, into):
        return make(Q.at[g, :, j], Q.at[g, :, j], device, out=q_out, into=into)

    q_x0 = q_copy(f, y, dev_x, None)
    q_c = [q_copy(f, j, dev_c, q_in) for j in (y, yo)]
    q_xc = [q_copy(fx, j, dev_c, q_in) for j in (y, yo)]
    q_xs = [make(Q.at[f, zz, yo], Q.at[f, zz, yo], dev_x, out=q_out) for zz in zk]
    o_x = make(O.at[f, z, y], O.at[f, z, y], dev_x)
    o_out, o_in = leaving(O.at[pl.ds(0, 2)]), arriving(O.at[pl.ds(0, 2)])

    def o_copy(g, j):
        return make(O.at[g, :, j], O.at[g, :, j], dev_c, out=o_out, into=o_in)

    o_c = [o_copy(f, j) for j in (y, yo)]
    op_c = [o_copy(fx, j) for j in (y, yo)]

    def token_gather(ref):
        out = leaving(ref.at[three])
        return (
            make(ref.at[f], ref.at[f], dev_x, out=out),
            make(ref.at[f], ref.at[f], dev_c, out=out),
            make(ref.at[fx], ref.at[fx], dev_c, out=out),
        )

    x_x, x_c, x_xc = token_gather(X)
    c_x, c_c, c_xc = token_gather(C)
    uf_out, uf_in = leaving(ub.at[three]), arriving(U.at[0, 0, three])
    u_f = [
        make(ub.at[g], U.at[z, y, f], dev, out=uf_out, into=uf_in)
        for g, dev in zip((fc, fx, fd), fsdp_devs)
    ]

    out = leaving(SK1)
    rk1 = [make(SK1.at[zz], RK1.at[zz], dev_y, out=out) for zz in zk]

    def to_z_peers(S, R):
        out, into = leaving(S), arriving(R)
        return [make(S.at[k], R.at[k], dev_z[k + 1], out=out, into=into) for k in range(3)], into

    rk2, rk2_in = to_z_peers(SK2, RK2)

    def to_core(ref, R):
        out, into = leaving(ref.at[pl.ds(0, 2)]), arriving(R)
        found = [
            make(ref.at[g], R.at[i], dev_c, out=out, into=into) for i, g in enumerate((fc, fd))
        ]
        return found, into

    out_c, out_in = to_core(OP, RO1)
    out_x = make(SO2, RO2, dev_x)
    nrm_c, nrm_in = to_core(NP, RN1)
    nrm_x = make(SN2, RN2, dev_x)

    def full_scatter(S1, R1, S2, R2, S3, R3, S4, R4):
        c_copy = make(S1, R1, dev_c)
        out = leaving(S2)
        x_copies = [make(S2.at[i], R2.at[i], dev_x, out=out) for i in range(2)]
        y_copy = make(S3, R3, dev_y)
        return (c_copy, x_copies, y_copy, *to_z_peers(S4, R4))

    q_sc = full_scatter(SQ1, RQ1, SQ2, RQ2, SQ3, RQ3, SQ4, RQ4)
    o_sc = full_scatter(SO1, QO1, SO2b, RO2b, SO3, RO3, SO4, RO4)
    p_c = make(SP1, RP1, dev_c)
    p_x = make(SP2, RP2, dev_x)
    out, p_in = leaving(SP3), arriving(RP3)
    p_s = [
        make(SP3.at[i], RP3.at[i], dev, out=out, into=p_in) for i, dev in enumerate(seq_devs)
    ]
    v_c = make(SV1, RV1, dev_c)
    v_x = make(SV2, RV2, dev_x)
    out, v_in = leaving(RV3), arriving(RV3)
    v_s = [make(SV3, RV3.at[i], dev, out=out, into=v_in) for i, dev in enumerate(seq_devs)]
    out = leaving(SU1)
    su_y = [make(SU1.at[zz], RU1.at[zz], dev_y, out=out) for zz in zk]
    inner = lax.div(z + 1, 2) == 1
    outer = lax.div(z + 1, 2) != 1

    def relayed(S2, R2, RX):
        to_z = [make(S2.at[k], R2.at[k], dev_z[k + 1]) for k in range(2)]
        to_z.append(make(S2.at[2], R2.at[2], dev_z[3], inner, inner))
        return to_z, make(S2.at[2], RX, dev_z[1], outer, inner)

    su_z, su_r = relayed(SU2, RU2, RXU)
    out, su_fin = leaving(SU3.at[three]), arriving(RU3)
    su_f = [
        make(SU3.at[g], RU3.at[i], dev, out=out, into=su_fin)
        for i, (g, dev) in enumerate(zip((fc, fx, fd), fsdp_devs))
    ]
    out = leaving(SD1)
    sd_y = [make(SD1.at[zz], RD1.at[zz], dev_y, out=out) for zz in zk]
    sd_z, sd_r = relayed(SD2, RD2, RXD)
    me = f * 8 + s
    everyone = [
        (g, zk[k] * 2 + yy) for k in (3, 2, 1, 0) for yy in (yo, y) for g in (fd, fx, fc, f)
    ][:-1]
    most = pl.ds(0, 31)
    out, n_in = leaving(NS1.at[most]), arriving(NS1.at[most])
    n_all = [make(NS1.at[me], NS1.at[me], dev, out=out, into=n_in) for dev in everyone]

    barrier = pltpu.get_barrier_semaphore()
    for dev in everyone:
        pl.semaphore_signal(barrier, inc=1, device_id=dev, device_id_type=pl.DeviceIdType.MESH)

    loads = []
    pairs = (
        (vec_in, vec), (kvb_in, kvb), (kw_in, kw), (qw_in, qw), (ow_in, ow),
        (x_in, x), (cot_in, cot), (uw_in, uw), (dw_in, dw),
    )
    for i, (source, target) in enumerate(pairs):
        copy = pltpu.make_async_copy(source, target, load_sems.at[i])
        copy.start()
        loads.append(copy)
    for copy in loads:
        copy.wait()

    vsq[...] = jnp.zeros((128, 128), F32)
    vsq[0:11, 0:24] = vec[...]
    vsq[11:12, 0:16] = kvb[...]
    KW[f, z, y, :, :128] = kw[...].astype(BF16)
    KW[f, z, y, :, 128:] = vsq[...].T[:24, :].astype(BF16)
    Q[f, z, y] = qw[...].astype(BF16)
    O[f, z, y] = ow[...].astype(BF16)
    for j in range(4):
        ub[j] = uw[:, j * D : (j + 1) * D].astype(BF16)
    U[z, y, f] = ub[f]
    Dn[z, y] = dw[...].astype(BF16)
    X[f] = x[...]
    C[f] = cot[...]

    @pl.when(outer)
    def _():
        RU2[2] = jnp.zeros((4, 24, D), BF16)
        RD2[2] = jnp.zeros((96, D), BF16)

    pl.semaphore_wait(barrier, 31)
    start(w_z[3], w_z[2], w_z[1], w_y[0])
    start(o_x, q_z[3], q_z[2], q_z[1], q_y[0])
    start(o_z[3], o_z[2], o_z[1], o_y[0])

    hat, scale = normalise(x[...].astype(F32))
    hat1[...] = hat
    scale1[...] = jnp.broadcast_to(scale, (tok, 128))
    own_span = span[0, s]
    lane = lax.broadcasted_iota(jnp.int32, (tok, 128), 1)
    spot = lax.broadcasted_iota(jnp.int32, (tok, 128), 0) + own_span * tok
    in_head = lax.rem(lane, 64)
    step = lax.rem(in_head, ROT_DIMS // 2).astype(F32)
    inverse = jnp.exp(step * (-2.0 * math.log(10000.0) / ROT_DIMS))
    angle = spot.astype(F32) * (0.25 * inverse)
    sine = jnp.sin(angle)
    cosine = jnp.where(in_head < ROT_DIMS, jnp.cos(angle), 1.0)
    sine_low = jnp.where(in_head < ROT_DIMS // 2, sine, 0.0)
    sine_high = jnp.where((in_head >= ROT_DIMS // 2) & (in_head < ROT_DIMS), sine, 0.0)
    key_lane = lane < 64
    key_cos = jnp.where(key_lane, cosine, 1.0)
    key_low = jnp.where(key_lane, sine_low, 0.0)
    key_high = jnp.where(key_lane, sine_high, 0.0)

    def turn(block, cos_t, low_t, high_t):
        up = pltpu.roll(block, 120, 1)
        down = pltpu.roll(block, 8, 1)
        return block * cos_t - up * low_t + down * high_t

    def turn_back(block, cos_t, low_t, high_t):
        up = pltpu.roll(block, 120, 1)
        down = pltpu.roll(block, 8, 1)
        return block * cos_t + up * low_t - down * high_t

    def forward(to_z, to_y, *which):
        for k in which:
            arrive(to_z[k])
            start(to_y[k])

    forward(w_z, w_y, *far)
    start(w_x[0], w_c[0])
    arrive(o_x)
    start(p_z[3], p_z[2], p_z[1], p_y[0])
    arrive(w_yin)
    start(w_x[1], w_c[1])
    forward(q_z, q_y, *far)
    start(q_x0, q_c[0])
    arrive(w_x[0])
    start(w_xc[0])
    arrive(w_x[1])
    start(w_xc[1])
    arrive(w_in)
    slabs = [KW[g, i, j].astype(F32) for g in range(4) for i in range(4) for j in range(2)]
    for i in range(16):
        pair = jnp.concatenate([slabs[2 * i][:, :128], slabs[2 * i + 1][:, :128]], 0)
        WKV[i * 48 : (i + 1) * 48, :] = pair.astype(BF16)
    gains[...] = jnp.concatenate([slab[:, 128:] for slab in slabs], 0).T
    vsq[...] = jnp.concatenate([slab[:16, 128:] for slab in slabs[:8]], 0).T
    kv_shift = vsq[11:12, :]
    n1[...] = (hat * gains[0:1, :] + gains[1:2, :]).astype(BF16)
    kv_pre = dot_nn(n1[...], WKV[...]) + kv_shift
    KV[z, y] = turn(kv_pre, key_cos, key_low, key_high).astype(BF16)
    start(k_z[3], k_z[2], k_z[1], k_y[0])
    for k in range(4):
        arrive(q_y[k])
        start(q_xs[k])
    start(q_c[1])
    forward(o_z, o_y, *far)
    start(o_c[0])
    forward(p_z, p_y, *far)
    start(op_c[0])
    arrive(q_x0)
    start(q_xc[0])
    vg[...] = jnp.zeros((128, D), F32)
    csum = jnp.sum(cot[...].astype(F32), 0, keepdims=True)
    vg[5:6, :] = csum
    vg[6:7, :] = csum
    key_iota = lax.broadcasted_iota(jnp.int32, (tok, tok), 0)
    row_iota = lax.broadcasted_iota(jnp.int32, (tok, tok), 1) + own_span * tok
    for i in range(8):
        bias[i * tok : (i + 1) * tok, :] = jnp.where(
            key_iota + span[0, i] * tok <= row_iota, 0.0, MASKED
        ).astype(F32)
    dkv[...] = jnp.zeros((8 * tok, 128), F32)
    start(*u_f)
    forward(k_z, k_y, *far)
    arrive(*q_xs)
    start(q_xc[1])
    arrive(o_yin)
    start(o_c[1])
    arrive(p_yin)
    start(op_c[1])
    arrive(uf_in)
    start(u_z[3], u_z[2], u_z[1], u_y[0])
    start(x_x, c_x, x_c, c_c)
    arrive(q_in)

    def join(ref, whole):
        def put(i, carry):
            g = lax.div(i, 4)
            zz = lax.rem(i, 4)
            pair = jnp.concatenate([ref[g, zz, 0].astype(F32), ref[g, zz, 1].astype(F32)], 0)
            whole[pl.ds(pl.multiple_of(i * 48, 16), 48), :] = pair.astype(BF16)
            return carry

        lax.fori_loop(0, 16, put, 0)

    join(Q, WQ)
    q_pre = dot_nn(n1[...], WQ[...]) + gains[4:5, :]
    gap = jnp.zeros((tok, 64), BF16)
    for j in range(6):
        cols = slice(j * 128, j * 128 + 128)
        turned = turn(q_pre[:, cols], cosine, sine_low, sine_high).astype(BF16).astype(F32)
        turned = (turned * HD ** (-0.5)).astype(BF16)
        qz[2 * j] = jnp.concatenate([turned[:, :64], gap], 1)
        qz[2 * j + 1] = jnp.concatenate([turned[:, 64:], gap], 1)
    arrive(o_in)
    join(O, WO)
    mixed_back = dot_nt(cot[...], WO[...]).astype(BF16)
    for j in range(6):
        pair = mixed_back[:, j * 128 : j * 128 + 128]
        doz[2 * j] = jnp.concatenate([gap, pair[:, :64]], 1)
        doz[2 * j + 1] = jnp.concatenate([gap, pair[:, 64:]], 1)
    doT[...] = mixed_back.astype(F32).T.astype(BF16).reshape(HQ, HD, tok)
    arrive(k_yin)
    KVF = KV.reshape(8 * tok, 128)
    kvT[...] = KVF[...].astype(F32).T.astype(BF16)

    span_rows = 2 * tok
    chunks = 8 * tok // span_rows

    def fold(values, reduce):
        return reduce(values.reshape(span_rows // 8, 8, tok), axis=0)

    def attend(step_index):
        heads = [step_index * 2, step_index * 2 + 1]
        top, total, share, delta, acc = {}, {}, {}, {}, {}

        def rows_of(i):
            return pl.ds(i * span_rows, span_rows)

        def held_of(j, i):
            return pl.ds((j * chunks + i) * span_rows, span_rows)

        def score(j, i):
            scores = dot_nt(KVF[rows_of(i), :], qz[heads[j]]) + bias[rows_of(i), :]
            sbuf[held_of(j, i), :] = scores
            here = fold(scores, jnp.max)
            top[j] = here if i == 0 else jnp.maximum(top[j], here)
            if i == chunks - 1:
                top[j] = jnp.max(top[j], axis=0, keepdims=True)

        def weigh(j, i):
            weights = jnp.exp(sbuf[held_of(j, i), :] - top[j])
            sbuf[held_of(j, i), :] = weights
            here = fold(weights, jnp.sum)
            total[j] = here if i == 0 else total[j] + here
            if i == chunks - 1:
                share[j] = 1.0 / jnp.sum(total[j], axis=0, keepdims=True)

        def mix(j, i):
            rows = rows_of(i)
            probs = sbuf[held_of(j, i), :] * share[j]
            probs_low = probs.astype(BF16)
            sbuf[held_of(j, i), :] = probs
            here = dot_nn(kvT[:, rows], probs_low)
            acc[j] = here if i == 0 else acc[j] + here
            dkv[rows, :] += dot_nn(probs_low, doz[heads[j]])
            if i == chunks - 1:
                mixed = acc[j][64:, :]
                mixT[heads[j]] = mixed.astype(BF16)
                delta[j] = jnp.sum(mixed * doT[heads[j]].astype(F32), axis=0, keepdims=True)

        def back(j, i):
            rows = rows_of(i)
            prob_grad = dot_nt(KVF[rows, :], doz[heads[j]])
            score_low = (sbuf[held_of(j, i), :] * (prob_grad - delta[j])).astype(BF16)
            here = dot_nn(kvT[:, rows], score_low)
            acc[j] = here if i == 0 else acc[j] + here
            dkv[rows, :] += dot_nn(score_low, qz[heads[j]])
            if i == chunks - 1:
                dqT[heads[j]] = acc[j][:64, :] * HD ** (-0.5)

        for stage in (
            ((score, 0),),
            ((weigh, 0), (score, 1)),
            ((mix, 0), (weigh, 1)),
            ((back, 0), (mix, 1)),
            ((back, 1),),
        ):
            for i in range(chunks):
                for part, j in stage:
                    part(j, i)

    def attend_all(first, last, meanwhile):
        def body_step(step_index, carry):
            for at, action in meanwhile:
                pl.when(step_index == at)(action)
            attend(step_index)
            return carry

        lax.fori_loop(first, last, body_step, 0)


    def pump_two():
        forward(u_z, u_y, 1)

    def pump_three():
        forward(u_z, u_y, 3, 2)

    def pump_four():
        forward(d_z, d_y, 1)
        arrive(x_x, c_x)
        start(x_xc, c_xc)

    def pump_five():
        forward(d_z, d_y, 3)

    attend_all(
        0, HQ // 2,
        (
            (1, lambda: start(d_z[3], d_z[2], d_z[1], d_y[0])),
            (2, pump_two), (3, pump_three), (4, pump_four), (5, pump_five),
        ),
    )

    for k in (3, 2, 1, 0):
        rows = pl.ds(pl.multiple_of((2 * zk[k] + yo) * tok, 8), tok)
        SK1[zk[k]] = dkv[rows, :].astype(BF16)
        start(rk1[k])
    mix_low = mixT.reshape(D, tok)[...]
    for c in range(3):
        sbuf[(3 + c) * D : (4 + c) * D, :] = dot_nn(mix_low, cot[:, c * 256 : c * 256 + 256])
    GQ = Panels(sbuf, D, 0, 3)
    GO = Panels(sbuf, D, 3, 3)

    def scatter_c(G, S1, copy):
        def put(i, carry):
            for j, g in enumerate((fc, fd)):
                S1[j, i] = G.get(g, i).astype(S1.dtype)
            return carry

        lax.fori_loop(0, 8, put, 0)
        start(copy)

    def scatter_x(G, R1, S2, copies_):
        arrive(copies_[0])
        for j, yy in enumerate((yo, y)):
            for i in range(4):
                slab = 2 * i + yy
                S2[j, i] = (G.get(fx, slab) + R1[1, slab].astype(F32)).astype(S2.dtype)
                G.put(f, slab, G.get(f, slab) + R1[0, slab].astype(F32))
            start(copies_[1][j])

    def scatter_y(G, R2, S3, copies_):
        arrive(copies_[1][0])
        for i in range(4):
            S3[i] = (G.get(f, 2 * i + yo) + R2[0, i].astype(F32)).astype(S3.dtype)
        start(copies_[2])

    def scatter_z(G, R2, R3, S4, copies_):
        arrive(copies_[1][1], copies_[2])
        for k in far:
            total = G.get(f, 2 * zk[k] + y) + R2[1, zk[k]].astype(F32) + R3[zk[k]].astype(F32)
            S4[k - 1] = total.astype(S4.dtype)
            start(copies_[3][k - 1])

    def scatter_end(G, R2, R3, R4, copies_):
        total = G.get(f, 2 * z + y) + R2[1, z].astype(F32) + R3[z].astype(F32)
        arrive(copies_[4])
        for k in range(3):
            total = total + R4[k].astype(F32)
        return total

    scatter_c(GO, SO1, o_sc[0])
    q_back = dqT.reshape(D, tok)[...].T
    parts = []
    for j in range(6):
        parts.append(
            turn_back(q_back[:, j * 128 : j * 128 + 128], cosine, sine_low, sine_high).astype(BF16)
        )
    q_low = jnp.concatenate(parts, 1)
    vg[4:5, :] = jnp.sum(q_low.astype(F32), 0, keepdims=True)
    for c in range(3):
        sbuf[c * D : (c + 1) * D, :] = dot_tn(n1[...], q_low[:, c * 256 : c * 256 + 256])
    scatter_c(GQ, SQ1, q_sc[0])
    forward(d_z, d_y, 2)
    arrive(u_yin, x_c, x_xc)

    def pair_step(k):
        arrive(rk1[k])
        rows = pl.ds(pl.multiple_of((2 * zk[k] + y) * tok, 8), tok)
        SK2[k - 1] = (dkv[rows, :] + RK1[zk[k]].astype(F32)).astype(BF16)
        start(rk2[k - 1])

    def lift_one():
        pair_step(3)

    def lift_two():
        pair_step(2)
        scatter_x(GO, QO1, SO2b, o_sc)

    def lift_three():
        pair_step(1)
        scatter_x(GQ, RQ1, SQ2, q_sc)

    def tokens_to_x():
        arrive(out_in, nrm_in)
        SO2[...] = (OP[fx].astype(F32) + RO1[1].astype(F32)).astype(BF16)
        start(out_x)
        SN2[...] = (NP[fx].astype(F32) + RN1[1].astype(F32)).astype(BF16)
        start(nrm_x)

    def down_rows(k):
        return pl.ds(pl.multiple_of((zk[k] * 2 + y) * 96, 8), 96)

    def down_step(k):
        arrive(sd_y[k])
        total = GD[down_rows(k), :] + RD1[zk[k]].astype(F32)
        if k in (0, 2):
            GD[down_rows(k), :] = total
        if k:
            SD2[k - 1] = total.astype(BF16)
        if k == 2:
            pl.when(outer)(lambda: start(sd_z[1]))
        elif k:
            start(sd_z[k - 1])
        if k == 3:
            start(sd_r)

    def down_relay():
        arrive(sd_r)

        @pl.when(inner)
        def _():
            SD2[1] = (GD[down_rows(2), :] + RXD[...].astype(F32)).astype(BF16)
            start(sd_z[1])

    def up_step(k):
        arrive(su_y[k])
        for g in range(4):
            rows = slab_rows(g, zk[k] * 2 + y)
            total = GU[rows, :] + RU1[zk[k], g].astype(F32)
            if k in (0, 2):
                GU[rows, :] = total
            if k:
                SU2[k - 1, g] = total.astype(BF16)
        if k == 2:
            pl.when(outer)(lambda: start(su_z[1]))
        elif k:
            start(su_z[k - 1])
        if k == 3:
            start(su_r)

    def up_relay():
        arrive(su_r)

        @pl.when(inner)
        def _():
            for g in range(4):
                total = GU[slab_rows(g, zk[2] * 2 + y), :] + RXU[g].astype(F32)
                SU2[1, g] = total.astype(BF16)
            start(su_z[1])

    up_totals = []

    def up_end():
        arrive(*su_z)
        for g in range(4):
            total = GU[slab_rows(g, s), :]
            for k in range(3):
                total = total + RU2[k, g].astype(F32)
            up_totals.append(total)
            g_up[g] = total
            SU3[g] = total.astype(BF16)
        start(*su_f)

    for g in range(4):
        for i in range(4):
            pair = jnp.concatenate([U[i, j, g].astype(F32) for j in range(2)], 0)
            WU[(g * 4 + i) * 48 : (g * 4 + i + 1) * 48, :] = pair.astype(BF16)
    WD = Dn.reshape(D, D)
    up_bias = gains[pl.ds(7 + f, 1), :]

    def slope_rows(c, t):
        return pl.ds(pl.multiple_of(c * 4 * tok + t * tok, tok), tok)

    def lift_block(t, carry):
        for at, action in ((1, lift_one), (2, lift_two), (3, lift_three)):
            pl.when(t == at)(action)
        rows = pl.ds(pl.multiple_of(t * tok, tok), tok)
        hat2, _ = normalise(X[t].astype(F32))
        low2 = (hat2 * gains[2:3, :] + gains[3:4, :]).astype(BF16)
        N2[rows, :] = low2
        for c in range(3):
            units = slice(c * 256, c * 256 + 256)
            lifted = dot_nn(low2, WU[:, units]) + up_bias[:, units]
            half = 0.5 + 0.5 * lax.erf(lifted * (0.5**0.5))
            act[rows, units] = (lifted * half).astype(BF16)
            bell = jnp.exp(lifted * lifted * -0.5) * (1.0 / math.sqrt(2.0 * math.pi))
            bias[slope_rows(c, t), :] = half + lifted * bell
        return carry

    lax.fori_loop(0, 4, lift_block, 0)
    arrive(c_c, c_xc)
    CF = C.reshape(4 * tok, D)
    for c in range(3):
        units = slice(c * 256, c * 256 + 256)
        GD[units, :] = dot_tn(act[:, units], CF[...])
    for k in (3, 2, 1, 0):
        SD1[zk[k]] = GD[pl.ds(pl.multiple_of((zk[k] * 2 + yo) * 96, 8), 96), :].astype(BF16)
        start(sd_y[k])
    arrive(d_yin)

    def back_one():
        scatter_y(GO, RO2b, SO3, o_sc)

    def back_two():
        down_step(3)

    def back_three():
        scatter_y(GQ, RQ2, SQ3, q_sc)

    def back_block(t, carry):
        for at, action in ((1, back_one), (2, back_two), (3, back_three)):
            pl.when(t == at)(action)
        two_gain, two_shift, up_sum = carry
        rows = pl.ds(pl.multiple_of(t * tok, tok), tok)
        back = C[t]
        sums = []
        for c in range(3):
            units = slice(c * 256, c * 256 + 256)
            low = (bias[slope_rows(c, t), :] * dot_nt(back, WD[units, :])).astype(BF16)
            dl[rows, units] = low
            sums.append(jnp.sum(low.astype(F32), 0, keepdims=True))
        OP[t] = dot_nn(act[rows, :], WD[...]).astype(BF16)
        grad2 = dot_nt(dl[rows, :], WU[...])
        NP[t] = grad2.astype(BF16)
        hat2, _ = normalise(X[t].astype(F32))
        return (
            two_gain + jnp.sum(grad2 * hat2, 0, keepdims=True),
            two_shift + jnp.sum(grad2, 0, keepdims=True),
            up_sum + jnp.concatenate(sums, 1),
        )

    zero_row = jnp.zeros((1, D), F32)
    two_gain, two_shift, up_sum = lax.fori_loop(0, 4, back_block, (zero_row,) * 3)
    vg[2:3, :] = two_gain
    vg[3:4, :] = two_shift
    vg[pl.ds(7 + f, 1), :] = up_sum
    start(*out_c, *nrm_c)
    down_step(2)
    for c in range(3):
        units = slice(c * 256, c * 256 + 256)
        GU[units, :] = dot_tn(N2[:, units], dl[...])
    for k in (3, 2, 1, 0):
        for g in range(4):
            SU1[zk[k], g] = GU[slab_rows(g, zk[k] * 2 + yo), :].astype(BF16)
        start(su_y[k])
    down_step(1)
    grad1 = dot_nt(q_low, WQ[...])
    arrive(rk1[0])
    kv_back = dkv[pl.ds(pl.multiple_of((2 * z + y) * tok, 8), tok), :] + RK1[z].astype(F32)
    arrive(rk2_in)
    for k in range(3):
        kv_back = kv_back + RK2[k].astype(F32)
    kv_low = turn_back(kv_back, key_cos, key_low, key_high).astype(BF16)
    grad1 = grad1 + dot_nt(kv_low, WKV[...])
    vg[0:1, :] = jnp.sum(grad1 * hat1[...], 0, keepdims=True)
    vg[1:2, :] = jnp.sum(grad1, 0, keepdims=True)
    kv_sum = jnp.sum(kv_low.astype(F32), 0, keepdims=True)
    short = jnp.zeros((1, 8), F32)
    spread = jnp.concatenate(
        [part for i in range(8) for part in (kv_sum[:, i * 16 : i * 16 + 16], short)], 1
    )
    vg[11:12, :] = jnp.concatenate([spread] * 4, 1)
    GP[...] = dot_tn(n1[...], kv_low)
    flipped = vg[...].T

    def packed(g):
        parts = [flipped[(g * 8 + i) * 24 : (g * 8 + i + 1) * 24, :16] for i in range(8)]
        return jnp.concatenate(parts, 1)

    for g in range(4):
        GV[g] = packed(g)
    for i in range(8):
        for j, g in enumerate((fc, fd)):
            SP1[j, i] = GP[slab_rows(g, i), :].astype(BF16)
    for j, g in enumerate((fc, fd)):
        SV1[j] = GV[g]
    start(p_c, v_c)
    down_relay()
    down_step(0)
    arrive(p_c, v_c)
    for i in range(8):
        SP2[i] = (GP[slab_rows(fx, i), :] + RP1[1, i].astype(F32)).astype(BF16)
    SV2[...] = GV[fx] + RV1[1]
    start(p_x, v_x)
    tokens_to_x()
    scatter_z(GO, RO2b, RO3, SO4, o_sc)
    arrive(p_x, v_x)

    def kv_sum_of(slab):
        return GP[slab_rows(f, slab), :] + RP1[0, slab].astype(F32) + RP2[slab].astype(F32)

    seq_slabs = [2 * zk[k] + y for k in (1, 2, 3)] + [2 * zk[k] + yo for k in range(4)]
    for i, slab in enumerate(seq_slabs):
        SP3[i] = kv_sum_of(slab).astype(BF16)
    SV3[...] = GV[f] + RV1[0] + RV2[...]
    start(*p_s, *v_s)
    up_step(3)
    scatter_z(GQ, RQ2, RQ3, SQ4, q_sc)
    up_step(2)
    up_step(1)
    up_relay()
    up_step(0)
    mixed_rows = mix_low.astype(F32).T.astype(BF16)
    arrive(out_x)
    bo[...] = (
        x[...].astype(F32)
        + (dot_nn(mixed_rows, WO[...]) + gains[5:6, :])
        + (OP[f].astype(F32) + RO1[0].astype(F32) + RO2[...].astype(F32) + gains[6:7, :])
    ).astype(BF16)
    save(bo, to_bo)
    arrive(nrm_x)
    grad2 = NP[f].astype(F32) + RN1[0].astype(F32) + RN2[...].astype(F32)
    hat_rows = hat1[...]
    scale_rows = scale1[:, 0:1]
    ig[...] = (
        cot[...].astype(F32)
        + norm_back(grad1, hat_rows, scale_rows, gains[0:1, :])
        + norm_back(grad2, hat_rows, scale_rows, gains[2:3, :])
    )
    save(ig, to_ig)
    copies.settle()
    q_grad = scatter_end(GQ, RQ2, RQ3, RQ4, q_sc)
    g_q[...] = q_grad
    save(g_q, to_q)
    o_grad = scatter_end(GO, RO2b, RO3, RO4, o_sc)
    g_o[...] = o_grad
    save(g_o, to_o)
    kv_grad = kv_sum_of(s)
    vec_sum = SV3[...]
    arrive(p_in, v_in)
    for i in range(7):
        kv_grad = kv_grad + RP3[i].astype(F32)
        vec_sum = vec_sum + RV3[i]
    vec_own = jnp.zeros((24, 16), F32)
    for i in range(8):
        vec_own = vec_own + jnp.where(s == i, vec_sum[:, i * 16 : i * 16 + 16], 0.0)
    vec_grad = jnp.concatenate([vec_own, jnp.zeros((24, 112), F32)], 1)
    g_kv[...] = kv_grad
    g_vec[...] = vec_grad
    save(g_kv, to_kv)
    save(g_vec, to_vec)
    rows = pl.ds(pl.multiple_of(s * 96, 8), 96)
    down_grad = GD[rows, :]
    for k in range(3):
        arrive(sd_z[k])
        down_grad = down_grad + RD2[k].astype(F32)
    g_dn[...] = down_grad
    save(g_dn, to_dn)
    def energy(values):
        return jnp.sum(jnp.sum(values * values, 0, keepdims=True), 1, keepdims=True)

    lanes = lax.broadcasted_iota(jnp.int32, (24, 128), 1)
    squares = energy(q_grad) + energy(o_grad) + energy(kv_grad) + energy(jnp.where(lanes == 11, 0.0, vec_grad)) + energy(g_dn[...])
    kv_rows = jnp.concatenate([vec_grad, jnp.zeros((104, 128), F32)], 0).T
    line = lax.broadcasted_iota(jnp.int32, (8, 128), 0)
    column = lax.broadcasted_iota(jnp.int32, (8, 128), 1)
    kv_line = jnp.where(column < 16, jnp.broadcast_to(kv_rows[11:12, :], (8, 128)), 0.0)
    up_end()
    save(g_up.at[f], to_up.at[f])

    for total in up_totals:
        squares = squares + energy(total)
    NS1[me] = jnp.where(line == 0, squares, kv_line)
    start(*n_all)
    arrive(su_fin)
    for i, g in enumerate((fc, fx, fd)):
        g_up[g] = RU3[i].astype(F32)
        save(g_up.at[g], to_up.at[g])
    arrive(n_in)
    everything = NS1[0]
    pieces = jnp.zeros((1, 128), F32)
    for i in range(8):
        kv_piece = NS1[i][1:2, :]
        pieces = pieces + kv_piece * kv_piece
    for i in range(1, 32):
        everything = everything + NS1[i]
    whole = everything[0:1, 0:1] + jnp.sum(pieces, 1, keepdims=True)
    kv_piece = NS1[s][1:2, :]
    g_small[...] = jnp.where(line == 0, whole, jnp.broadcast_to(kv_piece, (8, 128)))
    save(g_small, to_small)
    copies.settle()
    assert (copies.sends, copies.recvs) == N_SEMS, (copies.sends, copies.recvs)
    for copy in saved:
        copy.wait()


def update_kernel(
    small, g_q, g_o, g_kv, g_vec, g_up, g_dn, bo_in, ig_in,
    mq, mk, mo, mu, md, mv, mb,
    fq, fk, fo, fu, fdn, fv, fb,
    sq, sk, so, su, sd, sv, sb,
    bo, ig, norm,
    nmq, nmk, nmo, nmu, nmd, nmv, nmb,
    nfq, nfk, nfo, nfu, nfd, nfv, nfb,
    nsq, nsk, nso, nsu, nsd, nsv, nsb,
    residual,
):
    bo[...] = bo_in[...]
    ig[...] = ig_in[...]
    size = jnp.sqrt(small[0:1, 0:1])
    norm[...] = size
    factor = jnp.minimum(1.0, CLIP_NORM / (size + 1e-06))

    def update(grad, master, first, second, new_master, new_first, new_second, rate, decay):
        clipped = grad * factor
        values = adamw(master, clipped, first, second, rate, decay)
        for ref, value in zip((new_master, new_first, new_second), values):
            ref[...] = value

    rates = (MATRIX_RATE, MATRIX_DECAY)
    update(g_q[...], mq[...], fq[...], sq[...], nmq, nfq, nsq, *rates)
    update(g_o[...], mo[...], fo[...], so[...], nmo, nfo, nso, *rates)
    update(g_kv[...], mk[...], fk[...], sk[...], nmk, nfk, nsk, *rates)
    for g in range(4):
        cols = slice(g * D, (g + 1) * D)
        update(
            g_up[g], mu[:, cols], fu[:, cols], su[:, cols],
            nmu.at[:, cols], nfu.at[:, cols], nsu.at[:, cols], *rates,
        )
    update(g_dn[...], md[...], fdn[...], sd[...], nmd, nfd, nsd, *rates)
    flipped = jnp.concatenate([g_vec[...], jnp.zeros((104, 128), F32)], 0).T
    vector_grad = flipped[:11, :24]
    update(vector_grad, mv[...], fv[...], sv[...], nmv, nfv, nsv, VECTOR_RATE, 0.0)
    residual[...] = flipped[5:7, :24] * factor
    update(small[1:2, :16], mb[...], fb[...], sb[...], nmb, nfb, nsb, VECTOR_RATE, 0.0)


def fast_body(
    inputs, cotangent, span_order,
    query_weight, keyval_weight, output_weight, up_weight, down_weight, vectors, kv_bias,
    *moments,
):
    tok = inputs.shape[0]
    smem = pl.BlockSpec(memory_space=pltpu.SMEM)
    shape = jax.ShapeDtypeStruct
    V = pltpu.VMEM
    results_here = (
        shape((tok, D), BF16),
        shape((tok, D), F32),
        shape((24, D), F32),
        shape((24, D), F32),
        shape((24, 128), F32),
        shape((24, 128), F32),
        shape((4, 24, D), F32),
        shape((96, D), F32),
        shape((8, 128), F32),
    )
    operands_here = (
        inputs, cotangent, query_weight, keyval_weight, output_weight, up_weight, down_weight,
        vectors, kv_bias.reshape(1, -1),
    )
    scratch = [V(a.shape, a.dtype) for a in operands_here + results_here]
    scratch += [
        V((4, 4, 2, 24, 256), BF16),
        V((4, 4, 2, 24, D), BF16),
        V((4, 4, 2, 24, D), BF16),
        V((4, 2, 4, 24, D), BF16),
        V((4, 2, 96, D), BF16),
        V((4, tok, D), BF16),
        V((4, tok, D), BF16),
        V((4, 2, tok, 128), BF16),
        V((4, 24, D), BF16),
        V((D, D), BF16),
        V((D, 128), BF16),
        V((D, D), BF16),
        V((D, D), BF16),
        V((128, D), F32),
        V((128, 128), F32),
        V((tok, D), BF16),
        V((tok, D), F32),
        V((tok, 128), F32),
        V((4 * tok, D), BF16),
        V((4 * tok, D), BF16),
        V((4 * tok, D), BF16),
        V((4, tok, D), BF16),
        V((4, tok, D), BF16),
        V((HQ, tok, 128), BF16),
        V((HQ, tok, 128), BF16),
        V((HQ, HD, tok), BF16),
        V((128, 8 * tok), BF16),
        V((12 * tok, tok), F32),
        V((6 * D, 256), F32),
        V((HQ, HD, tok), BF16),
        V((HQ, HD, tok), F32),
        V((8 * tok, 128), F32),
        V((D, 128), F32),
        V((4, 24, 128), F32),
        V((D, D), F32),
        V((D, D), F32),
        V((128, D), F32),
        V((4, tok, 128), BF16), V((4, tok, 128), BF16),
        V((3, tok, 128), BF16), V((3, tok, 128), BF16),
        V((2, tok, D), BF16), V((tok, D), BF16), V((tok, D), BF16),
        V((2, tok, D), BF16), V((tok, D), BF16), V((tok, D), BF16),
    ]
    def scatter_buffers(width):
        found = []
        for lead in ((2, 8), (2, 4), (4,), (3,)):
            found += [V(lead + (24, width), BF16)] * 2
        return found

    scratch += scatter_buffers(D)
    scratch += scatter_buffers(D)
    for lead in ((2, 8), (8,), (7,)):
        scratch += [V(lead + (24, 128), BF16)] * 2
    scratch += [V((2, 24, 128), F32)] * 2 + [V((24, 128), F32)] * 3 + [V((7, 24, 128), F32)]
    scratch += [V((4, 4, 24, D), BF16)] * 2 + [V((3, 4, 24, D), BF16)] * 2
    scratch += [V((4, 24, D), BF16), V((3, 24, D), BF16), V((4, 24, D), BF16)]
    scratch += [V((4, 96, D), BF16)] * 2 + [V((3, 96, D), BF16)] * 2 + [V((96, D), BF16)]
    scratch += [V((32, 8, 128), F32)]
    scratch += [pltpu.SemaphoreType.DMA((n,)) for n in N_SEMS] + [pltpu.SemaphoreType.DMA((12,)), pltpu.SemaphoreType.DMA((9,))]
    kv_row = kv_bias.reshape(1, -1)
    bo, ig, g_q, g_o, g_kv, g_vec, g_up, g_dn, small = pl.pallas_call(
        layer_kernel,
        name="layer",
        out_shape=results_here,
        in_specs=[smem] + [pl.BlockSpec(memory_space=pl.ANY)] * 9,
        out_specs=(pl.BlockSpec(memory_space=pl.ANY),) * 9,
        scratch_shapes=scratch,
        compiler_params=pltpu.CompilerParams(
            collective_id=0, has_side_effects=True, vmem_limit_bytes=62 * 2**20
        ),
    )(
        span_order, inputs, cotangent,
        query_weight, keyval_weight, output_weight, up_weight, down_weight, vectors, kv_row,
    )
    masters = (query_weight, keyval_weight, output_weight, up_weight, down_weight, vectors, kv_row)
    firsts = tuple(moments[:6]) + (moments[6].reshape(1, -1),)
    seconds = tuple(moments[7:13]) + (moments[13].reshape(1, -1),)
    state = [shape(a.shape, F32) for a in masters]
    operands = (small, g_q, g_o, g_kv, g_vec, g_up, g_dn, bo, ig) + masters + firsts + seconds
    outcomes = [shape((tok, D), BF16), shape((tok, D), F32), shape((1, 1), F32)]
    outcomes += state * 3 + [shape((2, vectors.shape[1]), F32)]

    def whole(a):
        return pl.BlockSpec(a.shape, lambda i: (0,) * len(a.shape))

    results = pl.pallas_call(
        update_kernel,
        name="update",
        grid=(1,),
        out_shape=outcomes,
        in_specs=[whole(a) for a in operands],
        out_specs=[whole(a) for a in outcomes],
        compiler_params=pltpu.CompilerParams(vmem_limit_bytes=62 * 2**20),
    )(*operands)
    results = list(results)
    results[2] = results[2].reshape(())
    for i in (9, 16, 23):
        results[i] = results[i].reshape(-1)
    return tuple(results)


def solution(mesh):
    grid = (mesh.shape["fsdp"], mesh.shape["seq"])
    return jax.shard_map(
        fast_body if grid == (4, 8) else body,
        mesh=mesh,
        in_specs=(
            P(("fsdp", "seq"), None),
            P(("fsdp", "seq"), None),
            P("fsdp", None),
            P(("fsdp", "seq"), None),
            P(("fsdp", "seq"), None),
            P(("fsdp", "seq"), None),
            P(("fsdp", "seq"), None),
            P(("fsdp", "seq"), None),
            P(None, ("fsdp", "seq")),
            P("seq"),
            P(("fsdp", "seq"), None),
            P(("fsdp", "seq"), None),
            P(("fsdp", "seq"), None),
            P(("fsdp", "seq"), None),
            P(("fsdp", "seq"), None),
            P(None, ("fsdp", "seq")),
            P("seq"),
            P(("fsdp", "seq"), None),
            P(("fsdp", "seq"), None),
            P(("fsdp", "seq"), None),
            P(("fsdp", "seq"), None),
            P(("fsdp", "seq"), None),
            P(None, ("fsdp", "seq")),
            P("seq"),
        ),
        out_specs=(
            P(("fsdp", "seq"), None),
            P(("fsdp", "seq"), None),
            P(),
            P(("fsdp", "seq"), None),
            P(("fsdp", "seq"), None),
            P(("fsdp", "seq"), None),
            P(("fsdp", "seq"), None),
            P(("fsdp", "seq"), None),
            P(None, ("fsdp", "seq")),
            P("seq"),
            P(("fsdp", "seq"), None),
            P(("fsdp", "seq"), None),
            P(("fsdp", "seq"), None),
            P(("fsdp", "seq"), None),
            P(("fsdp", "seq"), None),
            P(None, ("fsdp", "seq")),
            P("seq"),
            P(("fsdp", "seq"), None),
            P(("fsdp", "seq"), None),
            P(("fsdp", "seq"), None),
            P(("fsdp", "seq"), None),
            P(("fsdp", "seq"), None),
            P(None, ("fsdp", "seq")),
            P("seq"),
            P(None, ("fsdp", "seq")),
        ),
        check_vma=False,
    )
```
